128 devices in a mesh: dp: 64 (over z, x, y_hi, core), tensor: 2 (over y_lo).
Axes of the slice: x: 4, y: 4 (y_hi: 2, y_lo: 2; y = y_hi * 2 + y_lo), z: 4, core: 2. Of those that a mesh axis runs over, the one named last changes fastest.
Arguments:
- tokens: bfloat16 [16384, 768], P(('dp', 'tensor')), may hold values from -6 to 6
- cotangent: bfloat16 [16384, 768], P(('dp', 'tensor')), may hold values from -6 to 6
- qkv_weight: float32 [3, 768, 2, 384], P(None, None, 'tensor', 'dp'), may hold values from -0.21875 to 0.21875
- out_weight: float32 [768, 2, 384], P(None, 'tensor', 'dp'), may hold values from -0.875 to 0.875
- fc_weight: float32 [2, 768, 2, 1536], P(None, None, 'tensor', 'dp'), may hold values from -0.21875 to 0.21875
- vectors: float32 [5376], replicated, may hold values from -2 to 2, as said below
- qkv_momentum: float32 [3, 768, 2, 384], P(None, None, 'tensor', 'dp'), may hold values from -2048 to 2048
- out_momentum: float32 [768, 2, 384], P(None, 'tensor', 'dp'), may hold values from -128 to 128
- fc_momentum: float32 [2, 768, 2, 1536], P(None, None, 'tensor', 'dp'), may hold values from -384 to 384
- vector_first: float32 [5376], replicated, may hold values from -256 to 256
- vector_second: float32 [5376], replicated, may hold values from 163 to 65536, as said below
Outputs:
- mixed: bfloat16 [16384, 768], P(('dp', 'tensor'))
- input_grad: float32 [16384, 768], P(('dp', 'tensor'))
- qkv_new: float32 [3, 768, 2, 384], P(None, None, 'tensor', 'dp')
- out_new: float32 [768, 2, 384], P(None, 'tensor', 'dp')
- fc_new: float32 [2, 768, 2, 1536], P(None, None, 'tensor', 'dp')
- qkv_moment: float32 [3, 768, 2, 384], P(None, None, 'tensor', 'dp')
- out_moment: float32 [768, 2, 384], P(None, 'tensor', 'dp')
- fc_moment: float32 [2, 768, 2, 1536], P(None, None, 'tensor', 'dp')
- vector_first_new: float32 [5376], replicated
- vector_second_new: float32 [5376], replicated
- vector_new: float32 [5376], replicated
The draws below stay inside these ranges and needn't reach their ends.
Inputs may be any that keep to these rules, and one draw needn't show every extreme that they name: `vectors`: entries are gains near 1 for the first 768, then shifts and biases of both signs. `vector_second`: every entry is positive.
All inputs are finite; a program needn't handle non-finite values.
Results may differ from the reference program's by a relative error of at most 0.011.
The reference program's roundings to bfloat16 on the way count: a program that leaves them out, or rounds other values in their place, can miss the bound.
Values may be sent and summed in bfloat16 or wider, within the bound.
No kernel may reach another device: no remote copies, remote signals or barrier semaphores. Data moves between devices by JAX's collectives and lax.ppermute only.
A program may use at most 192 MiB of HBM per device.

```python
import math
import jax
import jax.numpy as jnp
from jax import lax

D = 768
H = 12
HD = 64
ROT = 16
FF = 3072
LEN = 256
SWEEPS = 5
STEP = 10
SPLIT = 2
TOKENS = 16384
VEC = 5376
N_DP = 64


def segment_scales():
    root = math.sqrt(TOKENS)
    parts_list = [jnp.full((D,), 4.0), jnp.full((D,), 4.0), jnp.full((FF,), 0.5), jnp.full((D,), 1.0)]
    return jnp.concatenate(parts_list).astype(jnp.float32) * root


def draw_vectors(key, part):
    key = jax.random.fold_in(key, 1)
    sample = jnp.clip(jax.random.normal(key, (VEC,), jnp.float32), -4.0, 4.0)
    spread = jnp.concatenate([jnp.full((D,), 0.1), jnp.full((D,), 0.2), jnp.full((FF + D,), 0.3)]).astype(jnp.float32)
    centre = jnp.concatenate([jnp.ones((D,)), jnp.zeros((2 * D + FF,))]).astype(jnp.float32)
    return centre + spread * sample


def draw_qkv_momentum(key, part):
    key = jax.random.fold_in(key, 2)
    shape = (3, D, SPLIT, D // SPLIT)
    sample = jnp.clip(jax.random.normal(key, shape, jnp.float32), -4.0, 4.0)
    scales = jnp.array([0.4, 0.4, 4.0], jnp.float32)[:, None, None, None] * math.sqrt(TOKENS)
    return sample * scales


def draw_out_momentum(key, part):
    key = jax.random.fold_in(key, 3)
    shape = (D, SPLIT, D // SPLIT)
    sample = jnp.clip(jax.random.normal(key, shape, jnp.float32), -4.0, 4.0)
    return sample * (0.2 * math.sqrt(TOKENS))


def draw_fc_momentum(key, part):
    key = jax.random.fold_in(key, 4)
    shape = (2, D, SPLIT, FF // SPLIT)
    sample = jnp.clip(jax.random.normal(key, shape, jnp.float32), -4.0, 4.0)
    scales = jnp.array([0.5, 0.6], jnp.float32)[:, None, None, None] * math.sqrt(TOKENS)
    return sample * scales


def draw_vector_first(key, part):
    key = jax.random.fold_in(key, 5)
    sample = jnp.clip(jax.random.normal(key, (VEC,), jnp.float32), -4.0, 4.0)
    return sample * (0.11 * segment_scales())


def draw_vector_second(key, part):
    key = jax.random.fold_in(key, 6)
    factor = jnp.exp(jax.random.uniform(key, (VEC,), jnp.float32, 0.0, math.log(4.0)))
    scales = segment_scales()
    return factor * (0.0526 * scales * scales)


def shard_levels(key, shape, cuts, smallest, high):
    def one(axis_at, parts):
        steps = jax.random.uniform(jax.random.fold_in(jax.random.fold_in(key, 6), axis_at), (parts,), jnp.float32, smallest / len(cuts), high / len(cuts))
        return jnp.repeat(jnp.exp(steps), shape[axis_at] // parts).reshape((-1,) + (1,) * (len(shape) - axis_at - 1))

    level = one(*cuts[0])
    for cut in cuts[1:]:
        level = level * one(*cut)
    return level


def noise(stream_key, shape, scale, bound, pieces=(), kind=jnp.bfloat16):
    entries = jax.random.normal(stream_key, shape, jnp.float32) * scale
    if len(pieces) > 0:
        entries = shard_levels(stream_key, shape, pieces, -0.22, 0.18) * entries
    return jnp.clip(entries, min=-bound, max=bound).astype(kind)


def setup_inputs(seed: int = 0) -> dict:
    arg_keys = jax.random.split(jax.random.key(seed), 12)
    tokens = noise(arg_keys[0], (TOKENS, D), 1.0, 6.0, ((0, 128),))
    cotangent = noise(arg_keys[1], (TOKENS, D), 1.0, 6.0, ((0, 128),))
    qkv_weight = noise(arg_keys[2], (3, D, SPLIT, D // SPLIT), D ** -0.5, 0.21875, ((2, 2), (3, 64)), jnp.float32)
    out_weight = noise(arg_keys[3], (D, SPLIT, D // SPLIT), (16 * D // LEN) ** -0.5, 0.875, ((1, 2), (2, 64)), jnp.float32)
    fc_weight = noise(arg_keys[4], (2, D, SPLIT, FF // SPLIT), D ** -0.5, 0.21875, ((2, 2), (3, 64)), jnp.float32)
    vectors = draw_vectors(jax.random.fold_in(arg_keys[11], 71), 0)
    qkv_momentum = draw_qkv_momentum(jax.random.fold_in(arg_keys[11], 71), 0)
    out_momentum = draw_out_momentum(jax.random.fold_in(arg_keys[11], 71), 0)
    fc_momentum = draw_fc_momentum(jax.random.fold_in(arg_keys[11], 71), 0)
    vector_first = draw_vector_first(jax.random.fold_in(arg_keys[11], 71), 0)
    vector_second = draw_vector_second(jax.random.fold_in(arg_keys[11], 71), 0)
    return dict(tokens=tokens, cotangent=cotangent, qkv_weight=qkv_weight, out_weight=out_weight, fc_weight=fc_weight, vectors=vectors, qkv_momentum=qkv_momentum, out_momentum=out_momentum, fc_momentum=fc_momentum, vector_first=vector_first, vector_second=vector_second)


@jax.custom_vjp
def low(v):
    return lax.optimization_barrier(v.astype(jnp.bfloat16)).astype(jnp.float32)

@jax.custom_vjp
def low_back(v):
    return v

def low_keep(v):
    return (low(v), None)

def low_pass(kept, grad):
    return (grad,)

def back_keep(v):
    return (v, None)

def back_low(kept, grad):
    return (low(grad),)
low.defvjp(low_keep, low_pass)
low_back.defvjp(back_keep, back_low)
highest_value = lax.Precision.HIGHEST
ns_first = 3.4445
ns_second = -4.775
ns_third = 2.0315

def tables():
    position = jnp.arange(LEN, dtype=jnp.float32)
    frequency = 10000.0 ** (-2.0 * jnp.arange(ROT // 2, dtype=jnp.float32) / ROT)
    angles = position[:, None] * frequency[None, :]
    return (jnp.cos(angles)[:, None, :], jnp.sin(angles)[:, None, :])

def rotate(values, cos_table, sin_table):
    half_rot = ROT // 2
    leading = values[..., :half_rot]
    trailing = values[..., half_rot:ROT]
    return jnp.concatenate([leading * cos_table - trailing * sin_table, trailing * cos_table + leading * sin_table, values[..., ROT:]], axis=-1)

def block(inputs, params):
    gain, shift, input_bias, bias_out, w_qkv, w_out, w_fc = params
    average = lax.optimization_barrier(jnp.mean(inputs, axis=-1, keepdims=True))
    deviation = inputs - average
    variance = lax.optimization_barrier(jnp.mean(deviation * deviation, axis=-1, keepdims=True))
    centred = deviation * lax.rsqrt(variance + 1e-05)
    normed_input = low(centred * gain + shift)
    reduced_qkv_weight = low(w_qkv)
    reduced_out_weight = low(w_out)
    reduced_fc_weight = low(w_fc)
    seq_count = inputs.shape[0]
    head_shape = (seq_count, LEN, H, HD)
    cos_table, sin_table = tables()
    projected_output = jnp.einsum('nvc,ocu->onvu', normed_input, reduced_qkv_weight, precision=highest_value)
    query = low(rotate(low_back(projected_output[0]).reshape(head_shape), cos_table, sin_table))
    keyed = low(rotate(low_back(projected_output[1]).reshape(head_shape), cos_table, sin_table))
    value = low(low_back(projected_output[2])).reshape(head_shape)
    scores = low_back(jnp.einsum('sqhd,skhd->shqk', query, keyed, precision=highest_value) * HD ** (-0.5))
    causal = jnp.arange(LEN)[:, None] >= jnp.arange(LEN)[None, :]
    scores = jnp.where(causal, scores, -1e+30)
    chance = low(jax.nn.softmax(scores, axis=-1))
    attention_output = jnp.einsum('shqk,skhd->sqhd', chance, value, precision=highest_value).reshape(seq_count, LEN, D)
    attention_output = low(low_back(attention_output))
    hidden_before_act = low_back(jnp.einsum('xou,ue->xoe', normed_input, reduced_fc_weight[0], precision=highest_value) + input_bias)
    hidden_state = low(jax.nn.gelu(hidden_before_act, approximate=True))
    branch_output = jnp.einsum('wnb,jb->wnj', attention_output, reduced_out_weight, precision=highest_value)
    branch_output = branch_output + jnp.einsum('owy,gy->owg', hidden_state, reduced_fc_weight[1], precision=highest_value)
    return inputs + branch_output + bias_out

def orthogonal(update):
    norm_value = jnp.sqrt(jnp.sum(update * update))
    matrix = update / (norm_value + 1e-07)
    for sweep_index in range(SWEEPS):
        gram = jnp.dot(matrix, matrix.T, precision=highest_value)
        applied = jnp.dot(gram, matrix, precision=highest_value)
        matrix = ns_first * matrix + ns_second * applied + ns_third * jnp.dot(gram, applied, precision=highest_value)
    return matrix

def muon(weight, gradient, momentum, factor):
    moment = 0.95 * momentum + gradient
    update = gradient + 0.95 * moment
    return (weight * 0.99 - factor * orthogonal(update), moment)

def reference(tokens, cotangent, qkv_weight, out_weight, fc_weight, vectors, qkv_momentum, out_momentum, fc_momentum, vector_first, vector_second):
    w_qkv = qkv_weight.reshape(3, D, D)
    w_out = out_weight.reshape(D, D)
    w_fc = fc_weight.reshape(2, D, FF)
    gain = vectors[:D]
    shift = vectors[D:2 * D]
    input_bias = vectors[2 * D:2 * D + FF]
    bias_out = vectors[2 * D + FF:]
    params = (gain, shift, input_bias, bias_out, w_qkv, w_out, w_fc)
    group = math.gcd(N_DP, max(1, 4096 // LEN))
    inputs = tokens.astype(jnp.float32).reshape(N_DP // group, group, LEN, D)
    cot = cotangent.astype(jnp.float32).reshape(N_DP // group, group, LEN, D)
    zeros = jax.tree.map(jnp.zeros_like, params)

    def one_group(running, rows_pair):
        rows_in, rows_cot = rows_pair
        result, pullback = jax.vjp(block, rows_in, params)
        grad_rows, grad_params = pullback(rows_cot)
        return (jax.tree.map(jnp.add, running, grad_params), (result.astype(jnp.bfloat16), grad_rows))
    grads, (mixed, input_grad) = lax.scan(one_group, zeros, (inputs, cot))
    mixed = mixed.reshape(TOKENS, D)
    input_grad = input_grad.reshape(TOKENS, D)
    grad_gain, grad_shift, grad_bias_in, grad_bias_out, grad_qkv, grad_out, grad_fc = grads
    vector_grad = jnp.concatenate([grad_gain, grad_shift, grad_bias_in, grad_bias_out])
    first_new = 0.9 * vector_first + 0.1 * vector_grad
    second_new = 0.95 * vector_second + 0.05 * vector_grad * vector_grad
    step_size = first_new / (1.0 - 0.9 ** STEP) / (jnp.sqrt(second_new / (1.0 - 0.95 ** STEP)) + 1e-08)
    vector_new = vectors - 0.2 * step_size
    mom_qkv = qkv_momentum.reshape(3, D, D)
    mom_fc = fc_momentum.reshape(2, D, FF)
    qkv_pairs = [muon(w_qkv[index], grad_qkv[index], mom_qkv[index], 1.0) for index in range(3)]
    out_updated, out_moment = muon(w_out, grad_out, out_momentum.reshape(D, D), 1.0)
    fc_factor = math.sqrt(FF / D)
    fc_pairs = [muon(w_fc[index], grad_fc[index], mom_fc[index], fc_factor) for index in range(2)]
    qkv_new = jnp.stack([entry[0] for entry in qkv_pairs]).reshape(3, D, SPLIT, D // SPLIT)
    qkv_moment = jnp.stack([entry[1] for entry in qkv_pairs]).reshape(3, D, SPLIT, D // SPLIT)
    fc_new = jnp.stack([entry[0] for entry in fc_pairs]).reshape(2, D, SPLIT, FF // SPLIT)
    fc_moment = jnp.stack([entry[1] for entry in fc_pairs]).reshape(2, D, SPLIT, FF // SPLIT)
    out_new = out_updated.reshape(D, SPLIT, D // SPLIT)
    out_moment = out_moment.reshape(D, SPLIT, D // SPLIT)
    return (mixed, input_grad, qkv_new, out_new, fc_new, qkv_moment, out_moment, fc_moment, first_new, second_new, vector_new)
```

```python
import math

import jax
import jax.numpy as jnp
from jax import lax
from jax.sharding import Mesh, PartitionSpec as P

D = 768
H = 12
HD = 64
ROT = 16
FF = 3072
SWEEPS = 5
STEP = 10
LEN = 256

NS = (3.4445, -4.775, 2.0315)
BF = jnp.bfloat16
F32 = jnp.float32
HIGH = lax.Precision.HIGH
HIGHEST = lax.Precision.HIGHEST

DP = ("z", "x", "yh", "c")
ALL = ("z", "x", "yh", "c", "t")


def pull(value, axis, k):
    n = lax.axis_size(axis)
    return lax.ppermute(value, axis, [((i + k) % n, i) for i in range(n)])


def gather_ring(value, axis):
    n = lax.axis_size(axis)
    return jnp.stack([value] + [pull(value, axis, k) for k in range(1, n)])


def sum_ring(parts, axis):
    n = lax.axis_size(axis)
    total = parts[0].astype(F32)
    for k in range(1, n):
        total = total + pull(parts[k].astype(BF), axis, n - k).astype(F32)
    return total


def dot(a, b, dims, precision=None):
    return lax.dot_general(a, b, ((dims[0], dims[1]), ((), ())), precision=precision, preferred_element_type=F32)


def gelu_parts(u):
    k0 = math.sqrt(2.0 / math.pi)
    th = jnp.tanh(k0 * (u + 0.044715 * (u * u * u)))
    value = 0.5 * u * (1.0 + th)
    slope = 0.5 * (1.0 + th) + 0.5 * u * (1.0 - th * th) * (k0 * (1.0 + 3.0 * 0.044715 * u * u))
    return value, slope


def body(tokens, cotangent, qkv_weight, out_weight, fc_weight, vectors, qkv_momentum, out_momentum, fc_momentum, vector_first, vector_second):
    zi, xi, yi, ci, ti = (lax.axis_index(a) for a in ALL)
    rows = tokens.shape[0]
    n_att = qkv_weight.shape[3]
    n_fc = fc_weight.shape[3]
    gain, shift = vectors[:D], vectors[D : 2 * D]
    bias_in, bias_out = vectors[2 * D : 2 * D + FF], vectors[2 * D + FF :]

    attn_rows = jnp.concatenate([jnp.transpose(qkv_weight[:, :, 0, :], (0, 2, 1)), jnp.transpose(out_weight[:, 0, :])[None]])
    fc_rows = jnp.transpose(fc_weight[:, :, 0, :], (0, 2, 1))
    own_rows = jnp.concatenate([attn_rows.reshape(4 * n_att, D), fc_rows.reshape(2 * n_fc, D)]).astype(BF)
    held = gather_ring(own_rows, "yh")
    held = gather_ring(held, "z")
    held = gather_ring(held, "x")
    held = held.reshape(32, 4 * n_att + 2 * n_fc, D)
    w_in = held[:, 4 * n_att : 4 * n_att + n_fc].reshape(32 * n_fc, D)
    w_back = held[:, 4 * n_att + n_fc :].reshape(32 * n_fc, D)
    att_mine = held[:, : 4 * n_att].reshape(32 * 4 * n_att, D)
    att_both = jnp.concatenate([att_mine, pull(att_mine, "c", 1)])
    r = jnp.arange(2 * 32 * 4 * n_att)
    lane = r % n_att
    mat = (r // n_att) % 4
    ry = (r // (4 * n_att)) % 2
    rz = (r // (8 * n_att)) % 4
    rx = (r // (32 * n_att)) % 4
    rc = r // (128 * n_att)
    column = (((((zi + rz) % 4) * 4 + (xi + rx) % 4) * 2 + (yi + ry) % 2) * 2 + (ci + rc) % 2) * n_att + lane
    place = jnp.where(column // 192 == ci, mat * 192 + column % 192, -1)
    pick = (jnp.arange(768)[:, None] == place[None, :]).astype(BF)
    w_att = dot(pick, att_both, ((1,), (0,))).astype(BF)
    w_qkv, w_out = w_att[:576], w_att[576:]

    inputs = tokens.astype(F32)
    average = jnp.mean(inputs, axis=-1, keepdims=True)
    deviation = inputs - average
    variance = jnp.mean(deviation * deviation, axis=-1, keepdims=True)
    inv_spread = lax.rsqrt(variance + 1e-05)
    centred = deviation * inv_spread
    normed_own = (centred * gain + shift).astype(BF)
    both = jnp.stack([normed_own, cotangent])
    both = jnp.stack([both, pull(both, "t", 1)], axis=1)
    both = jnp.stack([both, pull(both, "c", 1)], axis=1)
    n_all = 4 * rows
    normed, cot = both[0].reshape(n_all, D), both[1].reshape(n_all, D)

    half = jnp.arange(LEN) // rows
    position = ((ti + half) % 2) * rows + jnp.arange(LEN) % rows
    frequency = 10000.0 ** (-2.0 * jnp.arange(ROT // 2, dtype=F32) / ROT)
    angles = position.astype(F32)[:, None] * frequency[None, :]
    cos_t, sin_t = jnp.cos(angles), jnp.sin(angles)
    ones, zeros = jnp.ones((LEN, HD - ROT), F32), jnp.zeros((LEN, HD - ROT), F32)
    cos_full = jnp.concatenate([cos_t, cos_t, ones], axis=1)[None, :, None, :]
    sin_full = jnp.concatenate([-sin_t, sin_t, zeros], axis=1)[None, :, None, :]

    def swap(v):
        return jnp.concatenate([v[..., ROT // 2 : ROT], v[..., : ROT // 2], v[..., ROT:]], axis=-1)

    def rotate(v):
        return v * cos_full + swap(v) * sin_full

    def unrotate(v):
        return v * cos_full - swap(v) * sin_full

    projected = dot(normed, w_qkv, ((1,), (1,)))
    shape = (2, LEN, 3, HD)
    query = rotate(projected[:, :192].reshape(shape)).astype(BF)
    keyed = rotate(projected[:, 192:384].reshape(shape)).astype(BF)
    value = projected[:, 384:].reshape(shape).astype(BF)
    causal = position[:, None] >= position[None, :]
    scale = HD ** (-0.5)
    scores = jnp.einsum("sqhd,skhd->shqk", query, keyed, preferred_element_type=F32) * scale
    scores = jnp.where(causal, scores, -1e30)
    raised = jnp.exp(scores - jnp.max(scores, axis=-1, keepdims=True))
    chance = raised / jnp.sum(raised, axis=-1, keepdims=True)
    chance_low = chance.astype(BF)
    attended = jnp.einsum("shqk,skhd->sqhd", chance_low, value, preferred_element_type=F32).reshape(n_all, 192).astype(BF)

    bias6 = bias_in.reshape(2, 4, 4, 2, 2, n_fc)
    bias6 = jnp.concatenate([bias6, bias6], axis=1)
    bias6 = jnp.concatenate([bias6, bias6], axis=2)
    bias6 = jnp.concatenate([bias6, bias6], axis=3)
    bias_own = lax.dynamic_slice(bias6, (ti, zi, xi, yi, ci, 0), (1, 4, 4, 2, 1, n_fc))[0, :, :, :, 0]
    bias_own = jnp.transpose(bias_own, (1, 0, 2, 3)).reshape(32 * n_fc)
    hidden_pre = dot(normed, w_in, ((1,), (1,))) + bias_own
    hidden_f, slope = gelu_parts(hidden_pre)
    hidden = hidden_f.astype(BF)

    branch = dot(attended, w_out, ((1,), (0,))) + dot(hidden, w_back, ((1,), (0,)))

    def own_rows_of(v):
        v = v.reshape(2, 2, rows, D)
        v = v[0] + pull(v[1], "c", 1)
        return v[0] + pull(v[1].astype(BF), "t", 1).astype(F32)

    mixed = (inputs + own_rows_of(branch) + bias_out).astype(BF)

    grad_out = dot(attended, cot, ((0,), (0,)))
    grad_back = dot(hidden, cot, ((0,), (0,)))
    d_attended = dot(cot, w_out, ((1,), (1,))).astype(BF).reshape(shape)
    d_pre = (dot(cot, w_back, ((1,), (1,))) * slope).astype(BF)
    d_value = jnp.einsum("shqk,sqhd->skhd", chance_low, d_attended, preferred_element_type=F32).astype(BF)
    d_chance = jnp.einsum("sqhd,skhd->shqk", d_attended, value, preferred_element_type=F32)
    d_scores = (chance * (d_chance - jnp.sum(chance * d_chance, axis=-1, keepdims=True))).astype(BF)
    d_query = unrotate(jnp.einsum("shqk,skhd->sqhd", d_scores, keyed, preferred_element_type=F32) * scale).astype(BF)
    d_key = unrotate(jnp.einsum("shqk,sqhd->skhd", d_scores, query, preferred_element_type=F32) * scale).astype(BF)
    d_proj = jnp.concatenate([v.reshape(n_all, 192) for v in (d_query, d_key, d_value)], axis=1)
    grad_qkv = dot(d_proj, normed, ((0,), (0,)))
    grad_in = dot(d_pre, normed, ((0,), (0,)))
    grad_bias_in = jnp.sum(d_pre.astype(F32), axis=0)
    d_normed = dot(d_proj, w_qkv, ((1,), (0,))) + dot(d_pre, w_in, ((1,), (0,)))
    d_rows = own_rows_of(d_normed)
    d_hat = d_rows * gain
    correction = d_hat - jnp.mean(d_hat, axis=-1, keepdims=True) - centred * jnp.mean(d_hat * centred, axis=-1, keepdims=True)
    own_cot = cotangent.astype(F32)
    input_grad = own_cot + correction * inv_spread

    spread = jnp.zeros((2, 8, 8, 4, 2, n_fc), F32)
    bias_grad = jnp.transpose(grad_bias_in.reshape(4, 4, 2, n_fc), (1, 0, 2, 3))[None, :, :, :, None]
    spread = lax.dynamic_update_slice(spread, bias_grad, (ti, zi, xi, yi, ci, 0))
    spread = spread.reshape(2, 2, 4, 2, 4, 2, 2, 2, n_fc).sum(axis=(1, 3, 5))
    vector_part = jnp.concatenate([jnp.sum(d_rows * centred, axis=0), jnp.sum(d_rows, axis=0), spread.reshape(FF), jnp.sum(own_cot, axis=0)])
    vector_grad = lax.psum(vector_part, ALL)
    first_new = 0.9 * vector_first + 0.1 * vector_grad
    second_new = 0.95 * vector_second + 0.05 * vector_grad * vector_grad
    step_size = first_new / (1.0 - 0.9**STEP) / (jnp.sqrt(second_new / (1.0 - 0.95**STEP)) + 1e-08)
    vector_new = vectors - 0.2 * step_size

    grad_att = jnp.concatenate([grad_qkv, grad_out]).astype(BF)
    att_home = dot(pick, grad_att, ((0,), (0,))).astype(BF)
    n_half = 32 * 4 * n_att
    att_rel = att_home[:n_half] + pull(att_home[n_half:], "c", 1)
    parts = jnp.concatenate(
        [
            att_rel.reshape(32, 4 * n_att, D),
            grad_in.astype(BF).reshape(32, n_fc, D),
            grad_back.astype(BF).reshape(32, n_fc, D),
        ],
        axis=1,
    )
    width = 4 * n_att + 2 * n_fc
    total = sum_ring(parts.reshape(4, 8, width, D), "x")
    total = sum_ring(total.reshape(4, 2, width, D), "z")
    total = sum_ring(total, "yh")

    mom_rows = jnp.concatenate(
        [
            jnp.transpose(qkv_momentum[:, :, 0, :], (0, 2, 1)).reshape(3 * n_att, D),
            jnp.transpose(out_momentum[:, 0, :]),
            jnp.transpose(fc_momentum[:, :, 0, :], (0, 2, 1)).reshape(2 * n_fc, D),
        ]
    )
    moment = 0.95 * mom_rows + total
    update = total + 0.95 * moment

    half_fc = n_fc // 2
    att_u = update[: 4 * n_att].reshape(4, n_att, D)
    att_u = jnp.concatenate([att_u, jnp.zeros((4, half_fc - n_att, D), F32)], axis=1)
    fc_u = update[4 * n_att :].reshape(4, half_fc, D)
    chunks = jnp.concatenate([att_u, fc_u]).reshape(8 * half_fc, D)
    mine = lax.all_to_all(chunks, ("z", "t"), split_axis=0, concat_axis=0, tiled=True)
    wide = gather_ring(mine, "yh").reshape(2 * 8 * half_fc, D)
    wide = gather_ring(wide, "x").reshape(8 * 8 * half_fc, D)
    gram = dot(wide, wide, ((0,), (0,)), HIGHEST)
    top, bottom = gram[: D // 2], gram[D // 2 :]
    keep = jnp.where(ci == 0, top, bottom)
    give = jnp.where(ci == 0, bottom, top)
    part = keep + pull(give, "c", 1)
    other = pull(part, "t", 1)
    part = jnp.where(zi >= 2, part + other, part)
    rest = pull(part, "c", 1)
    gram = jnp.where(ci == 0, jnp.concatenate([part, rest]), jnp.concatenate([rest, part]))
    factor = 1.0 / (jnp.sqrt(jnp.trace(gram)) + 1e-07)
    gram = gram * (factor * factor)
    x_rows = mine * factor
    eye = jnp.eye(D, dtype=F32)
    for sweep in range(SWEEPS):
        precision = HIGHEST if sweep == 0 else HIGH
        square = dot(gram, gram, ((1,), (0,)), precision)
        poly = NS[0] * eye + NS[1] * gram + NS[2] * square
        x_rows = dot(x_rows, poly, ((1,), (0,)), HIGHEST)
        if sweep + 1 < SWEEPS:
            gram = dot(dot(gram, poly, ((1,), (0,)), precision), poly, ((1,), (0,)), precision)
    back = lax.all_to_all(x_rows, ("z", "t"), split_axis=0, concat_axis=0, tiled=True).reshape(8, half_fc, D)
    att_x = back[:4, :n_att]
    fc_x = back[4:].reshape(2, n_fc, D)

    def cols(v):
        return jnp.transpose(v, (0, 2, 1))[:, :, None, :]

    fc_factor = math.sqrt(FF / D)
    qkv_new = qkv_weight * 0.99 - cols(att_x[:3])
    out_new = out_weight * 0.99 - cols(att_x[3:])[0]
    fc_new = fc_weight * 0.99 - fc_factor * cols(fc_x)
    att_m = moment[: 4 * n_att].reshape(4, n_att, D)
    fc_m = moment[4 * n_att :].reshape(2, n_fc, D)
    return (mixed, input_grad, qkv_new, out_new, fc_new, cols(att_m[:3]), cols(att_m[3:])[0], cols(fc_m), first_new, second_new, vector_new)


def solution(mesh):
    mesh = Mesh(mesh.devices.reshape(4, 4, 2, 2, 2), ALL)
    rows = P(ALL, None)
    w3 = P(None, None, "t", DP)
    w2 = P(None, "t", DP)
    vec = P()
    in_specs = (rows, rows, w3, w2, w3, vec, w3, w2, w3, vec, vec)
    out_specs = (rows, rows, w3, w2, w3, w3, w2, w3, vec, vec, vec)
    return jax.shard_map(body, mesh=mesh, in_specs=in_specs, out_specs=out_specs, check_vma=False)
```

```python
import math

import jax
import jax.numpy as jnp
from jax import lax
from jax.experimental import pallas as pl
from jax.experimental.pallas import tpu as pltpu
from jax.sharding import Mesh, PartitionSpec as P

D = 768
H = 12
HD = 64
ROT = 16
FF = 3072
SWEEPS = 5
STEP = 10
LEN = 256
VEC = 2 * D + FF + D
VEC_ROWS = 12

NS = (3.4445, -4.775, 2.0315)
BF = jnp.bfloat16
F32 = jnp.float32
BLK = 256
NB = D // BLK

DP = ("z", "x", "yh", "c")
ALL = ("z", "x", "yh", "c", "t")


def pull(value, axis, k):
    n = lax.axis_size(axis)
    return lax.ppermute(value, axis, [((i + k) % n, i) for i in range(n)])


def gather_ring(value, axis, dim=0):
    n = lax.axis_size(axis)
    return jnp.stack([value] + [pull(value, axis, k) for k in range(1, n)], axis=dim)


def sum_ring(parts, axis, dim=0):
    n = lax.axis_size(axis)
    entry = lambda k: lax.index_in_dim(parts, k, dim, keepdims=False)
    total = entry(0).astype(F32)
    for k in range(1, n):
        total = total + pull(entry(k).astype(BF), axis, n - k).astype(F32)
    return total


def dot(a, b, dims):
    return lax.dot_general(a, b, (dims, ((), ())), preferred_element_type=F32)


def pieces(value, n):
    out = []
    for _ in range(n):
        low = value.astype(BF)
        out.append(low)
        value = value - low.astype(F32)
    return out


def mul(xs, ys, dims=((1,), (0,))):
    n = len(xs)
    total = None
    for order in reversed(range(n)):
        for i in range(order + 1):
            term = lax.dot_general(xs[i], ys[order - i], (dims, ((), ())), preferred_element_type=F32)
            total = term if total is None else total + term
    return total


def gram_kernel(core_ref, wide_ref, keep_ref, give_ref):
    xs = pieces(wide_ref[...], 3)
    dims = ((0,), (0,))
    cut = lambda i: slice(i * BLK, (i + 1) * BLK)
    top = mul([x[:, cut(0)] for x in xs], xs, dims)
    mid = mul([x[:, cut(1)] for x in xs], [x[:, BLK:] for x in xs], dims)
    low = mul([x[:, cut(2)] for x in xs], [x[:, 2 * BLK :] for x in xs], dims)
    first = core_ref[0] == 0

    @pl.when(first)
    def _():
        keep_ref[...] = top
        give_ref[:, : 2 * BLK] = mid
        give_ref[:, 2 * BLK :] = low

    @pl.when(jnp.logical_not(first))
    def _():
        give_ref[...] = top
        keep_ref[:, : 2 * BLK] = mid
        keep_ref[:, 2 * BLK :] = low


def blocks(i, j):
    return (slice(i * BLK, (i + 1) * BLK), slice(j * BLK, (j + 1) * BLK))


def put(refs, i, j, value):
    for ref, piece in zip(refs, pieces(value, len(refs))):
        ref[blocks(i, j)] = piece


def put_both(refs, i, j, value):
    put(refs, i, j, value)
    if i != j:
        put(refs, j, i, value.T)


def symmetric_product(xs, ys, emit):
    for i in range(NB):
        rows = slice(i * BLK, (i + 1) * BLK)
        wide = mul([x[rows, :] for x in xs], [y[:, i * BLK :] for y in ys])
        for j in range(i, NB):
            emit(i, j, wide[:, (j - i) * BLK : (j - i + 1) * BLK])


def sweeps_kernel(core_ref, mine_ref, rest_ref, x_ref, out_ref, top_ref, bottom_ref, gram_ref, a_ref, p_ref, b_ref):
    first = core_ref[0] == 0

    @pl.when(first)
    def _():
        top_ref[...] = mine_ref[...]
        bottom_ref[...] = rest_ref[...]

    @pl.when(jnp.logical_not(first))
    def _():
        top_ref[...] = rest_ref[...]
        bottom_ref[...] = mine_ref[...]

    def packed(i, j):
        if i == 0:
            return top_ref[:, j * BLK : (j + 1) * BLK]
        at = (j - 1) if i == 1 else 2
        return bottom_ref[:, at * BLK : (at + 1) * BLK]

    eye = (lax.broadcasted_iota(jnp.int32, (BLK, BLK), 0) == lax.broadcasted_iota(jnp.int32, (BLK, BLK), 1)).astype(F32)
    trace = sum(jnp.sum(packed(i, i) * eye) for i in range(NB))
    norm = jnp.sqrt(jnp.full((8, 128), trace, F32)) + 1e-07
    factor = (1.0 / norm)[0:1, 0:1]
    square = factor * factor

    for i in range(NB):
        for j in range(i, NB):
            value = packed(i, j) * square
            gram_ref[blocks(i, j)] = value
            put_both([a_ref.at[k] for k in range(3)], i, j, value)
    out_ref[...] = x_ref[...] * factor

    def poly(n, n_p):
        a = [a_ref.at[k] for k in range(n)]

        def emit(i, j, block):
            value = NS[1] * gram_ref[blocks(i, j)] + NS[2] * block
            if i == j:
                value = value + NS[0] * eye
            put_both([p_ref.at[k] for k in range(n_p)], i, j, value)

        symmetric_product(a, a, emit)

    def apply():
        out_ref[...] = mul(pieces(out_ref[...], 2), [p_ref.at[k][...] for k in range(2)])

    def next_gram(n, keep):
        p = [p_ref.at[k] for k in range(n)]
        symmetric_product([a_ref.at[k] for k in range(n)], p, lambda i, j, block: put_both([b_ref.at[k] for k in range(n)], i, j, block))

        def emit(i, j, block):
            gram_ref[blocks(i, j)] = block
            put_both([a_ref.at[k] for k in range(keep)], i, j, block)

        symmetric_product([b_ref.at[k] for k in range(n)], p, emit)

    poly(3, 3)
    apply()
    next_gram(3, 2)

    @pl.loop(1, SWEEPS - 1)
    def _(_):
        poly(2, 2)
        apply()
        next_gram(2, 2)

    poly(2, 2)
    apply()


SMEM = pl.BlockSpec(memory_space=pltpu.SMEM)
VM = pl.BlockSpec(memory_space=pltpu.VMEM)


def gram_parts(core, wide):
    return pl.pallas_call(
        gram_kernel,
        out_shape=[jax.ShapeDtypeStruct((BLK, D), F32)] * 2,
        in_specs=[SMEM, VM],
        out_specs=[VM, VM],
        compiler_params=pltpu.CompilerParams(vmem_limit_bytes=48 << 20),
        cost_estimate=pl.CostEstimate(flops=2 * D * D * D * 4, bytes_accessed=4 * D * D * 2, transcendentals=0),
    )(core, wide)


def sweeps(core, mine, rest, x_rows):
    return pl.pallas_call(
        sweeps_kernel,
        out_shape=jax.ShapeDtypeStruct(x_rows.shape, F32),
        in_specs=[SMEM, VM, VM, VM],
        out_specs=VM,
        scratch_shapes=[
            pltpu.VMEM((BLK, D), F32),
            pltpu.VMEM((BLK, D), F32),
            pltpu.VMEM((D, D), F32),
            pltpu.VMEM((3, D, D), BF),
            pltpu.VMEM((3, D, D), BF),
            pltpu.VMEM((3, D, D), BF),
        ],
        compiler_params=pltpu.CompilerParams(vmem_limit_bytes=48 << 20),
        cost_estimate=pl.CostEstimate(flops=2 * D * D * D * 32, bytes_accessed=4 * D * D, transcendentals=0),
    )(core, mine, rest, x_rows)


def gelu_parts(u):
    k0 = math.sqrt(2.0 / math.pi)
    th = jnp.tanh(k0 * (u + 0.044715 * (u * u * u)))
    value = 0.5 * u * (1.0 + th)
    slope = 0.5 * (1.0 + th) + 0.5 * u * (1.0 - th * th) * (k0 * (1.0 + 3.0 * 0.044715 * u * u))
    return value, slope


def body(tokens, cotangent, qkv_weight, out_weight, fc_weight, vectors, qkv_momentum, out_momentum, fc_momentum, vector_first, vector_second):
    zi, xi, yi, ci, ti = (lax.axis_index(a) for a in ALL)
    rows = tokens.shape[0]
    n_att = qkv_weight.shape[3]
    n_fc = fc_weight.shape[3]
    gain, shift = vectors[:D], vectors[D : 2 * D]
    bias_in, bias_out = vectors[2 * D : 2 * D + FF], vectors[2 * D + FF :]

    attn_rows = jnp.concatenate([jnp.transpose(qkv_weight[:, :, 0, :], (0, 2, 1)), jnp.transpose(out_weight[:, 0, :])[None]])
    fc_rows = jnp.transpose(fc_weight[:, :, 0, :], (0, 2, 1))
    own_rows = jnp.concatenate([attn_rows.reshape(4 * n_att, D), fc_rows.reshape(2 * n_fc, D)]).astype(BF)
    held = gather_ring(own_rows, "yh")
    left = gather_ring(gather_ring(held[..., : D // 2], "z"), "x")
    right = gather_ring(gather_ring(held[..., D // 2 :], "x"), "z", 1)
    held = jnp.concatenate([left, right], axis=-1)
    held = held.reshape(32, 4 * n_att + 2 * n_fc, D)
    w_in = held[:, 4 * n_att : 4 * n_att + n_fc].reshape(32 * n_fc, D)
    w_back = held[:, 4 * n_att + n_fc :].reshape(32 * n_fc, D)
    att_mine = held[:, : 4 * n_att].reshape(32 * 4 * n_att, D)
    att_both = jnp.concatenate([att_mine, pull(att_mine, "c", 1)])
    r = jnp.arange(2 * 32 * 4 * n_att)
    lane = r % n_att
    mat = (r // n_att) % 4
    ry = (r // (4 * n_att)) % 2
    rz = (r // (8 * n_att)) % 4
    rx = (r // (32 * n_att)) % 4
    rc = r // (128 * n_att)
    column = (((((zi + rz) % 4) * 4 + (xi + rx) % 4) * 2 + (yi + ry) % 2) * 2 + (ci + rc) % 2) * n_att + lane
    place = jnp.where(column // 192 == ci, mat * 192 + column % 192, -1)
    pick = (jnp.arange(768)[:, None] == place[None, :]).astype(BF)
    w_att = dot(pick, att_both, ((1,), (0,))).astype(BF)
    w_qkv, w_out = w_att[:576], w_att[576:]

    inputs = tokens.astype(F32)
    average = jnp.mean(inputs, axis=-1, keepdims=True)
    deviation = inputs - average
    variance = jnp.mean(deviation * deviation, axis=-1, keepdims=True)
    inv_spread = lax.rsqrt(variance + 1e-05)
    centred = deviation * inv_spread
    normed_own = (centred * gain + shift).astype(BF)
    both = jnp.stack([normed_own, cotangent])
    both = jnp.stack([both, pull(both, "t", 1)], axis=1)
    both = jnp.stack([both, pull(both, "c", 1)], axis=1)
    n_all = 4 * rows
    normed, cot = both[0].reshape(n_all, D), both[1].reshape(n_all, D)

    half = jnp.arange(LEN) // rows
    position = ((ti + half) % 2) * rows + jnp.arange(LEN) % rows
    frequency = 10000.0 ** (-2.0 * jnp.arange(ROT // 2, dtype=F32) / ROT)
    angles = position.astype(F32)[:, None] * frequency[None, :]
    cos_t, sin_t = jnp.cos(angles), jnp.sin(angles)
    ones, zeros = jnp.ones((LEN, HD - ROT), F32), jnp.zeros((LEN, HD - ROT), F32)
    cos_full = jnp.concatenate([cos_t, cos_t, ones], axis=1)[None, :, None, :]
    sin_full = jnp.concatenate([-sin_t, sin_t, zeros], axis=1)[None, :, None, :]

    def swap(v):
        return jnp.concatenate([v[..., ROT // 2 : ROT], v[..., : ROT // 2], v[..., ROT:]], axis=-1)

    def rotate(v):
        return v * cos_full + swap(v) * sin_full

    def unrotate(v):
        return v * cos_full - swap(v) * sin_full

    projected = dot(normed, w_qkv, ((1,), (1,)))
    shape = (2, LEN, 3, HD)
    query = rotate(projected[:, :192].reshape(shape)).astype(BF)
    keyed = rotate(projected[:, 192:384].reshape(shape)).astype(BF)
    value = projected[:, 384:].reshape(shape).astype(BF)
    causal = position[:, None] >= position[None, :]
    scale = HD ** (-0.5)
    scores = jnp.einsum("sqhd,skhd->shqk", query, keyed, preferred_element_type=F32) * scale
    scores = jnp.where(causal, scores, -1e30)
    raised = jnp.exp(scores - jnp.max(scores, axis=-1, keepdims=True))
    chance = raised / jnp.sum(raised, axis=-1, keepdims=True)
    chance_low = chance.astype(BF)
    attended = jnp.einsum("shqk,skhd->sqhd", chance_low, value, preferred_element_type=F32).reshape(n_all, 192).astype(BF)

    bias6 = bias_in.reshape(2, 4, 4, 2, 2, n_fc)
    bias6 = jnp.concatenate([bias6, bias6], axis=1)
    bias6 = jnp.concatenate([bias6, bias6], axis=2)
    bias6 = jnp.concatenate([bias6, bias6], axis=3)
    bias_own = lax.dynamic_slice(bias6, (ti, zi, xi, yi, ci, 0), (1, 4, 4, 2, 1, n_fc))[0, :, :, :, 0]
    bias_own = jnp.transpose(bias_own, (1, 0, 2, 3)).reshape(32 * n_fc)
    hidden_pre = dot(normed, w_in, ((1,), (1,))) + bias_own
    hidden_f, slope = gelu_parts(hidden_pre)
    hidden = hidden_f.astype(BF)

    branch = dot(attended, w_out, ((1,), (0,))) + dot(hidden, w_back, ((1,), (0,)))

    def own_rows_of(v):
        v = v.reshape(2, 2, rows, D)
        v = v[0] + pull(v[1], "c", 1)
        return v[0] + pull(v[1].astype(BF), "t", 1).astype(F32)

    mixed = (inputs + own_rows_of(branch) + bias_out).astype(BF)

    grad_out = dot(attended, cot, ((0,), (0,)))
    grad_back = dot(hidden, cot, ((0,), (0,)))
    d_attended = dot(cot, w_out, ((1,), (1,))).astype(BF).reshape(shape)
    d_pre = (dot(cot, w_back, ((1,), (1,))) * slope).astype(BF)
    d_value = jnp.einsum("shqk,sqhd->skhd", chance_low, d_attended, preferred_element_type=F32).astype(BF)
    d_chance = jnp.einsum("sqhd,skhd->shqk", d_attended, value, preferred_element_type=F32)
    d_scores = (chance * (d_chance - jnp.sum(chance * d_chance, axis=-1, keepdims=True))).astype(BF)
    d_query = unrotate(jnp.einsum("shqk,skhd->sqhd", d_scores, keyed, preferred_element_type=F32) * scale).astype(BF)
    d_key = unrotate(jnp.einsum("shqk,sqhd->skhd", d_scores, query, preferred_element_type=F32) * scale).astype(BF)
    d_proj = jnp.concatenate([v.reshape(n_all, 192) for v in (d_query, d_key, d_value)], axis=1)
    grad_qkv = dot(d_proj, normed, ((0,), (0,)))
    grad_in = dot(d_pre, normed, ((0,), (0,)))
    grad_bias_in = jnp.sum(d_pre.astype(F32), axis=0)
    d_normed = dot(d_proj, w_qkv, ((1,), (0,))) + dot(d_pre, w_in, ((1,), (0,)))
    d_rows = own_rows_of(d_normed)
    d_hat = d_rows * gain
    correction = d_hat - jnp.mean(d_hat, axis=-1, keepdims=True) - centred * jnp.mean(d_hat * centred, axis=-1, keepdims=True)
    own_cot = cotangent.astype(F32)
    input_grad = own_cot + correction * inv_spread

    spread = jnp.zeros((2, 8, 8, 4, 2, n_fc), F32)
    bias_grad = jnp.transpose(grad_bias_in.reshape(4, 4, 2, n_fc), (1, 0, 2, 3))[None, :, :, :, None]
    spread = lax.dynamic_update_slice(spread, bias_grad, (ti, zi, xi, yi, ci, 0))
    spread = spread.reshape(2, 2, 4, 2, 4, 2, 2, 2, n_fc).sum(axis=(1, 3, 5))
    vector_part = jnp.concatenate([jnp.sum(d_rows * centred, axis=0), jnp.sum(d_rows, axis=0), spread.reshape(FF), jnp.sum(own_cot, axis=0)])

    grad_att = jnp.concatenate([grad_qkv, grad_out]).astype(BF)
    att_home = dot(pick, grad_att, ((0,), (0,))).astype(BF)
    n_half = 32 * 4 * n_att
    att_rel = att_home[:n_half] + pull(att_home[n_half:], "c", 1)
    parts = jnp.concatenate(
        [
            att_rel.reshape(32, 4 * n_att, D),
            grad_in.astype(BF).reshape(32, n_fc, D),
            grad_back.astype(BF).reshape(32, n_fc, D),
        ],
        axis=1,
    )
    width = 4 * n_att + 2 * n_fc
    parts = parts.reshape(4, 4, 2, width, D)
    left = sum_ring(sum_ring(parts[..., : D // 2], "x"), "z")
    right = sum_ring(sum_ring(parts[..., D // 2 :], "z", 1), "x")
    total = sum_ring(jnp.concatenate([left, right], axis=-1), "yh")

    mom_rows = jnp.concatenate(
        [
            jnp.transpose(qkv_momentum[:, :, 0, :], (0, 2, 1)).reshape(3 * n_att, D),
            jnp.transpose(out_momentum[:, 0, :]),
            jnp.transpose(fc_momentum[:, :, 0, :], (0, 2, 1)).reshape(2 * n_fc, D),
        ]
    )
    moment = 0.95 * mom_rows + total
    update = total + 0.95 * moment

    half_fc = n_fc // 2
    att_u = update[: 4 * n_att].reshape(4, n_att, D)
    att_u = jnp.concatenate([att_u, jnp.zeros((4, half_fc - n_att, D), F32)], axis=1)
    fc_u = update[4 * n_att :].reshape(4, half_fc, D)
    vec_rows = jnp.concatenate([vector_part.reshape(VEC // D, D), jnp.zeros((VEC_ROWS - VEC // D, D), F32)])
    chunks = jnp.concatenate([att_u, fc_u])
    chunks = jnp.concatenate([chunks, jnp.broadcast_to(vec_rows, (8, VEC_ROWS, D))], axis=1)
    got = lax.all_to_all(chunks, ("z", "t"), split_axis=0, concat_axis=0, tiled=True)
    mine = got[:, :half_fc].reshape(8 * half_fc, D)
    vec_sum = jnp.sum(got[:, half_fc:], axis=0)[:8]
    wide = mine
    for axis in ("yh", "x"):
        n = wide.shape[0]
        ring = gather_ring(jnp.concatenate([wide, vec_sum]), axis)
        wide = ring[:, :n].reshape(-1, D)
        vec_sum = jnp.sum(ring[:, n:], axis=0)
    core = ci.astype(jnp.int32)[None]
    keep, give = gram_parts(core, wide)
    from_core = pull(jnp.concatenate([give, vec_sum]), "c", 1)
    part = keep + from_core[:BLK]
    vec_sum = vec_sum + from_core[BLK:]
    other = pull(part, "t", 1)
    part = jnp.where(zi >= 2, part + other, part)
    rest = pull(part, "c", 1)
    x_rows = sweeps(core, part, rest, mine)
    vector_grad = vec_sum[: VEC // D].reshape(VEC)
    first_new = 0.9 * vector_first + 0.1 * vector_grad
    second_new = 0.95 * vector_second + 0.05 * vector_grad * vector_grad
    step_size = first_new / (1.0 - 0.9**STEP) / (jnp.sqrt(second_new / (1.0 - 0.95**STEP)) + 1e-08)
    vector_new = vectors - 0.2 * step_size

    back = lax.all_to_all(x_rows, ("z", "t"), split_axis=0, concat_axis=0, tiled=True).reshape(8, half_fc, D)
    att_x = back[:4, :n_att]
    fc_x = back[4:].reshape(2, n_fc, D)

    def cols(v):
        return jnp.transpose(v, (0, 2, 1))[:, :, None, :]

    fc_factor = math.sqrt(FF / D)
    qkv_new = qkv_weight * 0.99 - cols(att_x[:3])
    out_new = out_weight * 0.99 - cols(att_x[3:])[0]
    fc_new = fc_weight * 0.99 - fc_factor * cols(fc_x)
    att_m = moment[: 4 * n_att].reshape(4, n_att, D)
    fc_m = moment[4 * n_att :].reshape(2, n_fc, D)
    return (mixed, input_grad, qkv_new, out_new, fc_new, cols(att_m[:3]), cols(att_m[3:])[0], cols(fc_m), first_new, second_new, vector_new)


def solution(mesh):
    mesh = Mesh(mesh.devices.reshape(4, 4, 2, 2, 2), ALL)
    rows = P(ALL, None)
    w3 = P(None, None, "t", DP)
    w2 = P(None, "t", DP)
    vec = P()
    in_specs = (rows, rows, w3, w2, w3, vec, w3, w2, w3, vec, vec)
    out_specs = (rows, rows, w3, w2, w3, w3, w2, w3, vec, vec, vec)
    return jax.shard_map(body, mesh=mesh, in_specs=in_specs, out_specs=out_specs, check_vma=False)
```

```python
import math

import jax
import jax.numpy as jnp
from jax import lax
from jax.experimental import pallas as pl
from jax.experimental.pallas import tpu as pltpu
from jax.sharding import Mesh, PartitionSpec as P

D = 768
H = 12
HD = 64
ROT = 16
FF = 3072
SWEEPS = 5
STEP = 10
LEN = 256
VEC = 2 * D + FF + D
VEC_ROWS = 12

NS = (3.4445, -4.775, 2.0315)
BF = jnp.bfloat16
F32 = jnp.float32
BLK = 256
NB = D // BLK

DP = ("z", "x", "yh", "c")
ALL = ("z", "x", "yh", "c", "t")


def pull(value, axis, k):
    n = lax.axis_size(axis)
    return lax.ppermute(value, axis, [((i + k) % n, i) for i in range(n)])


def gather_ring(value, axis, dim=0):
    n = lax.axis_size(axis)
    return jnp.stack([value] + [pull(value, axis, k) for k in range(1, n)], axis=dim)


def sum_ring(parts, axis, dim=0):
    n = lax.axis_size(axis)
    entry = lambda k: lax.index_in_dim(parts, k, dim, keepdims=False)
    total = entry(0).astype(F32)
    for k in range(1, n):
        total = total + pull(entry(k).astype(BF), axis, n - k).astype(F32)
    return total


def dot(a, b, dims):
    return lax.dot_general(a, b, (dims, ((), ())), preferred_element_type=F32)


def pieces(value, n):
    out = []
    for _ in range(n):
        low = value.astype(BF)
        out.append(low)
        value = value - low.astype(F32)
    return out


def mul(xs, ys, dims=((1,), (0,))):
    n = len(xs)
    total = None
    for order in reversed(range(n)):
        for i in range(order + 1):
            term = lax.dot_general(xs[i], ys[order - i], (dims, ((), ())), preferred_element_type=F32)
            total = term if total is None else total + term
    return total


def gram_kernel(core_ref, wide_ref, keep_ref, give_ref):
    xs = pieces(wide_ref[...], 3)
    dims = ((0,), (0,))
    cut = lambda i: slice(i * BLK, (i + 1) * BLK)
    top = mul([x[:, cut(0)] for x in xs], xs, dims)
    mid = mul([x[:, cut(1)] for x in xs], [x[:, BLK:] for x in xs], dims)
    low = mul([x[:, cut(2)] for x in xs], [x[:, 2 * BLK :] for x in xs], dims)
    first = core_ref[0] == 0

    @pl.when(first)
    def _():
        keep_ref[...] = top
        give_ref[:, : 2 * BLK] = mid
        give_ref[:, 2 * BLK :] = low

    @pl.when(jnp.logical_not(first))
    def _():
        give_ref[...] = top
        keep_ref[:, : 2 * BLK] = mid
        keep_ref[:, 2 * BLK :] = low


def blocks(i, j):
    return (slice(i * BLK, (i + 1) * BLK), slice(j * BLK, (j + 1) * BLK))


def put(refs, i, j, value):
    for ref, piece in zip(refs, pieces(value, len(refs))):
        ref[blocks(i, j)] = piece


def put_both(refs, i, j, value):
    put(refs, i, j, value)
    if i != j:
        put(refs, j, i, value.T)


def symmetric_product(xs, ys, emit):
    for i in range(NB):
        rows = slice(i * BLK, (i + 1) * BLK)
        wide = mul([x[rows, :] for x in xs], [y[:, i * BLK :] for y in ys])
        for j in range(i, NB):
            emit(i, j, wide[:, (j - i) * BLK : (j - i + 1) * BLK])


def sweeps_kernel(core_ref, mine_ref, rest_ref, x_ref, out_ref, top_ref, bottom_ref, gram_ref, a_ref, p_ref, b_ref):
    first = core_ref[0] == 0

    @pl.when(first)
    def _():
        top_ref[...] = mine_ref[...]
        bottom_ref[...] = rest_ref[...]

    @pl.when(jnp.logical_not(first))
    def _():
        top_ref[...] = rest_ref[...]
        bottom_ref[...] = mine_ref[...]

    def packed(i, j):
        if i == 0:
            return top_ref[:, j * BLK : (j + 1) * BLK]
        at = (j - 1) if i == 1 else 2
        return bottom_ref[:, at * BLK : (at + 1) * BLK]

    eye = (lax.broadcasted_iota(jnp.int32, (BLK, BLK), 0) == lax.broadcasted_iota(jnp.int32, (BLK, BLK), 1)).astype(F32)
    trace = sum(jnp.sum(packed(i, i) * eye) for i in range(NB))
    norm = jnp.sqrt(jnp.full((8, 128), trace, F32)) + 1e-07
    factor = (1.0 / norm)[0:1, 0:1]
    square = factor * factor

    for i in range(NB):
        for j in range(i, NB):
            value = packed(i, j) * square
            gram_ref[blocks(i, j)] = value
            put_both([a_ref.at[k] for k in range(3)], i, j, value)
    out_ref[...] = x_ref[...] * factor

    def poly(n, n_p):
        a = [a_ref.at[k] for k in range(n)]

        def emit(i, j, block):
            value = NS[1] * gram_ref[blocks(i, j)] + NS[2] * block
            if i == j:
                value = value + NS[0] * eye
            put_both([p_ref.at[k] for k in range(n_p)], i, j, value)

        symmetric_product(a, a, emit)

    def apply():
        out_ref[...] = mul(pieces(out_ref[...], 2), [p_ref.at[k][...] for k in range(2)])

    def next_gram(n, keep):
        p = [p_ref.at[k] for k in range(n)]
        symmetric_product([a_ref.at[k] for k in range(n)], p, lambda i, j, block: put_both([b_ref.at[k] for k in range(n)], i, j, block))

        def emit(i, j, block):
            gram_ref[blocks(i, j)] = block
            put_both([a_ref.at[k] for k in range(keep)], i, j, block)

        symmetric_product([b_ref.at[k] for k in range(n)], p, emit)

    poly(3, 3)
    apply()
    next_gram(3, 2)

    @pl.loop(1, SWEEPS - 1)
    def _(_):
        poly(2, 2)
        apply()
        next_gram(2, 2)

    poly(2, 2)
    apply()


SMEM = pl.BlockSpec(memory_space=pltpu.SMEM)
VM = pl.BlockSpec(memory_space=pltpu.VMEM)


def gram_parts(core, wide):
    return pl.pallas_call(
        gram_kernel,
        out_shape=[jax.ShapeDtypeStruct((BLK, D), F32)] * 2,
        in_specs=[SMEM, VM],
        out_specs=[VM, VM],
        compiler_params=pltpu.CompilerParams(vmem_limit_bytes=48 << 20),
        cost_estimate=pl.CostEstimate(flops=2 * D * D * D * 4, bytes_accessed=4 * D * D * 2, transcendentals=0),
    )(core, wide)


def sweeps(core, mine, rest, x_rows):
    return pl.pallas_call(
        sweeps_kernel,
        out_shape=jax.ShapeDtypeStruct(x_rows.shape, F32),
        in_specs=[SMEM, VM, VM, VM],
        out_specs=VM,
        scratch_shapes=[
            pltpu.VMEM((BLK, D), F32),
            pltpu.VMEM((BLK, D), F32),
            pltpu.VMEM((D, D), F32),
            pltpu.VMEM((3, D, D), BF),
            pltpu.VMEM((3, D, D), BF),
            pltpu.VMEM((3, D, D), BF),
        ],
        compiler_params=pltpu.CompilerParams(vmem_limit_bytes=48 << 20),
        cost_estimate=pl.CostEstimate(flops=2 * D * D * D * 32, bytes_accessed=4 * D * D, transcendentals=0),
    )(core, mine, rest, x_rows)


def gelu_parts(u):
    k0 = math.sqrt(2.0 / math.pi)
    th = jnp.tanh(k0 * (u + 0.044715 * (u * u * u)))
    value = 0.5 * u * (1.0 + th)
    slope = 0.5 * (1.0 + th) + 0.5 * u * (1.0 - th * th) * (k0 * (1.0 + 3.0 * 0.044715 * u * u))
    return value, slope


HEADS = 3
PAD = 128
HC = HEADS * HD
HP = HEADS * PAD
NN = ((1,), (0,))
NT = ((1,), (1,))
TN = ((0,), (0,))


def iota(shape, dim):
    return lax.broadcasted_iota(jnp.int32, shape, dim)


def one_hot(cond):
    return jnp.where(cond, 1.0, 0.0).astype(BF)


def layer_kernel(
    tensor_ref, row_ref, col_ref, att_ref, win_ref, wback_ref, normed_ref, cot_ref, bias_ref, cos_ref, sin_ref,
    branch_ref, dnorm_ref, keep_ref, give_ref, gin_ref, gback_ref, gbias_ref,
    wq_ref, wk_ref, wv_ref, wo_ref, q_ref, k_ref, v_ref, da_ref, at_ref, dq_ref, dk_ref, dv_ref, nat_ref,
):
    n_rows = 4 * HC
    pick = one_hot(iota((n_rows, row_ref.shape[1]), 0) == row_ref[...])
    w_att = dot(pick, att_ref[...], NN).astype(BF)
    r = iota((HC, HC), 0)
    e = jnp.bitwise_and(r, HD - 1)
    half = ROT // 2
    source = jnp.where(e < half, r + half, jnp.where(e < ROT, r - half, -1))
    exchange = one_hot(iota((HC, HC), 1) == source)
    blank = jnp.zeros((HD, D), BF)
    for m, ref in enumerate((wq_ref, wk_ref)):
        own = w_att[m * HC : (m + 1) * HC]
        swapped = dot(exchange, own, NN).astype(BF)
        for h in range(HEADS):
            base = h * 2 * PAD
            ref[base : base + HD] = own[h * HD : (h + 1) * HD]
            ref[base + HD : base + PAD] = blank
            ref[base + PAD : base + PAD + HD] = swapped[h * HD : (h + 1) * HD]
            ref[base + PAD + HD : base + 2 * PAD] = blank
    for m, ref in ((2, wv_ref), (3, wo_ref)):
        for h in range(HEADS):
            ref[h * PAD : h * PAD + HD] = w_att[m * HC + h * HD : m * HC + (h + 1) * HD]
            ref[h * PAD + HD : (h + 1) * PAD] = blank

    cos, sin = cos_ref[...], sin_ref[...]
    for w_ref, ref in ((wq_ref, q_ref), (wk_ref, k_ref)):
        lin = dot(normed_ref[...], w_ref[...], NT)
        for s in range(2):
            rows = slice(s * LEN, (s + 1) * LEN)
            for h in range(HEADS):
                base = h * 2 * PAD
                own, other = lin[rows, base : base + PAD], lin[rows, base + PAD : base + 2 * PAD]
                ref[rows, base : base + PAD] = (own * cos + other * sin).astype(BF)
                ref[rows, base + PAD : base + 2 * PAD] = (other * cos - own * sin).astype(BF)
    v_ref[...] = dot(normed_ref[...], wv_ref[...], NT).astype(BF)
    da_ref[...] = dot(cot_ref[...], wo_ref[...], NT).astype(BF)

    turn = tensor_ref[0] * (LEN // 2)
    at_q = jnp.bitwise_xor(iota((LEN, LEN), 0), turn)
    at_k = jnp.bitwise_xor(iota((LEN, LEN), 1), turn)
    causal = at_q >= at_k
    scale = HD ** (-0.5)
    for s in range(2):
        rows = slice(s * LEN, (s + 1) * LEN)
        for h in range(HEADS):
            two = slice(h * 2 * PAD, (h + 1) * 2 * PAD)
            one = slice(h * 2 * PAD, h * 2 * PAD + PAD)
            lanes = slice(h * PAD, (h + 1) * PAD)
            value, d_att = v_ref[rows, lanes], da_ref[rows, lanes]
            scores = jnp.where(causal, dot(q_ref[rows, one], k_ref[rows, one], NT) * scale, -1e30)
            raised = jnp.exp(scores - jnp.max(scores, axis=1, keepdims=True))
            probs = raised / jnp.sum(raised, axis=1, keepdims=True)
            low = probs.astype(BF)
            at_ref[rows, lanes] = dot(low, value, NN).astype(BF)
            dv_ref[rows, lanes] = dot(low, d_att, TN).astype(BF)
            d_probs = dot(d_att, value, NT)
            d_scores = (probs * (d_probs - jnp.sum(probs * d_probs, axis=1, keepdims=True))).astype(BF)
            d_q = dot(d_scores, k_ref[rows, two], NN) * scale
            d_k = dot(d_scores, q_ref[rows, two], TN) * scale
            dq_ref[rows, lanes] = (d_q[:, :PAD] * cos - d_q[:, PAD:] * sin).astype(BF)
            dk_ref[rows, lanes] = (d_k[:, :PAD] * cos - d_k[:, PAD:] * sin).astype(BF)

    hidden, slope = gelu_parts(dot(normed_ref[...], win_ref[...], NT) + bias_ref[...])
    hidden = hidden.astype(BF)
    branch_ref[...] = dot(at_ref[...], wo_ref[...], NN) + dot(hidden, wback_ref[...], NN)
    gback_ref[...] = dot(hidden, cot_ref[...], TN).astype(BF)
    d_pre = (dot(cot_ref[...], wback_ref[...], NT) * slope).astype(BF)
    gbias_ref[...] = jnp.sum(d_pre.astype(F32), axis=0, keepdims=True)
    gin_ref[...] = dot(d_pre, normed_ref[...], TN).astype(BF)
    total = dot(d_pre, win_ref[...], NN) + dot(dv_ref[...], wv_ref[...], NN)
    for h in range(HEADS):
        one = slice(h * 2 * PAD, h * 2 * PAD + PAD)
        lanes = slice(h * PAD, (h + 1) * PAD)
        total = total + dot(dq_ref[:, lanes], wq_ref[one], NN) + dot(dk_ref[:, lanes], wk_ref[one], NN)
    dnorm_ref[...] = total

    for m, (ref, with_ref) in enumerate(((dq_ref, normed_ref), (dk_ref, normed_ref), (dv_ref, normed_ref), (at_ref, cot_ref))):
        grad = dot(ref[...], with_ref[...], TN).astype(BF)
        for h in range(HEADS):
            nat_ref[m * HC + h * HD : m * HC + (h + 1) * HD] = grad[h * PAD : h * PAD + HD]
    half_rows = keep_ref.shape[0]
    for k, ref in enumerate((keep_ref, give_ref)):
        place = one_hot(iota((half_rows, n_rows), 1) == col_ref[k * half_rows : (k + 1) * half_rows, :])
        ref[...] = dot(place, nat_ref[...], NN).astype(BF)


def layer(tensor, row, col, att, w_in, w_back, normed, cot, bias, cos, sin):
    n = normed.shape[0]
    out = lambda shape, dtype: jax.ShapeDtypeStruct(shape, dtype)
    low = lambda *shape: pltpu.VMEM(shape, BF)
    half_rows = att.shape[0] // 2
    return pl.pallas_call(
        layer_kernel,
        out_shape=[out((n, D), F32), out((n, D), F32), out((half_rows, D), BF), out((half_rows, D), BF), out(w_in.shape, BF), out(w_back.shape, BF), out(bias.shape, F32)],
        in_specs=[SMEM] + [VM] * 10,
        out_specs=[VM] * 7,
        scratch_shapes=[low(2 * HP, D), low(2 * HP, D), low(HP, D), low(HP, D), low(n, 2 * HP), low(n, 2 * HP)] + [low(n, HP)] * 6 + [low(4 * HC, D)],
        compiler_params=pltpu.CompilerParams(vmem_limit_bytes=56 << 20),
        cost_estimate=pl.CostEstimate(flops=12 * 10**9, bytes_accessed=16 << 20, transcendentals=10**6),
    )(tensor, row, col, att, w_in, w_back, normed, cot, bias, cos, sin)


def body(tokens, cotangent, qkv_weight, out_weight, fc_weight, vectors, qkv_momentum, out_momentum, fc_momentum, vector_first, vector_second):
    zi, xi, yi, ci, ti = (lax.axis_index(a) for a in ALL)
    rows = tokens.shape[0]
    n_att = qkv_weight.shape[3]
    n_fc = fc_weight.shape[3]
    gain, shift = vectors[:D], vectors[D : 2 * D]
    bias_in, bias_out = vectors[2 * D : 2 * D + FF], vectors[2 * D + FF :]

    attn_rows = jnp.concatenate([jnp.transpose(qkv_weight[:, :, 0, :], (0, 2, 1)), jnp.transpose(out_weight[:, 0, :])[None]])
    fc_rows = jnp.transpose(fc_weight[:, :, 0, :], (0, 2, 1))
    own_rows = jnp.concatenate([attn_rows.reshape(4 * n_att, D), fc_rows.reshape(2 * n_fc, D)]).astype(BF)
    held = gather_ring(own_rows, "yh")
    left = gather_ring(gather_ring(held[..., : D // 2], "z"), "x")
    right = gather_ring(gather_ring(held[..., D // 2 :], "x"), "z", 1)
    held = jnp.concatenate([left, right], axis=-1)
    held = held.reshape(32, 4 * n_att + 2 * n_fc, D)
    w_in = held[:, 4 * n_att : 4 * n_att + n_fc].reshape(32 * n_fc, D)
    w_back = held[:, 4 * n_att + n_fc :].reshape(32 * n_fc, D)
    att_mine = held[:, : 4 * n_att].reshape(32 * 4 * n_att, D)
    att_both = jnp.concatenate([att_mine, pull(att_mine, "c", 1)])
    r = jnp.arange(2 * 32 * 4 * n_att)
    lane = r % n_att
    mat = (r // n_att) % 4
    ry = (r // (4 * n_att)) % 2
    rz = (r // (8 * n_att)) % 4
    rx = (r // (32 * n_att)) % 4
    rc = r // (128 * n_att)
    column = (((((zi + rz) % 4) * 4 + (xi + rx) % 4) * 2 + (yi + ry) % 2) * 2 + (ci + rc) % 2) * n_att + lane
    place = jnp.where(column // HC == ci, mat * HC + column % HC, -1).astype(jnp.int32)

    inputs = tokens.astype(F32)
    average = jnp.mean(inputs, axis=-1, keepdims=True)
    deviation = inputs - average
    variance = jnp.mean(deviation * deviation, axis=-1, keepdims=True)
    inv_spread = lax.rsqrt(variance + 1e-05)
    centred = deviation * inv_spread
    normed_own = (centred * gain + shift).astype(BF)
    both = jnp.stack([normed_own, cotangent])
    both = jnp.stack([both, pull(both, "t", 1)], axis=1)
    both = jnp.stack([both, pull(both, "c", 1)], axis=1)
    n_all = 4 * rows
    normed, cot = both[0].reshape(n_all, D), both[1].reshape(n_all, D)

    half = jnp.arange(LEN) // rows
    position = ((ti + half) % 2) * rows + jnp.arange(LEN) % rows
    frequency = 10000.0 ** (-2.0 * jnp.arange(ROT // 2, dtype=F32) / ROT)
    angles = position.astype(F32)[:, None] * frequency[None, :]
    cos_t, sin_t = jnp.cos(angles), jnp.sin(angles)
    pad = lambda a, b, fill: jnp.concatenate([a, b, jnp.full((LEN, PAD - ROT), fill, F32)], axis=1)
    cos_full, sin_full = pad(cos_t, cos_t, 1.0), pad(-sin_t, sin_t, 0.0)

    bias6 = bias_in.reshape(2, 4, 4, 2, 2, n_fc)
    bias6 = jnp.concatenate([bias6, bias6], axis=1)
    bias6 = jnp.concatenate([bias6, bias6], axis=2)
    bias6 = jnp.concatenate([bias6, bias6], axis=3)
    bias_own = lax.dynamic_slice(bias6, (ti, zi, xi, yi, ci, 0), (1, 4, 4, 2, 1, n_fc))[0, :, :, :, 0]
    bias_own = jnp.transpose(bias_own, (1, 0, 2, 3)).reshape(32 * n_fc)
    branch, d_normed, att_keep, att_give, grad_in, grad_back, grad_bias_in = layer(
        ti.astype(jnp.int32)[None], place[None, :], place[:, None], att_both, w_in, w_back, normed, cot, bias_own[None, :], cos_full, sin_full
    )

    def own_rows_of(v):
        v = v.reshape(2, 2, rows, D)
        v = v[0] + pull(v[1], "c", 1)
        return v[0] + pull(v[1].astype(BF), "t", 1).astype(F32)

    mixed = (inputs + own_rows_of(branch) + bias_out).astype(BF)

    d_rows = own_rows_of(d_normed)
    d_hat = d_rows * gain
    correction = d_hat - jnp.mean(d_hat, axis=-1, keepdims=True) - centred * jnp.mean(d_hat * centred, axis=-1, keepdims=True)
    own_cot = cotangent.astype(F32)
    input_grad = own_cot + correction * inv_spread

    spread = jnp.zeros((2, 8, 8, 4, 2, n_fc), F32)
    bias_grad = jnp.transpose(grad_bias_in.reshape(4, 4, 2, n_fc), (1, 0, 2, 3))[None, :, :, :, None]
    spread = lax.dynamic_update_slice(spread, bias_grad, (ti, zi, xi, yi, ci, 0))
    spread = spread.reshape(2, 2, 4, 2, 4, 2, 2, 2, n_fc).sum(axis=(1, 3, 5))
    vector_part = jnp.concatenate([jnp.sum(d_rows * centred, axis=0), jnp.sum(d_rows, axis=0), spread.reshape(FF), jnp.sum(own_cot, axis=0)])

    att_rel = att_keep + pull(att_give, "c", 1)
    parts = jnp.concatenate(
        [
            att_rel.reshape(32, 4 * n_att, D),
            grad_in.reshape(32, n_fc, D),
            grad_back.reshape(32, n_fc, D),
        ],
        axis=1,
    )
    width = 4 * n_att + 2 * n_fc
    parts = parts.reshape(4, 4, 2, width, D)
    left = sum_ring(sum_ring(parts[..., : D // 2], "x"), "z")
    right = sum_ring(sum_ring(parts[..., D // 2 :], "z", 1), "x")
    total = sum_ring(jnp.concatenate([left, right], axis=-1), "yh")

    mom_rows = jnp.concatenate(
        [
            jnp.transpose(qkv_momentum[:, :, 0, :], (0, 2, 1)).reshape(3 * n_att, D),
            jnp.transpose(out_momentum[:, 0, :]),
            jnp.transpose(fc_momentum[:, :, 0, :], (0, 2, 1)).reshape(2 * n_fc, D),
        ]
    )
    moment = 0.95 * mom_rows + total
    update = total + 0.95 * moment

    half_fc = n_fc // 2
    att_u = update[: 4 * n_att].reshape(4, n_att, D)
    att_u = jnp.concatenate([att_u, jnp.zeros((4, half_fc - n_att, D), F32)], axis=1)
    fc_u = update[4 * n_att :].reshape(4, half_fc, D)
    vec_rows = jnp.concatenate([vector_part.reshape(VEC // D, D), jnp.zeros((VEC_ROWS - VEC // D, D), F32)])
    chunks = jnp.concatenate([att_u, fc_u])
    chunks = jnp.concatenate([chunks, jnp.broadcast_to(vec_rows, (8, VEC_ROWS, D))], axis=1)
    got = lax.all_to_all(chunks, ("z", "t"), split_axis=0, concat_axis=0, tiled=True)
    mine = got[:, :half_fc].reshape(8 * half_fc, D)
    vec_sum = jnp.sum(got[:, half_fc:], axis=0)[:8]
    wide = mine
    for axis in ("yh", "x"):
        n = wide.shape[0]
        ring = gather_ring(jnp.concatenate([wide, vec_sum]), axis)
        wide = ring[:, :n].reshape(-1, D)
        vec_sum = jnp.sum(ring[:, n:], axis=0)
    core = ci.astype(jnp.int32)[None]
    keep, give = gram_parts(core, wide)
    from_core = pull(jnp.concatenate([give, vec_sum]), "c", 1)
    part = keep + from_core[:BLK]
    vec_sum = vec_sum + from_core[BLK:]
    other = pull(part, "t", 1)
    part = jnp.where(zi >= 2, part + other, part)
    rest = pull(part, "c", 1)
    x_rows = sweeps(core, part, rest, mine)
    vector_grad = vec_sum[: VEC // D].reshape(VEC)
    first_new = 0.9 * vector_first + 0.1 * vector_grad
    second_new = 0.95 * vector_second + 0.05 * vector_grad * vector_grad
    step_size = first_new / (1.0 - 0.9**STEP) / (jnp.sqrt(second_new / (1.0 - 0.95**STEP)) + 1e-08)
    vector_new = vectors - 0.2 * step_size

    back = lax.all_to_all(x_rows, ("z", "t"), split_axis=0, concat_axis=0, tiled=True).reshape(8, half_fc, D)
    att_x = back[:4, :n_att]
    fc_x = back[4:].reshape(2, n_fc, D)

    def cols(v):
        return jnp.transpose(v, (0, 2, 1))[:, :, None, :]

    fc_factor = math.sqrt(FF / D)
    qkv_new = qkv_weight * 0.99 - cols(att_x[:3])
    out_new = out_weight * 0.99 - cols(att_x[3:])[0]
    fc_new = fc_weight * 0.99 - fc_factor * cols(fc_x)
    att_m = moment[: 4 * n_att].reshape(4, n_att, D)
    fc_m = moment[4 * n_att :].reshape(2, n_fc, D)
    return (mixed, input_grad, qkv_new, out_new, fc_new, cols(att_m[:3]), cols(att_m[3:])[0], cols(fc_m), first_new, second_new, vector_new)


def solution(mesh):
    mesh = Mesh(mesh.devices.reshape(4, 4, 2, 2, 2), ALL)
    rows = P(ALL, None)
    w3 = P(None, None, "t", DP)
    w2 = P(None, "t", DP)
    vec = P()
    in_specs = (rows, rows, w3, w2, w3, vec, w3, w2, w3, vec, vec)
    out_specs = (rows, rows, w3, w2, w3, w3, w2, w3, vec, vec, vec)
    return jax.shard_map(body, mesh=mesh, in_specs=in_specs, out_specs=out_specs, check_vma=False)
```

```python
import functools
import itertools
import math

import jax
import jax.numpy as jnp
from jax import lax
from jax.experimental import pallas as pl
from jax.experimental.pallas import tpu as pltpu
from jax.sharding import Mesh, PartitionSpec as P

D = 768
H = 12
HD = 64
ROT = 16
FF = 3072
SWEEPS = 5
STEP = 10
LEN = 256
VEC = 2 * D + FF + D
VEC_ROWS = 12

NS = (3.4445, -4.775, 2.0315)
BF = jnp.bfloat16
F32 = jnp.float32
BLK = 256
BLK_ROWS = 96
NB = D // BLK

DP = ("z", "x", "yh", "c")
ALL = ("z", "x", "yh", "c", "t")


def pull(value, axis, k):
    n = lax.axis_size(axis)
    return lax.ppermute(value, axis, [((i + k) % n, i) for i in range(n)])


def move(value, source):
    sizes = [lax.axis_size(a) for a in ALL]
    index = lambda at: functools.reduce(lambda total, one: total * one[0] + one[1] % one[0], zip(sizes, at), 0)
    pairs = []
    for here in itertools.product(*map(range, sizes)):
        there = source(*here)
        if there is not None:
            pairs.append((index(there), index(here)))
    return lax.ppermute(value, ALL, pairs)


def pull_outer(value, k):
    return move(value, lambda z, x, y, c, t: (z, x + k, y, c, t) if c == 0 else (z + k, x, y, c, t))


def pull_inner(value, k):
    return move(value, lambda z, x, y, c, t: (z + k, x, y, c, t) if c == 0 else (z, x + k, y, c, t))


def pull_yh(value, k):
    return pull(value, "yh", k)


def sum_ring(parts, pulls):
    n = len(parts)
    total = parts[0].astype(F32)
    for k in range(1, n):
        total = total + pulls(parts[k].astype(BF), n - k).astype(F32)
    return total


def dot(a, b, dims):
    return lax.dot_general(a, b, (dims, ((), ())), preferred_element_type=F32)


def pieces(value, n):
    out = []
    for _ in range(n):
        low = value.astype(BF)
        out.append(low)
        value = value - low.astype(F32)
    return out


def mul(xs, ys, dims=((1,), (0,))):
    n = len(xs)
    total = None
    for order in reversed(range(n)):
        for i in range(order + 1):
            term = lax.dot_general(xs[i], ys[order - i], (dims, ((), ())), preferred_element_type=F32)
            total = term if total is None else total + term
    return total


def gram_kernel(core_ref, *refs):
    *in_refs, keep_ref, give_ref, wide_ref = refs
    at = 0
    for ref in in_refs:
        n = ref.shape[0] // BLK_ROWS * BLK_ROWS
        for k, piece in enumerate(pieces(ref[:n], 3)):
            wide_ref[k, at : at + n] = piece
        at += n
    xs = [wide_ref[k] for k in range(3)]
    dims = ((0,), (0,))
    cut = lambda i: slice(i * BLK, (i + 1) * BLK)
    top = mul([x[:, cut(0)] for x in xs], xs, dims)
    mid = mul([x[:, cut(1)] for x in xs], [x[:, BLK:] for x in xs], dims)
    low = mul([x[:, cut(2)] for x in xs], [x[:, 2 * BLK :] for x in xs], dims)
    first = core_ref[0] == 0

    @pl.when(first)
    def _():
        keep_ref[...] = top
        give_ref[:, : 2 * BLK] = mid
        give_ref[:, 2 * BLK :] = low

    @pl.when(jnp.logical_not(first))
    def _():
        give_ref[...] = top
        keep_ref[:, : 2 * BLK] = mid
        keep_ref[:, 2 * BLK :] = low


def blocks(i, j):
    return (slice(i * BLK, (i + 1) * BLK), slice(j * BLK, (j + 1) * BLK))


def put(refs, i, j, value):
    for ref, piece in zip(refs, pieces(value, len(refs))):
        ref[blocks(i, j)] = piece


def put_both(refs, i, j, value):
    put(refs, i, j, value)
    if i != j:
        put(refs, j, i, value.T)


def symmetric_product(xs, ys, emit):
    for i in range(NB):
        rows = slice(i * BLK, (i + 1) * BLK)
        wide = mul([x[rows, :] for x in xs], [y[:, i * BLK :] for y in ys])
        for j in range(i, NB):
            emit(i, j, wide[:, (j - i) * BLK : (j - i + 1) * BLK])


def sweeps_kernel(core_ref, mine_ref, rest_ref, x_ref, out_ref, top_ref, bottom_ref, gram_ref, a_ref, p_ref, b_ref):
    first = core_ref[0] == 0

    @pl.when(first)
    def _():
        top_ref[...] = mine_ref[...]
        bottom_ref[...] = rest_ref[...]

    @pl.when(jnp.logical_not(first))
    def _():
        top_ref[...] = rest_ref[...]
        bottom_ref[...] = mine_ref[...]

    def packed(i, j):
        if i == 0:
            return top_ref[:, j * BLK : (j + 1) * BLK]
        at = (j - 1) if i == 1 else 2
        return bottom_ref[:, at * BLK : (at + 1) * BLK]

    eye = (lax.broadcasted_iota(jnp.int32, (BLK, BLK), 0) == lax.broadcasted_iota(jnp.int32, (BLK, BLK), 1)).astype(F32)
    trace = sum(jnp.sum(packed(i, i) * eye) for i in range(NB))
    norm = jnp.sqrt(jnp.full((8, 128), trace, F32)) + 1e-07
    factor = (1.0 / norm)[0:1, 0:1]
    square = factor * factor

    for i in range(NB):
        for j in range(i, NB):
            value = packed(i, j) * square
            gram_ref[blocks(i, j)] = value
            put_both([a_ref.at[k] for k in range(3)], i, j, value)
    out_ref[...] = x_ref[...] * factor

    def poly(n, n_p):
        a = [a_ref.at[k] for k in range(n)]

        def emit(i, j, block):
            value = NS[1] * gram_ref[blocks(i, j)] + NS[2] * block
            if i == j:
                value = value + NS[0] * eye
            put_both([p_ref.at[k] for k in range(n_p)], i, j, value)

        symmetric_product(a, a, emit)

    def apply():
        out_ref[...] = mul(pieces(out_ref[...], 2), [p_ref.at[k][...] for k in range(2)])

    def next_gram(n, keep):
        p = [p_ref.at[k] for k in range(n)]
        symmetric_product([a_ref.at[k] for k in range(n)], p, lambda i, j, block: put_both([b_ref.at[k] for k in range(n)], i, j, block))

        def emit(i, j, block):
            gram_ref[blocks(i, j)] = block
            put_both([a_ref.at[k] for k in range(keep)], i, j, block)

        symmetric_product([b_ref.at[k] for k in range(n)], p, emit)

    poly(3, 3)
    apply()
    next_gram(3, 2)

    @pl.loop(1, SWEEPS - 1)
    def _(_):
        poly(2, 2)
        apply()
        next_gram(2, 2)

    poly(2, 2)
    apply()


SMEM = pl.BlockSpec(memory_space=pltpu.SMEM)
VM = pl.BlockSpec(memory_space=pltpu.VMEM)


def gram_parts(core, held):
    rows = sum(v.shape[0] // BLK_ROWS * BLK_ROWS for v in held)
    return pl.pallas_call(
        gram_kernel,
        out_shape=[jax.ShapeDtypeStruct((BLK, D), F32)] * 2,
        in_specs=[SMEM] + [VM] * len(held),
        out_specs=[VM, VM],
        scratch_shapes=[pltpu.VMEM((3, rows, D), BF)],
        compiler_params=pltpu.CompilerParams(vmem_limit_bytes=48 << 20),
        cost_estimate=pl.CostEstimate(flops=2 * D * D * D * 4, bytes_accessed=4 * D * D * 2, transcendentals=0),
    )(core, *held)


def sweeps(core, mine, rest, x_rows):
    return pl.pallas_call(
        sweeps_kernel,
        out_shape=jax.ShapeDtypeStruct(x_rows.shape, F32),
        in_specs=[SMEM, VM, VM, VM],
        out_specs=VM,
        scratch_shapes=[
            pltpu.VMEM((BLK, D), F32),
            pltpu.VMEM((BLK, D), F32),
            pltpu.VMEM((D, D), F32),
            pltpu.VMEM((3, D, D), BF),
            pltpu.VMEM((3, D, D), BF),
            pltpu.VMEM((3, D, D), BF),
        ],
        compiler_params=pltpu.CompilerParams(vmem_limit_bytes=48 << 20),
        cost_estimate=pl.CostEstimate(flops=2 * D * D * D * 32, bytes_accessed=4 * D * D, transcendentals=0),
    )(core, mine, rest, x_rows)


def gelu_parts(u):
    k0 = math.sqrt(2.0 / math.pi)
    th = jnp.tanh(k0 * (u + 0.044715 * (u * u * u)))
    value = 0.5 * u * (1.0 + th)
    slope = 0.5 * (1.0 + th) + 0.5 * u * (1.0 - th * th) * (k0 * (1.0 + 3.0 * 0.044715 * u * u))
    return value, slope


HEADS = 3
PAD = 128
HC = HEADS * HD
HP = HEADS * PAD
NN = ((1,), (0,))
NT = ((1,), (1,))
TN = ((0,), (0,))


def iota(shape, dim):
    return lax.broadcasted_iota(jnp.int32, shape, dim)


def one_hot(cond):
    return jnp.where(cond, 1.0, 0.0).astype(BF)


def home_place(at_ref, r):
    zi, xi, yi, ci = (at_ref[k] for k in range(4))
    n = 6
    group = jnp.right_shift(r * 10923, 16)
    lane = r - n * group
    mat = jnp.bitwise_and(group, 3)
    y = jnp.bitwise_and(jnp.right_shift(group, 2) + yi, 1)
    inner = jnp.bitwise_and(jnp.right_shift(group, 3), 3)
    outer = jnp.bitwise_and(jnp.right_shift(group, 5), 3)
    core = jnp.bitwise_and(jnp.right_shift(group, 7) + ci, 1)
    first = ci == 0
    z = jnp.bitwise_and(jnp.where(first, inner, outer) + zi, 3)
    x = jnp.bitwise_and(jnp.where(first, outer, inner) + xi, 3)
    column = (((z * 4 + x) * 2 + y) * 2 + core) * n + lane - HC * ci
    return jnp.where((column >= 0) & (column < HC), mat * HC + column, -1)


def layer_kernel(
    at_ref, own0_ref, own1_ref, own2_ref, own3_ref, got_ref, normed_ref, cot_ref, bias_ref, cos_ref, sin_ref,
    branch_ref, dnorm_ref, mine_ref, theirs_ref, gbias_ref,
    att_ref, win_ref, wback_ref, wq_ref, wk_ref, wv_ref, wo_ref, q_ref, k_ref, v_ref, da_ref, at_heads_ref, dq_ref, dk_ref, dv_ref, nat_ref,
):
    span = got_ref.shape[2]
    small = span // 4
    half_d = D // 2
    for s, ref in enumerate((own0_ref, own1_ref, own2_ref, own3_ref)):
        for to_ref, base, c, own_group, got_group in (
            (att_ref, 0, 0, 0, 0), (att_ref, 4 * span, 1, 0, 3), (win_ref, 0, 0, 1, 1), (wback_ref, 0, 0, 2, 2),
        ):
            at = base + s * span
            to_ref[at : at + span, :half_d] = ref[c, own_group]
            for p in range(4):
                to_ref[at + p * small : at + (p + 1) * small, half_d:] = got_ref[p, got_group, s * small : (s + 1) * small]
    n_rows, n_all = 4 * HC, att_ref.shape[0]

    pick = one_hot(iota((n_rows, n_all), 0) == home_place(at_ref, iota((8, n_all), 1))[:1])
    w_att = dot(pick, att_ref[...], NN).astype(BF)
    r = iota((HC, HC), 0)
    e = jnp.bitwise_and(r, HD - 1)
    half = ROT // 2
    source = jnp.where(e < half, r + half, jnp.where(e < ROT, r - half, -1))
    exchange = one_hot(iota((HC, HC), 1) == source)
    blank = jnp.zeros((HD, D), BF)
    for m, ref in enumerate((wq_ref, wk_ref)):
        own = w_att[m * HC : (m + 1) * HC]
        swapped = dot(exchange, own, NN).astype(BF)
        for h in range(HEADS):
            base = h * 2 * PAD
            ref[base : base + HD] = own[h * HD : (h + 1) * HD]
            ref[base + HD : base + PAD] = blank
            ref[base + PAD : base + PAD + HD] = swapped[h * HD : (h + 1) * HD]
            ref[base + PAD + HD : base + 2 * PAD] = blank
    for m, ref in ((2, wv_ref), (3, wo_ref)):
        for h in range(HEADS):
            ref[h * PAD : h * PAD + HD] = w_att[m * HC + h * HD : m * HC + (h + 1) * HD]
            ref[h * PAD + HD : (h + 1) * PAD] = blank

    cos, sin = cos_ref[...], sin_ref[...]
    for w_ref, ref in ((wq_ref, q_ref), (wk_ref, k_ref)):
        lin = dot(normed_ref[...], w_ref[...], NT)
        for s in range(2):
            rows = slice(s * LEN, (s + 1) * LEN)
            for h in range(HEADS):
                base = h * 2 * PAD
                own, other = lin[rows, base : base + PAD], lin[rows, base + PAD : base + 2 * PAD]
                ref[rows, base : base + PAD] = (own * cos + other * sin).astype(BF)
                ref[rows, base + PAD : base + 2 * PAD] = (other * cos - own * sin).astype(BF)
    v_ref[...] = dot(normed_ref[...], wv_ref[...], NT).astype(BF)
    da_ref[...] = dot(cot_ref[...], wo_ref[...], NT).astype(BF)

    turn = at_ref[4] * (LEN // 2)
    at_q = jnp.bitwise_xor(iota((LEN, LEN), 0), turn)
    at_k = jnp.bitwise_xor(iota((LEN, LEN), 1), turn)
    causal = at_q >= at_k
    scale = HD ** (-0.5)
    for s in range(2):
        rows = slice(s * LEN, (s + 1) * LEN)
        for h in range(HEADS):
            two = slice(h * 2 * PAD, (h + 1) * 2 * PAD)
            one = slice(h * 2 * PAD, h * 2 * PAD + PAD)
            lanes = slice(h * PAD, (h + 1) * PAD)
            value, d_att = v_ref[rows, lanes], da_ref[rows, lanes]
            scores = jnp.where(causal, dot(q_ref[rows, one], k_ref[rows, one], NT) * scale, -1e30)
            raised = jnp.exp(scores - jnp.max(scores, axis=1, keepdims=True))
            probs = raised / jnp.sum(raised, axis=1, keepdims=True)
            low = probs.astype(BF)
            at_heads_ref[rows, lanes] = dot(low, value, NN).astype(BF)
            dv_ref[rows, lanes] = dot(low, d_att, TN).astype(BF)
            d_probs = dot(d_att, value, NT)
            d_scores = (probs * (d_probs - jnp.sum(probs * d_probs, axis=1, keepdims=True))).astype(BF)
            d_q = dot(d_scores, k_ref[rows, two], NN) * scale
            d_k = dot(d_scores, q_ref[rows, two], TN) * scale
            dq_ref[rows, lanes] = (d_q[:, :PAD] * cos - d_q[:, PAD:] * sin).astype(BF)
            dk_ref[rows, lanes] = (d_k[:, :PAD] * cos - d_k[:, PAD:] * sin).astype(BF)

    def send(group, grad):
        for s in range(4):
            mine_ref[s, group] = grad[s * span : (s + 1) * span, :half_d]
            for p in range(4):
                at = s * span + p * small
                theirs_ref[p, group, s * small : (s + 1) * small] = grad[at : at + small, half_d:]

    hidden, slope = gelu_parts(dot(normed_ref[...], win_ref[...], NT) + bias_ref[...])
    hidden = hidden.astype(BF)
    branch_ref[...] = dot(at_heads_ref[...], wo_ref[...], NN) + dot(hidden, wback_ref[...], NN)
    send(2, dot(hidden, cot_ref[...], TN).astype(BF))
    d_pre = (dot(cot_ref[...], wback_ref[...], NT) * slope).astype(BF)
    gbias_ref[...] = jnp.sum(d_pre.astype(F32), axis=0, keepdims=True)
    send(1, dot(d_pre, normed_ref[...], TN).astype(BF))
    total = dot(d_pre, win_ref[...], NN) + dot(dv_ref[...], wv_ref[...], NN)
    for h in range(HEADS):
        one = slice(h * 2 * PAD, h * 2 * PAD + PAD)
        lanes = slice(h * PAD, (h + 1) * PAD)
        total = total + dot(dq_ref[:, lanes], wq_ref[one], NN) + dot(dk_ref[:, lanes], wk_ref[one], NN)
    dnorm_ref[...] = total

    for m, (ref, with_ref) in enumerate(((dq_ref, normed_ref), (dk_ref, normed_ref), (dv_ref, normed_ref), (at_heads_ref, cot_ref))):
        grad = dot(ref[...], with_ref[...], TN).astype(BF)
        for h in range(HEADS):
            nat_ref[m * HC + h * HD : m * HC + (h + 1) * HD] = grad[h * PAD : h * PAD + HD]
    half_rows = n_all // 2
    for group, base in ((0, 0), (3, half_rows)):
        place = home_place(at_ref, iota((half_rows, 128), 0) + base)
        pick = jnp.concatenate([one_hot(iota((half_rows, 128), 1) + b == place) for b in range(0, n_rows, 128)], axis=1)
        send(group, dot(pick, nat_ref[...], NN).astype(BF))


def layer(at, own, got, normed, cot, bias, cos, sin):
    n = normed.shape[0]
    out = lambda shape, dtype: jax.ShapeDtypeStruct(shape, dtype)
    low = lambda *shape: pltpu.VMEM(shape, BF)
    span = got.shape[2]
    units = 4 * span
    return pl.pallas_call(
        layer_kernel,
        out_shape=[out((n, D), F32), out((n, D), F32), out(got.shape, BF), out(got.shape, BF), out(bias.shape, F32)],
        in_specs=[SMEM] + [VM] * 10,
        out_specs=[VM] * 5,
        scratch_shapes=[low(2 * units, D), low(units, D), low(units, D), low(2 * HP, D), low(2 * HP, D), low(HP, D), low(HP, D)]
        + [low(n, 2 * HP), low(n, 2 * HP)]
        + [low(n, HP)] * 6
        + [low(4 * HC, D)],
        compiler_params=pltpu.CompilerParams(vmem_limit_bytes=56 << 20),
        cost_estimate=pl.CostEstimate(flops=12 * 10**9, bytes_accessed=16 << 20, transcendentals=10**6),
    )(at, *own, got, normed, cot, bias, cos, sin)


def body(tokens, cotangent, qkv_weight, out_weight, fc_weight, vectors, qkv_momentum, out_momentum, fc_momentum, vector_first, vector_second):
    zi, xi, yi, ci, ti = (lax.axis_index(a) for a in ALL)
    rows = tokens.shape[0]
    n_att = qkv_weight.shape[3]
    n_fc = fc_weight.shape[3]
    gain, shift = vectors[:D], vectors[D : 2 * D]
    bias_in, bias_out = vectors[2 * D : 2 * D + FF], vectors[2 * D + FF :]

    first = ci == 0
    half_d = D // 2
    left, right = (lambda v: v[..., :half_d]), (lambda v: v[..., half_d:])
    turned = lambda v: jnp.concatenate([right(v), left(v)], axis=-1)
    own_first = lambda v: jnp.where(first, v, turned(v))

    attn_rows = jnp.concatenate([jnp.transpose(qkv_weight[:, :, 0, :], (0, 2, 1)), jnp.transpose(out_weight[:, 0, :])[None]])
    fc_rows = jnp.transpose(fc_weight[:, :, 0, :], (0, 2, 1))
    own_rows = own_first(jnp.concatenate([attn_rows.reshape(1, n_fc, D), fc_rows]).astype(BF))
    held = jnp.stack([left(own_rows), pull(right(own_rows), "c", 1)])
    held = jnp.stack([held, pull_yh(held, 1)], axis=2)
    held = jnp.stack([held] + [pull_inner(held, k) for k in (1, 2, 3)], axis=2)
    span = 8 * n_fc
    held = held.reshape(2, 3, span, half_d)
    held = [held] + [pull_outer(held, k) for k in (1, 2, 3)]
    got = pull(jnp.stack([jnp.concatenate([v[1], v[0, :1]]) for v in held]), "c", 1)

    inputs = tokens.astype(F32)
    average = jnp.mean(inputs, axis=-1, keepdims=True)
    deviation = inputs - average
    variance = jnp.mean(deviation * deviation, axis=-1, keepdims=True)
    inv_spread = lax.rsqrt(variance + 1e-05)
    centred = deviation * inv_spread
    normed_own = (centred * gain + shift).astype(BF)
    both = own_first(jnp.stack([normed_own, cotangent]))
    both = jnp.stack([both, pull(both, "t", 1)], axis=1)
    both = jnp.stack([both, turned(pull(both, "c", 1))], axis=1)
    n_all = 4 * rows
    normed, cot = both[0].reshape(n_all, D), both[1].reshape(n_all, D)

    half = jnp.arange(LEN) // rows
    position = ((ti + half) % 2) * rows + jnp.arange(LEN) % rows
    frequency = 10000.0 ** (-2.0 * jnp.arange(ROT // 2, dtype=F32) / ROT)
    angles = position.astype(F32)[:, None] * frequency[None, :]
    cos_t, sin_t = jnp.cos(angles), jnp.sin(angles)
    pad = lambda a, b, fill: jnp.concatenate([a, b, jnp.full((LEN, PAD - ROT), fill, F32)], axis=1)
    cos_full, sin_full = pad(cos_t, cos_t, 1.0), pad(-sin_t, sin_t, 0.0)

    bias6 = bias_in.reshape(2, 4, 4, 2, 2, n_fc)
    bias6 = jnp.concatenate([bias6, bias6], axis=1)
    bias6 = jnp.concatenate([bias6, bias6], axis=2)
    bias6 = jnp.concatenate([bias6, bias6], axis=3)
    bias_own = lax.dynamic_slice(bias6, (ti, zi, xi, yi, ci, 0), (1, 4, 4, 2, 1, n_fc))[0, :, :, :, 0]
    by_turn = lambda v: jnp.where(first, jnp.swapaxes(v, 0, 1), v)
    bias_own = by_turn(bias_own).reshape(1, 32 * n_fc)
    at = jnp.stack([zi, xi, yi, ci, ti]).astype(jnp.int32)
    branch, d_normed, sent_mine, sent_theirs, grad_bias_in = layer(at, held, got, normed, cot, bias_own, cos_full, sin_full)

    from_core = pull(sent_theirs, "c", 1)
    parts = [
        jnp.stack(
            [
                jnp.concatenate([mine[:1] + other[3:], mine[1:3]]),
                jnp.concatenate([mine[3:] + other[:1], other[1:3]]),
            ]
        )
        for mine, other in zip(sent_mine, from_core)
    ]
    total = sum_ring(parts, pull_outer).reshape(2, 3, 4, 2, n_fc, half_d)
    total = sum_ring([total[:, :, k] for k in range(4)], pull_inner)
    total = sum_ring([total[:, :, k] for k in range(2)], pull_yh)
    total = own_first(jnp.concatenate([total[0], pull(total[1], "c", 1)], axis=-1)).reshape(3 * n_fc, D)

    def own_rows_of(v):
        v = v.reshape(2, 2, rows, D)
        v = v[0] + turned(pull(v[1], "c", 1))
        return own_first(v[0] + pull(v[1].astype(BF), "t", 1).astype(F32))

    mixed = (inputs + own_rows_of(branch) + bias_out).astype(BF)

    d_rows = own_rows_of(d_normed)
    d_hat = d_rows * gain
    correction = d_hat - jnp.mean(d_hat, axis=-1, keepdims=True) - centred * jnp.mean(d_hat * centred, axis=-1, keepdims=True)
    own_cot = cotangent.astype(F32)
    input_grad = own_cot + correction * inv_spread

    spread = jnp.zeros((2, 8, 8, 4, 2, n_fc), F32)
    bias_grad = by_turn(grad_bias_in.reshape(4, 4, 2, n_fc))[None, :, :, :, None]
    spread = lax.dynamic_update_slice(spread, bias_grad, (ti, zi, xi, yi, ci, 0))
    spread = spread.reshape(2, 2, 4, 2, 4, 2, 2, 2, n_fc).sum(axis=(1, 3, 5))
    vector_part = jnp.concatenate([jnp.sum(d_rows * centred, axis=0), jnp.sum(d_rows, axis=0), spread.reshape(FF), jnp.sum(own_cot, axis=0)])

    mom_rows = jnp.concatenate(
        [
            jnp.transpose(qkv_momentum[:, :, 0, :], (0, 2, 1)).reshape(3 * n_att, D),
            jnp.transpose(out_momentum[:, 0, :]),
            jnp.transpose(fc_momentum[:, :, 0, :], (0, 2, 1)).reshape(2 * n_fc, D),
        ]
    )
    moment = 0.95 * mom_rows + total
    update = total + 0.95 * moment

    half_fc = n_fc // 2
    att_u = update[: 4 * n_att].reshape(4, n_att, D)
    att_u = jnp.concatenate([att_u, jnp.zeros((4, half_fc - n_att, D), F32)], axis=1)
    fc_u = update[4 * n_att :].reshape(4, half_fc, D)
    vec_rows = jnp.concatenate([vector_part.reshape(VEC // D, D), jnp.zeros((VEC_ROWS - VEC // D, D), F32)])
    chunks = jnp.concatenate([att_u, fc_u])
    chunks = jnp.concatenate([chunks, jnp.broadcast_to(vec_rows, (8, VEC_ROWS, D))], axis=1)
    got = lax.all_to_all(chunks, ("z", "t"), split_axis=0, concat_axis=0, tiled=True)
    mine = got[:, :half_fc].reshape(8 * half_fc, D)
    vec_sum = jnp.sum(got[:, half_fc:], axis=0)[:8]
    to_yh_x = lambda k: lambda z, x, y, c, t: (z, x, y + 1, c, t) if c == 0 else (z, x + k, y, c, t)
    to_x_yh = lambda k: lambda z, x, y, c, t: (z, x + k, y, c, t) if c == 0 else (z, x, y + 1, c, t)
    only = lambda core, source: lambda z, x, y, c, t: source(z, x, y, c, t) if c == core else None
    n = mine.shape[0]
    load = jnp.concatenate([mine, vec_sum])
    near = [load, move(load, to_yh_x(1)), move(load, only(1, to_yh_x(2))), move(load, only(1, to_yh_x(3)))]
    vec_sum = sum(v[n:] for v in near)
    load = jnp.concatenate([near[0][:n], near[1][:n], vec_sum])
    load_2 = jnp.where(first, load, jnp.concatenate([near[2][:n], near[3][:n], jnp.zeros_like(vec_sum)]))
    far = [move(load, to_x_yh(1)), move(load_2, to_x_yh(2)), move(load, only(0, to_x_yh(3)))]
    vec_sum = vec_sum + sum(v[2 * n :] for v in far)
    core = ci.astype(jnp.int32)[None]
    keep, give = gram_parts(core, near + far)
    from_core = pull(jnp.concatenate([give, vec_sum]), "c", 1)
    part = keep + from_core[:BLK]
    vec_sum = vec_sum + from_core[BLK:]
    other = pull(part, "t", 1)
    part = jnp.where(zi >= 2, part + other, part)
    rest = pull(part, "c", 1)
    x_rows = sweeps(core, part, rest, mine)
    vector_grad = vec_sum[: VEC // D].reshape(VEC)
    first_new = 0.9 * vector_first + 0.1 * vector_grad
    second_new = 0.95 * vector_second + 0.05 * vector_grad * vector_grad
    step_size = first_new / (1.0 - 0.9**STEP) / (jnp.sqrt(second_new / (1.0 - 0.95**STEP)) + 1e-08)
    vector_new = vectors - 0.2 * step_size

    back = lax.all_to_all(x_rows, ("z", "t"), split_axis=0, concat_axis=0, tiled=True).reshape(8, half_fc, D)
    att_x = back[:4, :n_att]
    fc_x = back[4:].reshape(2, n_fc, D)

    def cols(v):
        return jnp.transpose(v, (0, 2, 1))[:, :, None, :]

    fc_factor = math.sqrt(FF / D)
    qkv_new = qkv_weight * 0.99 - cols(att_x[:3])
    out_new = out_weight * 0.99 - cols(att_x[3:])[0]
    fc_new = fc_weight * 0.99 - fc_factor * cols(fc_x)
    att_m = moment[: 4 * n_att].reshape(4, n_att, D)
    fc_m = moment[4 * n_att :].reshape(2, n_fc, D)
    return (mixed, input_grad, qkv_new, out_new, fc_new, cols(att_m[:3]), cols(att_m[3:])[0], cols(fc_m), first_new, second_new, vector_new)


def solution(mesh):
    mesh = Mesh(mesh.devices.reshape(4, 4, 2, 2, 2), ALL)
    rows = P(ALL, None)
    w3 = P(None, None, "t", DP)
    w2 = P(None, "t", DP)
    vec = P()
    in_specs = (rows, rows, w3, w2, w3, vec, w3, w2, w3, vec, vec)
    out_specs = (rows, rows, w3, w2, w3, w3, w2, w3, vec, vec, vec)
    return jax.shard_map(body, mesh=mesh, in_specs=in_specs, out_specs=out_specs, check_vma=False)
```

```python
import functools
import itertools
import math

import jax
import jax.numpy as jnp
from jax import lax
from jax.experimental import pallas as pl
from jax.experimental.pallas import tpu as pltpu
from jax.sharding import Mesh, PartitionSpec as P

D = 768
H = 12
HD = 64
ROT = 16
FF = 3072
SWEEPS = 5
STEP = 10
LEN = 256
VEC = 2 * D + FF + D
VEC_ROWS = 12

NS = (3.4445, -4.775, 2.0315)
BF = jnp.bfloat16
F32 = jnp.float32
BLK = 256
BLK_ROWS = 96
NB = D // BLK

DP = ("z", "x", "yh", "c")
ALL = ("z", "x", "yh", "c", "t")


def pull(value, axis, k):
    n = lax.axis_size(axis)
    return lax.ppermute(value, axis, [((i + k) % n, i) for i in range(n)])


def move(value, source):
    sizes = [lax.axis_size(a) for a in ALL]
    index = lambda at: functools.reduce(lambda total, one: total * one[0] + one[1] % one[0], zip(sizes, at), 0)
    pairs = []
    for here in itertools.product(*map(range, sizes)):
        there = source(*here)
        if there is not None:
            pairs.append((index(there), index(here)))
    return lax.ppermute(value, ALL, pairs)


def pull_outer(value, k):
    return move(value, lambda z, x, y, c, t: (z, x + k, y, c, t) if c == 0 else (z + k, x, y, c, t))


def pull_inner(value, k):
    return move(value, lambda z, x, y, c, t: (z + k, x, y, c, t) if c == 0 else (z, x + k, y, c, t))


def pull_yh(value, k):
    return pull(value, "yh", k)


def sum_ring(parts, pulls):
    n = len(parts)
    total = parts[0].astype(F32)
    for k in range(1, n):
        total = total + pulls(parts[k].astype(BF), n - k).astype(F32)
    return total


def dot(a, b, dims):
    return lax.dot_general(a, b, (dims, ((), ())), preferred_element_type=F32)


def pieces(value, n):
    out = []
    for _ in range(n):
        low = value.astype(BF)
        out.append(low)
        value = value - low.astype(F32)
    return out


def mul(xs, ys, dims=((1,), (0,))):
    n = len(xs)
    total = None
    for order in reversed(range(n)):
        for i in range(order + 1):
            term = lax.dot_general(xs[i], ys[order - i], (dims, ((), ())), preferred_element_type=F32)
            total = term if total is None else total + term
    return total


def gram_kernel(core_ref, *refs):
    *in_refs, keep_ref, give_ref, wide_ref = refs
    at = 0
    for ref in in_refs:
        n = ref.shape[0] // BLK_ROWS * BLK_ROWS
        for k, piece in enumerate(pieces(ref[:n], 3)):
            wide_ref[k, at : at + n] = piece
        at += n
    xs = [wide_ref[k] for k in range(3)]
    dims = ((0,), (0,))
    cut = lambda i: slice(i * BLK, (i + 1) * BLK)
    top = mul([x[:, cut(0)] for x in xs], xs, dims)
    mid = mul([x[:, cut(1)] for x in xs], [x[:, BLK:] for x in xs], dims)
    low = mul([x[:, cut(2)] for x in xs], [x[:, 2 * BLK :] for x in xs], dims)
    first = core_ref[0] == 0

    @pl.when(first)
    def _():
        keep_ref[...] = top
        give_ref[:, : 2 * BLK] = mid
        give_ref[:, 2 * BLK :] = low

    @pl.when(jnp.logical_not(first))
    def _():
        give_ref[...] = top
        keep_ref[:, : 2 * BLK] = mid
        keep_ref[:, 2 * BLK :] = low


def blocks(i, j):
    return (slice(i * BLK, (i + 1) * BLK), slice(j * BLK, (j + 1) * BLK))


def put(refs, i, j, value):
    for ref, piece in zip(refs, pieces(value, len(refs))):
        ref[blocks(i, j)] = piece


def put_both(refs, i, j, value):
    put(refs, i, j, value)
    if i != j:
        put(refs, j, i, value.T)


def symmetric_product(xs, ys, emit, start=0):
    for i in range(start, NB):
        rows = slice(i * BLK, (i + 1) * BLK)
        wide = mul([x[rows, :] for x in xs], [y[:, i * BLK :] for y in ys])
        for j in range(i, NB):
            emit(i, j, wide[:, (j - i) * BLK : (j - i + 1) * BLK])


def sweeps_kernel(core_ref, mine_ref, rest_ref, x_ref, out_ref, top_ref, bottom_ref, gram_ref, a_ref, p_ref, b_ref):
    first = core_ref[0] == 0
    n_x = x_ref.shape[0]

    @pl.when(first)
    def _():
        top_ref[...] = mine_ref[...]
        bottom_ref[...] = rest_ref[...]

    @pl.when(jnp.logical_not(first))
    def _():
        top_ref[...] = rest_ref[...]
        bottom_ref[...] = mine_ref[...]

    def packed(i, j):
        if i == 0:
            return top_ref[:, j * BLK : (j + 1) * BLK]
        at = (j - 1) if i == 1 else 2
        return bottom_ref[:, at * BLK : (at + 1) * BLK]

    eye = (lax.broadcasted_iota(jnp.int32, (BLK, BLK), 0) == lax.broadcasted_iota(jnp.int32, (BLK, BLK), 1)).astype(F32)
    trace = sum(jnp.sum(packed(i, i) * eye) for i in range(NB))
    norm = jnp.sqrt(jnp.full((8, 128), trace, F32)) + 1e-07
    factor = (1.0 / norm)[0:1, 0:1]
    square = factor * factor

    a_rows = lambda n: [a_ref.at[k, n_x : n_x + D] for k in range(n)]
    p_rows = lambda n: [p_ref.at[k] for k in range(n)]
    b_rows = lambda n: [b_ref.at[k] for k in range(n)]

    def put_x(n, value):
        for k, piece in enumerate(pieces(value, n)):
            a_ref[k, :n_x] = piece

    for i in range(NB):
        for j in range(i, NB):
            value = packed(i, j) * square
            gram_ref[blocks(i, j)] = value
            put_both(a_rows(3), i, j, value)
    put_x(3, x_ref[...] * factor)

    def poly(n_p):
        def emit(i, j, block):
            value = NS[1] * gram_ref[blocks(i, j)] + NS[2] * block
            if i == j:
                value = value + NS[0] * eye
            put_both(p_rows(n_p), i, j, value)

        a = a_rows(2)
        symmetric_product(a, a, emit)

    def next_gram(n, keep):
        p = p_rows(n)
        rows = slice(0, n_x + BLK)
        wide = mul([a_ref[k, rows] for k in range(n)], [y[...] for y in p])
        for j in range(NB):
            put_both(b_rows(n), 0, j, wide[n_x:, j * BLK : (j + 1) * BLK])
        symmetric_product(a_rows(n), p, lambda i, j, block: put_both(b_rows(n), i, j, block), 1)
        put_x(keep, wide[:n_x])

        def emit(i, j, block):
            gram_ref[blocks(i, j)] = block
            put_both(a_rows(keep), i, j, block)

        symmetric_product(b_rows(n), p, emit)

    poly(3)
    next_gram(3, 2)

    @pl.loop(1, SWEEPS - 1)
    def _(_):
        poly(2)
        next_gram(2, 2)

    poly(2)
    out_ref[...] = mul([a_ref[k, :n_x] for k in range(2)], [y[...] for y in p_rows(2)])


SMEM = pl.BlockSpec(memory_space=pltpu.SMEM)
VM = pl.BlockSpec(memory_space=pltpu.VMEM)


def gram_parts(core, held):
    rows = sum(v.shape[0] // BLK_ROWS * BLK_ROWS for v in held)
    return pl.pallas_call(
        gram_kernel,
        out_shape=[jax.ShapeDtypeStruct((BLK, D), F32)] * 2,
        in_specs=[SMEM] + [VM] * len(held),
        out_specs=[VM, VM],
        scratch_shapes=[pltpu.VMEM((3, rows, D), BF)],
        compiler_params=pltpu.CompilerParams(vmem_limit_bytes=48 << 20),
        cost_estimate=pl.CostEstimate(flops=2 * D * D * D * 4, bytes_accessed=4 * D * D * 2, transcendentals=0),
    )(core, *held)


def sweeps(core, mine, rest, x_rows):
    return pl.pallas_call(
        sweeps_kernel,
        out_shape=jax.ShapeDtypeStruct(x_rows.shape, F32),
        in_specs=[SMEM, VM, VM, VM],
        out_specs=VM,
        scratch_shapes=[
            pltpu.VMEM((BLK, D), F32),
            pltpu.VMEM((BLK, D), F32),
            pltpu.VMEM((D, D), F32),
            pltpu.VMEM((3, x_rows.shape[0] + D, D), BF),
            pltpu.VMEM((3, D, D), BF),
            pltpu.VMEM((3, D, D), BF),
        ],
        compiler_params=pltpu.CompilerParams(vmem_limit_bytes=48 << 20),
        cost_estimate=pl.CostEstimate(flops=2 * D * D * D * 32, bytes_accessed=4 * D * D, transcendentals=0),
    )(core, mine, rest, x_rows)


def gelu_parts(u):
    k0 = math.sqrt(2.0 / math.pi)
    th = jnp.tanh(k0 * (u + 0.044715 * (u * u * u)))
    value = 0.5 * u * (1.0 + th)
    slope = 0.5 * (1.0 + th) + 0.5 * u * (1.0 - th * th) * (k0 * (1.0 + 3.0 * 0.044715 * u * u))
    return value, slope


HEADS = 3
PAD = 128
HC = HEADS * HD
HP = HEADS * PAD
NN = ((1,), (0,))
NT = ((1,), (1,))
TN = ((0,), (0,))


def iota(shape, dim):
    return lax.broadcasted_iota(jnp.int32, shape, dim)


def one_hot(cond):
    return jnp.where(cond, 1.0, 0.0).astype(BF)


def home_place(at_ref, r):
    zi, xi, yi, ci = (at_ref[k] for k in range(4))
    n = 6
    group = jnp.right_shift(r * 10923, 16)
    lane = r - n * group
    mat = jnp.bitwise_and(group, 3)
    y = jnp.bitwise_and(jnp.right_shift(group, 2) + yi, 1)
    inner = jnp.bitwise_and(jnp.right_shift(group, 3), 3)
    outer = jnp.bitwise_and(jnp.right_shift(group, 5), 3)
    core = jnp.bitwise_and(jnp.right_shift(group, 7) + ci, 1)
    first = ci == 0
    z = jnp.bitwise_and(jnp.where(first, inner, outer) + zi, 3)
    x = jnp.bitwise_and(jnp.where(first, outer, inner) + xi, 3)
    column = (((z * 4 + x) * 2 + y) * 2 + core) * n + lane - HC * ci
    return jnp.where((column >= 0) & (column < HC), mat * HC + column, -1)


def layer_kernel(
    at_ref, own0_ref, own1_ref, own2_ref, own3_ref, got0_ref, got1_ref, got2_ref, got3_ref, normed_ref, cot_ref, bias_ref, cos_ref, sin_ref,
    branch_ref, dnorm_ref, mine_ref, theirs_ref, gbias_ref,
    att_ref, win_ref, wback_ref, wq_ref, wk_ref, wv_ref, wo_ref, q_ref, k_ref, v_ref, da_ref, at_heads_ref, dq_ref, dk_ref, dv_ref, nat_ref,
):
    got_refs = (got0_ref, got1_ref, got2_ref, got3_ref)
    span = got0_ref.shape[2]
    small = span // 4
    half_d = D // 2
    for s, ref in enumerate((own0_ref, own1_ref, own2_ref, own3_ref)):
        for to_ref, base, c, group in ((att_ref, 0, 0, 0), (att_ref, 4 * span, 1, 0), (win_ref, 0, 0, 1), (wback_ref, 0, 0, 2)):
            at = base + s * span
            to_ref[at : at + span, :half_d] = ref[c, group]
            for p, got_ref in enumerate(got_refs):
                to_ref[at + p * small : at + (p + 1) * small, half_d:] = got_ref[1 - c, group, s * small : (s + 1) * small]
    n_rows, n_all = 4 * HC, att_ref.shape[0]

    pick = one_hot(iota((n_rows, n_all), 0) == home_place(at_ref, iota((8, n_all), 1))[:1])
    w_att = dot(pick, att_ref[...], NN).astype(BF)
    r = iota((HC, HC), 0)
    e = jnp.bitwise_and(r, HD - 1)
    half = ROT // 2
    source = jnp.where(e < half, r + half, jnp.where(e < ROT, r - half, -1))
    exchange = one_hot(iota((HC, HC), 1) == source)
    blank = jnp.zeros((HD, D), BF)
    for m, ref in enumerate((wq_ref, wk_ref)):
        own = w_att[m * HC : (m + 1) * HC]
        swapped = dot(exchange, own, NN).astype(BF)
        for h in range(HEADS):
            base = h * 2 * PAD
            ref[base : base + HD] = own[h * HD : (h + 1) * HD]
            ref[base + HD : base + PAD] = blank
            ref[base + PAD : base + PAD + HD] = swapped[h * HD : (h + 1) * HD]
            ref[base + PAD + HD : base + 2 * PAD] = blank
    for m, ref in ((2, wv_ref), (3, wo_ref)):
        for h in range(HEADS):
            ref[h * PAD : h * PAD + HD] = w_att[m * HC + h * HD : m * HC + (h + 1) * HD]
            ref[h * PAD + HD : (h + 1) * PAD] = blank

    cos, sin = cos_ref[...], sin_ref[...]
    for w_ref, ref in ((wq_ref, q_ref), (wk_ref, k_ref)):
        lin = dot(normed_ref[...], w_ref[...], NT)
        for s in range(2):
            rows = slice(s * LEN, (s + 1) * LEN)
            for h in range(HEADS):
                base = h * 2 * PAD
                own, other = lin[rows, base : base + PAD], lin[rows, base + PAD : base + 2 * PAD]
                ref[rows, base : base + PAD] = (own * cos + other * sin).astype(BF)
                ref[rows, base + PAD : base + 2 * PAD] = (other * cos - own * sin).astype(BF)
    v_ref[...] = dot(normed_ref[...], wv_ref[...], NT).astype(BF)
    da_ref[...] = dot(cot_ref[...], wo_ref[...], NT).astype(BF)

    turn = at_ref[4] * (LEN // 2)
    at_q = jnp.bitwise_xor(iota((LEN, LEN), 0), turn)
    at_k = jnp.bitwise_xor(iota((LEN, LEN), 1), turn)
    causal = at_q >= at_k
    scale = HD ** (-0.5)
    for s in range(2):
        rows = slice(s * LEN, (s + 1) * LEN)
        for h in range(HEADS):
            two = slice(h * 2 * PAD, (h + 1) * 2 * PAD)
            one = slice(h * 2 * PAD, h * 2 * PAD + PAD)
            lanes = slice(h * PAD, (h + 1) * PAD)
            value, d_att = v_ref[rows, lanes], da_ref[rows, lanes]
            scores = jnp.where(causal, dot(q_ref[rows, one], k_ref[rows, one], NT) * scale, -1e30)
            raised = jnp.exp(scores - jnp.max(scores, axis=1, keepdims=True))
            probs = raised / jnp.sum(raised, axis=1, keepdims=True)
            low = probs.astype(BF)
            at_heads_ref[rows, lanes] = dot(low, value, NN).astype(BF)
            dv_ref[rows, lanes] = dot(low, d_att, TN).astype(BF)
            d_probs = dot(d_att, value, NT)
            d_scores = (probs * (d_probs - jnp.sum(probs * d_probs, axis=1, keepdims=True))).astype(BF)
            d_q = dot(d_scores, k_ref[rows, two], NN) * scale
            d_k = dot(d_scores, q_ref[rows, two], TN) * scale
            dq_ref[rows, lanes] = (d_q[:, :PAD] * cos - d_q[:, PAD:] * sin).astype(BF)
            dk_ref[rows, lanes] = (d_k[:, :PAD] * cos - d_k[:, PAD:] * sin).astype(BF)

    def send(group, grad):
        for s in range(4):
            mine_ref[s, group] = grad[s * span : (s + 1) * span, :half_d]
            for p in range(4):
                at = s * span + p * small
                theirs_ref[p, group, s * small : (s + 1) * small] = grad[at : at + small, half_d:]

    hidden, slope = gelu_parts(dot(normed_ref[...], win_ref[...], NT) + bias_ref[...])
    hidden = hidden.astype(BF)
    branch_ref[...] = dot(at_heads_ref[...], wo_ref[...], NN) + dot(hidden, wback_ref[...], NN)
    send(2, dot(hidden, cot_ref[...], TN).astype(BF))
    d_pre = (dot(cot_ref[...], wback_ref[...], NT) * slope).astype(BF)
    gbias_ref[...] = jnp.sum(d_pre.astype(F32), axis=0, keepdims=True)
    send(1, dot(d_pre, normed_ref[...], TN).astype(BF))
    total = dot(d_pre, win_ref[...], NN) + dot(dv_ref[...], wv_ref[...], NN)
    for h in range(HEADS):
        one = slice(h * 2 * PAD, h * 2 * PAD + PAD)
        lanes = slice(h * PAD, (h + 1) * PAD)
        total = total + dot(dq_ref[:, lanes], wq_ref[one], NN) + dot(dk_ref[:, lanes], wk_ref[one], NN)
    dnorm_ref[...] = total

    for m, (ref, with_ref) in enumerate(((dq_ref, normed_ref), (dk_ref, normed_ref), (dv_ref, normed_ref), (at_heads_ref, cot_ref))):
        grad = dot(ref[...], with_ref[...], TN).astype(BF)
        for h in range(HEADS):
            nat_ref[m * HC + h * HD : m * HC + (h + 1) * HD] = grad[h * PAD : h * PAD + HD]
    half_rows = n_all // 2
    for group, base in ((0, 0), (3, half_rows)):
        place = home_place(at_ref, iota((half_rows, 128), 0) + base)
        pick = jnp.concatenate([one_hot(iota((half_rows, 128), 1) + b == place) for b in range(0, n_rows, 128)], axis=1)
        send(group, dot(pick, nat_ref[...], NN).astype(BF))


def layer(at, own, got, normed, cot, bias, cos, sin):
    n = normed.shape[0]
    out = lambda shape, dtype: jax.ShapeDtypeStruct(shape, dtype)
    low = lambda *shape: pltpu.VMEM(shape, BF)
    span = got[0].shape[2]
    units = 4 * span
    return pl.pallas_call(
        layer_kernel,
        out_shape=[out((n, D), F32), out((n, D), F32), out((4, 4, span, D // 2), BF), out((4, 4, span, D // 2), BF), out(bias.shape, F32)],
        in_specs=[SMEM] + [VM] * 13,
        out_specs=[VM] * 5,
        scratch_shapes=[low(2 * units, D), low(units, D), low(units, D), low(2 * HP, D), low(2 * HP, D), low(HP, D), low(HP, D)]
        + [low(n, 2 * HP), low(n, 2 * HP)]
        + [low(n, HP)] * 6
        + [low(4 * HC, D)],
        compiler_params=pltpu.CompilerParams(vmem_limit_bytes=56 << 20),
        cost_estimate=pl.CostEstimate(flops=12 * 10**9, bytes_accessed=16 << 20, transcendentals=10**6),
    )(at, *own, *got, normed, cot, bias, cos, sin)


def pack_kernel(mine_ref, other_ref, *out_refs):
    for s, ref in enumerate(out_refs):
        ref[0, 0] = mine_ref[s, 0] + other_ref[s, 3]
        ref[1, 0] = mine_ref[s, 3] + other_ref[s, 0]
        for group in (1, 2):
            ref[0, group] = mine_ref[s, group]
            ref[1, group] = other_ref[s, group]


def pack(mine, other):
    shape = (2, 3) + mine.shape[2:]
    return pl.pallas_call(
        pack_kernel,
        out_shape=[jax.ShapeDtypeStruct(shape, BF)] * 4,
        in_specs=[VM] * 2,
        out_specs=[VM] * 4,
        compiler_params=pltpu.CompilerParams(vmem_limit_bytes=32 << 20),
        cost_estimate=pl.CostEstimate(flops=0, bytes_accessed=8 << 20, transcendentals=0),
    )(mine, other)


def body(tokens, cotangent, qkv_weight, out_weight, fc_weight, vectors, qkv_momentum, out_momentum, fc_momentum, vector_first, vector_second):
    zi, xi, yi, ci, ti = (lax.axis_index(a) for a in ALL)
    rows = tokens.shape[0]
    n_att = qkv_weight.shape[3]
    n_fc = fc_weight.shape[3]
    gain, shift = vectors[:D], vectors[D : 2 * D]
    bias_in, bias_out = vectors[2 * D : 2 * D + FF], vectors[2 * D + FF :]

    first = ci == 0
    half_d = D // 2
    left, right = (lambda v: v[..., :half_d]), (lambda v: v[..., half_d:])
    turned = lambda v: jnp.concatenate([right(v), left(v)], axis=-1)
    own_first = lambda v: jnp.where(first, v, turned(v))

    attn_rows = jnp.concatenate([jnp.transpose(qkv_weight[:, :, 0, :], (0, 2, 1)), jnp.transpose(out_weight[:, 0, :])[None]])
    fc_rows = jnp.transpose(fc_weight[:, :, 0, :], (0, 2, 1))
    own_rows = own_first(jnp.concatenate([attn_rows.reshape(1, n_fc, D), fc_rows]).astype(BF))
    held = jnp.stack([left(own_rows), pull(right(own_rows), "c", 1)])
    held = jnp.stack([held, pull_yh(held, 1)], axis=2)
    held = jnp.stack([held] + [pull_inner(held, k) for k in (1, 2, 3)], axis=2)

    inputs = tokens.astype(F32)
    average = jnp.mean(inputs, axis=-1, keepdims=True)
    deviation = inputs - average
    variance = jnp.mean(deviation * deviation, axis=-1, keepdims=True)
    inv_spread = lax.rsqrt(variance + 1e-05)
    centred = deviation * inv_spread
    normed_own = (centred * gain + shift).astype(BF)
    both = own_first(jnp.stack([normed_own, cotangent]))
    both = jnp.stack([both, pull(both, "t", 1)], axis=1)

    held, both = lax.optimization_barrier((held, both))
    span = 8 * n_fc
    held = held.reshape(2, 3, span, half_d)
    held = [held] + [pull_outer(held, k) for k in (1, 2, 3)]

    both = jnp.stack([both, turned(pull(both, "c", 1))], axis=1)
    n_all = 4 * rows
    normed, cot = both[0].reshape(n_all, D), both[1].reshape(n_all, D)

    half = jnp.arange(LEN) // rows
    position = ((ti + half) % 2) * rows + jnp.arange(LEN) % rows
    frequency = 10000.0 ** (-2.0 * jnp.arange(ROT // 2, dtype=F32) / ROT)
    angles = position.astype(F32)[:, None] * frequency[None, :]
    cos_t, sin_t = jnp.cos(angles), jnp.sin(angles)
    pad = lambda a, b, fill: jnp.concatenate([a, b, jnp.full((LEN, PAD - ROT), fill, F32)], axis=1)
    cos_full, sin_full = pad(cos_t, cos_t, 1.0), pad(-sin_t, sin_t, 0.0)

    bias6 = bias_in.reshape(2, 4, 4, 2, 2, n_fc)
    bias6 = jnp.concatenate([bias6, bias6], axis=1)
    bias6 = jnp.concatenate([bias6, bias6], axis=2)
    bias6 = jnp.concatenate([bias6, bias6], axis=3)
    bias_own = lax.dynamic_slice(bias6, (ti, zi, xi, yi, ci, 0), (1, 4, 4, 2, 1, n_fc))[0, :, :, :, 0]
    by_turn = lambda v: jnp.where(first, jnp.swapaxes(v, 0, 1), v)
    bias_own = by_turn(bias_own).reshape(1, 32 * n_fc)
    at = jnp.stack([zi, xi, yi, ci, ti]).astype(jnp.int32)
    far, normed, cot, bias_own, at, cos_full, sin_full = lax.optimization_barrier((held[1:], normed, cot, bias_own, at, cos_full, sin_full))
    held = [held[0]] + far
    got = [pull(v, "c", 1) for v in held]
    branch, d_normed, sent_mine, sent_theirs, grad_bias_in = layer(at, held, got, normed, cot, bias_own, cos_full, sin_full)

    from_core = pull(sent_theirs, "c", 1)
    parts = pack(sent_mine, from_core)
    parts, branch, d_normed = lax.optimization_barrier((parts, branch, d_normed))
    total = sum_ring(parts, pull_outer).reshape(2, 3, 4, 2, n_fc, half_d)
    total = sum_ring([total[:, :, k] for k in range(4)], pull_inner)
    total = sum_ring([total[:, :, k] for k in range(2)], pull_yh)
    total = own_first(jnp.concatenate([total[0], pull(total[1], "c", 1)], axis=-1)).reshape(3 * n_fc, D)

    def own_rows_of(v):
        v = v.reshape(2, 2, rows, D)
        v = v[0] + turned(pull(v[1], "c", 1))
        return own_first(v[0] + pull(v[1].astype(BF), "t", 1).astype(F32))

    mixed = (inputs + own_rows_of(branch) + bias_out).astype(BF)

    d_rows = own_rows_of(d_normed)
    d_hat = d_rows * gain
    correction = d_hat - jnp.mean(d_hat, axis=-1, keepdims=True) - centred * jnp.mean(d_hat * centred, axis=-1, keepdims=True)
    own_cot = cotangent.astype(F32)
    input_grad = own_cot + correction * inv_spread

    spread = jnp.zeros((2, 8, 8, 4, 2, n_fc), F32)
    bias_grad = by_turn(grad_bias_in.reshape(4, 4, 2, n_fc))[None, :, :, :, None]
    spread = lax.dynamic_update_slice(spread, bias_grad, (ti, zi, xi, yi, ci, 0))
    spread = spread.reshape(2, 2, 4, 2, 4, 2, 2, 2, n_fc).sum(axis=(1, 3, 5))
    vector_part = jnp.concatenate([jnp.sum(d_rows * centred, axis=0), jnp.sum(d_rows, axis=0), spread.reshape(FF), jnp.sum(own_cot, axis=0)])

    mom_rows = jnp.concatenate(
        [
            jnp.transpose(qkv_momentum[:, :, 0, :], (0, 2, 1)).reshape(3 * n_att, D),
            jnp.transpose(out_momentum[:, 0, :]),
            jnp.transpose(fc_momentum[:, :, 0, :], (0, 2, 1)).reshape(2 * n_fc, D),
        ]
    )
    moment = 0.95 * mom_rows + total
    update = total + 0.95 * moment

    half_fc = n_fc // 2
    att_u = update[: 4 * n_att].reshape(4, n_att, D)
    att_u = jnp.concatenate([att_u, jnp.zeros((4, half_fc - n_att, D), F32)], axis=1)
    fc_u = update[4 * n_att :].reshape(4, half_fc, D)
    vec_rows = jnp.concatenate([vector_part.reshape(VEC // D, D), jnp.zeros((VEC_ROWS - VEC // D, D), F32)])
    chunks = jnp.concatenate([att_u, fc_u])
    chunks = jnp.concatenate([chunks, jnp.broadcast_to(vec_rows, (8, VEC_ROWS, D))], axis=1)
    got = lax.all_to_all(chunks, ("z", "t"), split_axis=0, concat_axis=0, tiled=True)
    mine = got[:, :half_fc].reshape(8 * half_fc, D)
    vec_sum = jnp.sum(got[:, half_fc:], axis=0)[:8]
    to_yh_x = lambda k: lambda z, x, y, c, t: (z, x, y + 1, c, t) if c == 0 else (z, x + k, y, c, t)
    to_x_yh = lambda k: lambda z, x, y, c, t: (z, x + k, y, c, t) if c == 0 else (z, x, y + 1, c, t)
    only = lambda core, source: lambda z, x, y, c, t: source(z, x, y, c, t) if c == core else None
    n = mine.shape[0]
    load = jnp.concatenate([mine, vec_sum])
    near = [load, move(load, to_yh_x(1)), move(load, only(1, to_yh_x(2))), move(load, only(1, to_yh_x(3)))]
    vec_sum = sum(v[n:] for v in near)
    load = jnp.concatenate([near[0][:n], near[1][:n], vec_sum])
    load_2 = jnp.where(first, load, jnp.concatenate([near[2][:n], near[3][:n], jnp.zeros_like(vec_sum)]))
    far = [move(load, to_x_yh(1)), move(load_2, to_x_yh(2)), move(load, only(0, to_x_yh(3)))]
    vec_sum = vec_sum + sum(v[2 * n :] for v in far)
    core = ci.astype(jnp.int32)[None]
    keep, give = gram_parts(core, near + far)
    from_core = pull(jnp.concatenate([give, vec_sum]), "c", 1)
    part = keep + from_core[:BLK]
    vec_sum = vec_sum + from_core[BLK:]
    other = pull(part, "t", 1)
    part = jnp.where(zi >= 2, part + other, part)
    rest = pull(part, "c", 1)
    x_rows = sweeps(core, part, rest, mine)
    vector_grad = vec_sum[: VEC // D].reshape(VEC)
    first_new = 0.9 * vector_first + 0.1 * vector_grad
    second_new = 0.95 * vector_second + 0.05 * vector_grad * vector_grad
    step_size = first_new / (1.0 - 0.9**STEP) / (jnp.sqrt(second_new / (1.0 - 0.95**STEP)) + 1e-08)
    vector_new = vectors - 0.2 * step_size

    back = lax.all_to_all(x_rows, ("z", "t"), split_axis=0, concat_axis=0, tiled=True).reshape(8, half_fc, D)
    att_x = back[:4, :n_att]
    fc_x = back[4:].reshape(2, n_fc, D)

    def cols(v):
        return jnp.transpose(v, (0, 2, 1))[:, :, None, :]

    fc_factor = math.sqrt(FF / D)
    qkv_new = qkv_weight * 0.99 - cols(att_x[:3])
    out_new = out_weight * 0.99 - cols(att_x[3:])[0]
    fc_new = fc_weight * 0.99 - fc_factor * cols(fc_x)
    att_m = moment[: 4 * n_att].reshape(4, n_att, D)
    fc_m = moment[4 * n_att :].reshape(2, n_fc, D)
    return (mixed, input_grad, qkv_new, out_new, fc_new, cols(att_m[:3]), cols(att_m[3:])[0], cols(fc_m), first_new, second_new, vector_new)


def solution(mesh):
    mesh = Mesh(mesh.devices.reshape(4, 4, 2, 2, 2), ALL)
    rows = P(ALL, None)
    w3 = P(None, None, "t", DP)
    w2 = P(None, "t", DP)
    vec = P()
    in_specs = (rows, rows, w3, w2, w3, vec, w3, w2, w3, vec, vec)
    out_specs = (rows, rows, w3, w2, w3, w3, w2, w3, vec, vec, vec)
    return jax.shard_map(body, mesh=mesh, in_specs=in_specs, out_specs=out_specs, check_vma=False)
```

```python
import functools
import itertools
import math

import jax
import jax.numpy as jnp
from jax import lax
from jax.experimental import pallas as pl
from jax.experimental.pallas import tpu as pltpu
from jax.sharding import Mesh, PartitionSpec as P

D = 768
H = 12
HD = 64
ROT = 16
FF = 3072
SWEEPS = 5
STEP = 10
LEN = 256
VEC = 2 * D + FF + D
VEC_ROWS = 12

NS = (3.4445, -4.775, 2.0315)
BF = jnp.bfloat16
F32 = jnp.float32
BLK = 256
BLK_ROWS = 96
NB = D // BLK

DP = ("z", "x", "yh", "c")
ALL = ("z", "x", "yh", "c", "t")


def pull(value, axis, k):
    n = lax.axis_size(axis)
    return lax.ppermute(value, axis, [((i + k) % n, i) for i in range(n)])


def move(value, source):
    sizes = [lax.axis_size(a) for a in ALL]
    index = lambda at: functools.reduce(lambda total, one: total * one[0] + one[1] % one[0], zip(sizes, at), 0)
    pairs = []
    for here in itertools.product(*map(range, sizes)):
        there = source(*here)
        if there is not None:
            pairs.append((index(there), index(here)))
    return lax.ppermute(value, ALL, pairs)


def pull_outer(value, k):
    return move(value, lambda z, x, y, c, t: (z, x + k, y, c, t) if c == 0 else (z + k, x, y, c, t))


def pull_inner(value, k):
    return move(value, lambda z, x, y, c, t: (z + k, x, y, c, t) if c == 0 else (z, x + k, y, c, t))


def pull_yh(value, k):
    return pull(value, "yh", k)


def sum_ring(parts, pulls):
    n = len(parts)
    total = parts[0].astype(F32)
    for k in range(1, n):
        total = total + pulls(parts[k].astype(BF), n - k).astype(F32)
    return total


def dot(a, b, dims):
    return lax.dot_general(a, b, (dims, ((), ())), preferred_element_type=F32)


def pieces(value, n):
    out = []
    for _ in range(n):
        low = value.astype(BF)
        out.append(low)
        value = value - low.astype(F32)
    return out


def mul(xs, ys, dims=((1,), (0,))):
    n = len(xs)
    total = None
    for order in reversed(range(n)):
        for i in range(order + 1):
            term = lax.dot_general(xs[i], ys[order - i], (dims, ((), ())), preferred_element_type=F32)
            total = term if total is None else total + term
    return total


def gram_kernel(core_ref, *refs):
    *in_refs, keep_ref, give_ref, wide_ref = refs
    at = 0
    for ref in in_refs:
        n = ref.shape[0] // BLK_ROWS * BLK_ROWS
        for k, piece in enumerate(pieces(ref[:n], 3)):
            wide_ref[k, at : at + n] = piece
        at += n
    xs = [wide_ref[k] for k in range(3)]
    dims = ((0,), (0,))
    cut = lambda i: slice(i * BLK, (i + 1) * BLK)
    top = mul([x[:, cut(0)] for x in xs], xs, dims)
    mid = mul([x[:, cut(1)] for x in xs], [x[:, BLK:] for x in xs], dims)
    low = mul([x[:, cut(2)] for x in xs], [x[:, 2 * BLK :] for x in xs], dims)
    first = core_ref[0] == 0

    @pl.when(first)
    def _():
        keep_ref[...] = top
        give_ref[:, : 2 * BLK] = mid
        give_ref[:, 2 * BLK :] = low

    @pl.when(jnp.logical_not(first))
    def _():
        give_ref[...] = top
        keep_ref[:, : 2 * BLK] = mid
        keep_ref[:, 2 * BLK :] = low


def blocks(i, j):
    return (slice(i * BLK, (i + 1) * BLK), slice(j * BLK, (j + 1) * BLK))


def put(refs, i, j, value):
    for ref, piece in zip(refs, pieces(value, len(refs))):
        ref[blocks(i, j)] = piece


def put_both(refs, i, j, value):
    put(refs, i, j, value)
    if i != j:
        put(refs, j, i, value.T)


def symmetric_product(xs, ys, emit, start=0):
    for i in range(start, NB):
        rows = slice(i * BLK, (i + 1) * BLK)
        wide = mul([x[rows, :] for x in xs], [y[:, i * BLK :] for y in ys])
        for j in range(i, NB):
            emit(i, j, wide[:, (j - i) * BLK : (j - i + 1) * BLK])


def sweeps_kernel(core_ref, mine_ref, rest_ref, x_ref, out_ref, top_ref, bottom_ref, gram_ref, a_ref, p_ref, b_ref):
    first = core_ref[0] == 0
    n_x = x_ref.shape[0]

    @pl.when(first)
    def _():
        top_ref[...] = mine_ref[...]
        bottom_ref[...] = rest_ref[...]

    @pl.when(jnp.logical_not(first))
    def _():
        top_ref[...] = rest_ref[...]
        bottom_ref[...] = mine_ref[...]

    def packed(i, j):
        if i == 0:
            return top_ref[:, j * BLK : (j + 1) * BLK]
        at = (j - 1) if i == 1 else 2
        return bottom_ref[:, at * BLK : (at + 1) * BLK]

    eye = (lax.broadcasted_iota(jnp.int32, (BLK, BLK), 0) == lax.broadcasted_iota(jnp.int32, (BLK, BLK), 1)).astype(F32)
    trace = sum(jnp.sum(packed(i, i) * eye) for i in range(NB))
    norm = jnp.sqrt(jnp.full((8, 128), trace, F32)) + 1e-07
    factor = (1.0 / norm)[0:1, 0:1]
    square = factor * factor

    a_rows = lambda n: [a_ref.at[k, n_x : n_x + D] for k in range(n)]
    p_rows = lambda n: [p_ref.at[k] for k in range(n)]
    b_rows = lambda n: [b_ref.at[k] for k in range(n)]

    def put_x(n, value):
        for k, piece in enumerate(pieces(value, n)):
            a_ref[k, :n_x] = piece

    for i in range(NB):
        for j in range(i, NB):
            value = packed(i, j) * square
            gram_ref[blocks(i, j)] = value
            put_both(a_rows(3), i, j, value)
    put_x(3, x_ref[...] * factor)

    def poly(n_p):
        def emit(i, j, block):
            value = NS[1] * gram_ref[blocks(i, j)] + NS[2] * block
            if i == j:
                value = value + NS[0] * eye
            put_both(p_rows(n_p), i, j, value)

        a = a_rows(2)
        symmetric_product(a, a, emit)

    def next_gram(n, keep):
        p = p_rows(n)
        rows = slice(0, n_x + BLK)
        wide = mul([a_ref[k, rows] for k in range(n)], [y[...] for y in p])
        for j in range(NB):
            put_both(b_rows(n), 0, j, wide[n_x:, j * BLK : (j + 1) * BLK])
        symmetric_product(a_rows(n), p, lambda i, j, block: put_both(b_rows(n), i, j, block), 1)
        put_x(keep, wide[:n_x])

        def emit(i, j, block):
            gram_ref[blocks(i, j)] = block
            put_both(a_rows(keep), i, j, block)

        symmetric_product(b_rows(n), p, emit)

    poly(3)
    next_gram(3, 2)

    @pl.loop(1, SWEEPS - 1)
    def _(_):
        poly(2)
        next_gram(2, 2)

    poly(2)
    out_ref[...] = mul([a_ref[k, :n_x] for k in range(2)], [y[...] for y in p_rows(2)])


SMEM = pl.BlockSpec(memory_space=pltpu.SMEM)
VM = pl.BlockSpec(memory_space=pltpu.VMEM)


def gram_parts(core, held):
    rows = sum(v.shape[0] // BLK_ROWS * BLK_ROWS for v in held)
    return pl.pallas_call(
        gram_kernel,
        out_shape=[jax.ShapeDtypeStruct((BLK, D), F32)] * 2,
        in_specs=[SMEM] + [VM] * len(held),
        out_specs=[VM, VM],
        scratch_shapes=[pltpu.VMEM((3, rows, D), BF)],
        compiler_params=pltpu.CompilerParams(vmem_limit_bytes=48 << 20),
        cost_estimate=pl.CostEstimate(flops=2 * D * D * D * 4, bytes_accessed=4 * D * D * 2, transcendentals=0),
    )(core, *held)


def sweeps(core, mine, rest, x_rows):
    return pl.pallas_call(
        sweeps_kernel,
        out_shape=jax.ShapeDtypeStruct(x_rows.shape, F32),
        in_specs=[SMEM, VM, VM, VM],
        out_specs=VM,
        scratch_shapes=[
            pltpu.VMEM((BLK, D), F32),
            pltpu.VMEM((BLK, D), F32),
            pltpu.VMEM((D, D), F32),
            pltpu.VMEM((3, x_rows.shape[0] + D, D), BF),
            pltpu.VMEM((3, D, D), BF),
            pltpu.VMEM((3, D, D), BF),
        ],
        compiler_params=pltpu.CompilerParams(vmem_limit_bytes=48 << 20),
        cost_estimate=pl.CostEstimate(flops=2 * D * D * D * 32, bytes_accessed=4 * D * D, transcendentals=0),
    )(core, mine, rest, x_rows)


def gelu_parts(u):
    k0 = math.sqrt(2.0 / math.pi)
    th = jnp.tanh(k0 * (u + 0.044715 * (u * u * u)))
    value = 0.5 * u * (1.0 + th)
    slope = 0.5 * (1.0 + th) + 0.5 * u * (1.0 - th * th) * (k0 * (1.0 + 3.0 * 0.044715 * u * u))
    return value, slope


HEADS = 3
PAD = 128
HC = HEADS * HD
HP = HEADS * PAD
NN = ((1,), (0,))
NT = ((1,), (1,))
TN = ((0,), (0,))


def iota(shape, dim):
    return lax.broadcasted_iota(jnp.int32, shape, dim)


def one_hot(cond):
    return jnp.where(cond, 1.0, 0.0).astype(BF)


def home_place(at_ref, r):
    zi, xi, yi, ci = (at_ref[k] for k in range(4))
    n = 6
    group = jnp.right_shift(r * 10923, 16)
    lane = r - n * group
    mat = jnp.bitwise_and(group, 3)
    y = jnp.bitwise_and(jnp.right_shift(group, 2) + yi, 1)
    inner = jnp.bitwise_and(jnp.right_shift(group, 3), 3)
    outer = jnp.bitwise_and(jnp.right_shift(group, 5), 3)
    core = jnp.bitwise_and(jnp.right_shift(group, 7) + ci, 1)
    first = ci == 0
    z = jnp.bitwise_and(jnp.where(first, inner, outer) + zi, 3)
    x = jnp.bitwise_and(jnp.where(first, outer, inner) + xi, 3)
    column = (((z * 4 + x) * 2 + y) * 2 + core) * n + lane - HC * ci
    return jnp.where((column >= 0) & (column < HC), mat * HC + column, -1)


def unit_place(at_ref, n):
    zi, xi, yi, ci, ti = (at_ref[k] for k in range(5))
    width = 24
    group = jnp.right_shift(n * 2731, 16)
    lane = n - width * group
    y = jnp.bitwise_and(group + yi, 1)
    inner = jnp.bitwise_and(jnp.right_shift(group, 1), 3)
    outer = jnp.bitwise_and(jnp.right_shift(group, 3), 3)
    z = jnp.bitwise_and(jnp.where(ci == 0, inner, outer) + zi, 3)
    x = jnp.bitwise_and(jnp.where(ci == 0, outer, inner) + xi, 3)
    row = 2 * ti + jnp.right_shift(z, 1)
    return row, (((jnp.bitwise_and(z, 1) * 4 + x) * 2 + y) * 2 + ci) * width + lane


def layer_kernel(
    at_ref, own0_ref, own1_ref, own2_ref, own3_ref, got0_ref, got1_ref, got2_ref, got3_ref, normed_ref, cot_ref, bias_ref, cos_ref, sin_ref,
    own_ref, peer_ref, mine_ref, theirs_ref, gbias_ref,
    att_ref, win_ref, wback_ref, wq_ref, wk_ref, wv_ref, wo_ref, q_ref, k_ref, v_ref, da_ref, at_heads_ref, dq_ref, dk_ref, dv_ref, nat_ref,
):
    got_refs = (got0_ref, got1_ref, got2_ref, got3_ref)
    span = got0_ref.shape[2]
    small = span // 4
    half_d = D // 2
    for s, ref in enumerate((own0_ref, own1_ref, own2_ref, own3_ref)):
        for to_ref, base, c, group in ((att_ref, 0, 0, 0), (att_ref, 4 * span, 1, 0), (win_ref, 0, 0, 1), (wback_ref, 0, 0, 2)):
            at = base + s * span
            to_ref[at : at + span, :half_d] = ref[c, group]
            for p, got_ref in enumerate(got_refs):
                to_ref[at + p * small : at + (p + 1) * small, half_d:] = got_ref[1 - c, group, s * small : (s + 1) * small]
    n_rows, n_all = 4 * HC, att_ref.shape[0]

    pick = one_hot(iota((n_rows, n_all), 0) == home_place(at_ref, iota((8, n_all), 1))[:1])
    w_att = dot(pick, att_ref[...], NN).astype(BF)
    r = iota((HC, HC), 0)
    e = jnp.bitwise_and(r, HD - 1)
    half = ROT // 2
    source = jnp.where(e < half, r + half, jnp.where(e < ROT, r - half, -1))
    exchange = one_hot(iota((HC, HC), 1) == source)
    blank = jnp.zeros((HD, D), BF)
    for m, ref in enumerate((wq_ref, wk_ref)):
        own = w_att[m * HC : (m + 1) * HC]
        swapped = dot(exchange, own, NN).astype(BF)
        for h in range(HEADS):
            base = h * 2 * PAD
            ref[base : base + HD] = own[h * HD : (h + 1) * HD]
            ref[base + HD : base + PAD] = blank
            ref[base + PAD : base + PAD + HD] = swapped[h * HD : (h + 1) * HD]
            ref[base + PAD + HD : base + 2 * PAD] = blank
    for m, ref in ((2, wv_ref), (3, wo_ref)):
        for h in range(HEADS):
            ref[h * PAD : h * PAD + HD] = w_att[m * HC + h * HD : m * HC + (h + 1) * HD]
            ref[h * PAD + HD : (h + 1) * PAD] = blank

    cos, sin = cos_ref[...], sin_ref[...]
    for w_ref, ref in ((wq_ref, q_ref), (wk_ref, k_ref)):
        lin = dot(normed_ref[...], w_ref[...], NT)
        for s in range(2):
            rows = slice(s * LEN, (s + 1) * LEN)
            for h in range(HEADS):
                base = h * 2 * PAD
                own, other = lin[rows, base : base + PAD], lin[rows, base + PAD : base + 2 * PAD]
                ref[rows, base : base + PAD] = (own * cos + other * sin).astype(BF)
                ref[rows, base + PAD : base + 2 * PAD] = (other * cos - own * sin).astype(BF)
    v_ref[...] = dot(normed_ref[...], wv_ref[...], NT).astype(BF)
    da_ref[...] = dot(cot_ref[...], wo_ref[...], NT).astype(BF)

    turn = at_ref[4] * (LEN // 2)
    at_q = jnp.bitwise_xor(iota((LEN, LEN), 0), turn)
    at_k = jnp.bitwise_xor(iota((LEN, LEN), 1), turn)
    causal = at_q >= at_k
    scale = HD ** (-0.5)
    for s in range(2):
        rows = slice(s * LEN, (s + 1) * LEN)
        for h in range(HEADS):
            two = slice(h * 2 * PAD, (h + 1) * 2 * PAD)
            one = slice(h * 2 * PAD, h * 2 * PAD + PAD)
            lanes = slice(h * PAD, (h + 1) * PAD)
            value, d_att = v_ref[rows, lanes], da_ref[rows, lanes]
            scores = jnp.where(causal, dot(q_ref[rows, one], k_ref[rows, one], NT) * scale, -1e30)
            raised = jnp.exp(scores - jnp.max(scores, axis=1, keepdims=True))
            probs = raised / jnp.sum(raised, axis=1, keepdims=True)
            low = probs.astype(BF)
            at_heads_ref[rows, lanes] = dot(low, value, NN).astype(BF)
            dv_ref[rows, lanes] = dot(low, d_att, TN).astype(BF)
            d_probs = dot(d_att, value, NT)
            d_scores = (probs * (d_probs - jnp.sum(probs * d_probs, axis=1, keepdims=True))).astype(BF)
            d_q = dot(d_scores, k_ref[rows, two], NN) * scale
            d_k = dot(d_scores, q_ref[rows, two], TN) * scale
            dq_ref[rows, lanes] = (d_q[:, :PAD] * cos - d_q[:, PAD:] * sin).astype(BF)
            dk_ref[rows, lanes] = (d_k[:, :PAD] * cos - d_k[:, PAD:] * sin).astype(BF)

    def send(group, grad):
        for s in range(4):
            mine_ref[s, group] = grad[s * span : (s + 1) * span, :half_d]
            for p in range(4):
                at = s * span + p * small
                theirs_ref[p, group, s * small : (s + 1) * small] = grad[at : at + small, half_d:]

    hidden, slope = gelu_parts(dot(normed_ref[...], win_ref[...], NT) + bias_ref[...])
    hidden = hidden.astype(BF)


    def give_rows(k, value):
        own_ref[k] = value[:LEN]
        peer_ref[k, :, :half_d] = value[LEN:, half_d:]
        peer_ref[k, :, half_d:] = value[LEN:, :half_d]

    give_rows(0, dot(at_heads_ref[...], wo_ref[...], NN) + dot(hidden, wback_ref[...], NN))
    send(2, dot(hidden, cot_ref[...], TN).astype(BF))
    d_pre = (dot(cot_ref[...], wback_ref[...], NT) * slope).astype(BF)
    grad_bias = jnp.sum(d_pre.astype(F32), axis=0, keepdims=True)
    n_units = win_ref.shape[0]
    bias_row, _ = unit_place(at_ref, iota((8, n_units), 1))
    spread = pieces(jnp.where(bias_row == iota((8, n_units), 0), grad_bias, 0.0), 3)
    _, bias_lane = unit_place(at_ref, iota((n_units, 128), 0))
    to_lane = jnp.concatenate([one_hot(iota((n_units, 128), 1) + b == bias_lane) for b in range(0, D, 128)], axis=1)
    gbias_ref[...] = sum(dot(piece, to_lane, NN) for piece in reversed(spread))
    send(1, dot(d_pre, normed_ref[...], TN).astype(BF))
    total = dot(d_pre, win_ref[...], NN) + dot(dv_ref[...], wv_ref[...], NN)
    for h in range(HEADS):
        one = slice(h * 2 * PAD, h * 2 * PAD + PAD)
        lanes = slice(h * PAD, (h + 1) * PAD)
        total = total + dot(dq_ref[:, lanes], wq_ref[one], NN) + dot(dk_ref[:, lanes], wk_ref[one], NN)
    give_rows(1, total)

    for m, (ref, with_ref) in enumerate(((dq_ref, normed_ref), (dk_ref, normed_ref), (dv_ref, normed_ref), (at_heads_ref, cot_ref))):
        grad = dot(ref[...], with_ref[...], TN).astype(BF)
        for h in range(HEADS):
            nat_ref[m * HC + h * HD : m * HC + (h + 1) * HD] = grad[h * PAD : h * PAD + HD]
    half_rows = n_all // 2
    for group, base in ((0, 0), (3, half_rows)):
        place = home_place(at_ref, iota((half_rows, 128), 0) + base)
        pick = jnp.concatenate([one_hot(iota((half_rows, 128), 1) + b == place) for b in range(0, n_rows, 128)], axis=1)
        send(group, dot(pick, nat_ref[...], NN).astype(BF))


def layer(at, own, got, normed, cot, bias, cos, sin):
    n = normed.shape[0]
    out = lambda shape, dtype: jax.ShapeDtypeStruct(shape, dtype)
    low = lambda *shape: pltpu.VMEM(shape, BF)
    span = got[0].shape[2]
    units = 4 * span
    return pl.pallas_call(
        layer_kernel,
        out_shape=[out((2, n // 2, D), F32), out((2, n // 2, D), F32), out((4, 4, span, D // 2), BF), out((4, 4, span, D // 2), BF), out((8, D), F32)],
        in_specs=[SMEM] + [VM] * 13,
        out_specs=[VM] * 5,
        scratch_shapes=[low(2 * units, D), low(units, D), low(units, D), low(2 * HP, D), low(2 * HP, D), low(HP, D), low(HP, D)]
        + [low(n, 2 * HP), low(n, 2 * HP)]
        + [low(n, HP)] * 6
        + [low(4 * HC, D)],
        compiler_params=pltpu.CompilerParams(vmem_limit_bytes=56 << 20),
        cost_estimate=pl.CostEstimate(flops=12 * 10**9, bytes_accessed=16 << 20, transcendentals=10**6),
    )(at, *own, *got, normed, cot, bias, cos, sin)


def pack_kernel(mine_ref, other_ref, *out_refs):
    for s, ref in enumerate(out_refs):
        ref[0, 0] = mine_ref[s, 0] + other_ref[s, 3]
        ref[1, 0] = mine_ref[s, 3] + other_ref[s, 0]
        for group in (1, 2):
            ref[0, group] = mine_ref[s, group]
            ref[1, group] = other_ref[s, group]


def pack(mine, other):
    shape = (2, 3) + mine.shape[2:]
    return pl.pallas_call(
        pack_kernel,
        out_shape=[jax.ShapeDtypeStruct(shape, BF)] * 4,
        in_specs=[VM] * 2,
        out_specs=[VM] * 4,
        compiler_params=pltpu.CompilerParams(vmem_limit_bytes=32 << 20),
        cost_estimate=pl.CostEstimate(flops=0, bytes_accessed=8 << 20, transcendentals=0),
    )(mine, other)


def body(tokens, cotangent, qkv_weight, out_weight, fc_weight, vectors, qkv_momentum, out_momentum, fc_momentum, vector_first, vector_second):
    zi, xi, yi, ci, ti = (lax.axis_index(a) for a in ALL)
    rows = tokens.shape[0]
    n_att = qkv_weight.shape[3]
    n_fc = fc_weight.shape[3]
    gain, shift = vectors[:D], vectors[D : 2 * D]
    bias_in, bias_out = vectors[2 * D : 2 * D + FF], vectors[2 * D + FF :]

    first = ci == 0
    half_d = D // 2
    left, right = (lambda v: v[..., :half_d]), (lambda v: v[..., half_d:])
    turned = lambda v: jnp.concatenate([right(v), left(v)], axis=-1)
    own_first = lambda v: jnp.where(first, v, turned(v))

    attn_rows = jnp.concatenate([jnp.transpose(qkv_weight[:, :, 0, :], (0, 2, 1)), jnp.transpose(out_weight[:, 0, :])[None]])
    fc_rows = jnp.transpose(fc_weight[:, :, 0, :], (0, 2, 1))
    own_rows = own_first(jnp.concatenate([attn_rows.reshape(1, n_fc, D), fc_rows]).astype(BF))
    held = jnp.stack([left(own_rows), pull(right(own_rows), "c", 1)])
    held = jnp.stack([held, pull_yh(held, 1)], axis=2)
    inputs = tokens.astype(F32)
    average = jnp.mean(inputs, axis=-1, keepdims=True)
    deviation = inputs - average
    variance = jnp.mean(deviation * deviation, axis=-1, keepdims=True)
    inv_spread = lax.rsqrt(variance + 1e-05)
    centred = deviation * inv_spread
    normed_own = (centred * gain + shift).astype(BF)
    both = own_first(jnp.stack([normed_own, cotangent]))
    held, both = lax.optimization_barrier((held, both))
    held = jnp.stack([held] + [pull_inner(held, k) for k in (1, 2, 3)], axis=2)
    both = jnp.stack([both, pull(both, "t", 1)], axis=1)

    held, both = lax.optimization_barrier((held, both))
    span = 8 * n_fc
    held = held.reshape(2, 3, span, half_d)
    held = [held] + [pull_outer(held, k) for k in (1, 2, 3)]

    both = jnp.stack([both, turned(pull(both, "c", 1))], axis=1)
    n_all = 4 * rows
    normed, cot = both[0].reshape(n_all, D), both[1].reshape(n_all, D)

    half = jnp.arange(LEN) // rows
    position = ((ti + half) % 2) * rows + jnp.arange(LEN) % rows
    frequency = 10000.0 ** (-2.0 * jnp.arange(ROT // 2, dtype=F32) / ROT)
    angles = position.astype(F32)[:, None] * frequency[None, :]
    cos_t, sin_t = jnp.cos(angles), jnp.sin(angles)
    pad = lambda a, b, fill: jnp.concatenate([a, b, jnp.full((LEN, PAD - ROT), fill, F32)], axis=1)
    cos_full, sin_full = pad(cos_t, cos_t, 1.0), pad(-sin_t, sin_t, 0.0)

    bias6 = bias_in.reshape(2, 4, 4, 2, 2, n_fc)
    bias6 = jnp.concatenate([bias6, bias6], axis=1)
    bias6 = jnp.concatenate([bias6, bias6], axis=2)
    bias6 = jnp.concatenate([bias6, bias6], axis=3)
    bias_own = lax.dynamic_slice(bias6, (ti, zi, xi, yi, ci, 0), (1, 4, 4, 2, 1, n_fc))[0, :, :, :, 0]
    by_turn = lambda v: jnp.where(first, jnp.swapaxes(v, 0, 1), v)
    bias_own = by_turn(bias_own).reshape(1, 32 * n_fc)
    at = jnp.stack([zi, xi, yi, ci, ti]).astype(jnp.int32)
    far, normed, cot, bias_own, at, cos_full, sin_full = lax.optimization_barrier((held[1:], normed, cot, bias_own, at, cos_full, sin_full))
    held = [held[0]] + far
    got = [pull(v, "c", 1) for v in held]
    rows_own, rows_peer, sent_mine, sent_theirs, grad_bias_in = layer(at, held, got, normed, cot, bias_own, cos_full, sin_full)

    from_core = pull(sent_theirs, "c", 1)
    parts = pack(sent_mine, from_core)
    rows_own = (rows_own + pull(rows_peer, "c", 1)).reshape(2, 2, rows, D)
    parts, rows_own = lax.optimization_barrier((parts, rows_own))
    total = sum_ring(parts, pull_outer).reshape(2, 3, 4, 2, n_fc, half_d)
    total = sum_ring([total[:, :, k] for k in range(4)], pull_inner)
    total = sum_ring([total[:, :, k] for k in range(2)], pull_yh)
    total = own_first(jnp.concatenate([total[0], pull(total[1], "c", 1)], axis=-1)).reshape(3 * n_fc, D)

    rows_own = own_first(rows_own[:, 0] + pull(rows_own[:, 1].astype(BF), "t", 1).astype(F32))
    mixed = (inputs + rows_own[0] + bias_out).astype(BF)
    d_rows = rows_own[1]
    d_hat = d_rows * gain
    correction = d_hat - jnp.mean(d_hat, axis=-1, keepdims=True) - centred * jnp.mean(d_hat * centred, axis=-1, keepdims=True)
    own_cot = cotangent.astype(F32)
    input_grad = own_cot + correction * inv_spread

    total_of = lambda v: jnp.sum(v, axis=0, keepdims=True)
    vec_rows = [total_of(d_rows * centred), total_of(d_rows), grad_bias_in[: FF // D], total_of(own_cot), jnp.zeros((VEC_ROWS - VEC // D, D), F32)]

    mom_rows = jnp.concatenate(
        [
            jnp.transpose(qkv_momentum[:, :, 0, :], (0, 2, 1)).reshape(3 * n_att, D),
            jnp.transpose(out_momentum[:, 0, :]),
            jnp.transpose(fc_momentum[:, :, 0, :], (0, 2, 1)).reshape(2 * n_fc, D),
        ]
    )
    moment = 0.95 * mom_rows + total
    update = total + 0.95 * moment

    half_fc = n_fc // 2
    att_u = update[: 4 * n_att].reshape(4, n_att, D)
    att_u = jnp.concatenate([att_u, jnp.zeros((4, half_fc - n_att, D), F32)], axis=1)
    fc_u = update[4 * n_att :].reshape(4, half_fc, D)
    vec_rows = jnp.concatenate(vec_rows)
    chunks = jnp.concatenate([att_u, fc_u])
    chunks = jnp.concatenate([chunks, jnp.broadcast_to(vec_rows, (8, VEC_ROWS, D))], axis=1)
    got = lax.all_to_all(chunks, ("z", "t"), split_axis=0, concat_axis=0, tiled=True)
    mine = got[:, :half_fc].reshape(8 * half_fc, D)
    vec_sum = jnp.sum(got[:, half_fc:], axis=0)[:8]
    to_yh_x = lambda k: lambda z, x, y, c, t: (z, x, y + 1, c, t) if c == 0 else (z, x + k, y, c, t)
    to_x_yh = lambda k: lambda z, x, y, c, t: (z, x + k, y, c, t) if c == 0 else (z, x, y + 1, c, t)
    only = lambda core, source: lambda z, x, y, c, t: source(z, x, y, c, t) if c == core else None
    n = mine.shape[0]
    load = jnp.concatenate([mine, vec_sum])
    near = [load, move(load, to_yh_x(1)), move(load, only(1, to_yh_x(2))), move(load, only(1, to_yh_x(3)))]
    vec_sum = sum(v[n:] for v in near)
    load = jnp.concatenate([near[0][:n], near[1][:n], vec_sum])
    load_2 = jnp.where(first, load, jnp.concatenate([near[2][:n], near[3][:n], jnp.zeros_like(vec_sum)]))
    far = [move(load, to_x_yh(1)), move(load_2, to_x_yh(2)), move(load, only(0, to_x_yh(3)))]
    vec_sum = vec_sum + sum(v[2 * n :] for v in far)
    core = ci.astype(jnp.int32)[None]
    keep, give = gram_parts(core, near + far)
    from_core = pull(jnp.concatenate([give, vec_sum]), "c", 1)
    part = keep + from_core[:BLK]
    vec_sum = vec_sum + from_core[BLK:]
    other = pull(part, "t", 1)
    part = jnp.where(zi >= 2, part + other, part)
    rest = pull(part, "c", 1)
    x_rows = sweeps(core, part, rest, mine)
    vector_grad = vec_sum[: VEC // D].reshape(VEC)
    first_new = 0.9 * vector_first + 0.1 * vector_grad
    second_new = 0.95 * vector_second + 0.05 * vector_grad * vector_grad
    step_size = first_new / (1.0 - 0.9**STEP) / (jnp.sqrt(second_new / (1.0 - 0.95**STEP)) + 1e-08)
    vector_new = vectors - 0.2 * step_size

    back = lax.all_to_all(x_rows, ("z", "t"), split_axis=0, concat_axis=0, tiled=True).reshape(8, half_fc, D)
    att_x = back[:4, :n_att]
    fc_x = back[4:].reshape(2, n_fc, D)

    def cols(v):
        return jnp.transpose(v, (0, 2, 1))[:, :, None, :]

    fc_factor = math.sqrt(FF / D)
    qkv_new = qkv_weight * 0.99 - cols(att_x[:3])
    out_new = out_weight * 0.99 - cols(att_x[3:])[0]
    fc_new = fc_weight * 0.99 - fc_factor * cols(fc_x)
    att_m = moment[: 4 * n_att].reshape(4, n_att, D)
    fc_m = moment[4 * n_att :].reshape(2, n_fc, D)
    return (mixed, input_grad, qkv_new, out_new, fc_new, cols(att_m[:3]), cols(att_m[3:])[0], cols(fc_m), first_new, second_new, vector_new)


def solution(mesh):
    mesh = Mesh(mesh.devices.reshape(4, 4, 2, 2, 2), ALL)
    rows = P(ALL, None)
    w3 = P(None, None, "t", DP)
    w2 = P(None, "t", DP)
    vec = P()
    in_specs = (rows, rows, w3, w2, w3, vec, w3, w2, w3, vec, vec)
    out_specs = (rows, rows, w3, w2, w3, w3, w2, w3, vec, vec, vec)
    return jax.shard_map(body, mesh=mesh, in_specs=in_specs, out_specs=out_specs, check_vma=False)
```

```python
import functools
import itertools
import math

import jax
import jax.numpy as jnp
from jax import lax
from jax.experimental import pallas as pl
from jax.experimental.pallas import tpu as pltpu
from jax.sharding import Mesh, PartitionSpec as P

D = 768
H = 12
HD = 64
ROT = 16
FF = 3072
SWEEPS = 5
STEP = 10
LEN = 256
VEC = 2 * D + FF + D
VEC_ROWS = 12

NS = (3.4445, -4.775, 2.0315)
BF = jnp.bfloat16
F32 = jnp.float32
BLK = 256
BLK_ROWS = 96
NB = D // BLK

DP = ("z", "x", "yh", "c")
ALL = ("z", "x", "yh", "c", "t")


def pull(value, axis, k):
    n = lax.axis_size(axis)
    return lax.ppermute(value, axis, [((i + k) % n, i) for i in range(n)])


def move(value, source):
    sizes = [lax.axis_size(a) for a in ALL]
    index = lambda at: functools.reduce(lambda total, one: total * one[0] + one[1] % one[0], zip(sizes, at), 0)
    pairs = []
    for here in itertools.product(*map(range, sizes)):
        there = source(*here)
        if there is not None:
            pairs.append((index(there), index(here)))
    return lax.ppermute(value, ALL, pairs)


def pull_outer(value, k):
    return move(value, lambda z, x, y, c, t: (z, x + k, y, c, t) if c == 0 else (z + k, x, y, c, t))


def pull_near(value, k):
    step = lambda z, x, y, c, t: (z + k // 2, x, y + k, c, t) if c == 0 else (z, x + k // 2, y + k, c, t)
    return move(value, step)


def push_near(value, k):
    step = lambda z, x, y, c, t: (z + 4 - k // 2, x, y + k, c, t) if c == 0 else (z, x + 4 - k // 2, y + k, c, t)
    return move(value, step)


def push_outer(value, k):
    return pull_outer(value, 4 - k)


def sum_ring(parts, push):
    total = parts[0].astype(F32)
    for k in range(1, len(parts)):
        total = total + push(parts[k].astype(BF), k).astype(F32)
    return total


def dot(a, b, dims):
    return lax.dot_general(a, b, (dims, ((), ())), preferred_element_type=F32)


def pieces(value, n):
    out = []
    for _ in range(n):
        low = value.astype(BF)
        out.append(low)
        value = value - low.astype(F32)
    return out


def mul(xs, ys, dims=((1,), (0,))):
    n = len(xs)
    total = None
    for order in reversed(range(n)):
        for i in range(order + 1):
            term = lax.dot_general(xs[i], ys[order - i], (dims, ((), ())), preferred_element_type=F32)
            total = term if total is None else total + term
    return total


def gram_kernel(core_ref, *refs):
    *in_refs, keep_ref, give_ref, wide_ref = refs
    at = 0
    for ref in in_refs:
        n = ref.shape[0] // BLK_ROWS * BLK_ROWS
        for k, piece in enumerate(pieces(ref[:n], 3)):
            wide_ref[k, at : at + n] = piece
        at += n
    xs = [wide_ref[k] for k in range(3)]
    dims = ((0,), (0,))
    cut = lambda i: slice(i * BLK, (i + 1) * BLK)
    top = mul([x[:, cut(0)] for x in xs], xs, dims)
    mid = mul([x[:, cut(1)] for x in xs], [x[:, BLK:] for x in xs], dims)
    low = mul([x[:, cut(2)] for x in xs], [x[:, 2 * BLK :] for x in xs], dims)
    first = core_ref[0] == 0

    @pl.when(first)
    def _():
        keep_ref[...] = top
        give_ref[:, : 2 * BLK] = mid
        give_ref[:, 2 * BLK :] = low

    @pl.when(jnp.logical_not(first))
    def _():
        give_ref[...] = top
        keep_ref[:, : 2 * BLK] = mid
        keep_ref[:, 2 * BLK :] = low


def blocks(i, j):
    return (slice(i * BLK, (i + 1) * BLK), slice(j * BLK, (j + 1) * BLK))


def put(refs, i, j, value):
    for ref, piece in zip(refs, pieces(value, len(refs))):
        ref[blocks(i, j)] = piece


def put_both(refs, i, j, value):
    put(refs, i, j, value)
    if i != j:
        put(refs, j, i, value.T)


def symmetric_product(xs, ys, emit, start=0):
    for i in range(start, NB):
        rows = slice(i * BLK, (i + 1) * BLK)
        wide = mul([x[rows, :] for x in xs], [y[:, i * BLK :] for y in ys])
        for j in range(i, NB):
            emit(i, j, wide[:, (j - i) * BLK : (j - i + 1) * BLK])


def sweeps_kernel(core_ref, mine_ref, rest_ref, x_ref, out_ref, top_ref, bottom_ref, gram_ref, a_ref, p_ref, b_ref):
    first = core_ref[0] == 0
    n_x = x_ref.shape[0]

    @pl.when(first)
    def _():
        top_ref[...] = mine_ref[...]
        bottom_ref[...] = rest_ref[...]

    @pl.when(jnp.logical_not(first))
    def _():
        top_ref[...] = rest_ref[...]
        bottom_ref[...] = mine_ref[...]

    def packed(i, j):
        if i == 0:
            return top_ref[:, j * BLK : (j + 1) * BLK]
        at = (j - 1) if i == 1 else 2
        return bottom_ref[:, at * BLK : (at + 1) * BLK]

    eye = (lax.broadcasted_iota(jnp.int32, (BLK, BLK), 0) == lax.broadcasted_iota(jnp.int32, (BLK, BLK), 1)).astype(F32)
    trace = sum(jnp.sum(packed(i, i) * eye) for i in range(NB))
    norm = jnp.sqrt(jnp.full((8, 128), trace, F32)) + 1e-07
    factor = (1.0 / norm)[0:1, 0:1]
    square = factor * factor

    a_rows = lambda n: [a_ref.at[k, n_x : n_x + D] for k in range(n)]
    p_rows = lambda n: [p_ref.at[k] for k in range(n)]
    b_rows = lambda n: [b_ref.at[k] for k in range(n)]

    def put_x(n, value):
        for k, piece in enumerate(pieces(value, n)):
            a_ref[k, :n_x] = piece

    for i in range(NB):
        for j in range(i, NB):
            value = packed(i, j) * square
            gram_ref[blocks(i, j)] = value
            put_both(a_rows(3), i, j, value)
    put_x(3, x_ref[...] * factor)

    def poly(n_p):
        def emit(i, j, block):
            value = NS[1] * gram_ref[blocks(i, j)] + NS[2] * block
            if i == j:
                value = value + NS[0] * eye
            put_both(p_rows(n_p), i, j, value)

        a = a_rows(2)
        symmetric_product(a, a, emit)

    def next_gram(n, keep):
        p = p_rows(n)
        rows = slice(0, n_x + BLK)
        wide = mul([a_ref[k, rows] for k in range(n)], [y[...] for y in p])
        for j in range(NB):
            put_both(b_rows(n), 0, j, wide[n_x:, j * BLK : (j + 1) * BLK])
        symmetric_product(a_rows(n), p, lambda i, j, block: put_both(b_rows(n), i, j, block), 1)
        put_x(keep, wide[:n_x])

        def emit(i, j, block):
            gram_ref[blocks(i, j)] = block
            put_both(a_rows(keep), i, j, block)

        symmetric_product(b_rows(n), p, emit)

    poly(3)
    next_gram(3, 2)

    @pl.loop(1, SWEEPS - 1)
    def _(_):
        poly(2)
        next_gram(2, 2)

    poly(2)
    out_ref[...] = mul([a_ref[k, :n_x] for k in range(2)], [y[...] for y in p_rows(2)])


SMEM = pl.BlockSpec(memory_space=pltpu.SMEM)
VM = pl.BlockSpec(memory_space=pltpu.VMEM)


def gram_parts(core, held):
    rows = sum(v.shape[0] // BLK_ROWS * BLK_ROWS for v in held)
    return pl.pallas_call(
        gram_kernel,
        out_shape=[jax.ShapeDtypeStruct((BLK, D), F32)] * 2,
        in_specs=[SMEM] + [VM] * len(held),
        out_specs=[VM, VM],
        scratch_shapes=[pltpu.VMEM((3, rows, D), BF)],
        compiler_params=pltpu.CompilerParams(vmem_limit_bytes=48 << 20),
        cost_estimate=pl.CostEstimate(flops=2 * D * D * D * 4, bytes_accessed=4 * D * D * 2, transcendentals=0),
    )(core, *held)


def sweeps(core, mine, rest, x_rows):
    return pl.pallas_call(
        sweeps_kernel,
        out_shape=jax.ShapeDtypeStruct(x_rows.shape, F32),
        in_specs=[SMEM, VM, VM, VM],
        out_specs=VM,
        scratch_shapes=[
            pltpu.VMEM((BLK, D), F32),
            pltpu.VMEM((BLK, D), F32),
            pltpu.VMEM((D, D), F32),
            pltpu.VMEM((3, x_rows.shape[0] + D, D), BF),
            pltpu.VMEM((3, D, D), BF),
            pltpu.VMEM((3, D, D), BF),
        ],
        compiler_params=pltpu.CompilerParams(vmem_limit_bytes=48 << 20),
        cost_estimate=pl.CostEstimate(flops=2 * D * D * D * 32, bytes_accessed=4 * D * D, transcendentals=0),
    )(core, mine, rest, x_rows)


def gelu_parts(u):
    k0 = math.sqrt(2.0 / math.pi)
    th = jnp.tanh(k0 * (u + 0.044715 * (u * u * u)))
    value = 0.5 * u * (1.0 + th)
    slope = 0.5 * (1.0 + th) + 0.5 * u * (1.0 - th * th) * (k0 * (1.0 + 3.0 * 0.044715 * u * u))
    return value, slope


HEADS = 3
PAD = 128
HC = HEADS * HD
HP = HEADS * PAD
NN = ((1,), (0,))
NT = ((1,), (1,))
TN = ((0,), (0,))


def iota(shape, dim):
    return lax.broadcasted_iota(jnp.int32, shape, dim)


def one_hot(cond):
    return jnp.where(cond, 1.0, 0.0).astype(BF)


def home_place(at_ref, r):
    zi, xi, yi, ci = (at_ref[k] for k in range(4))
    n = 6
    group = jnp.right_shift(r * 10923, 16)
    lane = r - n * group
    mat = jnp.bitwise_and(group, 3)
    y = jnp.bitwise_and(jnp.right_shift(group, 2) + yi, 1)
    inner = jnp.bitwise_and(jnp.right_shift(group, 3), 3)
    outer = jnp.bitwise_and(jnp.right_shift(group, 5), 3)
    core = jnp.bitwise_and(jnp.right_shift(group, 7) + ci, 1)
    first = ci == 0
    z = jnp.bitwise_and(jnp.where(first, inner, outer) + zi, 3)
    x = jnp.bitwise_and(jnp.where(first, outer, inner) + xi, 3)
    column = (((z * 4 + x) * 2 + y) * 2 + core) * n + lane - HC * ci
    return jnp.where((column >= 0) & (column < HC), mat * HC + column, -1)


def unit_place(at_ref, n):
    zi, xi, yi, ci, ti = (at_ref[k] for k in range(5))
    width = 24
    group = jnp.right_shift(n * 2731, 16)
    lane = n - width * group
    y = jnp.bitwise_and(group + yi, 1)
    inner = jnp.bitwise_and(jnp.right_shift(group, 1), 3)
    outer = jnp.bitwise_and(jnp.right_shift(group, 3), 3)
    z = jnp.bitwise_and(jnp.where(ci == 0, inner, outer) + zi, 3)
    x = jnp.bitwise_and(jnp.where(ci == 0, outer, inner) + xi, 3)
    row = 2 * ti + jnp.right_shift(z, 1)
    return row, (((jnp.bitwise_and(z, 1) * 4 + x) * 2 + y) * 2 + ci) * width + lane


def layer_kernel(
    at_ref, *refs,
):
    held_refs, got_refs, refs = refs[:8], refs[8:16], refs[16:]
    layer_math(at_ref, held_refs, got_refs, *refs)


def layer_math(
    at_ref, held_refs, got_refs, normed_ref, cot_ref, bias_ref, cos_ref, sin_ref,
    own_ref, peer_ref, mine_ref, theirs_ref, gbias_ref,
    att_ref, win_ref, wback_ref, wq_ref, wk_ref, wv_ref, wo_ref, q_ref, k_ref, v_ref, da_ref, at_heads_ref, dq_ref, dk_ref, dv_ref, nat_ref,
):
    span = got_refs[0].shape[1]
    small = span // 4
    half_d = D // 2
    for to_ref, base, c, group in ((att_ref, 0, 0, 0), (att_ref, 4 * span, 1, 0), (win_ref, 0, 0, 1), (wback_ref, 0, 0, 2)):
        for s in range(4):
            at = base + s * span
            to_ref[at : at + span, :half_d] = held_refs[2 * s + c][group]
            for p in range(4):
                to_ref[at + p * small : at + (p + 1) * small, half_d:] = got_refs[2 * p + 1 - c][group, s * small : (s + 1) * small]
    n_rows, n_all = 4 * HC, att_ref.shape[0]

    pick = one_hot(iota((n_rows, n_all), 0) == home_place(at_ref, iota((8, n_all), 1))[:1])
    w_att = dot(pick, att_ref[...], NN).astype(BF)
    r = iota((HC, HC), 0)
    e = jnp.bitwise_and(r, HD - 1)
    half = ROT // 2
    source = jnp.where(e < half, r + half, jnp.where(e < ROT, r - half, -1))
    exchange = one_hot(iota((HC, HC), 1) == source)
    blank = jnp.zeros((HD, D), BF)
    for m, ref in enumerate((wq_ref, wk_ref)):
        own = w_att[m * HC : (m + 1) * HC]
        swapped = dot(exchange, own, NN).astype(BF)
        for h in range(HEADS):
            base = h * 2 * PAD
            ref[base : base + HD] = own[h * HD : (h + 1) * HD]
            ref[base + HD : base + PAD] = blank
            ref[base + PAD : base + PAD + HD] = swapped[h * HD : (h + 1) * HD]
            ref[base + PAD + HD : base + 2 * PAD] = blank
    for m, ref in ((2, wv_ref), (3, wo_ref)):
        for h in range(HEADS):
            ref[h * PAD : h * PAD + HD] = w_att[m * HC + h * HD : m * HC + (h + 1) * HD]
            ref[h * PAD + HD : (h + 1) * PAD] = blank

    cos, sin = cos_ref[...], sin_ref[...]
    for w_ref, ref in ((wq_ref, q_ref), (wk_ref, k_ref)):
        lin = dot(normed_ref[...], w_ref[...], NT)
        for s in range(2):
            rows = slice(s * LEN, (s + 1) * LEN)
            for h in range(HEADS):
                base = h * 2 * PAD
                own, other = lin[rows, base : base + PAD], lin[rows, base + PAD : base + 2 * PAD]
                ref[rows, base : base + PAD] = (own * cos + other * sin).astype(BF)
                ref[rows, base + PAD : base + 2 * PAD] = (other * cos - own * sin).astype(BF)
    v_ref[...] = dot(normed_ref[...], wv_ref[...], NT).astype(BF)
    da_ref[...] = dot(cot_ref[...], wo_ref[...], NT).astype(BF)

    turn = at_ref[4] * (LEN // 2)
    at_q = jnp.bitwise_xor(iota((LEN, LEN), 0), turn)
    at_k = jnp.bitwise_xor(iota((LEN, LEN), 1), turn)
    causal = at_q >= at_k
    scale = HD ** (-0.5)
    for s in range(2):
        rows = slice(s * LEN, (s + 1) * LEN)
        for h in range(HEADS):
            two = slice(h * 2 * PAD, (h + 1) * 2 * PAD)
            one = slice(h * 2 * PAD, h * 2 * PAD + PAD)
            lanes = slice(h * PAD, (h + 1) * PAD)
            value, d_att = v_ref[rows, lanes], da_ref[rows, lanes]
            scores = jnp.where(causal, dot(q_ref[rows, one], k_ref[rows, one], NT) * scale, -1e30)
            raised = jnp.exp(scores - jnp.max(scores, axis=1, keepdims=True))
            probs = raised / jnp.sum(raised, axis=1, keepdims=True)
            low = probs.astype(BF)
            at_heads_ref[rows, lanes] = dot(low, value, NN).astype(BF)
            dv_ref[rows, lanes] = dot(low, d_att, TN).astype(BF)
            d_probs = dot(d_att, value, NT)
            d_scores = (probs * (d_probs - jnp.sum(probs * d_probs, axis=1, keepdims=True))).astype(BF)
            d_q = dot(d_scores, k_ref[rows, two], NN) * scale
            d_k = dot(d_scores, q_ref[rows, two], TN) * scale
            dq_ref[rows, lanes] = (d_q[:, :PAD] * cos - d_q[:, PAD:] * sin).astype(BF)
            dk_ref[rows, lanes] = (d_k[:, :PAD] * cos - d_k[:, PAD:] * sin).astype(BF)

    def send(group, grad):
        for s in range(4):
            mine_ref[s, group] = grad[s * span : (s + 1) * span, :half_d]
            for p in range(4):
                at = s * span + p * small
                theirs_ref[p, group, s * small : (s + 1) * small] = grad[at : at + small, half_d:]

    hidden, slope = gelu_parts(dot(normed_ref[...], win_ref[...], NT) + bias_ref[...])
    hidden = hidden.astype(BF)


    def give_rows(k, value):
        own_ref[k] = value[:LEN]
        peer_ref[k, :, :half_d] = value[LEN:, half_d:]
        peer_ref[k, :, half_d:] = value[LEN:, :half_d]

    give_rows(0, dot(at_heads_ref[...], wo_ref[...], NN) + dot(hidden, wback_ref[...], NN))
    send(2, dot(hidden, cot_ref[...], TN).astype(BF))
    d_pre = (dot(cot_ref[...], wback_ref[...], NT) * slope).astype(BF)
    grad_bias = jnp.sum(d_pre.astype(F32), axis=0, keepdims=True)
    n_units = win_ref.shape[0]
    bias_row, _ = unit_place(at_ref, iota((8, n_units), 1))
    spread = pieces(jnp.where(bias_row == iota((8, n_units), 0), grad_bias, 0.0), 3)
    _, bias_lane = unit_place(at_ref, iota((n_units, 128), 0))
    to_lane = jnp.concatenate([one_hot(iota((n_units, 128), 1) + b == bias_lane) for b in range(0, D, 128)], axis=1)
    gbias_ref[...] = sum(dot(piece, to_lane, NN) for piece in reversed(spread))
    send(1, dot(d_pre, normed_ref[...], TN).astype(BF))
    total = dot(d_pre, win_ref[...], NN) + dot(dv_ref[...], wv_ref[...], NN)
    for h in range(HEADS):
        one = slice(h * 2 * PAD, h * 2 * PAD + PAD)
        lanes = slice(h * PAD, (h + 1) * PAD)
        total = total + dot(dq_ref[:, lanes], wq_ref[one], NN) + dot(dk_ref[:, lanes], wk_ref[one], NN)
    give_rows(1, total)

    for m, (ref, with_ref) in enumerate(((dq_ref, normed_ref), (dk_ref, normed_ref), (dv_ref, normed_ref), (at_heads_ref, cot_ref))):
        grad = dot(ref[...], with_ref[...], TN).astype(BF)
        for h in range(HEADS):
            nat_ref[m * HC + h * HD : m * HC + (h + 1) * HD] = grad[h * PAD : h * PAD + HD]
    half_rows = n_all // 2
    for group, base in ((0, 0), (3, half_rows)):
        place = home_place(at_ref, iota((half_rows, 128), 0) + base)
        pick = jnp.concatenate([one_hot(iota((half_rows, 128), 1) + b == place) for b in range(0, n_rows, 128)], axis=1)
        send(group, dot(pick, nat_ref[...], NN).astype(BF))


def layer(at, own, got, normed, cot, bias, cos, sin):
    n = normed.shape[0]
    out = lambda shape, dtype: jax.ShapeDtypeStruct(shape, dtype)
    low = lambda *shape: pltpu.VMEM(shape, BF)
    span = got[0].shape[1]
    units = 4 * span
    return pl.pallas_call(
        layer_kernel,
        out_shape=[out((2, n // 2, D), F32), out((2, n // 2, D), F32), out((4, 4, span, D // 2), BF), out((4, 4, span, D // 2), BF), out((8, D), F32)],
        in_specs=[SMEM] + [VM] * 21,
        out_specs=[VM] * 5,
        scratch_shapes=[low(2 * units, D), low(units, D), low(units, D), low(2 * HP, D), low(2 * HP, D), low(HP, D), low(HP, D)]
        + [low(n, 2 * HP), low(n, 2 * HP)]
        + [low(n, HP)] * 6
        + [low(4 * HC, D)],
        compiler_params=pltpu.CompilerParams(vmem_limit_bytes=56 << 20),
        cost_estimate=pl.CostEstimate(flops=12 * 10**9, bytes_accessed=16 << 20, transcendentals=10**6),
    )(at, *own, *got, normed, cot, bias, cos, sin)


def pack_kernel(mine_ref, other_ref, *out_refs):
    for s in range(4):
        out_refs[2 * s][0] = mine_ref[s, 0] + other_ref[s, 3]
        out_refs[2 * s + 1][0] = mine_ref[s, 3] + other_ref[s, 0]
        for group in (1, 2):
            out_refs[2 * s][group] = mine_ref[s, group]
            out_refs[2 * s + 1][group] = other_ref[s, group]


def pack(mine, other):
    shape = (3,) + mine.shape[2:]
    flat = pl.pallas_call(
        pack_kernel,
        out_shape=[jax.ShapeDtypeStruct(shape, BF)] * 8,
        in_specs=[VM] * 2,
        out_specs=[VM] * 8,
        compiler_params=pltpu.CompilerParams(vmem_limit_bytes=32 << 20),
        cost_estimate=pl.CostEstimate(flops=0, bytes_accessed=8 << 20, transcendentals=0),
    )(mine, other)
    return [flat[2 * s : 2 * s + 2] for s in range(4)]


def sum_outer(parts):
    (a0, b0), (a1, b1), (a2, b2), (a3, b3) = parts
    add = lambda *values: functools.reduce(jnp.add, [v.astype(F32) for v in values])
    a2, b2 = push_outer(a2, 1), push_outer(b2, 3)
    b1, a3 = push_outer(b1, 1), push_outer(a3, 3)
    a1, b3 = push_outer(add(a1, a2).astype(BF), 1), push_outer(add(b3, b2).astype(BF), 3)
    return jnp.stack([add(a0, a1, a3), add(b0, b1, b3)])


def body(tokens, cotangent, qkv_weight, out_weight, fc_weight, vectors, qkv_momentum, out_momentum, fc_momentum, vector_first, vector_second):
    zi, xi, yi, ci, ti = (lax.axis_index(a) for a in ALL)
    rows = tokens.shape[0]
    n_att = qkv_weight.shape[3]
    n_fc = fc_weight.shape[3]
    gain, shift = vectors[:D], vectors[D : 2 * D]
    bias_in, bias_out = vectors[2 * D : 2 * D + FF], vectors[2 * D + FF :]

    first = ci == 0
    half_d = D // 2
    left, right = (lambda v: v[..., :half_d]), (lambda v: v[..., half_d:])
    turned = lambda v: jnp.concatenate([right(v), left(v)], axis=-1)
    own_first = lambda v: jnp.where(first, v, turned(v))

    attn_rows = jnp.concatenate([jnp.transpose(qkv_weight[:, :, 0, :], (0, 2, 1)), jnp.transpose(out_weight[:, 0, :])[None]])
    fc_rows = jnp.transpose(fc_weight[:, :, 0, :], (0, 2, 1))
    own_rows = own_first(jnp.concatenate([attn_rows.reshape(1, n_fc, D), fc_rows]).astype(BF))
    held = jnp.stack([left(own_rows), pull(right(own_rows), "c", 1)])
    held = jnp.concatenate([held] + [pull_near(held, k) for k in range(1, 8)], axis=2)
    inputs = tokens.astype(F32)
    average = jnp.mean(inputs, axis=-1, keepdims=True)
    deviation = inputs - average
    variance = jnp.mean(deviation * deviation, axis=-1, keepdims=True)
    inv_spread = lax.rsqrt(variance + 1e-05)
    centred = deviation * inv_spread
    normed_own = (centred * gain + shift).astype(BF)
    both = own_first(jnp.stack([normed_own, cotangent]))
    held, both = lax.optimization_barrier((held, both))
    other_t = pull(both, "t", 1)
    a0, b0 = held[0], held[1]
    wave = [pull_outer(a0, 1), pull_outer(b0, 3), pull_outer(b0, 1), pull_outer(a0, 3)]

    half = jnp.arange(LEN) // rows
    position = ((ti + half) % 2) * rows + jnp.arange(LEN) % rows
    frequency = 10000.0 ** (-2.0 * jnp.arange(ROT // 2, dtype=F32) / ROT)
    angles = position.astype(F32)[:, None] * frequency[None, :]
    cos_t, sin_t = jnp.cos(angles), jnp.sin(angles)
    pad = lambda a, b, fill: jnp.concatenate([a, b, jnp.full((LEN, PAD - ROT), fill, F32)], axis=1)
    cos_full, sin_full = pad(cos_t, cos_t, 1.0), pad(-sin_t, sin_t, 0.0)

    bias6 = bias_in.reshape(2, 4, 4, 2, 2, n_fc)
    bias6 = jnp.concatenate([bias6, bias6], axis=1)
    bias6 = jnp.concatenate([bias6, bias6], axis=2)
    bias6 = jnp.concatenate([bias6, bias6], axis=3)
    bias_own = lax.dynamic_slice(bias6, (ti, zi, xi, yi, ci, 0), (1, 4, 4, 2, 1, n_fc))[0, :, :, :, 0]
    by_turn = lambda v: jnp.where(first, jnp.swapaxes(v, 0, 1), v)
    bias_own = by_turn(bias_own).reshape(1, 32 * n_fc)
    at = jnp.stack([zi, xi, yi, ci, ti]).astype(jnp.int32)
    mom_rows = jnp.concatenate(
        [
            jnp.transpose(qkv_momentum[:, :, 0, :], (0, 2, 1)).reshape(3 * n_att, D),
            jnp.transpose(out_momentum[:, 0, :]),
            jnp.transpose(fc_momentum[:, :, 0, :], (0, 2, 1)).reshape(2 * n_fc, D),
        ]
    )
    wave, other_t, bias_own, at, cos_full, sin_full, mom_rows = lax.optimization_barrier(
        (wave, other_t, bias_own, at, cos_full, sin_full, mom_rows)
    )
    a1, b3, b1, a3 = wave
    a2, b2 = pull_outer(a1, 1), pull_outer(b3, 3)
    both = jnp.stack([both, other_t], axis=1)
    both = jnp.stack([both, turned(pull(both, "c", 1))], axis=1)
    n_all = 4 * rows
    normed, cot = both[0].reshape(n_all, D), both[1].reshape(n_all, D)
    near_got = [pull(v, "c", 1) for v in (a0, b0, a1, b1, a3, b3)]
    a2, b2, normed, cot, near_got = lax.optimization_barrier((a2, b2, normed, cot, near_got))
    held = [a0, b0, a1, b1, a2, b2, a3, b3]
    got = near_got[:4] + [pull(a2, "c", 1), pull(b2, "c", 1)] + near_got[4:]
    rows_own, rows_peer, sent_mine, sent_theirs, grad_bias_in = layer(at, held, got, normed, cot, bias_own, cos_full, sin_full)

    from_core = pull(sent_theirs, "c", 1)
    parts = pack(sent_mine, from_core)
    parts, rows_peer = lax.optimization_barrier((parts, rows_peer))
    rows_own = (rows_own + pull(rows_peer, "c", 1)).reshape(2, 2, rows, D)
    rows_own = rows_own[:, 0] + pull(rows_own[:, 1].astype(BF), "t", 1).astype(F32)
    total, rows_own = lax.optimization_barrier((sum_outer(parts), rows_own))
    total = total.reshape(2, 3, 8, n_fc, half_d)
    total = sum_ring([total[:, :, k] for k in range(8)], push_near)
    total = own_first(jnp.concatenate([total[0], pull(total[1], "c", 1)], axis=-1)).reshape(3 * n_fc, D)

    rows_own = own_first(rows_own)
    mixed = (inputs + rows_own[0] + bias_out).astype(BF)
    d_rows = rows_own[1]
    d_hat = d_rows * gain
    correction = d_hat - jnp.mean(d_hat, axis=-1, keepdims=True) - centred * jnp.mean(d_hat * centred, axis=-1, keepdims=True)
    own_cot = cotangent.astype(F32)
    input_grad = own_cot + correction * inv_spread

    total_of = lambda v: jnp.sum(v, axis=0, keepdims=True)
    vec_rows = [total_of(d_rows * centred), total_of(d_rows), grad_bias_in[: FF // D], total_of(own_cot), jnp.zeros((VEC_ROWS - VEC // D, D), F32)]

    moment = 0.95 * mom_rows + total
    update = total + 0.95 * moment

    half_fc = n_fc // 2
    att_u = update[: 4 * n_att].reshape(4, n_att, D)
    att_u = jnp.concatenate([att_u, jnp.zeros((4, half_fc - n_att, D), F32)], axis=1)
    fc_u = update[4 * n_att :].reshape(4, half_fc, D)
    vec_rows = jnp.concatenate(vec_rows)
    chunks = jnp.concatenate([att_u, fc_u])
    chunks = jnp.concatenate([chunks, jnp.broadcast_to(vec_rows, (8, VEC_ROWS, D))], axis=1)
    got = lax.all_to_all(chunks, ("z", "t"), split_axis=0, concat_axis=0, tiled=True)
    mine = got[:, :half_fc].reshape(8 * half_fc, D)
    vec_sum = jnp.sum(got[:, half_fc:], axis=0)[:8]
    to_yh_x = lambda k: lambda z, x, y, c, t: (z, x, y + 1, c, t) if c == 0 else (z, x + k, y, c, t)
    to_x_yh = lambda k: lambda z, x, y, c, t: (z, x + k, y, c, t) if c == 0 else (z, x, y + 1, c, t)
    only = lambda core, source: lambda z, x, y, c, t: source(z, x, y, c, t) if c == core else None
    n = mine.shape[0]
    load = jnp.concatenate([mine, vec_sum])
    near = [load, move(load, to_yh_x(1)), move(load, only(1, to_yh_x(2))), move(load, only(1, to_yh_x(3)))]
    vec_sum = sum(v[n:] for v in near)
    load = jnp.concatenate([near[0][:n], near[1][:n], vec_sum])
    load_2 = jnp.where(first, load, jnp.concatenate([near[2][:n], near[3][:n], jnp.zeros_like(vec_sum)]))
    far = [move(load, to_x_yh(1)), move(load_2, to_x_yh(2)), move(load, only(0, to_x_yh(3)))]
    vec_sum = vec_sum + sum(v[2 * n :] for v in far)
    core = ci.astype(jnp.int32)[None]
    keep, give = gram_parts(core, near + far)
    from_core = pull(jnp.concatenate([give, vec_sum]), "c", 1)
    part = keep + from_core[:BLK]
    vec_sum = vec_sum + from_core[BLK:]
    other = pull(part, "t", 1)
    part = jnp.where(zi >= 2, part + other, part)
    rest = pull(part, "c", 1)
    x_rows = sweeps(core, part, rest, mine)
    vector_grad = vec_sum[: VEC // D].reshape(VEC)
    first_new = 0.9 * vector_first + 0.1 * vector_grad
    second_new = 0.95 * vector_second + 0.05 * vector_grad * vector_grad
    step_size = first_new / (1.0 - 0.9**STEP) / (jnp.sqrt(second_new / (1.0 - 0.95**STEP)) + 1e-08)
    vector_new = vectors - 0.2 * step_size

    back = lax.all_to_all(x_rows, ("z", "t"), split_axis=0, concat_axis=0, tiled=True).reshape(8, half_fc, D)
    att_x = back[:4, :n_att]
    fc_x = back[4:].reshape(2, n_fc, D)

    def cols(v):
        return jnp.transpose(v, (0, 2, 1))[:, :, None, :]

    fc_factor = math.sqrt(FF / D)
    qkv_new = qkv_weight * 0.99 - cols(att_x[:3])
    out_new = out_weight * 0.99 - cols(att_x[3:])[0]
    fc_new = fc_weight * 0.99 - fc_factor * cols(fc_x)
    att_m = moment[: 4 * n_att].reshape(4, n_att, D)
    fc_m = moment[4 * n_att :].reshape(2, n_fc, D)
    return (mixed, input_grad, qkv_new, out_new, fc_new, cols(att_m[:3]), cols(att_m[3:])[0], cols(fc_m), first_new, second_new, vector_new)


def solution(mesh):
    mesh = Mesh(mesh.devices.reshape(4, 4, 2, 2, 2), ALL)
    rows = P(ALL, None)
    w3 = P(None, None, "t", DP)
    w2 = P(None, "t", DP)
    vec = P()
    in_specs = (rows, rows, w3, w2, w3, vec, w3, w2, w3, vec, vec)
    out_specs = (rows, rows, w3, w2, w3, w3, w2, w3, vec, vec, vec)
    return jax.shard_map(body, mesh=mesh, in_specs=in_specs, out_specs=out_specs, check_vma=False)
```

```python
import functools
import itertools
import math

import jax
import jax.numpy as jnp
from jax import lax
from jax.experimental import pallas as pl
from jax.experimental.pallas import tpu as pltpu
from jax.sharding import Mesh, PartitionSpec as P

D = 768
H = 12
HD = 64
ROT = 16
FF = 3072
SWEEPS = 5
STEP = 10
LEN = 256
VEC = 2 * D + FF + D
VEC_ROWS = 12

NS = (3.4445, -4.775, 2.0315)
BF = jnp.bfloat16
F32 = jnp.float32
BLK = 256
BLK_ROWS = 96
NB = D // BLK

DP = ("z", "x", "yh", "c")
ALL = ("z", "x", "yh", "c", "t")


def pull(value, axis, k):
    n = lax.axis_size(axis)
    return lax.ppermute(value, axis, [((i + k) % n, i) for i in range(n)])


def move(value, source):
    sizes = [lax.axis_size(a) for a in ALL]
    index = lambda at: functools.reduce(lambda total, one: total * one[0] + one[1] % one[0], zip(sizes, at), 0)
    pairs = []
    for here in itertools.product(*map(range, sizes)):
        there = source(*here)
        if there is not None:
            pairs.append((index(there), index(here)))
    return lax.ppermute(value, ALL, pairs)


def pull_outer(value, k):
    return move(value, lambda z, x, y, c, t: (z, x + k, y, c, t) if c == 0 else (z + k, x, y, c, t))


def pull_inner(value, k):
    return move(value, lambda z, x, y, c, t: (z + k, x, y, c, t) if c == 0 else (z, x + k, y, c, t))


def pull_yh(value, k):
    return pull(value, "yh", k)


def gather_ring(value, pulls, n):
    return [value] + [pulls(value, k) for k in range(1, n)]


def sum_ring(parts, pulls):
    n = len(parts)
    total = parts[0].astype(F32)
    for k in range(1, n):
        total = total + pulls(parts[k].astype(BF), n - k).astype(F32)
    return total


def dot(a, b, dims):
    return lax.dot_general(a, b, (dims, ((), ())), preferred_element_type=F32)


def pieces(value, n):
    out = []
    for _ in range(n):
        low = value.astype(BF)
        out.append(low)
        value = value - low.astype(F32)
    return out


def mul(xs, ys, dims=((1,), (0,))):
    n = len(xs)
    total = None
    for order in reversed(range(n)):
        for i in range(order + 1):
            term = lax.dot_general(xs[i], ys[order - i], (dims, ((), ())), preferred_element_type=F32)
            total = term if total is None else total + term
    return total


def gram_kernel(core_ref, *refs):
    *in_refs, keep_ref, give_ref, wide_ref = refs
    at = 0
    for ref in in_refs:
        n = ref.shape[0] // BLK_ROWS * BLK_ROWS
        for k, piece in enumerate(pieces(ref[:n], 3)):
            wide_ref[k, at : at + n] = piece
        at += n
    xs = [wide_ref[k] for k in range(3)]
    dims = ((0,), (0,))
    cut = lambda i: slice(i * BLK, (i + 1) * BLK)
    top = mul([x[:, cut(0)] for x in xs], xs, dims)
    mid = mul([x[:, cut(1)] for x in xs], [x[:, BLK:] for x in xs], dims)
    low = mul([x[:, cut(2)] for x in xs], [x[:, 2 * BLK :] for x in xs], dims)
    first = core_ref[0] == 0

    @pl.when(first)
    def _():
        keep_ref[...] = top
        give_ref[:, : 2 * BLK] = mid
        give_ref[:, 2 * BLK :] = low

    @pl.when(jnp.logical_not(first))
    def _():
        give_ref[...] = top
        keep_ref[:, : 2 * BLK] = mid
        keep_ref[:, 2 * BLK :] = low


def blocks(i, j):
    return (slice(i * BLK, (i + 1) * BLK), slice(j * BLK, (j + 1) * BLK))


def put(refs, i, j, value):
    for ref, piece in zip(refs, pieces(value, len(refs))):
        ref[blocks(i, j)] = piece


def put_both(refs, i, j, value):
    put(refs, i, j, value)
    if i != j:
        put(refs, j, i, value.T)


def symmetric_product(xs, ys, emit, start=0):
    for i in range(start, NB):
        rows = slice(i * BLK, (i + 1) * BLK)
        wide = mul([x[rows, :] for x in xs], [y[:, i * BLK :] for y in ys])
        for j in range(i, NB):
            emit(i, j, wide[:, (j - i) * BLK : (j - i + 1) * BLK])


def sweeps_kernel(core_ref, mine_ref, rest_ref, x_ref, out_ref, top_ref, bottom_ref, gram_ref, a_ref, p_ref, b_ref):
    first = core_ref[0] == 0
    n_x = x_ref.shape[0]

    @pl.when(first)
    def _():
        top_ref[...] = mine_ref[...]
        bottom_ref[...] = rest_ref[...]

    @pl.when(jnp.logical_not(first))
    def _():
        top_ref[...] = rest_ref[...]
        bottom_ref[...] = mine_ref[...]

    def packed(i, j):
        if i == 0:
            return top_ref[:, j * BLK : (j + 1) * BLK]
        at = (j - 1) if i == 1 else 2
        return bottom_ref[:, at * BLK : (at + 1) * BLK]

    eye = (lax.broadcasted_iota(jnp.int32, (BLK, BLK), 0) == lax.broadcasted_iota(jnp.int32, (BLK, BLK), 1)).astype(F32)
    trace = sum(jnp.sum(packed(i, i) * eye) for i in range(NB))
    norm = jnp.sqrt(jnp.full((8, 128), trace, F32)) + 1e-07
    factor = (1.0 / norm)[0:1, 0:1]
    square = factor * factor

    a_rows = lambda n: [a_ref.at[k, n_x : n_x + D] for k in range(n)]
    p_rows = lambda n: [p_ref.at[k] for k in range(n)]
    b_rows = lambda n: [b_ref.at[k] for k in range(n)]

    def put_x(n, value):
        for k, piece in enumerate(pieces(value, n)):
            a_ref[k, :n_x] = piece

    for i in range(NB):
        for j in range(i, NB):
            value = packed(i, j) * square
            gram_ref[blocks(i, j)] = value
            put_both(a_rows(3), i, j, value)
    put_x(3, x_ref[...] * factor)

    def poly(n_p):
        def emit(i, j, block):
            value = NS[1] * gram_ref[blocks(i, j)] + NS[2] * block
            if i == j:
                value = value + NS[0] * eye
            put_both(p_rows(n_p), i, j, value)

        a = a_rows(2)
        symmetric_product(a, a, emit)

    def next_gram(n, keep):
        p = p_rows(n)
        rows = slice(0, n_x + BLK)
        wide = mul([a_ref[k, rows] for k in range(n)], [y[...] for y in p])
        for j in range(NB):
            put_both(b_rows(n), 0, j, wide[n_x:, j * BLK : (j + 1) * BLK])
        symmetric_product(a_rows(n), p, lambda i, j, block: put_both(b_rows(n), i, j, block), 1)
        put_x(keep, wide[:n_x])

        def emit(i, j, block):
            gram_ref[blocks(i, j)] = block
            put_both(a_rows(keep), i, j, block)

        symmetric_product(b_rows(n), p, emit)

    poly(3)
    next_gram(3, 2)

    @pl.loop(1, SWEEPS - 1)
    def _(_):
        poly(2)
        next_gram(2, 2)

    poly(2)
    out_ref[...] = mul([a_ref[k, :n_x] for k in range(2)], [y[...] for y in p_rows(2)])


SMEM = pl.BlockSpec(memory_space=pltpu.SMEM)
VM = pl.BlockSpec(memory_space=pltpu.VMEM)


def gram_parts(core, held):
    rows = sum(v.shape[0] // BLK_ROWS * BLK_ROWS for v in held)
    return pl.pallas_call(
        gram_kernel,
        out_shape=[jax.ShapeDtypeStruct((BLK, D), F32)] * 2,
        in_specs=[SMEM] + [VM] * len(held),
        out_specs=[VM, VM],
        scratch_shapes=[pltpu.VMEM((3, rows, D), BF)],
        compiler_params=pltpu.CompilerParams(vmem_limit_bytes=48 << 20),
        cost_estimate=pl.CostEstimate(flops=2 * D * D * D * 4, bytes_accessed=4 * D * D * 2, transcendentals=0),
    )(core, *held)


def sweeps(core, mine, rest, x_rows):
    return pl.pallas_call(
        sweeps_kernel,
        out_shape=jax.ShapeDtypeStruct(x_rows.shape, F32),
        in_specs=[SMEM, VM, VM, VM],
        out_specs=VM,
        scratch_shapes=[
            pltpu.VMEM((BLK, D), F32),
            pltpu.VMEM((BLK, D), F32),
            pltpu.VMEM((D, D), F32),
            pltpu.VMEM((3, x_rows.shape[0] + D, D), BF),
            pltpu.VMEM((3, D, D), BF),
            pltpu.VMEM((3, D, D), BF),
        ],
        compiler_params=pltpu.CompilerParams(vmem_limit_bytes=48 << 20),
        cost_estimate=pl.CostEstimate(flops=2 * D * D * D * 32, bytes_accessed=4 * D * D, transcendentals=0),
    )(core, mine, rest, x_rows)


def gelu_parts(u):
    k0 = math.sqrt(2.0 / math.pi)
    th = jnp.tanh(k0 * (u + 0.044715 * (u * u * u)))
    value = 0.5 * u * (1.0 + th)
    slope = 0.5 * (1.0 + th) + 0.5 * u * (1.0 - th * th) * (k0 * (1.0 + 3.0 * 0.044715 * u * u))
    return value, slope


HEADS = 3
PAD = 128
HC = HEADS * HD
HP = HEADS * PAD
NN = ((1,), (0,))
NT = ((1,), (1,))
TN = ((0,), (0,))


def iota(shape, dim):
    return lax.broadcasted_iota(jnp.int32, shape, dim)


def one_hot(cond):
    return jnp.where(cond, 1.0, 0.0).astype(BF)


def home_place(at_ref, r):
    zi, xi, yi, ci = (at_ref[k] for k in range(4))
    n = 6
    group = jnp.right_shift(r * 10923, 16)
    lane = r - n * group
    mat = jnp.bitwise_and(group, 3)
    y = jnp.bitwise_and(jnp.right_shift(group, 2) + yi, 1)
    inner = jnp.bitwise_and(jnp.right_shift(group, 3), 3)
    outer = jnp.bitwise_and(jnp.right_shift(group, 5), 3)
    core = jnp.bitwise_and(jnp.right_shift(group, 7) + ci, 1)
    first = core == 0
    z = jnp.bitwise_and(jnp.where(first, inner, outer) + zi, 3)
    x = jnp.bitwise_and(jnp.where(first, outer, inner) + xi, 3)
    column = (((z * 4 + x) * 2 + y) * 2 + core) * n + lane - HC * ci
    return jnp.where((column >= 0) & (column < HC), mat * HC + column, -1)


def unit_place(at_ref, n):
    zi, xi, yi, ci, ti = (at_ref[k] for k in range(5))
    width = 24
    group = jnp.right_shift(n * 2731, 16)
    lane = n - width * group
    y = jnp.bitwise_and(group + yi, 1)
    inner = jnp.bitwise_and(jnp.right_shift(group, 1), 3)
    outer = jnp.bitwise_and(jnp.right_shift(group, 3), 3)
    z = jnp.bitwise_and(jnp.where(ci == 0, inner, outer) + zi, 3)
    x = jnp.bitwise_and(jnp.where(ci == 0, outer, inner) + xi, 3)
    row = 2 * ti + jnp.right_shift(z, 1)
    return row, (((jnp.bitwise_and(z, 1) * 4 + x) * 2 + y) * 2 + ci) * width + lane


def attention_kernel(
    at_ref, own0_ref, own1_ref, own2_ref, own3_ref, got0_ref, got1_ref, got2_ref, got3_ref, normed_ref, cot_ref, cos_ref, sin_ref,
    sums_ref, keep_ref, give_ref,
    att_ref, wq_ref, wk_ref, wv_ref, wo_ref, q_ref, k_ref, v_ref, da_ref, heads_ref, dq_ref, dk_ref, dv_ref, nat_ref,
):
    span = own0_ref.shape[0]
    for k, ref in enumerate((own0_ref, own1_ref, own2_ref, own3_ref, got0_ref, got1_ref, got2_ref, got3_ref)):
        att_ref[k * span : (k + 1) * span] = ref[...]

    n_rows, n_all = 4 * HC, att_ref.shape[0]
    pick = one_hot(iota((n_rows, n_all), 0) == home_place(at_ref, iota((8, n_all), 1))[:1])
    w_att = dot(pick, att_ref[...], NN).astype(BF)
    r = iota((HC, HC), 0)
    e = jnp.bitwise_and(r, HD - 1)
    half = ROT // 2
    source = jnp.where(e < half, r + half, jnp.where(e < ROT, r - half, -1))
    exchange = one_hot(iota((HC, HC), 1) == source)
    blank = jnp.zeros((HD, D), BF)
    for m, ref in enumerate((wq_ref, wk_ref)):
        own = w_att[m * HC : (m + 1) * HC]
        swapped = dot(exchange, own, NN).astype(BF)
        for h in range(HEADS):
            base = h * 2 * PAD
            ref[base : base + HD] = own[h * HD : (h + 1) * HD]
            ref[base + HD : base + PAD] = blank
            ref[base + PAD : base + PAD + HD] = swapped[h * HD : (h + 1) * HD]
            ref[base + PAD + HD : base + 2 * PAD] = blank
    for m, ref in ((2, wv_ref), (3, wo_ref)):
        for h in range(HEADS):
            ref[h * PAD : h * PAD + HD] = w_att[m * HC + h * HD : m * HC + (h + 1) * HD]
            ref[h * PAD + HD : (h + 1) * PAD] = blank

    cos, sin = cos_ref[...], sin_ref[...]
    for w_ref, ref in ((wq_ref, q_ref), (wk_ref, k_ref)):
        lin = dot(normed_ref[...], w_ref[...], NT)
        for s in range(2):
            rows = slice(s * LEN, (s + 1) * LEN)
            for h in range(HEADS):
                base = h * 2 * PAD
                own, other = lin[rows, base : base + PAD], lin[rows, base + PAD : base + 2 * PAD]
                ref[rows, base : base + PAD] = (own * cos + other * sin).astype(BF)
                ref[rows, base + PAD : base + 2 * PAD] = (other * cos - own * sin).astype(BF)
    v_ref[...] = dot(normed_ref[...], wv_ref[...], NT).astype(BF)
    da_ref[...] = dot(cot_ref[...], wo_ref[...], NT).astype(BF)

    turn = at_ref[4] * (LEN // 2)
    at_q = jnp.bitwise_xor(iota((LEN, LEN), 0), turn)
    at_k = jnp.bitwise_xor(iota((LEN, LEN), 1), turn)
    causal = at_q >= at_k
    scale = HD ** (-0.5)
    for s in range(2):
        rows = slice(s * LEN, (s + 1) * LEN)
        for h in range(HEADS):
            two = slice(h * 2 * PAD, (h + 1) * 2 * PAD)
            one = slice(h * 2 * PAD, h * 2 * PAD + PAD)
            lanes = slice(h * PAD, (h + 1) * PAD)
            value, d_att = v_ref[rows, lanes], da_ref[rows, lanes]
            scores = jnp.where(causal, dot(q_ref[rows, one], k_ref[rows, one], NT) * scale, -1e30)
            raised = jnp.exp(scores - jnp.max(scores, axis=1, keepdims=True))
            probs = raised / jnp.sum(raised, axis=1, keepdims=True)
            low = probs.astype(BF)
            heads_ref[rows, lanes] = dot(low, value, NN).astype(BF)
            dv_ref[rows, lanes] = dot(low, d_att, TN).astype(BF)
            d_probs = dot(d_att, value, NT)
            d_scores = (probs * (d_probs - jnp.sum(probs * d_probs, axis=1, keepdims=True))).astype(BF)
            d_q = dot(d_scores, k_ref[rows, two], NN) * scale
            d_k = dot(d_scores, q_ref[rows, two], TN) * scale
            dq_ref[rows, lanes] = (d_q[:, :PAD] * cos - d_q[:, PAD:] * sin).astype(BF)
            dk_ref[rows, lanes] = (d_k[:, :PAD] * cos - d_k[:, PAD:] * sin).astype(BF)

    sums_ref[0] = dot(heads_ref[...], wo_ref[...], NN)
    total = dot(dv_ref[...], wv_ref[...], NN)
    for h in range(HEADS):
        one = slice(h * 2 * PAD, h * 2 * PAD + PAD)
        lanes = slice(h * PAD, (h + 1) * PAD)
        total = total + dot(dq_ref[:, lanes], wq_ref[one], NN) + dot(dk_ref[:, lanes], wk_ref[one], NN)
    sums_ref[1] = total

    for m, (ref, with_ref) in enumerate(((dq_ref, normed_ref), (dk_ref, normed_ref), (dv_ref, normed_ref), (heads_ref, cot_ref))):
        grad = dot(ref[...], with_ref[...], TN).astype(BF)
        for h in range(HEADS):
            nat_ref[m * HC + h * HD : m * HC + (h + 1) * HD] = grad[h * PAD : h * PAD + HD]
    half_rows = n_all // 2
    for ref, base in ((keep_ref, 0), (give_ref, half_rows)):
        place = home_place(at_ref, iota((half_rows, 128), 0) + base)
        pick = jnp.concatenate([one_hot(iota((half_rows, 128), 1) + b == place) for b in range(0, n_rows, 128)], axis=1)
        ref[...] = dot(pick, nat_ref[...], NN).astype(BF)


def forward_kernel(
    at_ref, held0_ref, held1_ref, held2_ref, held3_ref, normed_ref, cot_ref, bias_ref, sums_ref,
    own_ref, peer_ref, gbias_ref, out0_ref, out1_ref, out2_ref, out3_ref,
    win_ref, wback_ref,
):
    span = held0_ref.shape[1]
    for s, ref in enumerate((held0_ref, held1_ref, held2_ref, held3_ref)):
        win_ref[s * span : (s + 1) * span] = ref[0]
        wback_ref[s * span : (s + 1) * span] = ref[1]

    def send(group, grad):
        for s, ref in enumerate((out0_ref, out1_ref, out2_ref, out3_ref)):
            ref[group] = grad[s * span : (s + 1) * span]

    hidden, slope = gelu_parts(dot(normed_ref[...], win_ref[...], NT) + bias_ref[...])
    hidden = hidden.astype(BF)


    def give_rows(k, value):
        own_ref[k] = value[:LEN]
        peer_ref[k] = value[LEN:]

    give_rows(0, sums_ref[0] + dot(hidden, wback_ref[...], NN))
    send(1, dot(hidden, cot_ref[...], TN).astype(BF))
    d_pre = (dot(cot_ref[...], wback_ref[...], NT) * slope).astype(BF)
    grad_bias = jnp.sum(d_pre.astype(F32), axis=0, keepdims=True)
    n_units = win_ref.shape[0]
    bias_row, _ = unit_place(at_ref, iota((8, n_units), 1))
    spread = pieces(jnp.where(bias_row == iota((8, n_units), 0), grad_bias, 0.0), 3)
    _, bias_lane = unit_place(at_ref, iota((n_units, 128), 0))
    to_lane = jnp.concatenate([one_hot(iota((n_units, 128), 1) + b == bias_lane) for b in range(0, D, 128)], axis=1)
    gbias_ref[...] = sum(dot(piece, to_lane, NN) for piece in reversed(spread))
    send(0, dot(d_pre, normed_ref[...], TN).astype(BF))
    give_rows(1, sums_ref[1] + dot(d_pre, win_ref[...], NN))


def out(shape, dtype):
    return jax.ShapeDtypeStruct(shape, dtype)


def low(*shape):
    return pltpu.VMEM(shape, BF)


def attention(at, own, got, normed, cot, cos, sin):
    n = normed.shape[0]
    rows = 4 * own[0].shape[0]
    return pl.pallas_call(
        attention_kernel,
        out_shape=[out((2, n, D), F32), out((rows, D), BF), out((rows, D), BF)],
        in_specs=[SMEM] + [VM] * 12,
        out_specs=[VM] * 3,
        scratch_shapes=[low(2 * rows, D), low(2 * HP, D), low(2 * HP, D), low(HP, D), low(HP, D)]
        + [low(n, 2 * HP), low(n, 2 * HP)]
        + [low(n, HP)] * 6
        + [low(4 * HC, D)],
        compiler_params=pltpu.CompilerParams(vmem_limit_bytes=56 << 20),
        cost_estimate=pl.CostEstimate(flops=12 * 10**9, bytes_accessed=16 << 20, transcendentals=10**6),
    )(at, *own, *got, normed, cot, cos, sin)


def feed_forward(at, held, normed, cot, bias, sums):
    n = normed.shape[0]
    span = held[0].shape[1]
    units = 4 * span
    return pl.pallas_call(
        forward_kernel,
        out_shape=[out((2, n // 2, D), F32), out((2, n // 2, D), F32), out((8, D), F32)] + [out((2, span, D), BF)] * 4,
        in_specs=[SMEM] + [VM] * 8,
        out_specs=[VM] * 7,
        scratch_shapes=[low(units, D), low(units, D)],
        compiler_params=pltpu.CompilerParams(vmem_limit_bytes=56 << 20),
        cost_estimate=pl.CostEstimate(flops=10 * 10**9, bytes_accessed=16 << 20, transcendentals=10**6),
    )(at, *held, normed, cot, bias, sums)


def body(tokens, cotangent, qkv_weight, out_weight, fc_weight, vectors, qkv_momentum, out_momentum, fc_momentum, vector_first, vector_second):
    zi, xi, yi, ci, ti = (lax.axis_index(a) for a in ALL)
    rows = tokens.shape[0]
    n_att = qkv_weight.shape[3]
    n_fc = fc_weight.shape[3]
    gain, shift = vectors[:D], vectors[D : 2 * D]
    bias_in, bias_out = vectors[2 * D : 2 * D + FF], vectors[2 * D + FF :]

    first = ci == 0
    attn_rows = jnp.concatenate([jnp.transpose(qkv_weight[:, :, 0, :], (0, 2, 1)), jnp.transpose(out_weight[:, 0, :])[None]])
    fc_rows = jnp.transpose(fc_weight[:, :, 0, :], (0, 2, 1))
    own_rows = jnp.concatenate([attn_rows.reshape(1, n_fc, D), fc_rows]).astype(BF)
    held = jnp.stack(gather_ring(own_rows, pull_yh, 2), axis=1)

    inputs = tokens.astype(F32)
    average = jnp.mean(inputs, axis=-1, keepdims=True)
    deviation = inputs - average
    variance = jnp.mean(deviation * deviation, axis=-1, keepdims=True)
    inv_spread = lax.rsqrt(variance + 1e-05)
    centred = deviation * inv_spread
    normed_own = (centred * gain + shift).astype(BF)
    both = jnp.stack([normed_own, cotangent])
    held, both = lax.optimization_barrier((held, both))
    held = jnp.stack(gather_ring(held, pull_inner, 4), axis=1)
    both = jnp.stack([both, pull(both, "t", 1)], axis=1)
    held, both = lax.optimization_barrier((held, both))
    span = 8 * n_fc
    held = held.reshape(3, span, D)
    att_held = gather_ring(held[0], pull_outer, 4)
    fc_held = gather_ring(held[1:], pull_outer, 4)
    both = jnp.stack([both, pull(both, "c", 1)], axis=1)
    n_all = 4 * rows
    normed, cot = both[0].reshape(n_all, D), both[1].reshape(n_all, D)

    half = jnp.arange(LEN) // rows
    position = ((ti + half) % 2) * rows + jnp.arange(LEN) % rows
    frequency = 10000.0 ** (-2.0 * jnp.arange(ROT // 2, dtype=F32) / ROT)
    angles = position.astype(F32)[:, None] * frequency[None, :]
    cos_t, sin_t = jnp.cos(angles), jnp.sin(angles)
    pad = lambda a, b, fill: jnp.concatenate([a, b, jnp.full((LEN, PAD - ROT), fill, F32)], axis=1)
    cos_full, sin_full = pad(cos_t, cos_t, 1.0), pad(-sin_t, sin_t, 0.0)

    bias6 = bias_in.reshape(2, 4, 4, 2, 2, n_fc)
    bias6 = jnp.concatenate([bias6, bias6], axis=1)
    bias6 = jnp.concatenate([bias6, bias6], axis=2)
    bias6 = jnp.concatenate([bias6, bias6], axis=3)
    bias_own = lax.dynamic_slice(bias6, (ti, zi, xi, yi, ci, 0), (1, 4, 4, 2, 1, n_fc))[0, :, :, :, 0]
    by_turn = lambda v: jnp.where(first, jnp.swapaxes(v, 0, 1), v)
    bias_own = by_turn(bias_own).reshape(1, 32 * n_fc)
    at = jnp.stack([zi, xi, yi, ci, ti]).astype(jnp.int32)
    mom_rows = jnp.concatenate(
        [
            jnp.transpose(qkv_momentum[:, :, 0, :], (0, 2, 1)).reshape(3 * n_att, D),
            jnp.transpose(out_momentum[:, 0, :]),
            jnp.transpose(fc_momentum[:, :, 0, :], (0, 2, 1)).reshape(2 * n_fc, D),
        ]
    )
    far, normed, cot, bias_own, at, cos_full, sin_full, mom_rows = lax.optimization_barrier(
        (att_held[1:], normed, cot, bias_own, at, cos_full, sin_full, mom_rows)
    )
    att_held = att_held[:1] + far
    att_got = [pull(v, "c", 1) for v in att_held]
    sums, att_keep, att_give = attention(at, att_held, att_got, normed, cot, cos_full, sin_full)

    att_grad = (att_keep + pull(att_give, "c", 1)).reshape(4, span, D)
    att_parts = [att_grad[k] for k in range(4)]

    rows_own, rows_peer, grad_bias_in, *fc_parts = feed_forward(at, fc_held, normed, cot, bias_own, sums)
    att_total = sum_ring(att_parts, pull_outer)
    fc_total = sum_ring(fc_parts, pull_outer)
    rows_own = (rows_own + pull(rows_peer, "c", 1)).reshape(2, 2, rows, D)
    rows_own = rows_own[:, 0] + pull(rows_own[:, 1].astype(BF), "t", 1).astype(F32)
    att_total, fc_total, rows_own = lax.optimization_barrier((att_total, fc_total, rows_own))
    total = jnp.concatenate([att_total[None], fc_total]).reshape(3, 4, 2, n_fc, D)
    total = sum_ring([total[:, k] for k in range(4)], pull_inner)
    total = sum_ring([total[:, k] for k in range(2)], pull_yh).reshape(3 * n_fc, D)

    mixed = (inputs + rows_own[0] + bias_out).astype(BF)
    d_rows = rows_own[1]
    d_hat = d_rows * gain
    correction = d_hat - jnp.mean(d_hat, axis=-1, keepdims=True) - centred * jnp.mean(d_hat * centred, axis=-1, keepdims=True)
    own_cot = cotangent.astype(F32)
    input_grad = own_cot + correction * inv_spread

    total_of = lambda v: jnp.sum(v, axis=0, keepdims=True)
    vec_rows = [total_of(d_rows * centred), total_of(d_rows), grad_bias_in[: FF // D], total_of(own_cot), jnp.zeros((VEC_ROWS - VEC // D, D), F32)]

    moment = 0.95 * mom_rows + total
    update = total + 0.95 * moment

    half_fc = n_fc // 2
    att_u = update[: 4 * n_att].reshape(4, n_att, D)
    att_u = jnp.concatenate([att_u, jnp.zeros((4, half_fc - n_att, D), F32)], axis=1)
    fc_u = update[4 * n_att :].reshape(4, half_fc, D)
    vec_rows = jnp.concatenate(vec_rows)
    chunks = jnp.concatenate([att_u, fc_u])
    chunks = jnp.concatenate([chunks, jnp.broadcast_to(vec_rows, (8, VEC_ROWS, D))], axis=1)
    got = lax.all_to_all(chunks, ("z", "t"), split_axis=0, concat_axis=0, tiled=True)
    mine = got[:, :half_fc].reshape(8 * half_fc, D)
    vec_sum = jnp.sum(got[:, half_fc:], axis=0)[:8]
    to_yh_x = lambda k: lambda z, x, y, c, t: (z, x, y + 1, c, t) if c == 0 else (z, x + k, y, c, t)
    to_x_yh = lambda k: lambda z, x, y, c, t: (z, x + k, y, c, t) if c == 0 else (z, x, y + 1, c, t)
    only = lambda core, source: lambda z, x, y, c, t: source(z, x, y, c, t) if c == core else None
    n = mine.shape[0]
    load = jnp.concatenate([mine, vec_sum])
    near = [load, move(load, to_yh_x(1)), move(load, only(1, to_yh_x(2))), move(load, only(1, to_yh_x(3)))]
    vec_sum = sum(v[n:] for v in near)
    load = jnp.concatenate([near[0][:n], near[1][:n], vec_sum])
    load_2 = jnp.where(first, load, jnp.concatenate([near[2][:n], near[3][:n], jnp.zeros_like(vec_sum)]))
    far = [move(load, to_x_yh(1)), move(load_2, to_x_yh(2)), move(load, only(0, to_x_yh(3)))]
    vec_sum = vec_sum + sum(v[2 * n :] for v in far)
    core = ci.astype(jnp.int32)[None]
    keep, give = gram_parts(core, near + far)
    from_core = pull(jnp.concatenate([give, vec_sum]), "c", 1)
    part = keep + from_core[:BLK]
    vec_sum = vec_sum + from_core[BLK:]
    other = pull(part, "t", 1)
    part = jnp.where(zi >= 2, part + other, part)
    rest = pull(part, "c", 1)
    x_rows = sweeps(core, part, rest, mine)
    vector_grad = vec_sum[: VEC // D].reshape(VEC)
    first_new = 0.9 * vector_first + 0.1 * vector_grad
    second_new = 0.95 * vector_second + 0.05 * vector_grad * vector_grad
    step_size = first_new / (1.0 - 0.9**STEP) / (jnp.sqrt(second_new / (1.0 - 0.95**STEP)) + 1e-08)
    vector_new = vectors - 0.2 * step_size

    back = lax.all_to_all(x_rows, ("z", "t"), split_axis=0, concat_axis=0, tiled=True).reshape(8, half_fc, D)
    att_x = back[:4, :n_att]
    fc_x = back[4:].reshape(2, n_fc, D)

    def cols(v):
        return jnp.transpose(v, (0, 2, 1))[:, :, None, :]

    fc_factor = math.sqrt(FF / D)
    qkv_new = qkv_weight * 0.99 - cols(att_x[:3])
    out_new = out_weight * 0.99 - cols(att_x[3:])[0]
    fc_new = fc_weight * 0.99 - fc_factor * cols(fc_x)
    att_m = moment[: 4 * n_att].reshape(4, n_att, D)
    fc_m = moment[4 * n_att :].reshape(2, n_fc, D)
    return (mixed, input_grad, qkv_new, out_new, fc_new, cols(att_m[:3]), cols(att_m[3:])[0], cols(fc_m), first_new, second_new, vector_new)


def solution(mesh):
    mesh = Mesh(mesh.devices.reshape(4, 4, 2, 2, 2), ALL)
    rows = P(ALL, None)
    w3 = P(None, None, "t", DP)
    w2 = P(None, "t", DP)
    vec = P()
    in_specs = (rows, rows, w3, w2, w3, vec, w3, w2, w3, vec, vec)
    out_specs = (rows, rows, w3, w2, w3, w3, w2, w3, vec, vec, vec)
    return jax.shard_map(body, mesh=mesh, in_specs=in_specs, out_specs=out_specs, check_vma=False)
```

```python
import functools
import itertools
import math

import jax
import jax.numpy as jnp
from jax import lax
from jax.experimental import pallas as pl
from jax.experimental.pallas import tpu as pltpu
from jax.sharding import Mesh, PartitionSpec as P

D = 768
H = 12
HD = 64
ROT = 16
FF = 3072
SWEEPS = 5
STEP = 10
LEN = 256
VEC = 2 * D + FF + D
VEC_ROWS = 12

NS = (3.4445, -4.775, 2.0315)
BF = jnp.bfloat16
F32 = jnp.float32
BLK = 256
BLK_ROWS = 96
NB = D // BLK

DP = ("z", "x", "yh", "c")
ALL = ("z", "x", "yh", "c", "t")


def pull(value, axis, k):
    n = lax.axis_size(axis)
    return lax.ppermute(value, axis, [((i + k) % n, i) for i in range(n)])


def move(value, source):
    sizes = [lax.axis_size(a) for a in ALL]
    index = lambda at: functools.reduce(lambda total, one: total * one[0] + one[1] % one[0], zip(sizes, at), 0)
    pairs = []
    for here in itertools.product(*map(range, sizes)):
        there = source(*here)
        if there is not None:
            pairs.append((index(there), index(here)))
    return lax.ppermute(value, ALL, pairs)


def pull_outer(value, k):
    return move(value, lambda z, x, y, c, t: (z, x + k, y, c, t) if c == 0 else (z + k, x, y, c, t))


def pull_inner(value, k):
    return move(value, lambda z, x, y, c, t: (z + k, x, y, c, t) if c == 0 else (z, x + k, y, c, t))


def pull_yh(value, k):
    return pull(value, "yh", k)


def gather_ring(value, pulls, n):
    return [value] + [pulls(value, k) for k in range(1, n)]


def sum_ring(parts, pulls):
    n = len(parts)
    total = parts[0].astype(F32)
    for k in range(1, n):
        total = total + pulls(parts[k].astype(BF), n - k).astype(F32)
    return total


def dot(a, b, dims):
    return lax.dot_general(a, b, (dims, ((), ())), preferred_element_type=F32)


def pieces(value, n):
    out = []
    for _ in range(n):
        low = value.astype(BF)
        out.append(low)
        value = value - low.astype(F32)
    return out


def mul(xs, ys, dims=((1,), (0,))):
    n = len(xs)
    total = None
    for order in reversed(range(n)):
        for i in range(order + 1):
            term = lax.dot_general(xs[i], ys[order - i], (dims, ((), ())), preferred_element_type=F32)
            total = term if total is None else total + term
    return total


def gram_kernel(core_ref, *refs):
    *in_refs, keep_ref, give_ref, wide_ref = refs
    at = 0
    for ref in in_refs:
        n = ref.shape[0] // BLK_ROWS * BLK_ROWS
        for k, piece in enumerate(pieces(ref[:n], 3)):
            wide_ref[k, at : at + n] = piece
        at += n
    xs = [wide_ref[k] for k in range(3)]
    dims = ((0,), (0,))
    cut = lambda i: slice(i * BLK, (i + 1) * BLK)
    top = mul([x[:, cut(0)] for x in xs], xs, dims)
    mid = mul([x[:, cut(1)] for x in xs], [x[:, BLK:] for x in xs], dims)
    low = mul([x[:, cut(2)] for x in xs], [x[:, 2 * BLK :] for x in xs], dims)
    first = core_ref[0] == 0

    @pl.when(first)
    def _():
        keep_ref[...] = top
        give_ref[:, : 2 * BLK] = mid
        give_ref[:, 2 * BLK :] = low

    @pl.when(jnp.logical_not(first))
    def _():
        give_ref[...] = top
        keep_ref[:, : 2 * BLK] = mid
        keep_ref[:, 2 * BLK :] = low


def blocks(i, j):
    return (slice(i * BLK, (i + 1) * BLK), slice(j * BLK, (j + 1) * BLK))


def put(refs, i, j, value):
    for ref, piece in zip(refs, pieces(value, len(refs))):
        ref[blocks(i, j)] = piece


def put_both(refs, i, j, value):
    put(refs, i, j, value)
    if i != j:
        put(refs, j, i, value.T)


def symmetric_product(xs, ys, emit, start=0):
    for i in range(start, NB):
        rows = slice(i * BLK, (i + 1) * BLK)
        wide = mul([x[rows, :] for x in xs], [y[:, i * BLK :] for y in ys])
        for j in range(i, NB):
            emit(i, j, wide[:, (j - i) * BLK : (j - i + 1) * BLK])


def sweeps_kernel(core_ref, mine_ref, rest_ref, x_ref, out_ref, top_ref, bottom_ref, gram_ref, a_ref, p_ref, b_ref):
    first = core_ref[0] == 0
    n_x = x_ref.shape[0]

    @pl.when(first)
    def _():
        top_ref[...] = mine_ref[...]
        bottom_ref[...] = rest_ref[...]

    @pl.when(jnp.logical_not(first))
    def _():
        top_ref[...] = rest_ref[...]
        bottom_ref[...] = mine_ref[...]

    def packed(i, j):
        if i == 0:
            return top_ref[:, j * BLK : (j + 1) * BLK]
        at = (j - 1) if i == 1 else 2
        return bottom_ref[:, at * BLK : (at + 1) * BLK]

    eye = (lax.broadcasted_iota(jnp.int32, (BLK, BLK), 0) == lax.broadcasted_iota(jnp.int32, (BLK, BLK), 1)).astype(F32)
    trace = sum(jnp.sum(packed(i, i) * eye) for i in range(NB))
    norm = jnp.sqrt(jnp.full((8, 128), trace, F32)) + 1e-07
    factor = (1.0 / norm)[0:1, 0:1]
    square = factor * factor

    a_rows = lambda n: [a_ref.at[k, n_x : n_x + D] for k in range(n)]
    p_rows = lambda n: [p_ref.at[k] for k in range(n)]
    b_rows = lambda n: [b_ref.at[k] for k in range(n)]

    def put_x(n, value):
        for k, piece in enumerate(pieces(value, n)):
            a_ref[k, :n_x] = piece

    for i in range(NB):
        for j in range(i, NB):
            value = packed(i, j) * square
            gram_ref[blocks(i, j)] = value
            put_both(a_rows(3), i, j, value)
    put_x(3, x_ref[...] * factor)

    def poly(n_p):
        def emit(i, j, block):
            value = NS[1] * gram_ref[blocks(i, j)] + NS[2] * block
            if i == j:
                value = value + NS[0] * eye
            put_both(p_rows(n_p), i, j, value)

        a = a_rows(2)
        symmetric_product(a, a, emit)

    def next_gram(n, keep):
        p = p_rows(n)
        rows = slice(0, n_x + BLK)
        wide = mul([a_ref[k, rows] for k in range(n)], [y[...] for y in p])
        for j in range(NB):
            put_both(b_rows(n), 0, j, wide[n_x:, j * BLK : (j + 1) * BLK])
        symmetric_product(a_rows(n), p, lambda i, j, block: put_both(b_rows(n), i, j, block), 1)
        put_x(keep, wide[:n_x])

        def emit(i, j, block):
            gram_ref[blocks(i, j)] = block
            put_both(a_rows(keep), i, j, block)

        symmetric_product(b_rows(n), p, emit)

    poly(3)
    next_gram(3, 2)

    @pl.loop(1, SWEEPS - 1)
    def _(_):
        poly(2)
        next_gram(2, 2)

    poly(2)
    out_ref[...] = mul([a_ref[k, :n_x] for k in range(2)], [y[...] for y in p_rows(2)])


SMEM = pl.BlockSpec(memory_space=pltpu.SMEM)
VM = pl.BlockSpec(memory_space=pltpu.VMEM)


def gram_parts(core, held):
    rows = sum(v.shape[0] // BLK_ROWS * BLK_ROWS for v in held)
    return pl.pallas_call(
        gram_kernel,
        out_shape=[jax.ShapeDtypeStruct((BLK, D), F32)] * 2,
        in_specs=[SMEM] + [VM] * len(held),
        out_specs=[VM, VM],
        scratch_shapes=[pltpu.VMEM((3, rows, D), BF)],
        compiler_params=pltpu.CompilerParams(vmem_limit_bytes=48 << 20),
        cost_estimate=pl.CostEstimate(flops=2 * D * D * D * 4, bytes_accessed=4 * D * D * 2, transcendentals=0),
    )(core, *held)


def sweeps(core, mine, rest, x_rows):
    return pl.pallas_call(
        sweeps_kernel,
        out_shape=jax.ShapeDtypeStruct(x_rows.shape, F32),
        in_specs=[SMEM, VM, VM, VM],
        out_specs=VM,
        scratch_shapes=[
            pltpu.VMEM((BLK, D), F32),
            pltpu.VMEM((BLK, D), F32),
            pltpu.VMEM((D, D), F32),
            pltpu.VMEM((3, x_rows.shape[0] + D, D), BF),
            pltpu.VMEM((3, D, D), BF),
            pltpu.VMEM((3, D, D), BF),
        ],
        compiler_params=pltpu.CompilerParams(vmem_limit_bytes=48 << 20),
        cost_estimate=pl.CostEstimate(flops=2 * D * D * D * 32, bytes_accessed=4 * D * D, transcendentals=0),
    )(core, mine, rest, x_rows)


def gelu_parts(u):
    k0 = math.sqrt(2.0 / math.pi)
    th = jnp.tanh(k0 * (u + 0.044715 * (u * u * u)))
    value = 0.5 * u * (1.0 + th)
    slope = 0.5 * (1.0 + th) + 0.5 * u * (1.0 - th * th) * (k0 * (1.0 + 3.0 * 0.044715 * u * u))
    return value, slope


HEADS = 3
PAD = 128
HC = HEADS * HD
HP = HEADS * PAD
NN = ((1,), (0,))
NT = ((1,), (1,))
TN = ((0,), (0,))


def iota(shape, dim):
    return lax.broadcasted_iota(jnp.int32, shape, dim)


def one_hot(cond):
    return jnp.where(cond, 1.0, 0.0).astype(BF)


def home_place(at_ref, r):
    zi, xi, yi, ci = (at_ref[k] for k in range(4))
    n = 6
    group = jnp.right_shift(r * 10923, 16)
    lane = r - n * group
    mat = jnp.bitwise_and(group, 3)
    y = jnp.bitwise_and(jnp.right_shift(group, 2) + yi, 1)
    inner = jnp.bitwise_and(jnp.right_shift(group, 3), 3)
    outer = jnp.bitwise_and(jnp.right_shift(group, 5), 3)
    core = jnp.bitwise_and(jnp.right_shift(group, 7) + ci, 1)
    first = core == 0
    z = jnp.bitwise_and(jnp.where(first, inner, outer) + zi, 3)
    x = jnp.bitwise_and(jnp.where(first, outer, inner) + xi, 3)
    column = (((z * 4 + x) * 2 + y) * 2 + core) * n + lane - HC * ci
    return jnp.where((column >= 0) & (column < HC), mat * HC + column, -1)


def unit_place(at_ref, n):
    zi, xi, yi, ci, ti = (at_ref[k] for k in range(5))
    width = 24
    group = jnp.right_shift(n * 2731, 16)
    lane = n - width * group
    y = jnp.bitwise_and(group + yi, 1)
    inner = jnp.bitwise_and(jnp.right_shift(group, 1), 3)
    outer = jnp.bitwise_and(jnp.right_shift(group, 3), 3)
    z = jnp.bitwise_and(jnp.where(ci == 0, inner, outer) + zi, 3)
    x = jnp.bitwise_and(jnp.where(ci == 0, outer, inner) + xi, 3)
    row = 2 * ti + jnp.right_shift(z, 1)
    return row, (((jnp.bitwise_and(z, 1) * 4 + x) * 2 + y) * 2 + ci) * width + lane


def attention_kernel(
    at_ref, own0_ref, own1_ref, own2_ref, own3_ref, got0_ref, got1_ref, got2_ref, got3_ref, normed_ref, cot_ref, cos_ref, sin_ref,
    sums_ref, own_ref, peer_ref, keep_ref, give_ref,
    att_ref, wq_ref, wk_ref, wv_ref, wo_ref, q_ref, k_ref, v_ref, da_ref, heads_ref, dq_ref, dk_ref, dv_ref, nat_ref,
):
    span = own0_ref.shape[0]
    for k, ref in enumerate((own0_ref, own1_ref, own2_ref, own3_ref, got0_ref, got1_ref, got2_ref, got3_ref)):
        att_ref[k * span : (k + 1) * span] = ref[...]

    n_rows, n_all = 4 * HC, att_ref.shape[0]
    pick = one_hot(iota((n_rows, n_all), 0) == home_place(at_ref, iota((8, n_all), 1))[:1])
    w_att = dot(pick, att_ref[...], NN).astype(BF)
    r = iota((HC, HC), 0)
    e = jnp.bitwise_and(r, HD - 1)
    half = ROT // 2
    source = jnp.where(e < half, r + half, jnp.where(e < ROT, r - half, -1))
    exchange = one_hot(iota((HC, HC), 1) == source)
    blank = jnp.zeros((HD, D), BF)
    for m, ref in enumerate((wq_ref, wk_ref)):
        own = w_att[m * HC : (m + 1) * HC]
        swapped = dot(exchange, own, NN).astype(BF)
        for h in range(HEADS):
            base = h * 2 * PAD
            ref[base : base + HD] = own[h * HD : (h + 1) * HD]
            ref[base + HD : base + PAD] = blank
            ref[base + PAD : base + PAD + HD] = swapped[h * HD : (h + 1) * HD]
            ref[base + PAD + HD : base + 2 * PAD] = blank
    for m, ref in ((2, wv_ref), (3, wo_ref)):
        for h in range(HEADS):
            ref[h * PAD : h * PAD + HD] = w_att[m * HC + h * HD : m * HC + (h + 1) * HD]
            ref[h * PAD + HD : (h + 1) * PAD] = blank

    cos, sin = cos_ref[...], sin_ref[...]
    for w_ref, ref in ((wq_ref, q_ref), (wk_ref, k_ref)):
        lin = dot(normed_ref[...], w_ref[...], NT)
        for s in range(2):
            rows = slice(s * LEN, (s + 1) * LEN)
            for h in range(HEADS):
                base = h * 2 * PAD
                own, other = lin[rows, base : base + PAD], lin[rows, base + PAD : base + 2 * PAD]
                ref[rows, base : base + PAD] = (own * cos + other * sin).astype(BF)
                ref[rows, base + PAD : base + 2 * PAD] = (other * cos - own * sin).astype(BF)
    v_ref[...] = dot(normed_ref[...], wv_ref[...], NT).astype(BF)
    da_ref[...] = dot(cot_ref[...], wo_ref[...], NT).astype(BF)

    turn = at_ref[4] * (LEN // 2)
    at_q = jnp.bitwise_xor(iota((LEN, LEN), 0), turn)
    at_k = jnp.bitwise_xor(iota((LEN, LEN), 1), turn)
    causal = at_q >= at_k
    scale = HD ** (-0.5)
    for s in range(2):
        rows = slice(s * LEN, (s + 1) * LEN)
        for h in range(HEADS):
            two = slice(h * 2 * PAD, (h + 1) * 2 * PAD)
            one = slice(h * 2 * PAD, h * 2 * PAD + PAD)
            lanes = slice(h * PAD, (h + 1) * PAD)
            value, d_att = v_ref[rows, lanes], da_ref[rows, lanes]
            scores = jnp.where(causal, dot(q_ref[rows, one], k_ref[rows, one], NT) * scale, -1e30)
            raised = jnp.exp(scores - jnp.max(scores, axis=1, keepdims=True))
            probs = raised / jnp.sum(raised, axis=1, keepdims=True)
            low = probs.astype(BF)
            heads_ref[rows, lanes] = dot(low, value, NN).astype(BF)
            dv_ref[rows, lanes] = dot(low, d_att, TN).astype(BF)
            d_probs = dot(d_att, value, NT)
            d_scores = (probs * (d_probs - jnp.sum(probs * d_probs, axis=1, keepdims=True))).astype(BF)
            d_q = dot(d_scores, k_ref[rows, two], NN) * scale
            d_k = dot(d_scores, q_ref[rows, two], TN) * scale
            dq_ref[rows, lanes] = (d_q[:, :PAD] * cos - d_q[:, PAD:] * sin).astype(BF)
            dk_ref[rows, lanes] = (d_k[:, :PAD] * cos - d_k[:, PAD:] * sin).astype(BF)

    def give_rows(k, value):
        own_ref[k] = value[:LEN]
        peer_ref[k] = value[LEN:]

    give_rows(0, sums_ref[0] + dot(heads_ref[...], wo_ref[...], NN))
    total = sums_ref[1] + dot(dv_ref[...], wv_ref[...], NN)
    for h in range(HEADS):
        one = slice(h * 2 * PAD, h * 2 * PAD + PAD)
        lanes = slice(h * PAD, (h + 1) * PAD)
        total = total + dot(dq_ref[:, lanes], wq_ref[one], NN) + dot(dk_ref[:, lanes], wk_ref[one], NN)
    give_rows(1, total)

    for m, (ref, with_ref) in enumerate(((dq_ref, normed_ref), (dk_ref, normed_ref), (dv_ref, normed_ref), (heads_ref, cot_ref))):
        grad = dot(ref[...], with_ref[...], TN).astype(BF)
        for h in range(HEADS):
            nat_ref[m * HC + h * HD : m * HC + (h + 1) * HD] = grad[h * PAD : h * PAD + HD]
    half_rows = n_all // 2
    for ref, base in ((keep_ref, 0), (give_ref, half_rows)):
        place = home_place(at_ref, iota((half_rows, 128), 0) + base)
        pick = jnp.concatenate([one_hot(iota((half_rows, 128), 1) + b == place) for b in range(0, n_rows, 128)], axis=1)
        ref[...] = dot(pick, nat_ref[...], NN).astype(BF)


def forward_kernel(
    at_ref, held0_ref, held1_ref, held2_ref, held3_ref, normed_ref, cot_ref, bias_ref,
    sums_ref, gbias_ref, out0_ref, out1_ref, out2_ref, out3_ref,
    win_ref, wback_ref,
):
    span = held0_ref.shape[1]
    for s, ref in enumerate((held0_ref, held1_ref, held2_ref, held3_ref)):
        win_ref[s * span : (s + 1) * span] = ref[0]
        wback_ref[s * span : (s + 1) * span] = ref[1]

    def send(group, grad):
        for s, ref in enumerate((out0_ref, out1_ref, out2_ref, out3_ref)):
            ref[group] = grad[s * span : (s + 1) * span]

    hidden, slope = gelu_parts(dot(normed_ref[...], win_ref[...], NT) + bias_ref[...])
    hidden = hidden.astype(BF)


    sums_ref[0] = dot(hidden, wback_ref[...], NN)
    send(1, dot(hidden, cot_ref[...], TN).astype(BF))
    d_pre = (dot(cot_ref[...], wback_ref[...], NT) * slope).astype(BF)
    grad_bias = jnp.sum(d_pre.astype(F32), axis=0, keepdims=True)
    n_units = win_ref.shape[0]
    bias_row, _ = unit_place(at_ref, iota((8, n_units), 1))
    spread = pieces(jnp.where(bias_row == iota((8, n_units), 0), grad_bias, 0.0), 3)
    _, bias_lane = unit_place(at_ref, iota((n_units, 128), 0))
    to_lane = jnp.concatenate([one_hot(iota((n_units, 128), 1) + b == bias_lane) for b in range(0, D, 128)], axis=1)
    gbias_ref[...] = sum(dot(piece, to_lane, NN) for piece in reversed(spread))
    send(0, dot(d_pre, normed_ref[...], TN).astype(BF))
    sums_ref[1] = dot(d_pre, win_ref[...], NN)


def out(shape, dtype):
    return jax.ShapeDtypeStruct(shape, dtype)


def low(*shape):
    return pltpu.VMEM(shape, BF)


def attention(at, own, got, normed, cot, cos, sin, sums):
    n = normed.shape[0]
    rows = 4 * own[0].shape[0]
    return pl.pallas_call(
        attention_kernel,
        out_shape=[out((2, n // 2, D), F32), out((2, n // 2, D), F32), out((rows, D), BF), out((rows, D), BF)],
        in_specs=[SMEM] + [VM] * 13,
        out_specs=[VM] * 4,
        scratch_shapes=[low(2 * rows, D), low(2 * HP, D), low(2 * HP, D), low(HP, D), low(HP, D)]
        + [low(n, 2 * HP), low(n, 2 * HP)]
        + [low(n, HP)] * 6
        + [low(4 * HC, D)],
        compiler_params=pltpu.CompilerParams(vmem_limit_bytes=56 << 20),
        cost_estimate=pl.CostEstimate(flops=12 * 10**9, bytes_accessed=16 << 20, transcendentals=10**6),
    )(at, *own, *got, normed, cot, cos, sin, sums)


def feed_forward(at, held, normed, cot, bias):
    n = normed.shape[0]
    span = held[0].shape[1]
    units = 4 * span
    return pl.pallas_call(
        forward_kernel,
        out_shape=[out((2, n, D), F32), out((8, D), F32)] + [out((2, span, D), BF)] * 4,
        in_specs=[SMEM] + [VM] * 7,
        out_specs=[VM] * 6,
        scratch_shapes=[low(units, D), low(units, D)],
        compiler_params=pltpu.CompilerParams(vmem_limit_bytes=56 << 20),
        cost_estimate=pl.CostEstimate(flops=10 * 10**9, bytes_accessed=16 << 20, transcendentals=10**6),
    )(at, *held, normed, cot, bias)


def body(tokens, cotangent, qkv_weight, out_weight, fc_weight, vectors, qkv_momentum, out_momentum, fc_momentum, vector_first, vector_second):
    zi, xi, yi, ci, ti = (lax.axis_index(a) for a in ALL)
    rows = tokens.shape[0]
    n_att = qkv_weight.shape[3]
    n_fc = fc_weight.shape[3]
    gain, shift = vectors[:D], vectors[D : 2 * D]
    bias_in, bias_out = vectors[2 * D : 2 * D + FF], vectors[2 * D + FF :]

    first = ci == 0
    attn_rows = jnp.concatenate([jnp.transpose(qkv_weight[:, :, 0, :], (0, 2, 1)), jnp.transpose(out_weight[:, 0, :])[None]])
    fc_rows = jnp.transpose(fc_weight[:, :, 0, :], (0, 2, 1))
    own_rows = jnp.concatenate([attn_rows.reshape(1, n_fc, D), fc_rows]).astype(BF)
    held = jnp.stack(gather_ring(own_rows, pull_yh, 2), axis=1)

    inputs = tokens.astype(F32)
    average = jnp.mean(inputs, axis=-1, keepdims=True)
    deviation = inputs - average
    variance = jnp.mean(deviation * deviation, axis=-1, keepdims=True)
    inv_spread = lax.rsqrt(variance + 1e-05)
    centred = deviation * inv_spread
    normed_own = (centred * gain + shift).astype(BF)
    both = jnp.stack([normed_own, cotangent])
    held, both = lax.optimization_barrier((held, both))
    held = jnp.stack(gather_ring(held, pull_inner, 4), axis=1)
    both = jnp.stack([both, pull(both, "t", 1)], axis=1)
    held, both = lax.optimization_barrier((held, both))
    span = 8 * n_fc
    held = held.reshape(3, span, D)
    fc_held = gather_ring(held[1:], pull_outer, 4)
    att_held = gather_ring(held[0], pull_outer, 4)
    both = jnp.stack([both, pull(both, "c", 1)], axis=1)
    n_all = 4 * rows
    normed, cot = both[0].reshape(n_all, D), both[1].reshape(n_all, D)

    half = jnp.arange(LEN) // rows
    position = ((ti + half) % 2) * rows + jnp.arange(LEN) % rows
    frequency = 10000.0 ** (-2.0 * jnp.arange(ROT // 2, dtype=F32) / ROT)
    angles = position.astype(F32)[:, None] * frequency[None, :]
    cos_t, sin_t = jnp.cos(angles), jnp.sin(angles)
    pad = lambda a, b, fill: jnp.concatenate([a, b, jnp.full((LEN, PAD - ROT), fill, F32)], axis=1)
    cos_full, sin_full = pad(cos_t, cos_t, 1.0), pad(-sin_t, sin_t, 0.0)

    bias6 = bias_in.reshape(2, 4, 4, 2, 2, n_fc)
    bias6 = jnp.concatenate([bias6, bias6], axis=1)
    bias6 = jnp.concatenate([bias6, bias6], axis=2)
    bias6 = jnp.concatenate([bias6, bias6], axis=3)
    bias_own = lax.dynamic_slice(bias6, (ti, zi, xi, yi, ci, 0), (1, 4, 4, 2, 1, n_fc))[0, :, :, :, 0]
    by_turn = lambda v: jnp.where(first, jnp.swapaxes(v, 0, 1), v)
    bias_own = by_turn(bias_own).reshape(1, 32 * n_fc)
    at = jnp.stack([zi, xi, yi, ci, ti]).astype(jnp.int32)
    mom_rows = jnp.concatenate(
        [
            jnp.transpose(qkv_momentum[:, :, 0, :], (0, 2, 1)).reshape(3 * n_att, D),
            jnp.transpose(out_momentum[:, 0, :]),
            jnp.transpose(fc_momentum[:, :, 0, :], (0, 2, 1)).reshape(2 * n_fc, D),
        ]
    )
    far, normed, cot, bias_own, at, cos_full, sin_full, mom_rows = lax.optimization_barrier(
        (fc_held[1:], normed, cot, bias_own, at, cos_full, sin_full, mom_rows)
    )
    sums, grad_bias_in, *fc_parts = feed_forward(at, fc_held[:1] + far, normed, cot, bias_own)
    att_held, sums = lax.optimization_barrier((att_held, sums))
    att_got = [pull(v, "c", 1) for v in att_held]
    rows_own, rows_peer, att_keep, att_give = attention(at, att_held, att_got, normed, cot, cos_full, sin_full, sums)

    fc_total = sum_ring(fc_parts, pull_outer)
    att_give, fc_total = lax.optimization_barrier((att_give, fc_total))
    att_grad = (att_keep + pull(att_give, "c", 1)).reshape(4, span, D)
    att_total = sum_ring([att_grad[k] for k in range(4)], pull_outer)
    rows_own = (rows_own + pull(rows_peer, "c", 1)).reshape(2, 2, rows, D)
    rows_own = rows_own[:, 0] + pull(rows_own[:, 1].astype(BF), "t", 1).astype(F32)
    att_total, fc_total, rows_own = lax.optimization_barrier((att_total, fc_total, rows_own))
    total = jnp.concatenate([att_total[None], fc_total]).reshape(3, 4, 2, n_fc, D)
    total = sum_ring([total[:, k] for k in range(4)], pull_inner)
    total = sum_ring([total[:, k] for k in range(2)], pull_yh).reshape(3 * n_fc, D)

    mixed = (inputs + rows_own[0] + bias_out).astype(BF)
    d_rows = rows_own[1]
    d_hat = d_rows * gain
    correction = d_hat - jnp.mean(d_hat, axis=-1, keepdims=True) - centred * jnp.mean(d_hat * centred, axis=-1, keepdims=True)
    own_cot = cotangent.astype(F32)
    input_grad = own_cot + correction * inv_spread

    total_of = lambda v: jnp.sum(v, axis=0, keepdims=True)
    vec_rows = [total_of(d_rows * centred), total_of(d_rows), grad_bias_in[: FF // D], total_of(own_cot), jnp.zeros((VEC_ROWS - VEC // D, D), F32)]

    moment = 0.95 * mom_rows + total
    update = total + 0.95 * moment

    half_fc = n_fc // 2
    att_u = update[: 4 * n_att].reshape(4, n_att, D)
    att_u = jnp.concatenate([att_u, jnp.zeros((4, half_fc - n_att, D), F32)], axis=1)
    fc_u = update[4 * n_att :].reshape(4, half_fc, D)
    vec_rows = jnp.concatenate(vec_rows)
    chunks = jnp.concatenate([att_u, fc_u])
    chunks = jnp.concatenate([chunks, jnp.broadcast_to(vec_rows, (8, VEC_ROWS, D))], axis=1)
    got = lax.all_to_all(chunks, ("z", "t"), split_axis=0, concat_axis=0, tiled=True)
    mine = got[:, :half_fc].reshape(8 * half_fc, D)
    vec_sum = jnp.sum(got[:, half_fc:], axis=0)[:8]
    to_yh_x = lambda k: lambda z, x, y, c, t: (z, x, y + 1, c, t) if c == 0 else (z, x + k, y, c, t)
    to_x_yh = lambda k: lambda z, x, y, c, t: (z, x + k, y, c, t) if c == 0 else (z, x, y + 1, c, t)
    only = lambda core, source: lambda z, x, y, c, t: source(z, x, y, c, t) if c == core else None
    n = mine.shape[0]
    load = jnp.concatenate([mine, vec_sum])
    near = [load, move(load, to_yh_x(1)), move(load, only(1, to_yh_x(2))), move(load, only(1, to_yh_x(3)))]
    vec_sum = sum(v[n:] for v in near)
    load = jnp.concatenate([near[0][:n], near[1][:n], vec_sum])
    load_2 = jnp.where(first, load, jnp.concatenate([near[2][:n], near[3][:n], jnp.zeros_like(vec_sum)]))
    far = [move(load, to_x_yh(1)), move(load_2, to_x_yh(2)), move(load, only(0, to_x_yh(3)))]
    vec_sum = vec_sum + sum(v[2 * n :] for v in far)
    core = ci.astype(jnp.int32)[None]
    keep, give = gram_parts(core, near + far)
    from_core = pull(jnp.concatenate([give, vec_sum]), "c", 1)
    part = keep + from_core[:BLK]
    vec_sum = vec_sum + from_core[BLK:]
    other = pull(part, "t", 1)
    part = jnp.where(zi >= 2, part + other, part)
    rest = pull(part, "c", 1)
    x_rows = sweeps(core, part, rest, mine)
    vector_grad = vec_sum[: VEC // D].reshape(VEC)
    first_new = 0.9 * vector_first + 0.1 * vector_grad
    second_new = 0.95 * vector_second + 0.05 * vector_grad * vector_grad
    step_size = first_new / (1.0 - 0.9**STEP) / (jnp.sqrt(second_new / (1.0 - 0.95**STEP)) + 1e-08)
    vector_new = vectors - 0.2 * step_size

    back = lax.all_to_all(x_rows, ("z", "t"), split_axis=0, concat_axis=0, tiled=True).reshape(8, half_fc, D)
    att_x = back[:4, :n_att]
    fc_x = back[4:].reshape(2, n_fc, D)

    def cols(v):
        return jnp.transpose(v, (0, 2, 1))[:, :, None, :]

    fc_factor = math.sqrt(FF / D)
    qkv_new = qkv_weight * 0.99 - cols(att_x[:3])
    out_new = out_weight * 0.99 - cols(att_x[3:])[0]
    fc_new = fc_weight * 0.99 - fc_factor * cols(fc_x)
    att_m = moment[: 4 * n_att].reshape(4, n_att, D)
    fc_m = moment[4 * n_att :].reshape(2, n_fc, D)
    return (mixed, input_grad, qkv_new, out_new, fc_new, cols(att_m[:3]), cols(att_m[3:])[0], cols(fc_m), first_new, second_new, vector_new)


def solution(mesh):
    mesh = Mesh(mesh.devices.reshape(4, 4, 2, 2, 2), ALL)
    rows = P(ALL, None)
    w3 = P(None, None, "t", DP)
    w2 = P(None, "t", DP)
    vec = P()
    in_specs = (rows, rows, w3, w2, w3, vec, w3, w2, w3, vec, vec)
    out_specs = (rows, rows, w3, w2, w3, w3, w2, w3, vec, vec, vec)
    return jax.shard_map(body, mesh=mesh, in_specs=in_specs, out_specs=out_specs, check_vma=False)
```

```python
import functools
import itertools
import math

import jax
import jax.numpy as jnp
from jax import lax
from jax.experimental import pallas as pl
from jax.experimental.pallas import tpu as pltpu
from jax.sharding import Mesh, PartitionSpec as P

D = 768
H = 12
HD = 64
ROT = 16
FF = 3072
SWEEPS = 5
STEP = 10
LEN = 256
VEC = 2 * D + FF + D
VEC_ROWS = 12

NS = (3.4445, -4.775, 2.0315)
BF = jnp.bfloat16
F32 = jnp.float32
BLK = 256
BLK_ROWS = 96
NB = D // BLK

DP = ("z", "x", "yh", "c")
ALL = ("z", "x", "yh", "c", "t")


def pull(value, axis, k):
    n = lax.axis_size(axis)
    return lax.ppermute(value, axis, [((i + k) % n, i) for i in range(n)])


def move(value, source):
    sizes = [lax.axis_size(a) for a in ALL]
    index = lambda at: functools.reduce(lambda total, one: total * one[0] + one[1] % one[0], zip(sizes, at), 0)
    pairs = []
    for here in itertools.product(*map(range, sizes)):
        there = source(*here)
        if there is not None:
            pairs.append((index(there), index(here)))
    return lax.ppermute(value, ALL, pairs)


def pull_outer(value, k):
    return move(value, lambda z, x, y, c, t: (z, x + k, y, c, t) if c == 0 else (z + k, x, y, c, t))


def pull_inner(value, k):
    return move(value, lambda z, x, y, c, t: (z + k, x, y, c, t) if c == 0 else (z, x + k, y, c, t))


def pull_yh(value, k):
    return pull(value, "yh", k)


def gather_ring(value, pulls, n):
    return [value] + [pulls(value, k) for k in range(1, n)]


def sum_ring(parts, pulls):
    n = len(parts)
    total = parts[0].astype(F32)
    for k in range(1, n):
        total = total + pulls(parts[k].astype(BF), n - k).astype(F32)
    return total


def dot(a, b, dims):
    return lax.dot_general(a, b, (dims, ((), ())), preferred_element_type=F32)


def pieces(value, n):
    out = []
    for _ in range(n):
        low = value.astype(BF)
        out.append(low)
        value = value - low.astype(F32)
    return out


def mul(xs, ys, dims=((1,), (0,))):
    n = len(xs)
    total = None
    for order in reversed(range(n)):
        for i in range(order + 1):
            term = lax.dot_general(xs[i], ys[order - i], (dims, ((), ())), preferred_element_type=F32)
            total = term if total is None else total + term
    return total


def gram_kernel(core_ref, *refs):
    *in_refs, keep_ref, give_ref, wide_ref = refs
    at = 0
    for ref in in_refs:
        n = ref.shape[0] // BLK_ROWS * BLK_ROWS
        for k, piece in enumerate(pieces(ref[:n], 3)):
            wide_ref[k, at : at + n] = piece
        at += n
    xs = [wide_ref[k] for k in range(3)]
    dims = ((0,), (0,))
    cut = lambda i: slice(i * BLK, (i + 1) * BLK)
    top = mul([x[:, cut(0)] for x in xs], xs, dims)
    mid = mul([x[:, cut(1)] for x in xs], [x[:, BLK:] for x in xs], dims)
    low = mul([x[:, cut(2)] for x in xs], [x[:, 2 * BLK :] for x in xs], dims)
    first = core_ref[0] == 0

    @pl.when(first)
    def _():
        keep_ref[...] = top
        give_ref[:, : 2 * BLK] = mid
        give_ref[:, 2 * BLK :] = low

    @pl.when(jnp.logical_not(first))
    def _():
        give_ref[...] = top
        keep_ref[:, : 2 * BLK] = mid
        keep_ref[:, 2 * BLK :] = low


def blocks(i, j):
    return (slice(i * BLK, (i + 1) * BLK), slice(j * BLK, (j + 1) * BLK))


def put(refs, i, j, value):
    for ref, piece in zip(refs, pieces(value, len(refs))):
        ref[blocks(i, j)] = piece


def put_both(refs, i, j, value):
    put(refs, i, j, value)
    if i != j:
        put(refs, j, i, value.T)


def symmetric_product(xs, ys, emit, start=0):
    for i in range(start, NB):
        rows = slice(i * BLK, (i + 1) * BLK)
        wide = mul([x[rows, :] for x in xs], [y[:, i * BLK :] for y in ys])
        for j in range(i, NB):
            emit(i, j, wide[:, (j - i) * BLK : (j - i + 1) * BLK])


def sweeps_kernel(core_ref, mine_ref, rest_ref, x_ref, out_ref, top_ref, bottom_ref, gram_ref, a_ref, p_ref, b_ref):
    first = core_ref[0] == 0
    n_x = x_ref.shape[0]

    @pl.when(first)
    def _():
        top_ref[...] = mine_ref[...]
        bottom_ref[...] = rest_ref[...]

    @pl.when(jnp.logical_not(first))
    def _():
        top_ref[...] = rest_ref[...]
        bottom_ref[...] = mine_ref[...]

    def packed(i, j):
        if i == 0:
            return top_ref[:, j * BLK : (j + 1) * BLK]
        at = (j - 1) if i == 1 else 2
        return bottom_ref[:, at * BLK : (at + 1) * BLK]

    eye = (lax.broadcasted_iota(jnp.int32, (BLK, BLK), 0) == lax.broadcasted_iota(jnp.int32, (BLK, BLK), 1)).astype(F32)
    trace = sum(jnp.sum(packed(i, i) * eye) for i in range(NB))
    norm = jnp.sqrt(jnp.full((8, 128), trace, F32)) + 1e-07
    factor = (1.0 / norm)[0:1, 0:1]
    square = factor * factor

    a_rows = lambda n: [a_ref.at[k, n_x : n_x + D] for k in range(n)]
    p_rows = lambda n: [p_ref.at[k] for k in range(n)]
    b_rows = lambda n: [b_ref.at[k] for k in range(n)]

    def put_x(n, value):
        for k, piece in enumerate(pieces(value, n)):
            a_ref[k, :n_x] = piece

    for i in range(NB):
        for j in range(i, NB):
            value = packed(i, j) * square
            gram_ref[blocks(i, j)] = value
            put_both(a_rows(3), i, j, value)
    put_x(3, x_ref[...] * factor)

    def poly(n_p):
        def emit(i, j, block):
            value = NS[1] * gram_ref[blocks(i, j)] + NS[2] * block
            if i == j:
                value = value + NS[0] * eye
            put_both(p_rows(n_p), i, j, value)

        a = a_rows(2)
        symmetric_product(a, a, emit)

    def next_gram(n, keep):
        p = p_rows(n)
        rows = slice(0, n_x + BLK)
        wide = mul([a_ref[k, rows] for k in range(n)], [y[...] for y in p])
        for j in range(NB):
            put_both(b_rows(n), 0, j, wide[n_x:, j * BLK : (j + 1) * BLK])
        symmetric_product(a_rows(n), p, lambda i, j, block: put_both(b_rows(n), i, j, block), 1)
        put_x(keep, wide[:n_x])

        def emit(i, j, block):
            gram_ref[blocks(i, j)] = block
            put_both(a_rows(keep), i, j, block)

        symmetric_product(b_rows(n), p, emit)

    poly(3)
    next_gram(3, 2)

    @pl.loop(1, SWEEPS - 1)
    def _(_):
        poly(2)
        next_gram(2, 2)

    poly(2)
    out_ref[...] = mul([a_ref[k, :n_x] for k in range(2)], [y[...] for y in p_rows(2)])


SMEM = pl.BlockSpec(memory_space=pltpu.SMEM)
VM = pl.BlockSpec(memory_space=pltpu.VMEM)


def gram_parts(core, held):
    rows = sum(v.shape[0] // BLK_ROWS * BLK_ROWS for v in held)
    return pl.pallas_call(
        gram_kernel,
        out_shape=[jax.ShapeDtypeStruct((BLK, D), F32)] * 2,
        in_specs=[SMEM] + [VM] * len(held),
        out_specs=[VM, VM],
        scratch_shapes=[pltpu.VMEM((3, rows, D), BF)],
        compiler_params=pltpu.CompilerParams(vmem_limit_bytes=14 << 20),
        cost_estimate=pl.CostEstimate(flops=2 * D * D * D * 4, bytes_accessed=4 * D * D * 2, transcendentals=0),
    )(core, *held)


def sweeps(core, mine, rest, x_rows):
    return pl.pallas_call(
        sweeps_kernel,
        out_shape=jax.ShapeDtypeStruct(x_rows.shape, F32),
        in_specs=[SMEM, VM, VM, VM],
        out_specs=VM,
        scratch_shapes=[
            pltpu.VMEM((BLK, D), F32),
            pltpu.VMEM((BLK, D), F32),
            pltpu.VMEM((D, D), F32),
            pltpu.VMEM((3, x_rows.shape[0] + D, D), BF),
            pltpu.VMEM((3, D, D), BF),
            pltpu.VMEM((3, D, D), BF),
        ],
        compiler_params=pltpu.CompilerParams(vmem_limit_bytes=24 << 20),
        cost_estimate=pl.CostEstimate(flops=2 * D * D * D * 32, bytes_accessed=4 * D * D, transcendentals=0),
    )(core, mine, rest, x_rows)


def gelu_parts(u):
    k0 = math.sqrt(2.0 / math.pi)
    th = jnp.tanh(k0 * (u + 0.044715 * (u * u * u)))
    value = 0.5 * u * (1.0 + th)
    slope = 0.5 * (1.0 + th) + 0.5 * u * (1.0 - th * th) * (k0 * (1.0 + 3.0 * 0.044715 * u * u))
    return value, slope


HEADS = 3
PAD = 128
HC = HEADS * HD
HP = HEADS * PAD
NN = ((1,), (0,))
NT = ((1,), (1,))
TN = ((0,), (0,))


def iota(shape, dim):
    return lax.broadcasted_iota(jnp.int32, shape, dim)


def one_hot(cond):
    return jnp.where(cond, 1.0, 0.0).astype(BF)


def unit_place(at_ref, n):
    zi, xi, yi, ci, ti = (at_ref[k] for k in range(5))
    width = 24
    group = jnp.right_shift(n * 2731, 16)
    lane = n - width * group
    y = jnp.bitwise_and(group + yi, 1)
    inner = jnp.bitwise_and(jnp.right_shift(group, 1), 3)
    outer = jnp.bitwise_and(jnp.right_shift(group, 3), 3)
    z = jnp.bitwise_and(jnp.where(ci == 0, inner, outer) + zi, 3)
    x = jnp.bitwise_and(jnp.where(ci == 0, outer, inner) + xi, 3)
    row = 2 * ti + jnp.right_shift(z, 1)
    return row, (((jnp.bitwise_and(z, 1) * 4 + x) * 2 + y) * 2 + ci) * width + lane


def needed_blocks(at_ref):
    zi, ci = at_ref[0], at_ref[3]
    for rc in range(2):
        core_0 = jnp.bitwise_xor(ci, rc) == 0
        for x in range(4):
            for j in range(2):
                z = jnp.bitwise_and(2 * ci + j - zi, 3)
                outer, inner = jnp.where(core_0, x, z), jnp.where(core_0, z, x)
                yield rc, pl.multiple_of((outer * 4 + inner) * 48, 48)


def home_place(at_ref, r):
    xi, yi, ci = (at_ref[k] for k in range(1, 4))
    n = 6
    group = jnp.right_shift(r * 10923, 16)
    lane = r - n * group
    mat = jnp.bitwise_and(group, 3)
    y = jnp.bitwise_and(jnp.right_shift(group, 2) + yi, 1)
    j = jnp.bitwise_and(jnp.right_shift(group, 3), 1)
    x = jnp.bitwise_and(jnp.right_shift(group, 4) + xi, 3)
    core = jnp.bitwise_and(jnp.right_shift(group, 6) + ci, 1)
    return mat * HC + (((j * 4 + x) * 2 + y) * 2 + core) * n + lane


def attention_kernel(
    at_ref, own0_ref, own1_ref, own2_ref, own3_ref, got0_ref, got1_ref, got2_ref, got3_ref, normed_ref, cot_ref, cos_ref, sin_ref,
    sums_ref, keep_ref, give_ref,
    att_ref, near_ref, w_ref, wo_ref, q_ref, k_ref, v_ref, da_ref, heads_ref, d_ref, nat_ref,
):
    span = own0_ref.shape[0]
    for k, ref in enumerate((own0_ref, own1_ref, own2_ref, own3_ref, got0_ref, got1_ref, got2_ref, got3_ref)):
        att_ref[k // 4, k % 4 * span : (k % 4 + 1) * span] = ref[...]
    block = span // 4
    for k, (rc, at) in enumerate(needed_blocks(at_ref)):
        near_ref[k * block : (k + 1) * block] = att_ref[rc, pl.ds(at, block)]

    n_rows = 4 * HC
    pick = one_hot(iota((n_rows, n_rows), 0) == home_place(at_ref, iota((8, n_rows), 1))[:1])
    w_att = dot(pick, near_ref[...], NN).astype(BF)
    r = iota((HC, HC), 0)
    e = jnp.bitwise_and(r, HD - 1)
    half = ROT // 2
    source = jnp.where(e < half, r + half, jnp.where(e < ROT, r - half, -1))
    exchange = one_hot(iota((HC, HC), 1) == source)
    blank = jnp.zeros((HD, D), BF)

    def padded(ref, base, rows):
        for h in range(HEADS):
            at = base + h * PAD
            ref[at : at + HD] = rows[h * HD : (h + 1) * HD]
            ref[at + HD : at + PAD] = blank

    for m in range(3):
        padded(w_ref, m * HP, w_att[m * HC : (m + 1) * HC])
    for m in range(2):
        padded(w_ref, (3 + m) * HP, dot(exchange, w_att[m * HC : (m + 1) * HC], NN).astype(BF))
    padded(wo_ref, 0, w_att[3 * HC :])

    cos, sin = cos_ref[...], sin_ref[...]
    for m, ref in ((0, q_ref), (1, k_ref)):
        lin = dot(normed_ref[...], w_ref[m * HP : (m + 1) * HP], NT)
        lin_2 = dot(normed_ref[...], w_ref[(3 + m) * HP : (4 + m) * HP], NT)
        for s in range(2):
            rows = slice(s * LEN, (s + 1) * LEN)
            for h in range(HEADS):
                lanes = slice(h * PAD, (h + 1) * PAD)
                base = h * 2 * PAD
                own, other = lin[rows, lanes], lin_2[rows, lanes]
                ref[rows, base : base + PAD] = (own * cos + other * sin).astype(BF)
                ref[rows, base + PAD : base + 2 * PAD] = (other * cos - own * sin).astype(BF)
    v_ref[...] = dot(normed_ref[...], w_ref[2 * HP : 3 * HP], NT).astype(BF)
    da_ref[...] = dot(cot_ref[...], wo_ref[...], NT).astype(BF)

    turn = at_ref[4] * (LEN // 2)
    at_q = jnp.bitwise_xor(iota((LEN, LEN), 0), turn)
    at_k = jnp.bitwise_xor(iota((LEN, LEN), 1), turn)
    causal = at_q >= at_k
    scale = HD ** (-0.5)
    for s in range(2):
        rows = slice(s * LEN, (s + 1) * LEN)
        for h in range(HEADS):
            two = slice(h * 2 * PAD, (h + 1) * 2 * PAD)
            one = slice(h * 2 * PAD, h * 2 * PAD + PAD)
            lanes = slice(h * PAD, (h + 1) * PAD)
            value, d_att = v_ref[rows, lanes], da_ref[rows, lanes]
            scores = jnp.where(causal, dot(q_ref[rows, one], k_ref[rows, one], NT) * scale, -1e30)
            raised = jnp.exp(scores - jnp.max(scores, axis=1, keepdims=True))
            probs = raised / jnp.sum(raised, axis=1, keepdims=True)
            low = probs.astype(BF)
            heads_ref[rows, lanes] = dot(low, value, NN).astype(BF)
            d_ref[rows, 2 * HP + h * PAD : 2 * HP + (h + 1) * PAD] = dot(low, d_att, TN).astype(BF)
            d_probs = dot(d_att, value, NT)
            d_scores = (probs * (d_probs - jnp.sum(probs * d_probs, axis=1, keepdims=True))).astype(BF)
            d_q = dot(d_scores, k_ref[rows, two], NN) * scale
            d_k = dot(d_scores, q_ref[rows, two], TN) * scale
            for m, pair in ((0, d_q), (1, d_k)):
                at = m * HP + h * PAD
                d_ref[rows, at : at + PAD] = (pair[:, :PAD] * cos - pair[:, PAD:] * sin).astype(BF)

    sums_ref[0] = dot(heads_ref[...], wo_ref[...], NN)
    sums_ref[1] = dot(d_ref[...], w_ref[: 3 * HP], NN)

    for m in range(4):
        if m < 3:
            grad = dot(d_ref[:, m * HP : (m + 1) * HP], normed_ref[...], TN).astype(BF)
        else:
            grad = dot(heads_ref[...], cot_ref[...], TN).astype(BF)
        for h in range(HEADS):
            nat_ref[m * HC + h * HD : m * HC + (h + 1) * HD] = grad[h * PAD : h * PAD + HD]
    place = home_place(at_ref, iota((n_rows, 128), 0))
    pick = jnp.concatenate([one_hot(iota((n_rows, 128), 1) + b == place) for b in range(0, n_rows, 128)], axis=1)
    near_ref[...] = dot(pick, nat_ref[...], NN).astype(BF)
    keep_ref[...] = jnp.zeros_like(keep_ref)
    give_ref[...] = jnp.zeros_like(give_ref)
    for k, (rc, at) in enumerate(needed_blocks(at_ref)):
        (keep_ref, give_ref)[rc][pl.ds(at, block)] = near_ref[k * block : (k + 1) * block]


def forward_kernel(
    at_ref, held0_ref, held1_ref, held2_ref, held3_ref, normed_ref, cot_ref, bias_ref, sums_ref,
    own_ref, peer_ref, gbias_ref, out0_ref, out1_ref, out2_ref, out3_ref,
    win_ref, wback_ref,
):
    span = held0_ref.shape[1]
    for s, ref in enumerate((held0_ref, held1_ref, held2_ref, held3_ref)):
        win_ref[s * span : (s + 1) * span] = ref[0]
        wback_ref[s * span : (s + 1) * span] = ref[1]

    def send(group, grad):
        for s, ref in enumerate((out0_ref, out1_ref, out2_ref, out3_ref)):
            ref[group] = grad[s * span : (s + 1) * span]

    hidden, slope = gelu_parts(dot(normed_ref[...], win_ref[...], NT) + bias_ref[...])
    hidden = hidden.astype(BF)


    def give_rows(k, value):
        own_ref[k] = value[:LEN]
        peer_ref[k] = value[LEN:]

    give_rows(0, sums_ref[0] + dot(hidden, wback_ref[...], NN))
    send(1, dot(hidden, cot_ref[...], TN).astype(BF))
    d_pre = (dot(cot_ref[...], wback_ref[...], NT) * slope).astype(BF)
    grad_bias = jnp.sum(d_pre.astype(F32), axis=0, keepdims=True)
    n_units = win_ref.shape[0]
    bias_row, _ = unit_place(at_ref, iota((8, n_units), 1))
    spread = pieces(jnp.where(bias_row == iota((8, n_units), 0), grad_bias, 0.0), 3)
    _, bias_lane = unit_place(at_ref, iota((n_units, 128), 0))
    to_lane = jnp.concatenate([one_hot(iota((n_units, 128), 1) + b == bias_lane) for b in range(0, D, 128)], axis=1)
    gbias_ref[...] = sum(dot(piece, to_lane, NN) for piece in reversed(spread))
    send(0, dot(d_pre, normed_ref[...], TN).astype(BF))
    give_rows(1, sums_ref[1] + dot(d_pre, win_ref[...], NN))


def out(shape, dtype):
    return jax.ShapeDtypeStruct(shape, dtype)


def low(*shape):
    return pltpu.VMEM(shape, BF)


def attention(at, own, got, normed, cot, cos, sin):
    n = normed.shape[0]
    rows = 4 * own[0].shape[0]
    return pl.pallas_call(
        attention_kernel,
        out_shape=[out((2, n, D), F32), out((rows, D), BF), out((rows, D), BF)],
        in_specs=[SMEM] + [VM] * 12,
        out_specs=[VM] * 3,
        scratch_shapes=[low(2, rows, D), low(4 * HC, D), low(5 * HP, D), low(HP, D)]
        + [low(n, 2 * HP), low(n, 2 * HP)]
        + [low(n, HP)] * 3
        + [low(n, 3 * HP), low(4 * HC, D)],
        compiler_params=pltpu.CompilerParams(vmem_limit_bytes=32 << 20),
        cost_estimate=pl.CostEstimate(flops=12 * 10**9, bytes_accessed=16 << 20, transcendentals=10**6),
    )(at, *own, *got, normed, cot, cos, sin)


def feed_forward(at, held, normed, cot, bias, sums):
    n = normed.shape[0]
    span = held[0].shape[1]
    units = 4 * span
    return pl.pallas_call(
        forward_kernel,
        out_shape=[out((2, n // 2, D), F32), out((2, n // 2, D), F32), out((8, D), F32)] + [out((2, span, D), BF)] * 4,
        in_specs=[SMEM] + [VM] * 8,
        out_specs=[VM] * 7,
        scratch_shapes=[low(units, D), low(units, D)],
        compiler_params=pltpu.CompilerParams(vmem_limit_bytes=22 << 20),
        cost_estimate=pl.CostEstimate(flops=10 * 10**9, bytes_accessed=16 << 20, transcendentals=10**6),
    )(at, *held, normed, cot, bias, sums)


def body(tokens, cotangent, qkv_weight, out_weight, fc_weight, vectors, qkv_momentum, out_momentum, fc_momentum, vector_first, vector_second):
    zi, xi, yi, ci, ti = (lax.axis_index(a) for a in ALL)
    rows = tokens.shape[0]
    n_att = qkv_weight.shape[3]
    n_fc = fc_weight.shape[3]
    gain, shift = vectors[:D], vectors[D : 2 * D]
    bias_in, bias_out = vectors[2 * D : 2 * D + FF], vectors[2 * D + FF :]

    first = ci == 0
    attn_rows = jnp.concatenate([jnp.transpose(qkv_weight[:, :, 0, :], (0, 2, 1)), jnp.transpose(out_weight[:, 0, :])[None]])
    fc_rows = jnp.transpose(fc_weight[:, :, 0, :], (0, 2, 1))
    own_rows = jnp.concatenate([attn_rows.reshape(1, n_fc, D), fc_rows]).astype(BF)
    held = jnp.stack(gather_ring(own_rows, pull_yh, 2), axis=1)

    inputs = tokens.astype(F32)
    average = jnp.mean(inputs, axis=-1, keepdims=True)
    deviation = inputs - average
    variance = jnp.mean(deviation * deviation, axis=-1, keepdims=True)
    inv_spread = lax.rsqrt(variance + 1e-05)
    centred = deviation * inv_spread
    normed_own = (centred * gain + shift).astype(BF)
    both = jnp.stack([normed_own, cotangent])
    held, both = lax.optimization_barrier((held, both))
    held = jnp.stack(gather_ring(held, pull_inner, 4), axis=1)
    both = jnp.stack([both, pull(both, "t", 1)], axis=1)
    held, both = lax.optimization_barrier((held, both))
    span = 8 * n_fc
    held = held.reshape(3, span, D)
    att_held = gather_ring(held[0], pull_outer, 4)
    fc_held = gather_ring(held[1:], pull_outer, 4)
    both = jnp.stack([both, pull(both, "c", 1)], axis=1)
    n_all = 4 * rows
    normed, cot = both[0].reshape(n_all, D), both[1].reshape(n_all, D)

    half = jnp.arange(LEN) // rows
    position = ((ti + half) % 2) * rows + jnp.arange(LEN) % rows
    frequency = 10000.0 ** (-2.0 * jnp.arange(ROT // 2, dtype=F32) / ROT)
    angles = position.astype(F32)[:, None] * frequency[None, :]
    cos_t, sin_t = jnp.cos(angles), jnp.sin(angles)
    pad = lambda a, b, fill: jnp.concatenate([a, b, jnp.full((LEN, PAD - ROT), fill, F32)], axis=1)
    cos_full, sin_full = pad(cos_t, cos_t, 1.0), pad(-sin_t, sin_t, 0.0)

    bias6 = bias_in.reshape(2, 4, 4, 2, 2, n_fc)
    bias6 = jnp.concatenate([bias6, bias6], axis=1)
    bias6 = jnp.concatenate([bias6, bias6], axis=2)
    bias6 = jnp.concatenate([bias6, bias6], axis=3)
    bias_own = lax.dynamic_slice(bias6, (ti, zi, xi, yi, ci, 0), (1, 4, 4, 2, 1, n_fc))[0, :, :, :, 0]
    by_turn = lambda v: jnp.where(first, jnp.swapaxes(v, 0, 1), v)
    bias_own = by_turn(bias_own).reshape(1, 32 * n_fc)
    at = jnp.stack([zi, xi, yi, ci, ti]).astype(jnp.int32)
    mom_rows = jnp.concatenate(
        [
            jnp.transpose(qkv_momentum[:, :, 0, :], (0, 2, 1)).reshape(3 * n_att, D),
            jnp.transpose(out_momentum[:, 0, :]),
            jnp.transpose(fc_momentum[:, :, 0, :], (0, 2, 1)).reshape(2 * n_fc, D),
        ]
    )
    far, normed, cot, bias_own, at, cos_full, sin_full, mom_rows = lax.optimization_barrier(
        (att_held[1:], normed, cot, bias_own, at, cos_full, sin_full, mom_rows)
    )
    att_held = att_held[:1] + far
    att_got = [pull(v, "c", 1) for v in att_held]
    sums, att_keep, att_give = attention(at, att_held, att_got, normed, cot, cos_full, sin_full)

    att_grad = (att_keep + pull(att_give, "c", 1)).reshape(4, span, D)
    att_parts = [att_grad[k] for k in range(4)]

    rows_own, rows_peer, grad_bias_in, *fc_parts = feed_forward(at, fc_held, normed, cot, bias_own, sums)
    att_total = sum_ring(att_parts, pull_outer)
    fc_total = sum_ring(fc_parts, pull_outer)
    rows_own = (rows_own + pull(rows_peer, "c", 1)).reshape(2, 2, rows, D)
    rows_own = rows_own[:, 0] + pull(rows_own[:, 1].astype(BF), "t", 1).astype(F32)
    att_total, fc_total, rows_own = lax.optimization_barrier((att_total, fc_total, rows_own))
    total = jnp.concatenate([att_total[None], fc_total]).reshape(3, 4, 2, n_fc, D)
    total = sum_ring([total[:, k] for k in range(4)], pull_inner)
    total = sum_ring([total[:, k] for k in range(2)], pull_yh).reshape(3 * n_fc, D)

    mixed = (inputs + rows_own[0] + bias_out).astype(BF)
    d_rows = rows_own[1]
    d_hat = d_rows * gain
    correction = d_hat - jnp.mean(d_hat, axis=-1, keepdims=True) - centred * jnp.mean(d_hat * centred, axis=-1, keepdims=True)
    own_cot = cotangent.astype(F32)
    input_grad = own_cot + correction * inv_spread

    total_of = lambda v: jnp.sum(v, axis=0, keepdims=True)
    vec_rows = [total_of(d_rows * centred), total_of(d_rows), grad_bias_in[: FF // D], total_of(own_cot), jnp.zeros((VEC_ROWS - VEC // D, D), F32)]

    moment = 0.95 * mom_rows + total
    update = total + 0.95 * moment

    half_fc = n_fc // 2
    att_u = update[: 4 * n_att].reshape(4, n_att, D)
    att_u = jnp.concatenate([att_u, jnp.zeros((4, half_fc - n_att, D), F32)], axis=1)
    fc_u = update[4 * n_att :].reshape(4, half_fc, D)
    vec_rows = jnp.concatenate(vec_rows)
    chunks = jnp.concatenate([att_u, fc_u])
    chunks = jnp.concatenate([chunks, jnp.broadcast_to(vec_rows, (8, VEC_ROWS, D))], axis=1)
    got = lax.all_to_all(chunks, ("z", "t"), split_axis=0, concat_axis=0, tiled=True)
    mine = got[:, :half_fc].reshape(8 * half_fc, D)
    vec_sum = jnp.sum(got[:, half_fc:], axis=0)[:8]
    to_yh_x = lambda k: lambda z, x, y, c, t: (z, x, y + 1, c, t) if c == 0 else (z, x + k, y, c, t)
    to_x_yh = lambda k: lambda z, x, y, c, t: (z, x + k, y, c, t) if c == 0 else (z, x, y + 1, c, t)
    only = lambda core, source: lambda z, x, y, c, t: source(z, x, y, c, t) if c == core else None
    n = mine.shape[0]
    load = jnp.concatenate([mine, vec_sum])
    near = [load, move(load, to_yh_x(1)), move(load, only(1, to_yh_x(2))), move(load, only(1, to_yh_x(3)))]
    vec_sum = sum(v[n:] for v in near)
    load = jnp.concatenate([near[0][:n], near[1][:n], vec_sum])
    load_2 = jnp.where(first, load, jnp.concatenate([near[2][:n], near[3][:n], jnp.zeros_like(vec_sum)]))
    far = [move(load, to_x_yh(1)), move(load_2, to_x_yh(2)), move(load, only(0, to_x_yh(3)))]
    vec_sum = vec_sum + sum(v[2 * n :] for v in far)
    core = ci.astype(jnp.int32)[None]
    keep, give = gram_parts(core, near + far)
    from_core = pull(jnp.concatenate([give, vec_sum]), "c", 1)
    part = keep + from_core[:BLK]
    vec_sum = vec_sum + from_core[BLK:]
    other = pull(part, "t", 1)
    part = jnp.where(zi >= 2, part + other, part)
    rest = pull(part, "c", 1)
    x_rows = sweeps(core, part, rest, mine)
    vector_grad = vec_sum[: VEC // D].reshape(VEC)
    first_new = 0.9 * vector_first + 0.1 * vector_grad
    second_new = 0.95 * vector_second + 0.05 * vector_grad * vector_grad
    step_size = first_new / (1.0 - 0.9**STEP) / (jnp.sqrt(second_new / (1.0 - 0.95**STEP)) + 1e-08)
    vector_new = vectors - 0.2 * step_size

    back = lax.all_to_all(x_rows, ("z", "t"), split_axis=0, concat_axis=0, tiled=True).reshape(8, half_fc, D)
    att_x = back[:4, :n_att]
    fc_x = back[4:].reshape(2, n_fc, D)

    def cols(v):
        return jnp.transpose(v, (0, 2, 1))[:, :, None, :]

    fc_factor = math.sqrt(FF / D)
    qkv_new = qkv_weight * 0.99 - cols(att_x[:3])
    out_new = out_weight * 0.99 - cols(att_x[3:])[0]
    fc_new = fc_weight * 0.99 - fc_factor * cols(fc_x)
    att_m = moment[: 4 * n_att].reshape(4, n_att, D)
    fc_m = moment[4 * n_att :].reshape(2, n_fc, D)
    return (mixed, input_grad, qkv_new, out_new, fc_new, cols(att_m[:3]), cols(att_m[3:])[0], cols(fc_m), first_new, second_new, vector_new)


def solution(mesh):
    mesh = Mesh(mesh.devices.reshape(4, 4, 2, 2, 2), ALL)
    rows = P(ALL, None)
    w3 = P(None, None, "t", DP)
    w2 = P(None, "t", DP)
    vec = P()
    in_specs = (rows, rows, w3, w2, w3, vec, w3, w2, w3, vec, vec)
    out_specs = (rows, rows, w3, w2, w3, w3, w2, w3, vec, vec, vec)
    return jax.shard_map(body, mesh=mesh, in_specs=in_specs, out_specs=out_specs, check_vma=False)
```

```python
import functools
import itertools
import math

import jax
import jax.numpy as jnp
from jax import lax
from jax.experimental import pallas as pl
from jax.experimental.pallas import tpu as pltpu
from jax.sharding import Mesh, PartitionSpec as P

D = 768
H = 12
HD = 64
ROT = 16
FF = 3072
SWEEPS = 5
STEP = 10
LEN = 256
VEC = 2 * D + FF + D
VEC_ROWS = 12

NS = (3.4445, -4.775, 2.0315)
BF = jnp.bfloat16
F32 = jnp.float32
BLK = 256
QUARTER = 64
NB = D // BLK

DP = ("z", "x", "yh", "c")
ALL = ("z", "x", "yh", "c", "t")


def pull(value, axis, k):
    n = lax.axis_size(axis)
    return lax.ppermute(value, axis, [((i + k) % n, i) for i in range(n)])


def move(value, source):
    sizes = [lax.axis_size(a) for a in ALL]
    index = lambda at: functools.reduce(lambda total, one: total * one[0] + one[1] % one[0], zip(sizes, at), 0)
    pairs = []
    for here in itertools.product(*map(range, sizes)):
        there = source(*here)
        if there is not None:
            pairs.append((index(there), index(here)))
    return lax.ppermute(value, ALL, pairs)


def pull_outer(value, k):
    return move(value, lambda z, x, y, c, t: (z, x + k, y, c, t) if c == 0 else (z + k, x, y, c, t))


def pull_inner(value, k):
    return move(value, lambda z, x, y, c, t: (z + k, x, y, c, t) if c == 0 else (z, x + k, y, c, t))


def pull_yh(value, k):
    return pull(value, "yh", k)


def gather_ring(value, pulls, n):
    return [value] + [pulls(value, k) for k in range(1, n)]


def sum_ring(parts, pulls):
    n = len(parts)
    total = parts[0].astype(F32)
    for k in range(1, n):
        total = total + pulls(parts[k].astype(BF), n - k).astype(F32)
    return total


def dot(a, b, dims):
    return lax.dot_general(a, b, (dims, ((), ())), preferred_element_type=F32)


def pieces(value, n):
    out = []
    for _ in range(n):
        low = value.astype(BF)
        out.append(low)
        value = value - low.astype(F32)
    return out


def mul(xs, ys, dims=((1,), (0,))):
    n = len(xs)
    total = None
    for order in reversed(range(n)):
        for i in range(order + 1):
            term = lax.dot_general(xs[i], ys[order - i], (dims, ((), ())), preferred_element_type=F32)
            total = term if total is None else total + term
    return total


def gram_kernel(at_ref, rows_ref, keep_ref, give_ref, top_ref, bottom_ref):
    xs = pieces(rows_ref[...], 3)
    dims = ((0,), (0,))
    cut = lambda i: slice(i * BLK, (i + 1) * BLK)
    top_ref[...] = mul([x[:, cut(0)] for x in xs], xs, dims)
    bottom_ref[:, : 2 * BLK] = mul([x[:, cut(1)] for x in xs], [x[:, BLK:] for x in xs], dims)
    bottom_ref[:, 2 * BLK :] = mul([x[:, cut(2)] for x in xs], [x[:, 2 * BLK :] for x in xs], dims)

    def by_place(out_ref, in_ref):
        for k in range(4):
            place = pl.multiple_of(jnp.bitwise_and(at_ref[1] + k, 3) * QUARTER, QUARTER)
            out_ref[k * QUARTER : (k + 1) * QUARTER] = in_ref[pl.ds(place, QUARTER)]

    first = at_ref[3] == 0

    @pl.when(first)
    def _():
        by_place(keep_ref, top_ref)
        by_place(give_ref, bottom_ref)

    @pl.when(jnp.logical_not(first))
    def _():
        by_place(keep_ref, bottom_ref)
        by_place(give_ref, top_ref)


def blocks(i, j):
    return (slice(i * BLK, (i + 1) * BLK), slice(j * BLK, (j + 1) * BLK))


def put(refs, i, j, value):
    for ref, piece in zip(refs, pieces(value, len(refs))):
        ref[blocks(i, j)] = piece


def put_both(refs, i, j, value):
    put(refs, i, j, value)
    if i != j:
        put(refs, j, i, value.T)


def symmetric_product(xs, ys, emit, start=0):
    for i in range(start, NB):
        rows = slice(i * BLK, (i + 1) * BLK)
        wide = mul([x[rows, :] for x in xs], [y[:, i * BLK :] for y in ys])
        for j in range(i, NB):
            emit(i, j, wide[:, (j - i) * BLK : (j - i + 1) * BLK])


def sweeps_kernel(at_ref, mine_ref, rest_ref, x_ref, out_ref, top_ref, bottom_ref, gram_ref, a_ref, p_ref, b_ref):
    first = at_ref[3] == 0
    n_x = x_ref.shape[0]

    def by_place(out_ref, in_ref):
        for k in range(4):
            place = pl.multiple_of(jnp.bitwise_and(at_ref[1] + k, 3) * QUARTER, QUARTER)
            out_ref[pl.ds(place, QUARTER)] = in_ref[k * QUARTER : (k + 1) * QUARTER]

    @pl.when(first)
    def _():
        by_place(top_ref, mine_ref)
        by_place(bottom_ref, rest_ref)

    @pl.when(jnp.logical_not(first))
    def _():
        by_place(top_ref, rest_ref)
        by_place(bottom_ref, mine_ref)

    def packed(i, j):
        if i == 0:
            return top_ref[:, j * BLK : (j + 1) * BLK]
        at = (j - 1) if i == 1 else 2
        return bottom_ref[:, at * BLK : (at + 1) * BLK]

    eye = (lax.broadcasted_iota(jnp.int32, (BLK, BLK), 0) == lax.broadcasted_iota(jnp.int32, (BLK, BLK), 1)).astype(F32)
    trace = sum(jnp.sum(packed(i, i) * eye) for i in range(NB))
    norm = jnp.sqrt(jnp.full((8, 128), trace, F32)) + 1e-07
    factor = (1.0 / norm)[0:1, 0:1]
    square = factor * factor

    a_rows = lambda n: [a_ref.at[k, n_x : n_x + D] for k in range(n)]
    p_rows = lambda n: [p_ref.at[k] for k in range(n)]
    b_rows = lambda n: [b_ref.at[k] for k in range(n)]

    def put_x(n, value):
        for k, piece in enumerate(pieces(value, n)):
            a_ref[k, :n_x] = piece

    for i in range(NB):
        for j in range(i, NB):
            value = packed(i, j) * square
            gram_ref[blocks(i, j)] = value
            put_both(a_rows(3), i, j, value)
    put_x(3, x_ref[...] * factor)

    def poly(n_p):
        def emit(i, j, block):
            value = NS[1] * gram_ref[blocks(i, j)] + NS[2] * block
            if i == j:
                value = value + NS[0] * eye
            put_both(p_rows(n_p), i, j, value)

        a = a_rows(2)
        symmetric_product(a, a, emit)

    def next_gram(n, keep):
        p = p_rows(n)
        rows = slice(0, n_x + BLK)
        wide = mul([a_ref[k, rows] for k in range(n)], [y[...] for y in p])
        for j in range(NB):
            put_both(b_rows(n), 0, j, wide[n_x:, j * BLK : (j + 1) * BLK])
        symmetric_product(a_rows(n), p, lambda i, j, block: put_both(b_rows(n), i, j, block), 1)
        put_x(keep, wide[:n_x])

        def emit(i, j, block):
            gram_ref[blocks(i, j)] = block
            put_both(a_rows(keep), i, j, block)

        symmetric_product(b_rows(n), p, emit)

    poly(3)
    next_gram(3, 2)

    @pl.loop(1, SWEEPS - 1)
    def _(_):
        poly(2)
        next_gram(2, 2)

    poly(2)
    out_ref[...] = mul([a_ref[k, :n_x] for k in range(2)], [y[...] for y in p_rows(2)])


SMEM = pl.BlockSpec(memory_space=pltpu.SMEM)
VM = pl.BlockSpec(memory_space=pltpu.VMEM)


def gram_parts(at, rows):
    return pl.pallas_call(
        gram_kernel,
        out_shape=[jax.ShapeDtypeStruct((BLK, D), F32)] * 2,
        in_specs=[SMEM, VM],
        out_specs=[VM, VM],
        scratch_shapes=[pltpu.VMEM((BLK, D), F32)] * 2,
        compiler_params=pltpu.CompilerParams(vmem_limit_bytes=14 << 20),
        cost_estimate=pl.CostEstimate(flops=2 * 96 * D * D * 4, bytes_accessed=4 * D * D * 2, transcendentals=0),
    )(at, rows)


def sweeps(at, mine, rest, x_rows):
    return pl.pallas_call(
        sweeps_kernel,
        out_shape=jax.ShapeDtypeStruct(x_rows.shape, F32),
        in_specs=[SMEM, VM, VM, VM],
        out_specs=VM,
        scratch_shapes=[
            pltpu.VMEM((BLK, D), F32),
            pltpu.VMEM((BLK, D), F32),
            pltpu.VMEM((D, D), F32),
            pltpu.VMEM((3, x_rows.shape[0] + D, D), BF),
            pltpu.VMEM((3, D, D), BF),
            pltpu.VMEM((3, D, D), BF),
        ],
        compiler_params=pltpu.CompilerParams(vmem_limit_bytes=24 << 20),
        cost_estimate=pl.CostEstimate(flops=2 * D * D * D * 32, bytes_accessed=4 * D * D, transcendentals=0),
    )(at, mine, rest, x_rows)


def gelu_parts(u):
    k0 = math.sqrt(2.0 / math.pi)
    th = jnp.tanh(k0 * (u + 0.044715 * (u * u * u)))
    value = 0.5 * u * (1.0 + th)
    slope = 0.5 * (1.0 + th) + 0.5 * u * (1.0 - th * th) * (k0 * (1.0 + 3.0 * 0.044715 * u * u))
    return value, slope


HEADS = 3
PAD = 128
HC = HEADS * HD
HP = HEADS * PAD
NN = ((1,), (0,))
NT = ((1,), (1,))
TN = ((0,), (0,))


def iota(shape, dim):
    return lax.broadcasted_iota(jnp.int32, shape, dim)


def one_hot(cond):
    return jnp.where(cond, 1.0, 0.0).astype(BF)


def unit_place(at_ref, n):
    zi, xi, yi, ci, ti = (at_ref[k] for k in range(5))
    width = 24
    group = jnp.right_shift(n * 2731, 16)
    lane = n - width * group
    y = jnp.bitwise_and(group + yi, 1)
    inner = jnp.bitwise_and(jnp.right_shift(group, 1), 3)
    outer = jnp.bitwise_and(jnp.right_shift(group, 3), 3)
    z = jnp.bitwise_and(jnp.where(ci == 0, inner, outer) + zi, 3)
    x = jnp.bitwise_and(jnp.where(ci == 0, outer, inner) + xi, 3)
    row = 2 * ti + jnp.right_shift(z, 1)
    return row, (((jnp.bitwise_and(z, 1) * 4 + x) * 2 + y) * 2 + ci) * width + lane


def needed_blocks(at_ref):
    zi, ci = at_ref[0], at_ref[3]
    for rc in range(2):
        core_0 = jnp.bitwise_xor(ci, rc) == 0
        for x in range(4):
            for j in range(2):
                z = jnp.bitwise_and(2 * ci + j - zi, 3)
                outer, inner = jnp.where(core_0, x, z), jnp.where(core_0, z, x)
                yield rc, pl.multiple_of((outer * 4 + inner) * 48, 48)


def home_place(at_ref, r):
    xi, yi, ci = (at_ref[k] for k in range(1, 4))
    n = 6
    group = jnp.right_shift(r * 10923, 16)
    lane = r - n * group
    mat = jnp.bitwise_and(group, 3)
    y = jnp.bitwise_and(jnp.right_shift(group, 2) + yi, 1)
    j = jnp.bitwise_and(jnp.right_shift(group, 3), 1)
    x = jnp.bitwise_and(jnp.right_shift(group, 4) + xi, 3)
    core = jnp.bitwise_and(jnp.right_shift(group, 6) + ci, 1)
    return mat * HC + (((j * 4 + x) * 2 + y) * 2 + core) * n + lane


def attention_kernel(
    at_ref, own0_ref, own1_ref, own2_ref, own3_ref, got0_ref, got1_ref, got2_ref, got3_ref, normed_ref, cot_ref, cos_ref, sin_ref,
    sums_ref, keep_ref, give_ref,
    att_ref, near_ref, w_ref, wo_ref, q_ref, k_ref, v_ref, da_ref, heads_ref, d_ref, nat_ref,
):
    span = own0_ref.shape[0]
    for k, ref in enumerate((own0_ref, own1_ref, own2_ref, own3_ref, got0_ref, got1_ref, got2_ref, got3_ref)):
        att_ref[k // 4, k % 4 * span : (k % 4 + 1) * span] = ref[...]
    block = span // 4
    for k, (rc, at) in enumerate(needed_blocks(at_ref)):
        near_ref[k * block : (k + 1) * block] = att_ref[rc, pl.ds(at, block)]

    n_rows = 4 * HC
    pick = one_hot(iota((n_rows, n_rows), 0) == home_place(at_ref, iota((8, n_rows), 1))[:1])
    w_att = dot(pick, near_ref[...], NN).astype(BF)
    r = iota((HC, HC), 0)
    e = jnp.bitwise_and(r, HD - 1)
    half = ROT // 2
    source = jnp.where(e < half, r + half, jnp.where(e < ROT, r - half, -1))
    exchange = one_hot(iota((HC, HC), 1) == source)
    blank = jnp.zeros((HD, D), BF)

    def padded(ref, base, rows):
        for h in range(HEADS):
            at = base + h * PAD
            ref[at : at + HD] = rows[h * HD : (h + 1) * HD]
            ref[at + HD : at + PAD] = blank

    for m in range(3):
        padded(w_ref, m * HP, w_att[m * HC : (m + 1) * HC])
    for m in range(2):
        padded(w_ref, (3 + m) * HP, dot(exchange, w_att[m * HC : (m + 1) * HC], NN).astype(BF))
    padded(wo_ref, 0, w_att[3 * HC :])

    cos, sin = cos_ref[...], sin_ref[...]
    for m, ref in ((0, q_ref), (1, k_ref)):
        lin = dot(normed_ref[...], w_ref[m * HP : (m + 1) * HP], NT)
        lin_2 = dot(normed_ref[...], w_ref[(3 + m) * HP : (4 + m) * HP], NT)
        for s in range(2):
            rows = slice(s * LEN, (s + 1) * LEN)
            for h in range(HEADS):
                lanes = slice(h * PAD, (h + 1) * PAD)
                base = h * 2 * PAD
                own, other = lin[rows, lanes], lin_2[rows, lanes]
                ref[rows, base : base + PAD] = (own * cos + other * sin).astype(BF)
                ref[rows, base + PAD : base + 2 * PAD] = (other * cos - own * sin).astype(BF)
    v_ref[...] = dot(normed_ref[...], w_ref[2 * HP : 3 * HP], NT).astype(BF)
    da_ref[...] = dot(cot_ref[...], wo_ref[...], NT).astype(BF)

    turn = at_ref[4] * (LEN // 2)
    at_q = jnp.bitwise_xor(iota((LEN, LEN), 0), turn)
    at_k = jnp.bitwise_xor(iota((LEN, LEN), 1), turn)
    causal = at_q >= at_k
    scale = HD ** (-0.5)
    for s in range(2):
        rows = slice(s * LEN, (s + 1) * LEN)
        for h in range(HEADS):
            two = slice(h * 2 * PAD, (h + 1) * 2 * PAD)
            one = slice(h * 2 * PAD, h * 2 * PAD + PAD)
            lanes = slice(h * PAD, (h + 1) * PAD)
            value, d_att = v_ref[rows, lanes], da_ref[rows, lanes]
            scores = jnp.where(causal, dot(q_ref[rows, one], k_ref[rows, one], NT) * scale, -1e30)
            raised = jnp.exp(scores - jnp.max(scores, axis=1, keepdims=True))
            probs = raised / jnp.sum(raised, axis=1, keepdims=True)
            low = probs.astype(BF)
            heads_ref[rows, lanes] = dot(low, value, NN).astype(BF)
            d_ref[rows, 2 * HP + h * PAD : 2 * HP + (h + 1) * PAD] = dot(low, d_att, TN).astype(BF)
            d_probs = dot(d_att, value, NT)
            d_scores = (probs * (d_probs - jnp.sum(probs * d_probs, axis=1, keepdims=True))).astype(BF)
            d_q = dot(d_scores, k_ref[rows, two], NN) * scale
            d_k = dot(d_scores, q_ref[rows, two], TN) * scale
            for m, pair in ((0, d_q), (1, d_k)):
                at = m * HP + h * PAD
                d_ref[rows, at : at + PAD] = (pair[:, :PAD] * cos - pair[:, PAD:] * sin).astype(BF)

    sums_ref[0] = dot(heads_ref[...], wo_ref[...], NN)
    sums_ref[1] = dot(d_ref[...], w_ref[: 3 * HP], NN)

    for m in range(4):
        if m < 3:
            grad = dot(d_ref[:, m * HP : (m + 1) * HP], normed_ref[...], TN).astype(BF)
        else:
            grad = dot(heads_ref[...], cot_ref[...], TN).astype(BF)
        for h in range(HEADS):
            nat_ref[m * HC + h * HD : m * HC + (h + 1) * HD] = grad[h * PAD : h * PAD + HD]
    place = home_place(at_ref, iota((n_rows, 128), 0))
    pick = jnp.concatenate([one_hot(iota((n_rows, 128), 1) + b == place) for b in range(0, n_rows, 128)], axis=1)
    near_ref[...] = dot(pick, nat_ref[...], NN).astype(BF)
    keep_ref[...] = jnp.zeros_like(keep_ref)
    give_ref[...] = jnp.zeros_like(give_ref)
    for k, (rc, at) in enumerate(needed_blocks(at_ref)):
        (keep_ref, give_ref)[rc][pl.ds(at, block)] = near_ref[k * block : (k + 1) * block]


def forward_kernel(
    at_ref, held0_ref, held1_ref, held2_ref, held3_ref, normed_ref, cot_ref, bias_ref, sums_ref,
    own_ref, peer_ref, gbias_ref, out0_ref, out1_ref, out2_ref, out3_ref,
    win_ref, wback_ref,
):
    span = held0_ref.shape[1]
    for s, ref in enumerate((held0_ref, held1_ref, held2_ref, held3_ref)):
        win_ref[s * span : (s + 1) * span] = ref[0]
        wback_ref[s * span : (s + 1) * span] = ref[1]

    def send(group, grad):
        for s, ref in enumerate((out0_ref, out1_ref, out2_ref, out3_ref)):
            ref[group] = grad[s * span : (s + 1) * span]

    hidden, slope = gelu_parts(dot(normed_ref[...], win_ref[...], NT) + bias_ref[...])
    hidden = hidden.astype(BF)


    def give_rows(k, value):
        own_ref[k] = value[:LEN]
        peer_ref[k] = value[LEN:]

    give_rows(0, sums_ref[0] + dot(hidden, wback_ref[...], NN))
    send(1, dot(hidden, cot_ref[...], TN).astype(BF))
    d_pre = (dot(cot_ref[...], wback_ref[...], NT) * slope).astype(BF)
    grad_bias = jnp.sum(d_pre.astype(F32), axis=0, keepdims=True)
    n_units = win_ref.shape[0]
    bias_row, _ = unit_place(at_ref, iota((8, n_units), 1))
    spread = pieces(jnp.where(bias_row == iota((8, n_units), 0), grad_bias, 0.0), 3)
    _, bias_lane = unit_place(at_ref, iota((n_units, 128), 0))
    to_lane = jnp.concatenate([one_hot(iota((n_units, 128), 1) + b == bias_lane) for b in range(0, D, 128)], axis=1)
    gbias_ref[...] = sum(dot(piece, to_lane, NN) for piece in reversed(spread))
    send(0, dot(d_pre, normed_ref[...], TN).astype(BF))
    give_rows(1, sums_ref[1] + dot(d_pre, win_ref[...], NN))


def out(shape, dtype):
    return jax.ShapeDtypeStruct(shape, dtype)


def low(*shape):
    return pltpu.VMEM(shape, BF)


def attention(at, own, got, normed, cot, cos, sin):
    n = normed.shape[0]
    rows = 4 * own[0].shape[0]
    return pl.pallas_call(
        attention_kernel,
        out_shape=[out((2, n, D), F32), out((rows, D), BF), out((rows, D), BF)],
        in_specs=[SMEM] + [VM] * 12,
        out_specs=[VM] * 3,
        scratch_shapes=[low(2, rows, D), low(4 * HC, D), low(5 * HP, D), low(HP, D)]
        + [low(n, 2 * HP), low(n, 2 * HP)]
        + [low(n, HP)] * 3
        + [low(n, 3 * HP), low(4 * HC, D)],
        compiler_params=pltpu.CompilerParams(vmem_limit_bytes=32 << 20),
        cost_estimate=pl.CostEstimate(flops=12 * 10**9, bytes_accessed=16 << 20, transcendentals=10**6),
    )(at, *own, *got, normed, cot, cos, sin)


def feed_forward(at, held, normed, cot, bias, sums):
    n = normed.shape[0]
    span = held[0].shape[1]
    units = 4 * span
    return pl.pallas_call(
        forward_kernel,
        out_shape=[out((2, n // 2, D), F32), out((2, n // 2, D), F32), out((8, D), F32)] + [out((2, span, D), BF)] * 4,
        in_specs=[SMEM] + [VM] * 8,
        out_specs=[VM] * 7,
        scratch_shapes=[low(units, D), low(units, D)],
        compiler_params=pltpu.CompilerParams(vmem_limit_bytes=22 << 20),
        cost_estimate=pl.CostEstimate(flops=10 * 10**9, bytes_accessed=16 << 20, transcendentals=10**6),
    )(at, *held, normed, cot, bias, sums)


def body(tokens, cotangent, qkv_weight, out_weight, fc_weight, vectors, qkv_momentum, out_momentum, fc_momentum, vector_first, vector_second):
    zi, xi, yi, ci, ti = (lax.axis_index(a) for a in ALL)
    rows = tokens.shape[0]
    n_att = qkv_weight.shape[3]
    n_fc = fc_weight.shape[3]
    gain, shift = vectors[:D], vectors[D : 2 * D]
    bias_in, bias_out = vectors[2 * D : 2 * D + FF], vectors[2 * D + FF :]

    first = ci == 0
    attn_rows = jnp.concatenate([jnp.transpose(qkv_weight[:, :, 0, :], (0, 2, 1)), jnp.transpose(out_weight[:, 0, :])[None]])
    fc_rows = jnp.transpose(fc_weight[:, :, 0, :], (0, 2, 1))
    own_rows = jnp.concatenate([attn_rows.reshape(1, n_fc, D), fc_rows]).astype(BF)
    held = jnp.stack(gather_ring(own_rows, pull_yh, 2), axis=1)

    inputs = tokens.astype(F32)
    average = jnp.mean(inputs, axis=-1, keepdims=True)
    deviation = inputs - average
    variance = jnp.mean(deviation * deviation, axis=-1, keepdims=True)
    inv_spread = lax.rsqrt(variance + 1e-05)
    centred = deviation * inv_spread
    normed_own = (centred * gain + shift).astype(BF)
    both = jnp.stack([normed_own, cotangent])
    held, both = lax.optimization_barrier((held, both))
    held = jnp.stack(gather_ring(held, pull_inner, 4), axis=1)
    both = jnp.stack([both, pull(both, "t", 1)], axis=1)
    held, both = lax.optimization_barrier((held, both))
    span = 8 * n_fc
    held = held.reshape(3, span, D)
    att_held = gather_ring(held[0], pull_outer, 4)
    fc_held = gather_ring(held[1:], pull_outer, 4)
    both = jnp.stack([both, pull(both, "c", 1)], axis=1)
    n_all = 4 * rows
    normed, cot = both[0].reshape(n_all, D), both[1].reshape(n_all, D)

    half = jnp.arange(LEN) // rows
    position = ((ti + half) % 2) * rows + jnp.arange(LEN) % rows
    frequency = 10000.0 ** (-2.0 * jnp.arange(ROT // 2, dtype=F32) / ROT)
    angles = position.astype(F32)[:, None] * frequency[None, :]
    cos_t, sin_t = jnp.cos(angles), jnp.sin(angles)
    pad = lambda a, b, fill: jnp.concatenate([a, b, jnp.full((LEN, PAD - ROT), fill, F32)], axis=1)
    cos_full, sin_full = pad(cos_t, cos_t, 1.0), pad(-sin_t, sin_t, 0.0)

    bias6 = bias_in.reshape(2, 4, 4, 2, 2, n_fc)
    bias6 = jnp.concatenate([bias6, bias6], axis=1)
    bias6 = jnp.concatenate([bias6, bias6], axis=2)
    bias6 = jnp.concatenate([bias6, bias6], axis=3)
    bias_own = lax.dynamic_slice(bias6, (ti, zi, xi, yi, ci, 0), (1, 4, 4, 2, 1, n_fc))[0, :, :, :, 0]
    by_turn = lambda v: jnp.where(first, jnp.swapaxes(v, 0, 1), v)
    bias_own = by_turn(bias_own).reshape(1, 32 * n_fc)
    at = jnp.stack([zi, xi, yi, ci, ti]).astype(jnp.int32)
    mom_rows = jnp.concatenate(
        [
            jnp.transpose(qkv_momentum[:, :, 0, :], (0, 2, 1)).reshape(3 * n_att, D),
            jnp.transpose(out_momentum[:, 0, :]),
            jnp.transpose(fc_momentum[:, :, 0, :], (0, 2, 1)).reshape(2 * n_fc, D),
        ]
    )
    far, normed, cot, bias_own, at, cos_full, sin_full, mom_rows = lax.optimization_barrier(
        (att_held[1:], normed, cot, bias_own, at, cos_full, sin_full, mom_rows)
    )
    att_held = att_held[:1] + far
    att_got = [pull(v, "c", 1) for v in att_held]
    sums, att_keep, att_give = attention(at, att_held, att_got, normed, cot, cos_full, sin_full)

    att_grad = (att_keep + pull(att_give, "c", 1)).reshape(4, span, D)
    att_parts = [att_grad[k] for k in range(4)]

    rows_own, rows_peer, grad_bias_in, *fc_parts = feed_forward(at, fc_held, normed, cot, bias_own, sums)
    att_total = sum_ring(att_parts, pull_outer)
    fc_total = sum_ring(fc_parts, pull_outer)
    rows_own = (rows_own + pull(rows_peer, "c", 1)).reshape(2, 2, rows, D)
    rows_own = rows_own[:, 0] + pull(rows_own[:, 1].astype(BF), "t", 1).astype(F32)
    att_total, fc_total, rows_own = lax.optimization_barrier((att_total, fc_total, rows_own))
    total = jnp.concatenate([att_total[None], fc_total]).reshape(3, 4, 2, n_fc, D)
    total = sum_ring([total[:, k] for k in range(4)], pull_inner)
    total = sum_ring([total[:, k] for k in range(2)], pull_yh).reshape(3 * n_fc, D)

    mixed = (inputs + rows_own[0] + bias_out).astype(BF)
    d_rows = rows_own[1]
    d_hat = d_rows * gain
    correction = d_hat - jnp.mean(d_hat, axis=-1, keepdims=True) - centred * jnp.mean(d_hat * centred, axis=-1, keepdims=True)
    own_cot = cotangent.astype(F32)
    input_grad = own_cot + correction * inv_spread

    total_of = lambda v: jnp.sum(v, axis=0, keepdims=True)
    vec_rows = [total_of(d_rows * centred), total_of(d_rows), grad_bias_in[: FF // D], total_of(own_cot), jnp.zeros((VEC_ROWS - VEC // D, D), F32)]

    moment = 0.95 * mom_rows + total
    update = total + 0.95 * moment

    half_fc = n_fc // 2
    att_u = update[: 4 * n_att].reshape(4, n_att, D)
    att_u = jnp.concatenate([att_u, jnp.zeros((4, half_fc - n_att, D), F32)], axis=1)
    fc_u = update[4 * n_att :].reshape(4, half_fc, D)
    vec_rows = jnp.concatenate(vec_rows)
    chunks = jnp.concatenate([att_u, fc_u])
    chunks = jnp.concatenate([chunks, jnp.broadcast_to(vec_rows, (8, VEC_ROWS, D))], axis=1)
    got = lax.all_to_all(chunks, ("z", "t"), split_axis=0, concat_axis=0, tiled=True)
    mine = got[:, :half_fc].reshape(8 * half_fc, D)
    vec_sum = jnp.sum(got[:, half_fc:], axis=0)[:8]
    keep, give = gram_parts(at, mine)
    from_core = pull(jnp.concatenate([give, vec_sum]), "c", 1)
    part = keep + from_core[:BLK]
    vec_sum = vec_sum + from_core[BLK:]
    quarter = lambda k: part[k * QUARTER : (k + 1) * QUARTER]
    along_x = lambda v, k: pull(v, "x", k)
    load = jnp.concatenate([quarter(0), vec_sum])
    for k in (1, 2, 3):
        load = load + along_x(jnp.concatenate([quarter(k), vec_sum]), 4 - k)
    load = load + pull(load, "yh", 1)
    part, vec_sum = load[:QUARTER], load[QUARTER:]
    part = jnp.where(zi >= 2, part + pull(part, "t", 1), part)
    part = jnp.concatenate(gather_ring(part, along_x, 4))
    rest = pull(part, "c", 1)
    x_rows = sweeps(at, part, rest, mine)
    vector_grad = vec_sum[: VEC // D].reshape(VEC)
    first_new = 0.9 * vector_first + 0.1 * vector_grad
    second_new = 0.95 * vector_second + 0.05 * vector_grad * vector_grad
    step_size = first_new / (1.0 - 0.9**STEP) / (jnp.sqrt(second_new / (1.0 - 0.95**STEP)) + 1e-08)
    vector_new = vectors - 0.2 * step_size

    back = lax.all_to_all(x_rows, ("z", "t"), split_axis=0, concat_axis=0, tiled=True).reshape(8, half_fc, D)
    att_x = back[:4, :n_att]
    fc_x = back[4:].reshape(2, n_fc, D)

    def cols(v):
        return jnp.transpose(v, (0, 2, 1))[:, :, None, :]

    fc_factor = math.sqrt(FF / D)
    qkv_new = qkv_weight * 0.99 - cols(att_x[:3])
    out_new = out_weight * 0.99 - cols(att_x[3:])[0]
    fc_new = fc_weight * 0.99 - fc_factor * cols(fc_x)
    att_m = moment[: 4 * n_att].reshape(4, n_att, D)
    fc_m = moment[4 * n_att :].reshape(2, n_fc, D)
    return (mixed, input_grad, qkv_new, out_new, fc_new, cols(att_m[:3]), cols(att_m[3:])[0], cols(fc_m), first_new, second_new, vector_new)


def solution(mesh):
    mesh = Mesh(mesh.devices.reshape(4, 4, 2, 2, 2), ALL)
    rows = P(ALL, None)
    w3 = P(None, None, "t", DP)
    w2 = P(None, "t", DP)
    vec = P()
    in_specs = (rows, rows, w3, w2, w3, vec, w3, w2, w3, vec, vec)
    out_specs = (rows, rows, w3, w2, w3, w3, w2, w3, vec, vec, vec)
    return jax.shard_map(body, mesh=mesh, in_specs=in_specs, out_specs=out_specs, check_vma=False)
```

```python
import functools
import itertools
import math

import jax
import jax.numpy as jnp
from jax import lax
from jax.experimental import pallas as pl
from jax.experimental.pallas import tpu as pltpu
from jax.sharding import Mesh, PartitionSpec as P

D = 768
H = 12
HD = 64
ROT = 16
FF = 3072
SWEEPS = 5
STEP = 10
LEN = 256
VEC = 2 * D + FF + D
VEC_ROWS = 12

NS = (3.4445, -4.775, 2.0315)
BF = jnp.bfloat16
F32 = jnp.float32
BLK = 256
QUARTER = 64
NB = D // BLK

DP = ("z", "x", "yh", "c")
ALL = ("z", "x", "yh", "c", "t")


def pull(value, axis, k):
    n = lax.axis_size(axis)
    return lax.ppermute(value, axis, [((i + k) % n, i) for i in range(n)])


def move(value, source):
    sizes = [lax.axis_size(a) for a in ALL]
    index = lambda at: functools.reduce(lambda total, one: total * one[0] + one[1] % one[0], zip(sizes, at), 0)
    pairs = []
    for here in itertools.product(*map(range, sizes)):
        there = source(*here)
        if there is not None:
            pairs.append((index(there), index(here)))
    return lax.ppermute(value, ALL, pairs)


def pull_outer(value, k):
    return move(value, lambda z, x, y, c, t: (z, x + k, y, c, t) if c == 0 else (z + k, x, y, c, t))


def pull_inner(value, k):
    return move(value, lambda z, x, y, c, t: (z + k, x, y, c, t) if c == 0 else (z, x + k, y, c, t))


def pull_yh(value, k):
    return pull(value, "yh", k)


def gather_ring(value, pulls, n):
    return [value] + [pulls(value, k) for k in range(1, n)]


def sum_ring(parts, pulls):
    n = len(parts)
    total = parts[0].astype(F32)
    for k in range(1, n):
        total = total + pulls(parts[k].astype(BF), n - k).astype(F32)
    return total


def dot(a, b, dims):
    return lax.dot_general(a, b, (dims, ((), ())), preferred_element_type=F32)


def pieces(value, n):
    out = []
    for _ in range(n):
        low = value.astype(BF)
        out.append(low)
        value = value - low.astype(F32)
    return out


def mul(xs, ys, dims=((1,), (0,))):
    n = len(xs)
    total = None
    for order in reversed(range(n)):
        for i in range(order + 1):
            term = lax.dot_general(xs[i], ys[order - i], (dims, ((), ())), preferred_element_type=F32)
            total = term if total is None else total + term
    return total


def gram_kernel(at_ref, rows_ref, keep_ref, give_ref, top_ref, bottom_ref):
    xs = pieces(rows_ref[...], 3)
    dims = ((0,), (0,))
    cut = lambda i: slice(i * BLK, (i + 1) * BLK)
    top_ref[...] = mul([x[:, cut(0)] for x in xs], xs, dims)
    bottom_ref[:, : 2 * BLK] = mul([x[:, cut(1)] for x in xs], [x[:, BLK:] for x in xs], dims)
    bottom_ref[:, 2 * BLK :] = mul([x[:, cut(2)] for x in xs], [x[:, 2 * BLK :] for x in xs], dims)

    def by_place(out_ref, in_ref):
        for k in range(4):
            place = pl.multiple_of(jnp.bitwise_and(at_ref[1] + k, 3) * QUARTER, QUARTER)
            out_ref[k * QUARTER : (k + 1) * QUARTER] = in_ref[pl.ds(place, QUARTER)]

    first = at_ref[3] == 0

    @pl.when(first)
    def _():
        by_place(keep_ref, top_ref)
        by_place(give_ref, bottom_ref)

    @pl.when(jnp.logical_not(first))
    def _():
        by_place(keep_ref, bottom_ref)
        by_place(give_ref, top_ref)


def blocks(i, j):
    return (slice(i * BLK, (i + 1) * BLK), slice(j * BLK, (j + 1) * BLK))


def put(refs, i, j, value):
    for ref, piece in zip(refs, pieces(value, len(refs))):
        ref[blocks(i, j)] = piece


def put_both(refs, i, j, value):
    put(refs, i, j, value)
    if i != j:
        put(refs, j, i, value.T)


def symmetric_product(xs, ys, emit, start=0):
    for i in range(start, NB):
        rows = slice(i * BLK, (i + 1) * BLK)
        wide = mul([x[rows, :] for x in xs], [y[:, i * BLK :] for y in ys])
        for j in range(i, NB):
            emit(i, j, wide[:, (j - i) * BLK : (j - i + 1) * BLK])


def sweeps_kernel(at_ref, *refs):
    sweeps_math(at_ref, refs[:4], refs[4:8], *refs[8:])


def sweeps_math(at_ref, mine_refs, rest_refs, x_ref, out_ref, top_ref, bottom_ref, gram_ref, a_ref, p_ref, b_ref):
    first = at_ref[3] == 0
    n_x = x_ref.shape[0]

    def by_place(out_ref, in_refs):
        for k, ref in enumerate(in_refs):
            place = pl.multiple_of(jnp.bitwise_and(at_ref[1] + k, 3) * QUARTER, QUARTER)
            out_ref[pl.ds(place, QUARTER)] = ref[...]

    @pl.when(first)
    def _():
        by_place(top_ref, mine_refs)
        by_place(bottom_ref, rest_refs)

    @pl.when(jnp.logical_not(first))
    def _():
        by_place(top_ref, rest_refs)
        by_place(bottom_ref, mine_refs)

    def packed(i, j):
        if i == 0:
            return top_ref[:, j * BLK : (j + 1) * BLK]
        at = (j - 1) if i == 1 else 2
        return bottom_ref[:, at * BLK : (at + 1) * BLK]

    eye = (lax.broadcasted_iota(jnp.int32, (BLK, BLK), 0) == lax.broadcasted_iota(jnp.int32, (BLK, BLK), 1)).astype(F32)
    trace = sum(jnp.sum(packed(i, i) * eye) for i in range(NB))
    norm = jnp.sqrt(jnp.full((8, 128), trace, F32)) + 1e-07
    factor = (1.0 / norm)[0:1, 0:1]
    square = factor * factor

    a_rows = lambda n: [a_ref.at[k, n_x : n_x + D] for k in range(n)]
    p_rows = lambda n: [p_ref.at[k] for k in range(n)]
    b_rows = lambda n: [b_ref.at[k] for k in range(n)]

    def put_x(n, value):
        for k, piece in enumerate(pieces(value, n)):
            a_ref[k, :n_x] = piece

    spread = 0.0
    for i in range(NB):
        for j in range(i, NB):
            value = packed(i, j) * square
            gram_ref[blocks(i, j)] = value
            put_both(a_rows(3), i, j, value)
            spread = spread + jnp.sum(value * value) * (1.0 if i == j else 2.0)
    put_x(3, x_ref[...] * factor)

    def poly(n_p):
        def emit(i, j, block):
            value = NS[1] * gram_ref[blocks(i, j)] + NS[2] * block
            if i == j:
                value = value + NS[0] * eye
            put_both(p_rows(n_p), i, j, value)

        a = a_rows(2)
        symmetric_product(a, a, emit)

    def next_gram(n, keep):
        p = p_rows(n)
        rows = slice(0, n_x + BLK)
        wide = mul([a_ref[k, rows] for k in range(n)], [y[...] for y in p])
        for j in range(NB):
            put_both(b_rows(n), 0, j, wide[n_x:, j * BLK : (j + 1) * BLK])
        symmetric_product(a_rows(n), p, lambda i, j, block: put_both(b_rows(n), i, j, block), 1)
        put_x(keep, wide[:n_x])

        def emit(i, j, block):
            gram_ref[blocks(i, j)] = block
            put_both(a_rows(keep), i, j, block)

        symmetric_product(b_rows(n), p, emit)

    steep = spread > 0.02

    @pl.when(steep)
    def _():
        poly(3)
        next_gram(3, 2)

    @pl.when(jnp.logical_not(steep))
    def _():
        poly(2)
        next_gram(2, 2)

    @pl.loop(1, SWEEPS - 1)
    def _(_):
        poly(2)
        next_gram(2, 2)

    poly(2)
    out_ref[...] = mul([a_ref[k, :n_x] for k in range(2)], [y[...] for y in p_rows(2)])


SMEM = pl.BlockSpec(memory_space=pltpu.SMEM)
VM = pl.BlockSpec(memory_space=pltpu.VMEM)


def gram_parts(at, rows):
    return pl.pallas_call(
        gram_kernel,
        out_shape=[jax.ShapeDtypeStruct((BLK, D), F32)] * 2,
        in_specs=[SMEM, VM],
        out_specs=[VM, VM],
        scratch_shapes=[pltpu.VMEM((BLK, D), F32)] * 2,
        compiler_params=pltpu.CompilerParams(vmem_limit_bytes=14 << 20),
        cost_estimate=pl.CostEstimate(flops=2 * 96 * D * D * 4, bytes_accessed=4 * D * D * 2, transcendentals=0),
    )(at, rows)


def sweeps(at, mine, rest, x_rows):
    return pl.pallas_call(
        sweeps_kernel,
        out_shape=jax.ShapeDtypeStruct(x_rows.shape, F32),
        in_specs=[SMEM] + [VM] * 9,
        out_specs=VM,
        scratch_shapes=[
            pltpu.VMEM((BLK, D), F32),
            pltpu.VMEM((BLK, D), F32),
            pltpu.VMEM((D, D), F32),
            pltpu.VMEM((3, x_rows.shape[0] + D, D), BF),
            pltpu.VMEM((3, D, D), BF),
            pltpu.VMEM((3, D, D), BF),
        ],
        compiler_params=pltpu.CompilerParams(vmem_limit_bytes=24 << 20),
        cost_estimate=pl.CostEstimate(flops=2 * D * D * D * 32, bytes_accessed=4 * D * D, transcendentals=0),
    )(at, *mine, *rest, x_rows)


def gelu_parts(u):
    k0 = math.sqrt(2.0 / math.pi)
    th = jnp.tanh(k0 * (u + 0.044715 * (u * u * u)))
    value = 0.5 * u * (1.0 + th)
    slope = 0.5 * (1.0 + th) + 0.5 * u * (1.0 - th * th) * (k0 * (1.0 + 3.0 * 0.044715 * u * u))
    return value, slope


HEADS = 3
PAD = 128
HC = HEADS * HD
HP = HEADS * PAD
NN = ((1,), (0,))
NT = ((1,), (1,))
TN = ((0,), (0,))


def iota(shape, dim):
    return lax.broadcasted_iota(jnp.int32, shape, dim)


def one_hot(cond):
    return jnp.where(cond, 1.0, 0.0).astype(BF)


def unit_place(at_ref, n):
    zi, xi, yi, ci, ti = (at_ref[k] for k in range(5))
    width = 24
    group = jnp.right_shift(n * 2731, 16)
    lane = n - width * group
    y = jnp.bitwise_and(group + yi, 1)
    inner = jnp.bitwise_and(jnp.right_shift(group, 1), 3)
    outer = jnp.bitwise_and(jnp.right_shift(group, 3), 3)
    z = jnp.bitwise_and(jnp.where(ci == 0, inner, outer) + zi, 3)
    x = jnp.bitwise_and(jnp.where(ci == 0, outer, inner) + xi, 3)
    row = 2 * ti + jnp.right_shift(z, 1)
    return row, (((jnp.bitwise_and(z, 1) * 4 + x) * 2 + y) * 2 + ci) * width + lane


def needed_blocks(at_ref):
    zi, ci = at_ref[0], at_ref[3]
    for rc in range(2):
        core_0 = jnp.bitwise_xor(ci, rc) == 0
        for x in range(4):
            for j in range(2):
                z = jnp.bitwise_and(2 * ci + j - zi, 3)
                outer, inner = jnp.where(core_0, x, z), jnp.where(core_0, z, x)
                yield rc, pl.multiple_of((outer * 4 + inner) * 48, 48)


def home_place(at_ref, r):
    xi, yi, ci = (at_ref[k] for k in range(1, 4))
    n = 6
    group = jnp.right_shift(r * 10923, 16)
    lane = r - n * group
    mat = jnp.bitwise_and(group, 3)
    y = jnp.bitwise_and(jnp.right_shift(group, 2) + yi, 1)
    j = jnp.bitwise_and(jnp.right_shift(group, 3), 1)
    x = jnp.bitwise_and(jnp.right_shift(group, 4) + xi, 3)
    core = jnp.bitwise_and(jnp.right_shift(group, 6) + ci, 1)
    return mat * HC + (((j * 4 + x) * 2 + y) * 2 + core) * n + lane


def attention_kernel(
    at_ref, own0_ref, own1_ref, own2_ref, own3_ref, got0_ref, got1_ref, got2_ref, got3_ref, normed_ref, cot_ref, cos_ref, sin_ref,
    sums_ref, keep_ref, give_ref,
    att_ref, near_ref, w_ref, wo_ref, q_ref, k_ref, v_ref, da_ref, heads_ref, d_ref, nat_ref,
):
    span = own0_ref.shape[0]
    for k, ref in enumerate((own0_ref, own1_ref, own2_ref, own3_ref, got0_ref, got1_ref, got2_ref, got3_ref)):
        att_ref[k // 4, k % 4 * span : (k % 4 + 1) * span] = ref[...]
    block = span // 4
    for k, (rc, at) in enumerate(needed_blocks(at_ref)):
        near_ref[k * block : (k + 1) * block] = att_ref[rc, pl.ds(at, block)]

    n_rows = 4 * HC
    pick = one_hot(iota((n_rows, n_rows), 0) == home_place(at_ref, iota((8, n_rows), 1))[:1])
    w_att = dot(pick, near_ref[...], NN).astype(BF)
    r = iota((HC, HC), 0)
    e = jnp.bitwise_and(r, HD - 1)
    half = ROT // 2
    source = jnp.where(e < half, r + half, jnp.where(e < ROT, r - half, -1))
    exchange = one_hot(iota((HC, HC), 1) == source)
    blank = jnp.zeros((HD, D), BF)

    def padded(ref, base, rows):
        for h in range(HEADS):
            at = base + h * PAD
            ref[at : at + HD] = rows[h * HD : (h + 1) * HD]
            ref[at + HD : at + PAD] = blank

    for m in range(3):
        padded(w_ref, m * HP, w_att[m * HC : (m + 1) * HC])
    for m in range(2):
        padded(w_ref, (3 + m) * HP, dot(exchange, w_att[m * HC : (m + 1) * HC], NN).astype(BF))
    padded(wo_ref, 0, w_att[3 * HC :])

    cos, sin = cos_ref[...], sin_ref[...]
    for m, ref in ((0, q_ref), (1, k_ref)):
        lin = dot(normed_ref[...], w_ref[m * HP : (m + 1) * HP], NT)
        lin_2 = dot(normed_ref[...], w_ref[(3 + m) * HP : (4 + m) * HP], NT)
        for s in range(2):
            rows = slice(s * LEN, (s + 1) * LEN)
            for h in range(HEADS):
                lanes = slice(h * PAD, (h + 1) * PAD)
                base = h * 2 * PAD
                own, other = lin[rows, lanes], lin_2[rows, lanes]
                ref[rows, base : base + PAD] = (own * cos + other * sin).astype(BF)
                ref[rows, base + PAD : base + 2 * PAD] = (other * cos - own * sin).astype(BF)
    v_ref[...] = dot(normed_ref[...], w_ref[2 * HP : 3 * HP], NT).astype(BF)
    da_ref[...] = dot(cot_ref[...], wo_ref[...], NT).astype(BF)

    turn = at_ref[4] * (LEN // 2)
    at_q = jnp.bitwise_xor(iota((LEN, LEN), 0), turn)
    at_k = jnp.bitwise_xor(iota((LEN, LEN), 1), turn)
    causal = at_q >= at_k
    scale = HD ** (-0.5)
    for s in range(2):
        rows = slice(s * LEN, (s + 1) * LEN)
        for h in range(HEADS):
            two = slice(h * 2 * PAD, (h + 1) * 2 * PAD)
            one = slice(h * 2 * PAD, h * 2 * PAD + PAD)
            lanes = slice(h * PAD, (h + 1) * PAD)
            value, d_att = v_ref[rows, lanes], da_ref[rows, lanes]
            scores = jnp.where(causal, dot(q_ref[rows, one], k_ref[rows, one], NT) * scale, -1e30)
            raised = jnp.exp(scores - jnp.max(scores, axis=1, keepdims=True))
            probs = raised / jnp.sum(raised, axis=1, keepdims=True)
            low = probs.astype(BF)
            heads_ref[rows, lanes] = dot(low, value, NN).astype(BF)
            d_ref[rows, 2 * HP + h * PAD : 2 * HP + (h + 1) * PAD] = dot(low, d_att, TN).astype(BF)
            d_probs = dot(d_att, value, NT)
            d_scores = (probs * (d_probs - jnp.sum(probs * d_probs, axis=1, keepdims=True))).astype(BF)
            d_q = dot(d_scores, k_ref[rows, two], NN) * scale
            d_k = dot(d_scores, q_ref[rows, two], TN) * scale
            for m, pair in ((0, d_q), (1, d_k)):
                at = m * HP + h * PAD
                d_ref[rows, at : at + PAD] = (pair[:, :PAD] * cos - pair[:, PAD:] * sin).astype(BF)

    sums_ref[0] = dot(heads_ref[...], wo_ref[...], NN)
    sums_ref[1] = dot(d_ref[...], w_ref[: 3 * HP], NN)

    for m in range(4):
        if m < 3:
            grad = dot(d_ref[:, m * HP : (m + 1) * HP], normed_ref[...], TN).astype(BF)
        else:
            grad = dot(heads_ref[...], cot_ref[...], TN).astype(BF)
        for h in range(HEADS):
            nat_ref[m * HC + h * HD : m * HC + (h + 1) * HD] = grad[h * PAD : h * PAD + HD]
    place = home_place(at_ref, iota((n_rows, 128), 0))
    pick = jnp.concatenate([one_hot(iota((n_rows, 128), 1) + b == place) for b in range(0, n_rows, 128)], axis=1)
    near_ref[...] = dot(pick, nat_ref[...], NN).astype(BF)
    keep_ref[...] = jnp.zeros_like(keep_ref)
    give_ref[...] = jnp.zeros_like(give_ref)
    for k, (rc, at) in enumerate(needed_blocks(at_ref)):
        (keep_ref, give_ref)[rc][pl.ds(at, block)] = near_ref[k * block : (k + 1) * block]


def forward_kernel(
    at_ref, held0_ref, held1_ref, held2_ref, held3_ref, normed_ref, cot_ref, bias_ref, sums_ref,
    own_ref, peer_ref, gbias_ref, out0_ref, out1_ref, out2_ref, out3_ref,
    win_ref, wback_ref,
):
    span = held0_ref.shape[1]
    for s, ref in enumerate((held0_ref, held1_ref, held2_ref, held3_ref)):
        win_ref[s * span : (s + 1) * span] = ref[0]
        wback_ref[s * span : (s + 1) * span] = ref[1]

    def send(group, grad):
        for s, ref in enumerate((out0_ref, out1_ref, out2_ref, out3_ref)):
            ref[group] = grad[s * span : (s + 1) * span]

    hidden, slope = gelu_parts(dot(normed_ref[...], win_ref[...], NT) + bias_ref[...])
    hidden = hidden.astype(BF)


    def give_rows(k, value):
        own_ref[k] = value[:LEN]
        peer_ref[k] = value[LEN:]

    give_rows(0, sums_ref[0] + dot(hidden, wback_ref[...], NN))
    send(1, dot(hidden, cot_ref[...], TN).astype(BF))
    d_pre = (dot(cot_ref[...], wback_ref[...], NT) * slope).astype(BF)
    grad_bias = jnp.sum(d_pre.astype(F32), axis=0, keepdims=True)
    n_units = win_ref.shape[0]
    bias_row, _ = unit_place(at_ref, iota((8, n_units), 1))
    spread = pieces(jnp.where(bias_row == iota((8, n_units), 0), grad_bias, 0.0), 3)
    _, bias_lane = unit_place(at_ref, iota((n_units, 128), 0))
    to_lane = jnp.concatenate([one_hot(iota((n_units, 128), 1) + b == bias_lane) for b in range(0, D, 128)], axis=1)
    gbias_ref[...] = sum(dot(piece, to_lane, NN) for piece in reversed(spread))
    send(0, dot(d_pre, normed_ref[...], TN).astype(BF))
    give_rows(1, sums_ref[1] + dot(d_pre, win_ref[...], NN))


def out(shape, dtype):
    return jax.ShapeDtypeStruct(shape, dtype)


def low(*shape):
    return pltpu.VMEM(shape, BF)


def attention(at, own, got, normed, cot, cos, sin):
    n = normed.shape[0]
    rows = 4 * own[0].shape[0]
    return pl.pallas_call(
        attention_kernel,
        out_shape=[out((2, n, D), F32), out((rows, D), BF), out((rows, D), BF)],
        in_specs=[SMEM] + [VM] * 12,
        out_specs=[VM] * 3,
        scratch_shapes=[low(2, rows, D), low(4 * HC, D), low(5 * HP, D), low(HP, D)]
        + [low(n, 2 * HP), low(n, 2 * HP)]
        + [low(n, HP)] * 3
        + [low(n, 3 * HP), low(4 * HC, D)],
        compiler_params=pltpu.CompilerParams(vmem_limit_bytes=32 << 20),
        cost_estimate=pl.CostEstimate(flops=12 * 10**9, bytes_accessed=16 << 20, transcendentals=10**6),
    )(at, *own, *got, normed, cot, cos, sin)


def feed_forward(at, held, normed, cot, bias, sums):
    n = normed.shape[0]
    span = held[0].shape[1]
    units = 4 * span
    return pl.pallas_call(
        forward_kernel,
        out_shape=[out((2, n // 2, D), F32), out((2, n // 2, D), F32), out((8, D), F32)] + [out((2, span, D), BF)] * 4,
        in_specs=[SMEM] + [VM] * 8,
        out_specs=[VM] * 7,
        scratch_shapes=[low(units, D), low(units, D)],
        compiler_params=pltpu.CompilerParams(vmem_limit_bytes=22 << 20),
        cost_estimate=pl.CostEstimate(flops=10 * 10**9, bytes_accessed=16 << 20, transcendentals=10**6),
    )(at, *held, normed, cot, bias, sums)


def body(tokens, cotangent, qkv_weight, out_weight, fc_weight, vectors, qkv_momentum, out_momentum, fc_momentum, vector_first, vector_second):
    zi, xi, yi, ci, ti = (lax.axis_index(a) for a in ALL)
    rows = tokens.shape[0]
    n_att = qkv_weight.shape[3]
    n_fc = fc_weight.shape[3]
    gain, shift = vectors[:D], vectors[D : 2 * D]
    bias_in, bias_out = vectors[2 * D : 2 * D + FF], vectors[2 * D + FF :]

    first = ci == 0
    attn_rows = jnp.concatenate([jnp.transpose(qkv_weight[:, :, 0, :], (0, 2, 1)), jnp.transpose(out_weight[:, 0, :])[None]])
    fc_rows = jnp.transpose(fc_weight[:, :, 0, :], (0, 2, 1))
    own_rows = jnp.concatenate([attn_rows.reshape(1, n_fc, D), fc_rows]).astype(BF)
    held = jnp.stack(gather_ring(own_rows, pull_yh, 2), axis=1)

    inputs = tokens.astype(F32)
    average = jnp.mean(inputs, axis=-1, keepdims=True)
    deviation = inputs - average
    variance = jnp.mean(deviation * deviation, axis=-1, keepdims=True)
    inv_spread = lax.rsqrt(variance + 1e-05)
    centred = deviation * inv_spread
    normed_own = (centred * gain + shift).astype(BF)
    both = jnp.stack([normed_own, cotangent])
    held, both = lax.optimization_barrier((held, both))
    held = jnp.stack(gather_ring(held, pull_inner, 4), axis=1)
    both = jnp.stack([both, pull(both, "t", 1)], axis=1)
    held, both = lax.optimization_barrier((held, both))
    span = 8 * n_fc
    held = held.reshape(3, span, D)
    att_held = gather_ring(held[0], pull_outer, 4)
    fc_held = gather_ring(held[1:], pull_outer, 4)
    both = jnp.stack([both, pull(both, "c", 1)], axis=1)
    n_all = 4 * rows
    normed, cot = both[0].reshape(n_all, D), both[1].reshape(n_all, D)

    half = jnp.arange(LEN) // rows
    position = ((ti + half) % 2) * rows + jnp.arange(LEN) % rows
    frequency = 10000.0 ** (-2.0 * jnp.arange(ROT // 2, dtype=F32) / ROT)
    angles = position.astype(F32)[:, None] * frequency[None, :]
    cos_t, sin_t = jnp.cos(angles), jnp.sin(angles)
    pad = lambda a, b, fill: jnp.concatenate([a, b, jnp.full((LEN, PAD - ROT), fill, F32)], axis=1)
    cos_full, sin_full = pad(cos_t, cos_t, 1.0), pad(-sin_t, sin_t, 0.0)

    bias6 = bias_in.reshape(2, 4, 4, 2, 2, n_fc)
    bias6 = jnp.concatenate([bias6, bias6], axis=1)
    bias6 = jnp.concatenate([bias6, bias6], axis=2)
    bias6 = jnp.concatenate([bias6, bias6], axis=3)
    bias_own = lax.dynamic_slice(bias6, (ti, zi, xi, yi, ci, 0), (1, 4, 4, 2, 1, n_fc))[0, :, :, :, 0]
    by_turn = lambda v: jnp.where(first, jnp.swapaxes(v, 0, 1), v)
    bias_own = by_turn(bias_own).reshape(1, 32 * n_fc)
    at = jnp.stack([zi, xi, yi, ci, ti]).astype(jnp.int32)
    mom_rows = jnp.concatenate(
        [
            jnp.transpose(qkv_momentum[:, :, 0, :], (0, 2, 1)).reshape(3 * n_att, D),
            jnp.transpose(out_momentum[:, 0, :]),
            jnp.transpose(fc_momentum[:, :, 0, :], (0, 2, 1)).reshape(2 * n_fc, D),
        ]
    )
    att_held[2], normed, cot, bias_own, at, cos_full, sin_full, mom_rows = lax.optimization_barrier(
        (att_held[2], normed, cot, bias_own, at, cos_full, sin_full, mom_rows)
    )
    att_got = [pull(v, "c", 1) for v in att_held]
    sums, att_keep, att_give = attention(at, att_held, att_got, normed, cot, cos_full, sin_full)

    att_grad = (att_keep + pull(att_give, "c", 1)).reshape(4, span, D)
    att_parts = [att_grad[k] for k in range(4)]

    rows_own, rows_peer, grad_bias_in, *fc_parts = feed_forward(at, fc_held, normed, cot, bias_own, sums)
    att_total = sum_ring(att_parts, pull_outer)
    fc_total = sum_ring(fc_parts, pull_outer)
    rows_own = (rows_own + pull(rows_peer, "c", 1)).reshape(2, 2, rows, D)
    rows_own = rows_own[:, 0] + pull(rows_own[:, 1].astype(BF), "t", 1).astype(F32)
    att_total, fc_total, rows_own = lax.optimization_barrier((att_total, fc_total, rows_own))
    total = jnp.concatenate([att_total[None], fc_total]).reshape(3, 4, 2, n_fc, D)
    total = sum_ring([total[:, k] for k in range(4)], pull_inner)
    total = sum_ring([total[:, k] for k in range(2)], pull_yh).reshape(3 * n_fc, D)

    mixed = (inputs + rows_own[0] + bias_out).astype(BF)
    d_rows = rows_own[1]
    d_hat = d_rows * gain
    correction = d_hat - jnp.mean(d_hat, axis=-1, keepdims=True) - centred * jnp.mean(d_hat * centred, axis=-1, keepdims=True)
    own_cot = cotangent.astype(F32)
    input_grad = own_cot + correction * inv_spread

    total_of = lambda v: jnp.sum(v, axis=0, keepdims=True)
    vec_rows = [total_of(d_rows * centred), total_of(d_rows), grad_bias_in[: FF // D], total_of(own_cot), jnp.zeros((VEC_ROWS - VEC // D, D), F32)]

    moment = 0.95 * mom_rows + total
    update = total + 0.95 * moment

    half_fc = n_fc // 2
    att_u = update[: 4 * n_att].reshape(4, n_att, D)
    att_u = jnp.concatenate([att_u, jnp.zeros((4, half_fc - n_att, D), F32)], axis=1)
    fc_u = update[4 * n_att :].reshape(4, half_fc, D)
    vec_rows = jnp.concatenate(vec_rows)
    chunks = jnp.concatenate([att_u, fc_u])
    chunks = jnp.concatenate([chunks, jnp.broadcast_to(vec_rows, (8, VEC_ROWS, D))], axis=1)
    got = lax.all_to_all(chunks, ("z", "t"), split_axis=0, concat_axis=0, tiled=True)
    mine = got[:, :half_fc].reshape(8 * half_fc, D)
    vec_sum = jnp.sum(got[:, half_fc:], axis=0)[:8]
    keep, give = gram_parts(at, mine)
    from_core = pull(jnp.concatenate([give, vec_sum]), "c", 1)
    part = keep + from_core[:BLK]
    vec_sum = vec_sum + from_core[BLK:]
    quarter = lambda k: part[k * QUARTER : (k + 1) * QUARTER]
    along_x = lambda v, k: pull(v, "x", k)
    load = jnp.concatenate([quarter(0), vec_sum])
    for k in (1, 2, 3):
        load = load + along_x(jnp.concatenate([quarter(k), vec_sum]), 4 - k)
    load = load + pull(load, "yh", 1)
    part, vec_sum = load[:QUARTER], load[QUARTER:]
    part = jnp.where(zi >= 2, part + pull(part, "t", 1), part)
    part = gather_ring(part, along_x, 4)
    rest = [pull(v, "c", 1) for v in part]
    x_rows = sweeps(at, part, rest, mine)
    vector_grad = vec_sum[: VEC // D].reshape(VEC)
    first_new = 0.9 * vector_first + 0.1 * vector_grad
    second_new = 0.95 * vector_second + 0.05 * vector_grad * vector_grad
    step_size = first_new / (1.0 - 0.9**STEP) / (jnp.sqrt(second_new / (1.0 - 0.95**STEP)) + 1e-08)
    vector_new = vectors - 0.2 * step_size

    back = lax.all_to_all(x_rows.astype(BF).reshape(8, half_fc, D), ("z", "t"), split_axis=0, concat_axis=0, tiled=True).astype(F32)
    att_x = back[:4, :n_att]
    fc_x = back[4:].reshape(2, n_fc, D)

    def cols(v):
        return jnp.transpose(v, (0, 2, 1))[:, :, None, :]

    fc_factor = math.sqrt(FF / D)
    qkv_new = qkv_weight * 0.99 - cols(att_x[:3])
    out_new = out_weight * 0.99 - cols(att_x[3:])[0]
    fc_new = fc_weight * 0.99 - fc_factor * cols(fc_x)
    att_m = moment[: 4 * n_att].reshape(4, n_att, D)
    fc_m = moment[4 * n_att :].reshape(2, n_fc, D)
    return (mixed, input_grad, qkv_new, out_new, fc_new, cols(att_m[:3]), cols(att_m[3:])[0], cols(fc_m), first_new, second_new, vector_new)


def solution(mesh):
    mesh = Mesh(mesh.devices.reshape(4, 4, 2, 2, 2), ALL)
    rows = P(ALL, None)
    w3 = P(None, None, "t", DP)
    w2 = P(None, "t", DP)
    vec = P()
    in_specs = (rows, rows, w3, w2, w3, vec, w3, w2, w3, vec, vec)
    out_specs = (rows, rows, w3, w2, w3, w3, w2, w3, vec, vec, vec)
    return jax.shard_map(body, mesh=mesh, in_specs=in_specs, out_specs=out_specs, check_vma=False)
```

```python
import functools
import itertools
import math

import jax
import jax.numpy as jnp
from jax import lax
from jax.experimental import pallas as pl
from jax.experimental.pallas import tpu as pltpu
from jax.sharding import Mesh, PartitionSpec as P

D = 768
H = 12
HD = 64
ROT = 16
FF = 3072
SWEEPS = 5
STEP = 10
LEN = 256
VEC = 2 * D + FF + D
VEC_ROWS = 12

NS = (3.4445, -4.775, 2.0315)
BF = jnp.bfloat16
F32 = jnp.float32
BLK = 256
QUARTER = 64
NB = D // BLK

DP = ("z", "x", "yh", "c")
ALL = ("z", "x", "yh", "c", "t")


def pull(value, axis, k):
    n = lax.axis_size(axis)
    return lax.ppermute(value, axis, [((i + k) % n, i) for i in range(n)])


def move(value, source):
    sizes = [lax.axis_size(a) for a in ALL]
    index = lambda at: functools.reduce(lambda total, one: total * one[0] + one[1] % one[0], zip(sizes, at), 0)
    pairs = []
    for here in itertools.product(*map(range, sizes)):
        there = source(*here)
        if there is not None:
            pairs.append((index(there), index(here)))
    return lax.ppermute(value, ALL, pairs)


def pull_outer(value, k):
    return move(value, lambda z, x, y, c, t: (z, x + k, y, c, t) if c == 0 else (z + k, x, y, c, t))


def pull_inner(value, k):
    return move(value, lambda z, x, y, c, t: (z + k, x, y, c, t) if c == 0 else (z, x + k, y, c, t))


def pull_yh(value, k):
    return pull(value, "yh", k)


def gather_ring(value, pulls, n):
    return [value] + [pulls(value, k) for k in range(1, n)]


def sum_ring(parts, pulls):
    n = len(parts)
    total = parts[0].astype(F32)
    for k in range(1, n):
        total = total + pulls(parts[k].astype(BF), n - k).astype(F32)
    return total


def dot(a, b, dims):
    return lax.dot_general(a, b, (dims, ((), ())), preferred_element_type=F32)


def pieces(value, n):
    out = []
    for _ in range(n):
        low = value.astype(BF)
        out.append(low)
        value = value - low.astype(F32)
    return out


def mul(xs, ys, dims=((1,), (0,))):
    n = len(xs)
    total = None
    for order in reversed(range(n)):
        for i in range(order + 1):
            term = lax.dot_general(xs[i], ys[order - i], (dims, ((), ())), preferred_element_type=F32)
            total = term if total is None else total + term
    return total


def gram_kernel(at_ref, rows_ref, keep_ref, give_ref, top_ref, bottom_ref):
    xs = pieces(rows_ref[...], 3)
    dims = ((0,), (0,))
    cut = lambda i: slice(i * BLK, (i + 1) * BLK)
    top_ref[...] = mul([x[:, cut(0)] for x in xs], xs, dims)
    bottom_ref[:, : 2 * BLK] = mul([x[:, cut(1)] for x in xs], [x[:, BLK:] for x in xs], dims)
    bottom_ref[:, 2 * BLK :] = mul([x[:, cut(2)] for x in xs], [x[:, 2 * BLK :] for x in xs], dims)

    def by_place(out_ref, in_ref):
        for k in range(4):
            place = pl.multiple_of(jnp.bitwise_and(at_ref[1] + k, 3) * QUARTER, QUARTER)
            out_ref[k * QUARTER : (k + 1) * QUARTER] = in_ref[pl.ds(place, QUARTER)]

    first = at_ref[3] == 0

    @pl.when(first)
    def _():
        by_place(keep_ref, top_ref)
        by_place(give_ref, bottom_ref)

    @pl.when(jnp.logical_not(first))
    def _():
        by_place(keep_ref, bottom_ref)
        by_place(give_ref, top_ref)


def blocks(i, j):
    return (slice(i * BLK, (i + 1) * BLK), slice(j * BLK, (j + 1) * BLK))


def put(refs, i, j, value):
    for ref, piece in zip(refs, pieces(value, len(refs))):
        ref[blocks(i, j)] = piece


def put_both(refs, i, j, value):
    put(refs, i, j, value)
    if i != j:
        put(refs, j, i, value.T)


def symmetric_product(xs, ys, emit, start=0):
    for i in range(start, NB):
        rows = slice(i * BLK, (i + 1) * BLK)
        wide = mul([x[rows, :] for x in xs], [y[:, i * BLK :] for y in ys])
        for j in range(i, NB):
            emit(i, j, wide[:, (j - i) * BLK : (j - i + 1) * BLK])


def sweeps_kernel(at_ref, *refs):
    sweeps_math(at_ref, refs[:4], refs[4:8], *refs[8:])


def sweeps_math(at_ref, mine_refs, rest_refs, x_ref, out_ref, top_ref, bottom_ref, gram_ref, a_ref, p_ref, b_ref):
    first = at_ref[3] == 0
    n_x = x_ref.shape[0]

    def by_place(out_ref, in_refs):
        for k, ref in enumerate(in_refs):
            place = pl.multiple_of(jnp.bitwise_and(at_ref[1] + k, 3) * QUARTER, QUARTER)
            out_ref[pl.ds(place, QUARTER)] = ref[...]

    @pl.when(first)
    def _():
        by_place(top_ref, mine_refs)
        by_place(bottom_ref, rest_refs)

    @pl.when(jnp.logical_not(first))
    def _():
        by_place(top_ref, rest_refs)
        by_place(bottom_ref, mine_refs)

    def packed(i, j):
        if i == 0:
            return top_ref[:, j * BLK : (j + 1) * BLK]
        at = (j - 1) if i == 1 else 2
        return bottom_ref[:, at * BLK : (at + 1) * BLK]

    eye = (lax.broadcasted_iota(jnp.int32, (BLK, BLK), 0) == lax.broadcasted_iota(jnp.int32, (BLK, BLK), 1)).astype(F32)
    trace = sum(jnp.sum(packed(i, i) * eye) for i in range(NB))
    norm = jnp.sqrt(jnp.full((8, 128), trace, F32)) + 1e-07
    factor = (1.0 / norm)[0:1, 0:1]
    square = factor * factor

    a_rows = lambda n: [a_ref.at[k, n_x : n_x + D] for k in range(n)]
    p_rows = lambda n: [p_ref.at[k] for k in range(n)]
    b_rows = lambda n: [b_ref.at[k] for k in range(n)]

    def put_x(n, value):
        for k, piece in enumerate(pieces(value, n)):
            a_ref[k, :n_x] = piece

    spread = 0.0
    for i in range(NB):
        for j in range(i, NB):
            value = packed(i, j) * square
            gram_ref[blocks(i, j)] = value
            put_both(a_rows(3), i, j, value)
            spread = spread + jnp.sum(value * value) * (1.0 if i == j else 2.0)
    put_x(3, x_ref[...] * factor)

    def poly(n_p):
        def emit(i, j, block):
            value = NS[1] * gram_ref[blocks(i, j)] + NS[2] * block
            if i == j:
                value = value + NS[0] * eye
            put_both(p_rows(n_p), i, j, value)

        a = a_rows(2)
        symmetric_product(a, a, emit)

    def next_gram(n, keep):
        p = p_rows(n)
        rows = slice(0, n_x + BLK)
        wide = mul([a_ref[k, rows] for k in range(n)], [y[...] for y in p])
        for j in range(NB):
            put_both(b_rows(n), 0, j, wide[n_x:, j * BLK : (j + 1) * BLK])
        symmetric_product(a_rows(n), p, lambda i, j, block: put_both(b_rows(n), i, j, block), 1)
        put_x(keep, wide[:n_x])

        def emit(i, j, block):
            gram_ref[blocks(i, j)] = block
            put_both(a_rows(keep), i, j, block)

        symmetric_product(b_rows(n), p, emit)

    steep = spread > 0.02

    @pl.when(steep)
    def _():
        poly(3)
        next_gram(3, 2)

    @pl.loop(jnp.where(steep, 1, 0), SWEEPS - 1)
    def _(_):
        poly(2)
        next_gram(2, 2)

    poly(2)
    out_ref[...] = mul([a_ref[k, :n_x] for k in range(2)], [y[...] for y in p_rows(2)])


SMEM = pl.BlockSpec(memory_space=pltpu.SMEM)
VM = pl.BlockSpec(memory_space=pltpu.VMEM)


def gram_parts(at, rows):
    return pl.pallas_call(
        gram_kernel,
        out_shape=[jax.ShapeDtypeStruct((BLK, D), F32)] * 2,
        in_specs=[SMEM, VM],
        out_specs=[VM, VM],
        scratch_shapes=[pltpu.VMEM((BLK, D), F32)] * 2,
        compiler_params=pltpu.CompilerParams(vmem_limit_bytes=14 << 20),
        cost_estimate=pl.CostEstimate(flops=2 * 96 * D * D * 4, bytes_accessed=4 * D * D * 2, transcendentals=0),
    )(at, rows)


def sweeps(at, mine, rest, x_rows):
    return pl.pallas_call(
        sweeps_kernel,
        out_shape=jax.ShapeDtypeStruct(x_rows.shape, F32),
        in_specs=[SMEM] + [VM] * 9,
        out_specs=VM,
        scratch_shapes=[
            pltpu.VMEM((BLK, D), F32),
            pltpu.VMEM((BLK, D), F32),
            pltpu.VMEM((D, D), F32),
            pltpu.VMEM((3, x_rows.shape[0] + D, D), BF),
            pltpu.VMEM((3, D, D), BF),
            pltpu.VMEM((3, D, D), BF),
        ],
        compiler_params=pltpu.CompilerParams(vmem_limit_bytes=24 << 20),
        cost_estimate=pl.CostEstimate(flops=2 * D * D * D * 32, bytes_accessed=4 * D * D, transcendentals=0),
    )(at, *mine, *rest, x_rows)


def gelu_parts(u):
    k0 = math.sqrt(2.0 / math.pi)
    th = jnp.tanh(k0 * (u + 0.044715 * (u * u * u)))
    value = 0.5 * u * (1.0 + th)
    slope = 0.5 * (1.0 + th) + 0.5 * u * (1.0 - th * th) * (k0 * (1.0 + 3.0 * 0.044715 * u * u))
    return value, slope


HEADS = 3
PAD = 128
HC = HEADS * HD
HP = HEADS * PAD
NN = ((1,), (0,))
NT = ((1,), (1,))
TN = ((0,), (0,))


def iota(shape, dim):
    return lax.broadcasted_iota(jnp.int32, shape, dim)


def one_hot(cond):
    return jnp.where(cond, 1.0, 0.0).astype(BF)


def unit_place(at_ref, n):
    zi, xi, yi, ci, ti = (at_ref[k] for k in range(5))
    width = 24
    group = jnp.right_shift(n * 2731, 16)
    lane = n - width * group
    y = jnp.bitwise_and(group + yi, 1)
    inner = jnp.bitwise_and(jnp.right_shift(group, 1), 3)
    outer = jnp.bitwise_and(jnp.right_shift(group, 3), 3)
    z = jnp.bitwise_and(jnp.where(ci == 0, inner, outer) + zi, 3)
    x = jnp.bitwise_and(jnp.where(ci == 0, outer, inner) + xi, 3)
    row = 2 * ti + jnp.right_shift(z, 1)
    return row, (((jnp.bitwise_and(z, 1) * 4 + x) * 2 + y) * 2 + ci) * width + lane


def needed_blocks(at_ref):
    zi, ci = at_ref[0], at_ref[3]
    for rc in range(2):
        core_0 = jnp.bitwise_xor(ci, rc) == 0
        for x in range(4):
            for j in range(2):
                z = jnp.bitwise_and(2 * ci + j - zi, 3)
                outer, inner = jnp.where(core_0, x, z), jnp.where(core_0, z, x)
                yield rc, pl.multiple_of((outer * 4 + inner) * 48, 48)


def home_place(at_ref, r):
    xi, yi, ci = (at_ref[k] for k in range(1, 4))
    n = 6
    group = jnp.right_shift(r * 10923, 16)
    lane = r - n * group
    mat = jnp.bitwise_and(group, 3)
    y = jnp.bitwise_and(jnp.right_shift(group, 2) + yi, 1)
    j = jnp.bitwise_and(jnp.right_shift(group, 3), 1)
    x = jnp.bitwise_and(jnp.right_shift(group, 4) + xi, 3)
    core = jnp.bitwise_and(jnp.right_shift(group, 6) + ci, 1)
    return mat * HC + (((j * 4 + x) * 2 + y) * 2 + core) * n + lane


def attention_kernel(
    at_ref, own0_ref, own1_ref, own2_ref, own3_ref, got0_ref, got1_ref, got2_ref, got3_ref, normed_ref, cot_ref, cos_ref, sin_ref,
    sums_ref, keep_ref, give_ref,
    att_ref, near_ref, w_ref, wo_ref, q_ref, k_ref, v_ref, da_ref, heads_ref, d_ref, nat_ref,
):
    span = own0_ref.shape[0]
    for k, ref in enumerate((own0_ref, own1_ref, own2_ref, own3_ref, got0_ref, got1_ref, got2_ref, got3_ref)):
        att_ref[k // 4, k % 4 * span : (k % 4 + 1) * span] = ref[...]
    block = span // 4
    for k, (rc, at) in enumerate(needed_blocks(at_ref)):
        near_ref[k * block : (k + 1) * block] = att_ref[rc, pl.ds(at, block)]

    n_rows = 4 * HC
    pick = one_hot(iota((n_rows, n_rows), 0) == home_place(at_ref, iota((8, n_rows), 1))[:1])
    w_att = dot(pick, near_ref[...], NN).astype(BF)
    r = iota((HC, HC), 0)
    e = jnp.bitwise_and(r, HD - 1)
    half = ROT // 2
    source = jnp.where(e < half, r + half, jnp.where(e < ROT, r - half, -1))
    exchange = one_hot(iota((HC, HC), 1) == source)
    blank = jnp.zeros((HD, D), BF)

    def padded(ref, base, rows):
        for h in range(HEADS):
            at = base + h * PAD
            ref[at : at + HD] = rows[h * HD : (h + 1) * HD]
            ref[at + HD : at + PAD] = blank

    for m in range(3):
        padded(w_ref, m * HP, w_att[m * HC : (m + 1) * HC])
    for m in range(2):
        padded(w_ref, (3 + m) * HP, dot(exchange, w_att[m * HC : (m + 1) * HC], NN).astype(BF))
    padded(wo_ref, 0, w_att[3 * HC :])

    cos, sin = cos_ref[...], sin_ref[...]
    for m, ref in ((0, q_ref), (1, k_ref)):
        lin = dot(normed_ref[...], w_ref[m * HP : (m + 1) * HP], NT)
        lin_2 = dot(normed_ref[...], w_ref[(3 + m) * HP : (4 + m) * HP], NT)
        for s in range(2):
            rows = slice(s * LEN, (s + 1) * LEN)
            for h in range(HEADS):
                lanes = slice(h * PAD, (h + 1) * PAD)
                base = h * 2 * PAD
                own, other = lin[rows, lanes], lin_2[rows, lanes]
                ref[rows, base : base + PAD] = (own * cos + other * sin).astype(BF)
                ref[rows, base + PAD : base + 2 * PAD] = (other * cos - own * sin).astype(BF)
    v_ref[...] = dot(normed_ref[...], w_ref[2 * HP : 3 * HP], NT).astype(BF)
    da_ref[...] = dot(cot_ref[...], wo_ref[...], NT).astype(BF)

    turn = at_ref[4] * (LEN // 2)
    at_q = jnp.bitwise_xor(iota((LEN, LEN), 0), turn)
    at_k = jnp.bitwise_xor(iota((LEN, LEN), 1), turn)
    causal = at_q >= at_k
    scale = HD ** (-0.5)
    for s in range(2):
        rows = slice(s * LEN, (s + 1) * LEN)
        for h in range(HEADS):
            two = slice(h * 2 * PAD, (h + 1) * 2 * PAD)
            one = slice(h * 2 * PAD, h * 2 * PAD + PAD)
            lanes = slice(h * PAD, (h + 1) * PAD)
            value, d_att = v_ref[rows, lanes], da_ref[rows, lanes]
            scores = jnp.where(causal, dot(q_ref[rows, one], k_ref[rows, one], NT) * scale, -1e30)
            raised = jnp.exp(scores - jnp.max(scores, axis=1, keepdims=True))
            probs = raised / jnp.sum(raised, axis=1, keepdims=True)
            low = probs.astype(BF)
            heads_ref[rows, lanes] = dot(low, value, NN).astype(BF)
            d_ref[rows, 2 * HP + h * PAD : 2 * HP + (h + 1) * PAD] = dot(low, d_att, TN).astype(BF)
            d_probs = dot(d_att, value, NT)
            d_scores = (probs * (d_probs - jnp.sum(probs * d_probs, axis=1, keepdims=True))).astype(BF)
            d_q = dot(d_scores, k_ref[rows, two], NN) * scale
            d_k = dot(d_scores, q_ref[rows, two], TN) * scale
            for m, pair in ((0, d_q), (1, d_k)):
                at = m * HP + h * PAD
                d_ref[rows, at : at + PAD] = (pair[:, :PAD] * cos - pair[:, PAD:] * sin).astype(BF)

    sums_ref[0] = dot(heads_ref[...], wo_ref[...], NN)
    sums_ref[1] = dot(d_ref[...], w_ref[: 3 * HP], NN)

    for m in range(4):
        if m < 3:
            grad = dot(d_ref[:, m * HP : (m + 1) * HP], normed_ref[...], TN).astype(BF)
        else:
            grad = dot(heads_ref[...], cot_ref[...], TN).astype(BF)
        for h in range(HEADS):
            nat_ref[m * HC + h * HD : m * HC + (h + 1) * HD] = grad[h * PAD : h * PAD + HD]
    place = home_place(at_ref, iota((n_rows, 128), 0))
    pick = jnp.concatenate([one_hot(iota((n_rows, 128), 1) + b == place) for b in range(0, n_rows, 128)], axis=1)
    near_ref[...] = dot(pick, nat_ref[...], NN).astype(BF)
    keep_ref[...] = jnp.zeros_like(keep_ref)
    give_ref[...] = jnp.zeros_like(give_ref)
    for k, (rc, at) in enumerate(needed_blocks(at_ref)):
        (keep_ref, give_ref)[rc][pl.ds(at, block)] = near_ref[k * block : (k + 1) * block]


def forward_kernel(
    at_ref, held0_ref, held1_ref, held2_ref, held3_ref, normed_ref, cot_ref, bias_ref, sums_ref,
    own_ref, peer_ref, gbias_ref, out0_ref, out1_ref, out2_ref, out3_ref,
    win_ref, wback_ref,
):
    span = held0_ref.shape[1]
    for s, ref in enumerate((held0_ref, held1_ref, held2_ref, held3_ref)):
        win_ref[s * span : (s + 1) * span] = ref[0]
        wback_ref[s * span : (s + 1) * span] = ref[1]

    def send(group, grad):
        for s, ref in enumerate((out0_ref, out1_ref, out2_ref, out3_ref)):
            ref[group] = grad[s * span : (s + 1) * span]

    hidden, slope = gelu_parts(dot(normed_ref[...], win_ref[...], NT) + bias_ref[...])
    hidden = hidden.astype(BF)


    def give_rows(k, value):
        own_ref[k] = value[:LEN]
        peer_ref[k] = value[LEN:]

    give_rows(0, sums_ref[0] + dot(hidden, wback_ref[...], NN))
    send(1, dot(hidden, cot_ref[...], TN).astype(BF))
    d_pre = (dot(cot_ref[...], wback_ref[...], NT) * slope).astype(BF)
    grad_bias = jnp.sum(d_pre.astype(F32), axis=0, keepdims=True)
    n_units = win_ref.shape[0]
    bias_row, _ = unit_place(at_ref, iota((8, n_units), 1))
    spread = pieces(jnp.where(bias_row == iota((8, n_units), 0), grad_bias, 0.0), 3)
    _, bias_lane = unit_place(at_ref, iota((n_units, 128), 0))
    to_lane = jnp.concatenate([one_hot(iota((n_units, 128), 1) + b == bias_lane) for b in range(0, D, 128)], axis=1)
    gbias_ref[...] = sum(dot(piece, to_lane, NN) for piece in reversed(spread))
    send(0, dot(d_pre, normed_ref[...], TN).astype(BF))
    give_rows(1, sums_ref[1] + dot(d_pre, win_ref[...], NN))


def out(shape, dtype):
    return jax.ShapeDtypeStruct(shape, dtype)


def low(*shape):
    return pltpu.VMEM(shape, BF)


def attention(at, own, got, normed, cot, cos, sin):
    n = normed.shape[0]
    rows = 4 * own[0].shape[0]
    return pl.pallas_call(
        attention_kernel,
        out_shape=[out((2, n, D), F32), out((rows, D), BF), out((rows, D), BF)],
        in_specs=[SMEM] + [VM] * 12,
        out_specs=[VM] * 3,
        scratch_shapes=[low(2, rows, D), low(4 * HC, D), low(5 * HP, D), low(HP, D)]
        + [low(n, 2 * HP), low(n, 2 * HP)]
        + [low(n, HP)] * 3
        + [low(n, 3 * HP), low(4 * HC, D)],
        compiler_params=pltpu.CompilerParams(vmem_limit_bytes=32 << 20),
        cost_estimate=pl.CostEstimate(flops=12 * 10**9, bytes_accessed=16 << 20, transcendentals=10**6),
    )(at, *own, *got, normed, cot, cos, sin)


def feed_forward(at, held, normed, cot, bias, sums):
    n = normed.shape[0]
    span = held[0].shape[1]
    units = 4 * span
    return pl.pallas_call(
        forward_kernel,
        out_shape=[out((2, n // 2, D), F32), out((2, n // 2, D), F32), out((8, D), F32)] + [out((2, span, D), BF)] * 4,
        in_specs=[SMEM] + [VM] * 8,
        out_specs=[VM] * 7,
        scratch_shapes=[low(units, D), low(units, D)],
        compiler_params=pltpu.CompilerParams(vmem_limit_bytes=22 << 20),
        cost_estimate=pl.CostEstimate(flops=10 * 10**9, bytes_accessed=16 << 20, transcendentals=10**6),
    )(at, *held, normed, cot, bias, sums)


def body(tokens, cotangent, qkv_weight, out_weight, fc_weight, vectors, qkv_momentum, out_momentum, fc_momentum, vector_first, vector_second):
    zi, xi, yi, ci, ti = (lax.axis_index(a) for a in ALL)
    rows = tokens.shape[0]
    n_att = qkv_weight.shape[3]
    n_fc = fc_weight.shape[3]
    gain, shift = vectors[:D], vectors[D : 2 * D]
    bias_in, bias_out = vectors[2 * D : 2 * D + FF], vectors[2 * D + FF :]

    first = ci == 0
    attn_rows = jnp.concatenate([jnp.transpose(qkv_weight[:, :, 0, :], (0, 2, 1)), jnp.transpose(out_weight[:, 0, :])[None]])
    fc_rows = jnp.transpose(fc_weight[:, :, 0, :], (0, 2, 1))
    own_rows = jnp.concatenate([attn_rows.reshape(1, n_fc, D), fc_rows]).astype(BF)
    held = jnp.stack(gather_ring(own_rows, pull_yh, 2), axis=1)

    inputs = tokens.astype(F32)
    average = jnp.mean(inputs, axis=-1, keepdims=True)
    deviation = inputs - average
    variance = jnp.mean(deviation * deviation, axis=-1, keepdims=True)
    inv_spread = lax.rsqrt(variance + 1e-05)
    centred = deviation * inv_spread
    normed_own = (centred * gain + shift).astype(BF)
    both = jnp.stack([normed_own, cotangent])
    held, both = lax.optimization_barrier((held, both))
    held = jnp.stack(gather_ring(held, pull_inner, 4), axis=1)
    both = jnp.stack([both, pull(both, "t", 1)], axis=1)
    held, both = lax.optimization_barrier((held, both))
    span = 8 * n_fc
    held = held.reshape(3, span, D)
    att_held = gather_ring(held[0], pull_outer, 4)
    fc_held = gather_ring(held[1:], pull_outer, 4)
    both = jnp.stack([both, pull(both, "c", 1)], axis=1)
    n_all = 4 * rows
    normed, cot = both[0].reshape(n_all, D), both[1].reshape(n_all, D)

    half = jnp.arange(LEN) // rows
    position = ((ti + half) % 2) * rows + jnp.arange(LEN) % rows
    frequency = 10000.0 ** (-2.0 * jnp.arange(ROT // 2, dtype=F32) / ROT)
    angles = position.astype(F32)[:, None] * frequency[None, :]
    cos_t, sin_t = jnp.cos(angles), jnp.sin(angles)
    pad = lambda a, b, fill: jnp.concatenate([a, b, jnp.full((LEN, PAD - ROT), fill, F32)], axis=1)
    cos_full, sin_full = pad(cos_t, cos_t, 1.0), pad(-sin_t, sin_t, 0.0)

    bias6 = bias_in.reshape(2, 4, 4, 2, 2, n_fc)
    bias6 = jnp.concatenate([bias6, bias6], axis=1)
    bias6 = jnp.concatenate([bias6, bias6], axis=2)
    bias6 = jnp.concatenate([bias6, bias6], axis=3)
    bias_own = lax.dynamic_slice(bias6, (ti, zi, xi, yi, ci, 0), (1, 4, 4, 2, 1, n_fc))[0, :, :, :, 0]
    by_turn = lambda v: jnp.where(first, jnp.swapaxes(v, 0, 1), v)
    bias_own = by_turn(bias_own).reshape(1, 32 * n_fc)
    at = jnp.stack([zi, xi, yi, ci, ti]).astype(jnp.int32)
    mom_rows = jnp.concatenate(
        [
            jnp.transpose(qkv_momentum[:, :, 0, :], (0, 2, 1)).reshape(3 * n_att, D),
            jnp.transpose(out_momentum[:, 0, :]),
            jnp.transpose(fc_momentum[:, :, 0, :], (0, 2, 1)).reshape(2 * n_fc, D),
        ]
    )
    att_held[2], normed, cot, bias_own, at, cos_full, sin_full, mom_rows = lax.optimization_barrier(
        (att_held[2], normed, cot, bias_own, at, cos_full, sin_full, mom_rows)
    )
    att_got = [pull(v, "c", 1) for v in att_held]
    sums, att_keep, att_give = attention(at, att_held, att_got, normed, cot, cos_full, sin_full)

    att_grad = (att_keep + pull(att_give, "c", 1)).reshape(4, span, D)
    att_parts = [att_grad[k] for k in range(4)]

    rows_own, rows_peer, grad_bias_in, *fc_parts = feed_forward(at, fc_held, normed, cot, bias_own, sums)
    att_total = sum_ring(att_parts, pull_outer)
    fc_total = sum_ring(fc_parts, pull_outer)
    rows_own = (rows_own + pull(rows_peer, "c", 1)).reshape(2, 2, rows, D)
    rows_own = rows_own[:, 0] + pull(rows_own[:, 1].astype(BF), "t", 1).astype(F32)
    att_total, fc_total, rows_own = lax.optimization_barrier((att_total, fc_total, rows_own))
    total = jnp.concatenate([att_total[None], fc_total]).reshape(3, 4, 2, n_fc, D)
    total = sum_ring([total[:, k] for k in range(4)], pull_inner)
    total = sum_ring([total[:, k] for k in range(2)], pull_yh).reshape(3 * n_fc, D)

    mixed = (inputs + rows_own[0] + bias_out).astype(BF)
    d_rows = rows_own[1]
    d_hat = d_rows * gain
    correction = d_hat - jnp.mean(d_hat, axis=-1, keepdims=True) - centred * jnp.mean(d_hat * centred, axis=-1, keepdims=True)
    own_cot = cotangent.astype(F32)
    input_grad = own_cot + correction * inv_spread

    total_of = lambda v: jnp.sum(v, axis=0, keepdims=True)
    vec_rows = [total_of(d_rows * centred), total_of(d_rows), grad_bias_in[: FF // D], total_of(own_cot), jnp.zeros((VEC_ROWS - VEC // D, D), F32)]

    moment = 0.95 * mom_rows + total
    update = total + 0.95 * moment

    half_fc = n_fc // 2
    att_u = update[: 4 * n_att].reshape(4, n_att, D)
    att_u = jnp.concatenate([att_u, jnp.zeros((4, half_fc - n_att, D), F32)], axis=1)
    fc_u = update[4 * n_att :].reshape(4, half_fc, D)
    vec_rows = jnp.concatenate(vec_rows)
    chunks = jnp.concatenate([att_u, fc_u])
    chunks = jnp.concatenate([chunks, jnp.broadcast_to(vec_rows, (8, VEC_ROWS, D))], axis=1)
    got = lax.all_to_all(chunks, ("z", "t"), split_axis=0, concat_axis=0, tiled=True)
    mine = got[:, :half_fc].reshape(8 * half_fc, D)
    vec_sum = jnp.sum(got[:, half_fc:], axis=0)[:8]
    keep, give = gram_parts(at, mine)
    from_core = pull(jnp.concatenate([give, vec_sum]), "c", 1)
    part = keep + from_core[:BLK]
    vec_sum = vec_sum + from_core[BLK:]
    quarter = lambda k: part[k * QUARTER : (k + 1) * QUARTER]
    along_x = lambda v, k: pull(v, "x", k)
    load = jnp.concatenate([quarter(0), vec_sum])
    for k in (1, 2, 3):
        load = load + along_x(jnp.concatenate([quarter(k), vec_sum]), 4 - k)
    load = load + pull(load, "yh", 1)
    part, vec_sum = load[:QUARTER], load[QUARTER:]
    part = jnp.where(zi >= 2, part + pull(part, "t", 1), part)
    part = gather_ring(part, along_x, 4)
    rest = [pull(v, "c", 1) for v in part]
    x_rows = sweeps(at, part, rest, mine)
    vector_grad = vec_sum[: VEC // D].reshape(VEC)
    first_new = 0.9 * vector_first + 0.1 * vector_grad
    second_new = 0.95 * vector_second + 0.05 * vector_grad * vector_grad
    step_size = first_new / (1.0 - 0.9**STEP) / (jnp.sqrt(second_new / (1.0 - 0.95**STEP)) + 1e-08)
    vector_new = vectors - 0.2 * step_size

    back = lax.all_to_all(x_rows.astype(BF).reshape(8, half_fc, D), ("z", "t"), split_axis=0, concat_axis=0, tiled=True).astype(F32)
    att_x = back[:4, :n_att]
    fc_x = back[4:].reshape(2, n_fc, D)

    def cols(v):
        return jnp.transpose(v, (0, 2, 1))[:, :, None, :]

    fc_factor = math.sqrt(FF / D)
    qkv_new = qkv_weight * 0.99 - cols(att_x[:3])
    out_new = out_weight * 0.99 - cols(att_x[3:])[0]
    fc_new = fc_weight * 0.99 - fc_factor * cols(fc_x)
    att_m = moment[: 4 * n_att].reshape(4, n_att, D)
    fc_m = moment[4 * n_att :].reshape(2, n_fc, D)
    return (mixed, input_grad, qkv_new, out_new, fc_new, cols(att_m[:3]), cols(att_m[3:])[0], cols(fc_m), first_new, second_new, vector_new)


def solution(mesh):
    mesh = Mesh(mesh.devices.reshape(4, 4, 2, 2, 2), ALL)
    rows = P(ALL, None)
    w3 = P(None, None, "t", DP)
    w2 = P(None, "t", DP)
    vec = P()
    in_specs = (rows, rows, w3, w2, w3, vec, w3, w2, w3, vec, vec)
    out_specs = (rows, rows, w3, w2, w3, w3, w2, w3, vec, vec, vec)
    return jax.shard_map(body, mesh=mesh, in_specs=in_specs, out_specs=out_specs, check_vma=False)
```

```python
import functools
import itertools
import math

import jax
import jax.numpy as jnp
from jax import lax
from jax.experimental import pallas as pl
from jax.experimental.pallas import tpu as pltpu
from jax.sharding import Mesh, PartitionSpec as P

D = 768
H = 12
HD = 64
ROT = 16
FF = 3072
SWEEPS = 5
STEP = 10
LEN = 256
VEC = 2 * D + FF + D
VEC_ROWS = 12

NS = (3.4445, -4.775, 2.0315)
BF = jnp.bfloat16
F32 = jnp.float32
BLK = 256
QUARTER = 64
NB = D // BLK

DP = ("z", "x", "yh", "c")
ALL = ("z", "x", "yh", "c", "t")


def pull(value, axis, k):
    n = lax.axis_size(axis)
    return lax.ppermute(value, axis, [((i + k) % n, i) for i in range(n)])


def move(value, source):
    sizes = [lax.axis_size(a) for a in ALL]
    index = lambda at: functools.reduce(lambda total, one: total * one[0] + one[1] % one[0], zip(sizes, at), 0)
    pairs = []
    for here in itertools.product(*map(range, sizes)):
        there = source(*here)
        if there is not None:
            pairs.append((index(there), index(here)))
    return lax.ppermute(value, ALL, pairs)


def pull_outer(value, k):
    return move(value, lambda z, x, y, c, t: (z, x + k, y, c, t) if c == 0 else (z + k, x, y, c, t))


def pull_inner(value, k):
    return move(value, lambda z, x, y, c, t: (z + k, x, y, c, t) if c == 0 else (z, x + k, y, c, t))


def pull_yh(value, k):
    return pull(value, "yh", k)


def gather_ring(value, pulls, n):
    return [value] + [pulls(value, k) for k in range(1, n)]


def sum_ring(parts, pulls):
    n = len(parts)
    total = parts[0].astype(F32)
    for k in range(1, n):
        total = total + pulls(parts[k].astype(BF), n - k).astype(F32)
    return total


def dot(a, b, dims):
    return lax.dot_general(a, b, (dims, ((), ())), preferred_element_type=F32)


def pieces(value, n):
    out = []
    for _ in range(n):
        low = value.astype(BF)
        out.append(low)
        value = value - low.astype(F32)
    return out


def mul(xs, ys, dims=((1,), (0,))):
    n = len(xs)
    total = None
    for order in reversed(range(n)):
        for i in range(order + 1):
            term = lax.dot_general(xs[i], ys[order - i], (dims, ((), ())), preferred_element_type=F32)
            total = term if total is None else total + term
    return total


def gram_kernel(at_ref, rows_ref, keep_ref, give_ref, top_ref, bottom_ref):
    xs = pieces(rows_ref[...], 3)
    dims = ((0,), (0,))
    cut = lambda i: slice(i * BLK, (i + 1) * BLK)
    top_ref[...] = mul([x[:, cut(0)] for x in xs], xs, dims)
    bottom_ref[:, : 2 * BLK] = mul([x[:, cut(1)] for x in xs], [x[:, BLK:] for x in xs], dims)
    bottom_ref[:, 2 * BLK :] = mul([x[:, cut(2)] for x in xs], [x[:, 2 * BLK :] for x in xs], dims)

    def by_place(out_ref, in_ref):
        for k in range(4):
            place = pl.multiple_of(jnp.bitwise_and(at_ref[1] + k, 3) * QUARTER, QUARTER)
            out_ref[k * QUARTER : (k + 1) * QUARTER] = in_ref[pl.ds(place, QUARTER)]

    first = at_ref[3] == 0

    @pl.when(first)
    def _():
        by_place(keep_ref, top_ref)
        by_place(give_ref, bottom_ref)

    @pl.when(jnp.logical_not(first))
    def _():
        by_place(keep_ref, bottom_ref)
        by_place(give_ref, top_ref)


def blocks(i, j):
    return (slice(i * BLK, (i + 1) * BLK), slice(j * BLK, (j + 1) * BLK))


def put(refs, i, j, value):
    for ref, piece in zip(refs, pieces(value, len(refs))):
        ref[blocks(i, j)] = piece


def put_both(refs, i, j, value):
    put(refs, i, j, value)
    if i != j:
        put(refs, j, i, value.T)


def symmetric_product(xs, ys, emit, start=0):
    for i in range(start, NB):
        rows = slice(i * BLK, (i + 1) * BLK)
        wide = mul([x[rows, :] for x in xs], [y[:, i * BLK :] for y in ys])
        for j in range(i, NB):
            emit(i, j, wide[:, (j - i) * BLK : (j - i + 1) * BLK])


def sweeps_kernel(at_ref, *refs):
    sweeps_math(at_ref, refs[:4], refs[4:8], *refs[8:])


def sweeps_math(at_ref, mine_refs, rest_refs, x_ref, out_ref, top_ref, bottom_ref, gram_ref, a_ref, p_ref, b_ref):
    first = at_ref[3] == 0
    n_x = x_ref.shape[0]

    def by_place(out_ref, in_refs):
        for k, ref in enumerate(in_refs):
            place = pl.multiple_of(jnp.bitwise_and(at_ref[1] + k, 3) * QUARTER, QUARTER)
            out_ref[pl.ds(place, QUARTER)] = ref[...]

    @pl.when(first)
    def _():
        by_place(top_ref, mine_refs)
        by_place(bottom_ref, rest_refs)

    @pl.when(jnp.logical_not(first))
    def _():
        by_place(top_ref, rest_refs)
        by_place(bottom_ref, mine_refs)

    def packed(i, j):
        if i == 0:
            return top_ref[:, j * BLK : (j + 1) * BLK]
        at = (j - 1) if i == 1 else 2
        return bottom_ref[:, at * BLK : (at + 1) * BLK]

    eye = (lax.broadcasted_iota(jnp.int32, (BLK, BLK), 0) == lax.broadcasted_iota(jnp.int32, (BLK, BLK), 1)).astype(F32)
    trace = sum(jnp.sum(packed(i, i) * eye) for i in range(NB))
    norm = jnp.sqrt(jnp.full((8, 128), trace, F32)) + 1e-07
    factor = (1.0 / norm)[0:1, 0:1]
    square = factor * factor

    a_rows = lambda n: [a_ref.at[k, n_x : n_x + D] for k in range(n)]
    p_rows = lambda n: [p_ref.at[k] for k in range(n)]
    b_rows = lambda n: [b_ref.at[k] for k in range(n)]

    def put_x(n, value):
        for k, piece in enumerate(pieces(value, n)):
            a_ref[k, :n_x] = piece

    spread = 0.0
    for i in range(NB):
        for j in range(i, NB):
            value = packed(i, j) * square
            gram_ref[blocks(i, j)] = value
            put_both(a_rows(3), i, j, value)
            spread = spread + jnp.sum(value * value) * (1.0 if i == j else 2.0)
    put_x(3, x_ref[...] * factor)

    def poly(n_p):
        def emit(i, j, block):
            value = NS[1] * gram_ref[blocks(i, j)] + NS[2] * block
            if i == j:
                value = value + NS[0] * eye
            put_both(p_rows(n_p), i, j, value)

        a = a_rows(2)
        symmetric_product(a, a, emit)

    def next_gram(n, keep):
        p = p_rows(n)
        rows = slice(0, n_x + BLK)
        wide = mul([a_ref[k, rows] for k in range(n)], [y[...] for y in p])
        for j in range(NB):
            put_both(b_rows(n), 0, j, wide[n_x:, j * BLK : (j + 1) * BLK])
        symmetric_product(a_rows(n), p, lambda i, j, block: put_both(b_rows(n), i, j, block), 1)
        put_x(keep, wide[:n_x])

        def emit(i, j, block):
            gram_ref[blocks(i, j)] = block
            put_both(a_rows(keep), i, j, block)

        symmetric_product(b_rows(n), p, emit)

    steep = spread > 0.02

    @pl.when(steep)
    def _():
        poly(3)
        next_gram(3, 2)

    @pl.loop(jnp.where(steep, 1, 0), SWEEPS - 1)
    def _(_):
        poly(2)
        next_gram(2, 2)

    poly(2)
    out_ref[...] = mul([a_ref[k, :n_x] for k in range(2)], [y[...] for y in p_rows(2)])


SMEM = pl.BlockSpec(memory_space=pltpu.SMEM)
VM = pl.BlockSpec(memory_space=pltpu.VMEM)


def gram_parts(at, rows):
    return pl.pallas_call(
        gram_kernel,
        out_shape=[jax.ShapeDtypeStruct((BLK, D), F32)] * 2,
        in_specs=[SMEM, VM],
        out_specs=[VM, VM],
        scratch_shapes=[pltpu.VMEM((BLK, D), F32)] * 2,
        compiler_params=pltpu.CompilerParams(vmem_limit_bytes=14 << 20),
        cost_estimate=pl.CostEstimate(flops=2 * 96 * D * D * 4, bytes_accessed=4 * D * D * 2, transcendentals=0),
    )(at, rows)


def sweeps(at, mine, rest, x_rows):
    return pl.pallas_call(
        sweeps_kernel,
        out_shape=jax.ShapeDtypeStruct(x_rows.shape, F32),
        in_specs=[SMEM] + [VM] * 9,
        out_specs=VM,
        scratch_shapes=[
            pltpu.VMEM((BLK, D), F32),
            pltpu.VMEM((BLK, D), F32),
            pltpu.VMEM((D, D), F32),
            pltpu.VMEM((3, x_rows.shape[0] + D, D), BF),
            pltpu.VMEM((3, D, D), BF),
            pltpu.VMEM((3, D, D), BF),
        ],
        compiler_params=pltpu.CompilerParams(vmem_limit_bytes=24 << 20),
        cost_estimate=pl.CostEstimate(flops=2 * D * D * D * 32, bytes_accessed=4 * D * D, transcendentals=0),
    )(at, *mine, *rest, x_rows)


def gelu_parts(u):
    k0 = math.sqrt(2.0 / math.pi)
    th = jnp.tanh(k0 * (u + 0.044715 * (u * u * u)))
    value = 0.5 * u * (1.0 + th)
    slope = 0.5 * (1.0 + th) + 0.5 * u * (1.0 - th * th) * (k0 * (1.0 + 3.0 * 0.044715 * u * u))
    return value, slope


HEADS = 3
PAD = 128
HC = HEADS * HD
HP = HEADS * PAD
NN = ((1,), (0,))
NT = ((1,), (1,))
TN = ((0,), (0,))


def iota(shape, dim):
    return lax.broadcasted_iota(jnp.int32, shape, dim)


def one_hot(cond):
    return jnp.where(cond, 1.0, 0.0).astype(BF)


def unit_place(at_ref, n):
    zi, xi, yi, ci, ti = (at_ref[k] for k in range(5))
    width = 24
    group = jnp.right_shift(n * 2731, 16)
    lane = n - width * group
    y = jnp.bitwise_and(group + yi, 1)
    inner = jnp.bitwise_and(jnp.right_shift(group, 1), 3)
    outer = jnp.bitwise_and(jnp.right_shift(group, 3), 3)
    z = jnp.bitwise_and(jnp.where(ci == 0, inner, outer) + zi, 3)
    x = jnp.bitwise_and(jnp.where(ci == 0, outer, inner) + xi, 3)
    row = 2 * ti + jnp.right_shift(z, 1)
    return row, (((jnp.bitwise_and(z, 1) * 4 + x) * 2 + y) * 2 + ci) * width + lane


def needed_blocks(at_ref):
    zi, ci = at_ref[0], at_ref[3]
    for rc in range(2):
        core_0 = jnp.bitwise_xor(ci, rc) == 0
        for x in range(4):
            for j in range(2):
                z = jnp.bitwise_and(2 * ci + j - zi, 3)
                outer, inner = jnp.where(core_0, x, z), jnp.where(core_0, z, x)
                yield rc, pl.multiple_of((outer * 4 + inner) * 48, 48)


def home_place(at_ref, r):
    xi, yi, ci = (at_ref[k] for k in range(1, 4))
    n = 6
    group = jnp.right_shift(r * 10923, 16)
    lane = r - n * group
    mat = jnp.bitwise_and(group, 3)
    y = jnp.bitwise_and(jnp.right_shift(group, 2) + yi, 1)
    j = jnp.bitwise_and(jnp.right_shift(group, 3), 1)
    x = jnp.bitwise_and(jnp.right_shift(group, 4) + xi, 3)
    core = jnp.bitwise_and(jnp.right_shift(group, 6) + ci, 1)
    return mat * HC + (((j * 4 + x) * 2 + y) * 2 + core) * n + lane


def attention_kernel(
    at_ref, own0_ref, own1_ref, own2_ref, own3_ref, got0_ref, got1_ref, got2_ref, got3_ref, normed_ref, cot_ref, cos_ref, sin_ref,
    sums_ref, keep_ref, give_ref,
    att_ref, near_ref, w_ref, wo_ref, q_ref, k_ref, v_ref, da_ref, heads_ref, d_ref, nat_ref,
):
    span = own0_ref.shape[0]
    for k, ref in enumerate((own0_ref, own1_ref, own2_ref, own3_ref, got0_ref, got1_ref, got2_ref, got3_ref)):
        att_ref[k // 4, k % 4 * span : (k % 4 + 1) * span] = ref[...]
    block = span // 4
    for k, (rc, at) in enumerate(needed_blocks(at_ref)):
        near_ref[k * block : (k + 1) * block] = att_ref[rc, pl.ds(at, block)]

    n_rows = 4 * HC
    pick = one_hot(iota((n_rows, n_rows), 0) == home_place(at_ref, iota((8, n_rows), 1))[:1])
    w_att = dot(pick, near_ref[...], NN).astype(BF)
    r = iota((HC, HC), 0)
    e = jnp.bitwise_and(r, HD - 1)
    half = ROT // 2
    source = jnp.where(e < half, r + half, jnp.where(e < ROT, r - half, -1))
    exchange = one_hot(iota((HC, HC), 1) == source)
    blank = jnp.zeros((HD, D), BF)

    def padded(ref, base, rows):
        for h in range(HEADS):
            at = base + h * PAD
            ref[at : at + HD] = rows[h * HD : (h + 1) * HD]
            ref[at + HD : at + PAD] = blank

    for m in range(3):
        padded(w_ref, m * HP, w_att[m * HC : (m + 1) * HC])
    for m in range(2):
        padded(w_ref, (3 + m) * HP, dot(exchange, w_att[m * HC : (m + 1) * HC], NN).astype(BF))
    padded(wo_ref, 0, w_att[3 * HC :])

    cos, sin = cos_ref[...], sin_ref[...]
    turn = at_ref[4] * (LEN // 2)
    at_q = jnp.bitwise_xor(iota((LEN, LEN), 0), turn)
    at_k = jnp.bitwise_xor(iota((LEN, LEN), 1), turn)
    causal = at_q >= at_k
    scale = HD ** (-0.5)

    @pl.loop(0, 2)
    def _(s):
        rows = pl.ds(pl.multiple_of(s * LEN, LEN), LEN)
        normed = normed_ref[rows]
        for m, ref in ((0, q_ref), (1, k_ref)):
            lin = dot(normed, w_ref[m * HP : (m + 1) * HP], NT)
            lin_2 = dot(normed, w_ref[(3 + m) * HP : (4 + m) * HP], NT)
            for h in range(HEADS):
                lanes = slice(h * PAD, (h + 1) * PAD)
                base = h * 2 * PAD
                own, other = lin[:, lanes], lin_2[:, lanes]
                ref[:, base : base + PAD] = (own * cos + other * sin).astype(BF)
                ref[:, base + PAD : base + 2 * PAD] = (other * cos - own * sin).astype(BF)
        v_ref[...] = dot(normed, w_ref[2 * HP : 3 * HP], NT).astype(BF)
        da_ref[...] = dot(cot_ref[rows], wo_ref[...], NT).astype(BF)
        for h in range(HEADS):
            two = slice(h * 2 * PAD, (h + 1) * 2 * PAD)
            one = slice(h * 2 * PAD, h * 2 * PAD + PAD)
            lanes = slice(h * PAD, (h + 1) * PAD)
            value, d_att = v_ref[:, lanes], da_ref[:, lanes]
            scores = jnp.where(causal, dot(q_ref[:, one], k_ref[:, one], NT) * scale, -1e30)
            raised = jnp.exp(scores - jnp.max(scores, axis=1, keepdims=True))
            probs = raised / jnp.sum(raised, axis=1, keepdims=True)
            low = probs.astype(BF)
            heads_ref[rows, lanes] = dot(low, value, NN).astype(BF)
            d_ref[rows, 2 * HP + h * PAD : 2 * HP + (h + 1) * PAD] = dot(low, d_att, TN).astype(BF)
            d_probs = dot(d_att, value, NT)
            d_scores = (probs * (d_probs - jnp.sum(probs * d_probs, axis=1, keepdims=True))).astype(BF)
            d_q = dot(d_scores, k_ref[:, two], NN) * scale
            d_k = dot(d_scores, q_ref[:, two], TN) * scale
            for m, pair in ((0, d_q), (1, d_k)):
                at = m * HP + h * PAD
                d_ref[rows, at : at + PAD] = (pair[:, :PAD] * cos - pair[:, PAD:] * sin).astype(BF)

    sums_ref[0] = dot(heads_ref[...], wo_ref[...], NN)
    sums_ref[1] = dot(d_ref[...], w_ref[: 3 * HP], NN)

    for m in range(4):
        if m < 3:
            grad = dot(d_ref[:, m * HP : (m + 1) * HP], normed_ref[...], TN).astype(BF)
        else:
            grad = dot(heads_ref[...], cot_ref[...], TN).astype(BF)
        for h in range(HEADS):
            nat_ref[m * HC + h * HD : m * HC + (h + 1) * HD] = grad[h * PAD : h * PAD + HD]
    place = home_place(at_ref, iota((n_rows, 128), 0))
    pick = jnp.concatenate([one_hot(iota((n_rows, 128), 1) + b == place) for b in range(0, n_rows, 128)], axis=1)
    near_ref[...] = dot(pick, nat_ref[...], NN).astype(BF)
    keep_ref[...] = jnp.zeros_like(keep_ref)
    give_ref[...] = jnp.zeros_like(give_ref)
    for k, (rc, at) in enumerate(needed_blocks(at_ref)):
        (keep_ref, give_ref)[rc][pl.ds(at, block)] = near_ref[k * block : (k + 1) * block]


def forward_kernel(
    at_ref, held0_ref, held1_ref, held2_ref, held3_ref, normed_ref, cot_ref, bias_ref, sums_ref,
    own_ref, peer_ref, gbias_ref, out0_ref, out1_ref, out2_ref, out3_ref,
    win_ref, wback_ref,
):
    span = held0_ref.shape[1]
    for s, ref in enumerate((held0_ref, held1_ref, held2_ref, held3_ref)):
        win_ref[s * span : (s + 1) * span] = ref[0]
        wback_ref[s * span : (s + 1) * span] = ref[1]

    def send(group, grad):
        for s, ref in enumerate((out0_ref, out1_ref, out2_ref, out3_ref)):
            ref[group] = grad[s * span : (s + 1) * span]

    hidden, slope = gelu_parts(dot(normed_ref[...], win_ref[...], NT) + bias_ref[...])
    hidden = hidden.astype(BF)


    def give_rows(k, value):
        own_ref[k] = value[:LEN]
        peer_ref[k] = value[LEN:]

    give_rows(0, sums_ref[0] + dot(hidden, wback_ref[...], NN))
    send(1, dot(hidden, cot_ref[...], TN).astype(BF))
    d_pre = (dot(cot_ref[...], wback_ref[...], NT) * slope).astype(BF)
    grad_bias = jnp.sum(d_pre.astype(F32), axis=0, keepdims=True)
    n_units = win_ref.shape[0]
    bias_row, _ = unit_place(at_ref, iota((8, n_units), 1))
    spread = pieces(jnp.where(bias_row == iota((8, n_units), 0), grad_bias, 0.0), 3)
    _, bias_lane = unit_place(at_ref, iota((n_units, 128), 0))
    to_lane = jnp.concatenate([one_hot(iota((n_units, 128), 1) + b == bias_lane) for b in range(0, D, 128)], axis=1)
    gbias_ref[...] = sum(dot(piece, to_lane, NN) for piece in reversed(spread))
    send(0, dot(d_pre, normed_ref[...], TN).astype(BF))
    give_rows(1, sums_ref[1] + dot(d_pre, win_ref[...], NN))


def out(shape, dtype):
    return jax.ShapeDtypeStruct(shape, dtype)


def low(*shape):
    return pltpu.VMEM(shape, BF)


def attention(at, own, got, normed, cot, cos, sin):
    n = normed.shape[0]
    rows = 4 * own[0].shape[0]
    return pl.pallas_call(
        attention_kernel,
        out_shape=[out((2, n, D), F32), out((rows, D), BF), out((rows, D), BF)],
        in_specs=[SMEM] + [VM] * 12,
        out_specs=[VM] * 3,
        scratch_shapes=[low(2, rows, D), low(4 * HC, D), low(5 * HP, D), low(HP, D)]
        + [low(LEN, 2 * HP), low(LEN, 2 * HP), low(LEN, HP), low(LEN, HP)]
        + [low(n, HP), low(n, 3 * HP), low(4 * HC, D)],
        compiler_params=pltpu.CompilerParams(vmem_limit_bytes=32 << 20),
        cost_estimate=pl.CostEstimate(flops=12 * 10**9, bytes_accessed=16 << 20, transcendentals=10**6),
    )(at, *own, *got, normed, cot, cos, sin)


def feed_forward(at, held, normed, cot, bias, sums):
    n = normed.shape[0]
    span = held[0].shape[1]
    units = 4 * span
    return pl.pallas_call(
        forward_kernel,
        out_shape=[out((2, n // 2, D), F32), out((2, n // 2, D), F32), out((8, D), F32)] + [out((2, span, D), BF)] * 4,
        in_specs=[SMEM] + [VM] * 8,
        out_specs=[VM] * 7,
        scratch_shapes=[low(units, D), low(units, D)],
        compiler_params=pltpu.CompilerParams(vmem_limit_bytes=22 << 20),
        cost_estimate=pl.CostEstimate(flops=10 * 10**9, bytes_accessed=16 << 20, transcendentals=10**6),
    )(at, *held, normed, cot, bias, sums)


def body(tokens, cotangent, qkv_weight, out_weight, fc_weight, vectors, qkv_momentum, out_momentum, fc_momentum, vector_first, vector_second):
    zi, xi, yi, ci, ti = (lax.axis_index(a) for a in ALL)
    rows = tokens.shape[0]
    n_att = qkv_weight.shape[3]
    n_fc = fc_weight.shape[3]
    gain, shift = vectors[:D], vectors[D : 2 * D]
    bias_in, bias_out = vectors[2 * D : 2 * D + FF], vectors[2 * D + FF :]

    first = ci == 0
    attn_rows = jnp.concatenate([jnp.transpose(qkv_weight[:, :, 0, :], (0, 2, 1)), jnp.transpose(out_weight[:, 0, :])[None]])
    fc_rows = jnp.transpose(fc_weight[:, :, 0, :], (0, 2, 1))
    own_rows = jnp.concatenate([attn_rows.reshape(1, n_fc, D), fc_rows]).astype(BF)
    held = jnp.stack(gather_ring(own_rows, pull_yh, 2), axis=1)

    inputs = tokens.astype(F32)
    average = jnp.mean(inputs, axis=-1, keepdims=True)
    deviation = inputs - average
    variance = jnp.mean(deviation * deviation, axis=-1, keepdims=True)
    inv_spread = lax.rsqrt(variance + 1e-05)
    centred = deviation * inv_spread
    normed_own = (centred * gain + shift).astype(BF)
    both = jnp.stack([normed_own, cotangent])
    held, both = lax.optimization_barrier((held, both))
    held = jnp.stack(gather_ring(held, pull_inner, 4), axis=1)
    both = jnp.stack([both, pull(both, "t", 1)], axis=1)
    held, both = lax.optimization_barrier((held, both))
    span = 8 * n_fc
    held = held.reshape(3, span, D)
    att_held = gather_ring(held[0], pull_outer, 4)
    fc_held = gather_ring(held[1:], pull_outer, 4)
    both = jnp.stack([both, pull(both, "c", 1)], axis=1)
    n_all = 4 * rows
    normed, cot = both[0].reshape(n_all, D), both[1].reshape(n_all, D)

    half = jnp.arange(LEN) // rows
    position = ((ti + half) % 2) * rows + jnp.arange(LEN) % rows
    frequency = 10000.0 ** (-2.0 * jnp.arange(ROT // 2, dtype=F32) / ROT)
    angles = position.astype(F32)[:, None] * frequency[None, :]
    cos_t, sin_t = jnp.cos(angles), jnp.sin(angles)
    pad = lambda a, b, fill: jnp.concatenate([a, b, jnp.full((LEN, PAD - ROT), fill, F32)], axis=1)
    cos_full, sin_full = pad(cos_t, cos_t, 1.0), pad(-sin_t, sin_t, 0.0)

    bias6 = bias_in.reshape(2, 4, 4, 2, 2, n_fc)
    bias6 = jnp.concatenate([bias6, bias6], axis=1)
    bias6 = jnp.concatenate([bias6, bias6], axis=2)
    bias6 = jnp.concatenate([bias6, bias6], axis=3)
    bias_own = lax.dynamic_slice(bias6, (ti, zi, xi, yi, ci, 0), (1, 4, 4, 2, 1, n_fc))[0, :, :, :, 0]
    by_turn = lambda v: jnp.where(first, jnp.swapaxes(v, 0, 1), v)
    bias_own = by_turn(bias_own).reshape(1, 32 * n_fc)
    at = jnp.stack([zi, xi, yi, ci, ti]).astype(jnp.int32)
    mom_rows = jnp.concatenate(
        [
            jnp.transpose(qkv_momentum[:, :, 0, :], (0, 2, 1)).reshape(3 * n_att, D),
            jnp.transpose(out_momentum[:, 0, :]),
            jnp.transpose(fc_momentum[:, :, 0, :], (0, 2, 1)).reshape(2 * n_fc, D),
        ]
    )
    att_held[2], normed, cot, bias_own, at, cos_full, sin_full, mom_rows = lax.optimization_barrier(
        (att_held[2], normed, cot, bias_own, at, cos_full, sin_full, mom_rows)
    )
    att_got = [pull(v, "c", 1) for v in att_held]
    sums, att_keep, att_give = attention(at, att_held, att_got, normed, cot, cos_full, sin_full)

    att_grad = (att_keep + pull(att_give, "c", 1)).reshape(4, span, D)
    att_parts = [att_grad[k] for k in range(4)]

    rows_own, rows_peer, grad_bias_in, *fc_parts = feed_forward(at, fc_held, normed, cot, bias_own, sums)
    att_total = sum_ring(att_parts, pull_outer)
    fc_total = sum_ring(fc_parts, pull_outer)
    rows_own = (rows_own + pull(rows_peer, "c", 1)).reshape(2, 2, rows, D)
    rows_own = rows_own[:, 0] + pull(rows_own[:, 1].astype(BF), "t", 1).astype(F32)
    att_total, fc_total, rows_own = lax.optimization_barrier((att_total, fc_total, rows_own))
    total = jnp.concatenate([att_total[None], fc_total]).reshape(3, 4, 2, n_fc, D)
    total = sum_ring([total[:, k] for k in range(4)], pull_inner)
    total = sum_ring([total[:, k] for k in range(2)], pull_yh).reshape(3 * n_fc, D)

    mixed = (inputs + rows_own[0] + bias_out).astype(BF)
    d_rows = rows_own[1]
    d_hat = d_rows * gain
    correction = d_hat - jnp.mean(d_hat, axis=-1, keepdims=True) - centred * jnp.mean(d_hat * centred, axis=-1, keepdims=True)
    own_cot = cotangent.astype(F32)
    input_grad = own_cot + correction * inv_spread

    total_of = lambda v: jnp.sum(v, axis=0, keepdims=True)
    vec_rows = [total_of(d_rows * centred), total_of(d_rows), grad_bias_in[: FF // D], total_of(own_cot), jnp.zeros((VEC_ROWS - VEC // D, D), F32)]

    moment = 0.95 * mom_rows + total
    update = total + 0.95 * moment

    half_fc = n_fc // 2
    att_u = update[: 4 * n_att].reshape(4, n_att, D)
    att_u = jnp.concatenate([att_u, jnp.zeros((4, half_fc - n_att, D), F32)], axis=1)
    fc_u = update[4 * n_att :].reshape(4, half_fc, D)
    vec_rows = jnp.concatenate(vec_rows)
    chunks = jnp.concatenate([att_u, fc_u])
    chunks = jnp.concatenate([chunks, jnp.broadcast_to(vec_rows, (8, VEC_ROWS, D))], axis=1)
    got = lax.all_to_all(chunks, ("z", "t"), split_axis=0, concat_axis=0, tiled=True)
    mine = got[:, :half_fc].reshape(8 * half_fc, D)
    vec_sum = jnp.sum(got[:, half_fc:], axis=0)[:8]
    keep, give = gram_parts(at, mine)
    from_core = pull(jnp.concatenate([give, vec_sum]), "c", 1)
    part = keep + from_core[:BLK]
    vec_sum = vec_sum + from_core[BLK:]
    quarter = lambda k: part[k * QUARTER : (k + 1) * QUARTER]
    along_x = lambda v, k: pull(v, "x", k)
    load = jnp.concatenate([quarter(0), vec_sum])
    for k in (1, 2, 3):
        load = load + along_x(jnp.concatenate([quarter(k), vec_sum]), 4 - k)
    load = load + pull(load, "yh", 1)
    part, vec_sum = load[:QUARTER], load[QUARTER:]
    part = jnp.where(zi >= 2, part + pull(part, "t", 1), part)
    part = gather_ring(part, along_x, 4)
    rest = [pull(v, "c", 1) for v in part]
    x_rows = sweeps(at, part, rest, mine)
    vector_grad = vec_sum[: VEC // D].reshape(VEC)
    first_new = 0.9 * vector_first + 0.1 * vector_grad
    second_new = 0.95 * vector_second + 0.05 * vector_grad * vector_grad
    step_size = first_new / (1.0 - 0.9**STEP) / (jnp.sqrt(second_new / (1.0 - 0.95**STEP)) + 1e-08)
    vector_new = vectors - 0.2 * step_size

    back = lax.all_to_all(x_rows.astype(BF).reshape(8, half_fc, D), ("z", "t"), split_axis=0, concat_axis=0, tiled=True).astype(F32)
    att_x = back[:4, :n_att]
    fc_x = back[4:].reshape(2, n_fc, D)

    def cols(v):
        return jnp.transpose(v, (0, 2, 1))[:, :, None, :]

    fc_factor = math.sqrt(FF / D)
    qkv_new = qkv_weight * 0.99 - cols(att_x[:3])
    out_new = out_weight * 0.99 - cols(att_x[3:])[0]
    fc_new = fc_weight * 0.99 - fc_factor * cols(fc_x)
    att_m = moment[: 4 * n_att].reshape(4, n_att, D)
    fc_m = moment[4 * n_att :].reshape(2, n_fc, D)
    return (mixed, input_grad, qkv_new, out_new, fc_new, cols(att_m[:3]), cols(att_m[3:])[0], cols(fc_m), first_new, second_new, vector_new)


def solution(mesh):
    mesh = Mesh(mesh.devices.reshape(4, 4, 2, 2, 2), ALL)
    rows = P(ALL, None)
    w3 = P(None, None, "t", DP)
    w2 = P(None, "t", DP)
    vec = P()
    in_specs = (rows, rows, w3, w2, w3, vec, w3, w2, w3, vec, vec)
    out_specs = (rows, rows, w3, w2, w3, w3, w2, w3, vec, vec, vec)
    return jax.shard_map(body, mesh=mesh, in_specs=in_specs, out_specs=out_specs, check_vma=False)
```

```python
import functools
import itertools
import math

import jax
import jax.numpy as jnp
from jax import lax
from jax.experimental import pallas as pl
from jax.experimental.pallas import tpu as pltpu
from jax.sharding import Mesh, PartitionSpec as P

D = 768
H = 12
HD = 64
ROT = 16
FF = 3072
SWEEPS = 5
STEP = 10
LEN = 256
VEC = 2 * D + FF + D
VEC_ROWS = 12

NS = (3.4445, -4.775, 2.0315)
BF = jnp.bfloat16
F32 = jnp.float32
BLK = 256
QUARTER = 64
NB = D // BLK

DP = ("z", "x", "yh", "c")
ALL = ("z", "x", "yh", "c", "t")


def pull(value, axis, k):
    n = lax.axis_size(axis)
    return lax.ppermute(value, axis, [((i + k) % n, i) for i in range(n)])


def move(value, source):
    sizes = [lax.axis_size(a) for a in ALL]
    index = lambda at: functools.reduce(lambda total, one: total * one[0] + one[1] % one[0], zip(sizes, at), 0)
    pairs = []
    for here in itertools.product(*map(range, sizes)):
        there = source(*here)
        if there is not None:
            pairs.append((index(there), index(here)))
    return lax.ppermute(value, ALL, pairs)


def pull_outer(value, k):
    return move(value, lambda z, x, y, c, t: (z, x + k, y, c, t) if c == 0 else (z + k, x, y, c, t))


def pull_inner(value, k):
    return move(value, lambda z, x, y, c, t: (z + k, x, y, c, t) if c == 0 else (z, x + k, y, c, t))


def pull_yh(value, k):
    return pull(value, "yh", k)


def gather_ring(value, pulls, n):
    return [value] + [pulls(value, k) for k in range(1, n)]


def sum_ring(parts, pulls):
    n = len(parts)
    total = parts[0].astype(F32)
    for k in range(1, n):
        total = total + pulls(parts[k].astype(BF), n - k).astype(F32)
    return total


def dot(a, b, dims):
    return lax.dot_general(a, b, (dims, ((), ())), preferred_element_type=F32)


def pieces(value, n):
    out = []
    for _ in range(n):
        low = value.astype(BF)
        out.append(low)
        value = value - low.astype(F32)
    return out


def mul(xs, ys, dims=((1,), (0,))):
    n = len(xs)
    total = None
    for order in reversed(range(n)):
        for i in range(order + 1):
            term = lax.dot_general(xs[i], ys[order - i], (dims, ((), ())), preferred_element_type=F32)
            total = term if total is None else total + term
    return total


def gram_kernel(at_ref, rows_ref, keep_ref, give_ref, top_ref, bottom_ref):
    xs = pieces(rows_ref[...], 3)
    dims = ((0,), (0,))
    cut = lambda i: slice(i * BLK, (i + 1) * BLK)
    top_ref[...] = mul([x[:, cut(0)] for x in xs], xs, dims)
    bottom_ref[:, : 2 * BLK] = mul([x[:, cut(1)] for x in xs], [x[:, BLK:] for x in xs], dims)
    bottom_ref[:, 2 * BLK :] = mul([x[:, cut(2)] for x in xs], [x[:, 2 * BLK :] for x in xs], dims)

    def by_place(out_ref, in_ref):
        for k in range(4):
            place = pl.multiple_of(jnp.bitwise_and(at_ref[1] + k, 3) * QUARTER, QUARTER)
            out_ref[k * QUARTER : (k + 1) * QUARTER] = in_ref[pl.ds(place, QUARTER)]

    first = at_ref[3] == 0

    @pl.when(first)
    def _():
        by_place(keep_ref, top_ref)
        by_place(give_ref, bottom_ref)

    @pl.when(jnp.logical_not(first))
    def _():
        by_place(keep_ref, bottom_ref)
        by_place(give_ref, top_ref)


def blocks(i, j):
    return (slice(i * BLK, (i + 1) * BLK), slice(j * BLK, (j + 1) * BLK))


def put(refs, i, j, value):
    for ref, piece in zip(refs, pieces(value, len(refs))):
        ref[blocks(i, j)] = piece


def put_both(refs, i, j, value):
    put(refs, i, j, value)
    if i != j:
        put(refs, j, i, value.T)


def symmetric_product(xs, ys, emit, start=0):
    for i in range(start, NB):
        rows = slice(i * BLK, (i + 1) * BLK)
        wide = mul([x[rows, :] for x in xs], [y[:, i * BLK :] for y in ys])
        for j in range(i, NB):
            emit(i, j, wide[:, (j - i) * BLK : (j - i + 1) * BLK])


def sweeps_kernel(at_ref, *refs):
    sweeps_math(at_ref, refs[:4], refs[4:8], *refs[8:])


def sweeps_math(at_ref, mine_refs, rest_refs, x_ref, out_ref, top_ref, bottom_ref, gram_ref, a_ref, p_ref, b_ref):
    first = at_ref[3] == 0
    n_x = x_ref.shape[0]

    def by_place(out_ref, in_refs):
        for k, ref in enumerate(in_refs):
            place = pl.multiple_of(jnp.bitwise_and(at_ref[1] + k, 3) * QUARTER, QUARTER)
            out_ref[pl.ds(place, QUARTER)] = ref[...]

    @pl.when(first)
    def _():
        by_place(top_ref, mine_refs)
        by_place(bottom_ref, rest_refs)

    @pl.when(jnp.logical_not(first))
    def _():
        by_place(top_ref, rest_refs)
        by_place(bottom_ref, mine_refs)

    def packed(i, j):
        if i == 0:
            return top_ref[:, j * BLK : (j + 1) * BLK]
        at = (j - 1) if i == 1 else 2
        return bottom_ref[:, at * BLK : (at + 1) * BLK]

    eye = (lax.broadcasted_iota(jnp.int32, (BLK, BLK), 0) == lax.broadcasted_iota(jnp.int32, (BLK, BLK), 1)).astype(F32)
    trace = sum(jnp.sum(packed(i, i) * eye) for i in range(NB))
    norm = jnp.sqrt(jnp.full((8, 128), trace, F32)) + 1e-07
    factor = (1.0 / norm)[0:1, 0:1]
    square = factor * factor

    a_rows = lambda n: [a_ref.at[k, n_x : n_x + D] for k in range(n)]
    p_rows = lambda n: [p_ref.at[k] for k in range(n)]
    b_rows = lambda n: [b_ref.at[k] for k in range(n)]

    def put_x(n, value):
        for k, piece in enumerate(pieces(value, n)):
            a_ref[k, :n_x] = piece

    for i in range(NB):
        for j in range(i, NB):
            value = packed(i, j) * square
            gram_ref[blocks(i, j)] = value
            put_both(a_rows(2), i, j, value)
    put_x(2, x_ref[...] * factor)

    def poly(n_p):
        def emit(i, j, block):
            value = NS[1] * gram_ref[blocks(i, j)] + NS[2] * block
            if i == j:
                value = value + NS[0] * eye
            put_both(p_rows(n_p), i, j, value)

        a = a_rows(2)
        symmetric_product(a, a, emit)

    def next_gram(n, keep):
        p = p_rows(n)
        rows = slice(0, n_x + BLK)
        wide = mul([a_ref[k, rows] for k in range(n)], [y[...] for y in p])
        for j in range(NB):
            put_both(b_rows(n), 0, j, wide[n_x:, j * BLK : (j + 1) * BLK])
        symmetric_product(a_rows(n), p, lambda i, j, block: put_both(b_rows(n), i, j, block), 1)
        put_x(keep, wide[:n_x])

        def emit(i, j, block):
            gram_ref[blocks(i, j)] = block
            put_both(a_rows(keep), i, j, block)

        symmetric_product(b_rows(n), p, emit)

    @pl.loop(0, SWEEPS - 1)
    def _(_):
        poly(2)
        next_gram(2, 2)

    poly(2)
    last = mul([a_ref[k, :n_x] for k in range(2)], [y[...] for y in p_rows(2)]).astype(BF)
    n = out_ref.shape[1]
    for k in range(out_ref.shape[0]):
        out_ref[k] = last[k * n : (k + 1) * n]


SMEM = pl.BlockSpec(memory_space=pltpu.SMEM)
VM = pl.BlockSpec(memory_space=pltpu.VMEM)


def gram_parts(at, rows):
    return pl.pallas_call(
        gram_kernel,
        out_shape=[jax.ShapeDtypeStruct((BLK, D), F32)] * 2,
        in_specs=[SMEM, VM],
        out_specs=[VM, VM],
        scratch_shapes=[pltpu.VMEM((BLK, D), F32)] * 2,
        compiler_params=pltpu.CompilerParams(vmem_limit_bytes=14 << 20),
        cost_estimate=pl.CostEstimate(flops=2 * 96 * D * D * 4, bytes_accessed=4 * D * D * 2, transcendentals=0),
    )(at, rows)


def sweeps(at, mine, rest, x_rows):
    return pl.pallas_call(
        sweeps_kernel,
        out_shape=jax.ShapeDtypeStruct((8, x_rows.shape[0] // 8, D), BF),
        in_specs=[SMEM] + [VM] * 9,
        out_specs=VM,
        scratch_shapes=[
            pltpu.VMEM((BLK, D), F32),
            pltpu.VMEM((BLK, D), F32),
            pltpu.VMEM((D, D), F32),
            pltpu.VMEM((3, x_rows.shape[0] + D, D), BF),
            pltpu.VMEM((3, D, D), BF),
            pltpu.VMEM((3, D, D), BF),
        ],
        compiler_params=pltpu.CompilerParams(vmem_limit_bytes=24 << 20),
        cost_estimate=pl.CostEstimate(flops=2 * D * D * D * 32, bytes_accessed=4 * D * D, transcendentals=0),
    )(at, *mine, *rest, x_rows)


def gelu_parts(u):
    k0 = math.sqrt(2.0 / math.pi)
    th = jnp.tanh(k0 * (u + 0.044715 * (u * u * u)))
    value = 0.5 * u * (1.0 + th)
    slope = 0.5 * (1.0 + th) + 0.5 * u * (1.0 - th * th) * (k0 * (1.0 + 3.0 * 0.044715 * u * u))
    return value, slope


HEADS = 3
PAD = 128
HC = HEADS * HD
HP = HEADS * PAD
NN = ((1,), (0,))
NT = ((1,), (1,))
TN = ((0,), (0,))


def iota(shape, dim):
    return lax.broadcasted_iota(jnp.int32, shape, dim)


def one_hot(cond):
    return jnp.where(cond, 1.0, 0.0).astype(BF)


def unit_place(at_ref, n):
    zi, xi, yi, ci, ti = (at_ref[k] for k in range(5))
    width = 24
    group = jnp.right_shift(n * 2731, 16)
    lane = n - width * group
    y = jnp.bitwise_and(group + yi, 1)
    inner = jnp.bitwise_and(jnp.right_shift(group, 1), 3)
    outer = jnp.bitwise_and(jnp.right_shift(group, 3), 3)
    z = jnp.bitwise_and(jnp.where(ci == 0, inner, outer) + zi, 3)
    x = jnp.bitwise_and(jnp.where(ci == 0, outer, inner) + xi, 3)
    row = 2 * ti + jnp.right_shift(z, 1)
    return row, (((jnp.bitwise_and(z, 1) * 4 + x) * 2 + y) * 2 + ci) * width + lane


def needed_blocks(at_ref):
    zi, ci = at_ref[0], at_ref[3]
    for rc in range(2):
        core_0 = jnp.bitwise_xor(ci, rc) == 0
        for x in range(4):
            for j in range(2):
                z = jnp.bitwise_and(2 * ci + j - zi, 3)
                outer, inner = jnp.where(core_0, x, z), jnp.where(core_0, z, x)
                yield rc, pl.multiple_of((outer * 4 + inner) * 48, 48)


def home_place(at_ref, r):
    xi, yi, ci = (at_ref[k] for k in range(1, 4))
    n = 6
    group = jnp.right_shift(r * 10923, 16)
    lane = r - n * group
    mat = jnp.bitwise_and(group, 3)
    y = jnp.bitwise_and(jnp.right_shift(group, 2) + yi, 1)
    j = jnp.bitwise_and(jnp.right_shift(group, 3), 1)
    x = jnp.bitwise_and(jnp.right_shift(group, 4) + xi, 3)
    core = jnp.bitwise_and(jnp.right_shift(group, 6) + ci, 1)
    return mat * HC + (((j * 4 + x) * 2 + y) * 2 + core) * n + lane


def attention_kernel(
    at_ref, own0_ref, own1_ref, own2_ref, own3_ref, got0_ref, got1_ref, got2_ref, got3_ref, normed_ref, cot_ref, cos_ref, sin_ref,
    sums_ref, keep_ref, give_ref,
    att_ref, near_ref, w_ref, wo_ref, q_ref, k_ref, v_ref, da_ref, heads_ref, d_ref, nat_ref,
):
    span = own0_ref.shape[0]
    for k, ref in enumerate((own0_ref, own1_ref, own2_ref, own3_ref, got0_ref, got1_ref, got2_ref, got3_ref)):
        att_ref[k // 4, k % 4 * span : (k % 4 + 1) * span] = ref[...]
    block = span // 4
    for k, (rc, at) in enumerate(needed_blocks(at_ref)):
        near_ref[k * block : (k + 1) * block] = att_ref[rc, pl.ds(at, block)]

    n_rows = 4 * HC
    pick = one_hot(iota((n_rows, n_rows), 0) == home_place(at_ref, iota((8, n_rows), 1))[:1])
    w_att = dot(pick, near_ref[...], NN).astype(BF)
    r = iota((HC, HC), 0)
    e = jnp.bitwise_and(r, HD - 1)
    half = ROT // 2
    source = jnp.where(e < half, r + half, jnp.where(e < ROT, r - half, -1))
    exchange = one_hot(iota((HC, HC), 1) == source)
    blank = jnp.zeros((HD, D), BF)

    def padded(ref, base, rows):
        for h in range(HEADS):
            at = base + h * PAD
            ref[at : at + HD] = rows[h * HD : (h + 1) * HD]
            ref[at + HD : at + PAD] = blank

    for m in range(3):
        padded(w_ref, m * HP, w_att[m * HC : (m + 1) * HC])
    for m in range(2):
        padded(w_ref, (3 + m) * HP, dot(exchange, w_att[m * HC : (m + 1) * HC], NN).astype(BF))
    padded(wo_ref, 0, w_att[3 * HC :])

    cos, sin = cos_ref[...], sin_ref[...]
    turn = at_ref[4] * (LEN // 2)
    at_q = jnp.bitwise_xor(iota((LEN, LEN), 0), turn)
    at_k = jnp.bitwise_xor(iota((LEN, LEN), 1), turn)
    causal = at_q >= at_k
    scale = HD ** (-0.5)

    @pl.loop(0, 2)
    def _(s):
        rows = pl.ds(pl.multiple_of(s * LEN, LEN), LEN)
        normed = normed_ref[rows]
        for m, ref in ((0, q_ref), (1, k_ref)):
            lin = dot(normed, w_ref[m * HP : (m + 1) * HP], NT)
            lin_2 = dot(normed, w_ref[(3 + m) * HP : (4 + m) * HP], NT)
            for h in range(HEADS):
                lanes = slice(h * PAD, (h + 1) * PAD)
                base = h * 2 * PAD
                own, other = lin[:, lanes], lin_2[:, lanes]
                ref[:, base : base + PAD] = (own * cos + other * sin).astype(BF)
                ref[:, base + PAD : base + 2 * PAD] = (other * cos - own * sin).astype(BF)
        v_ref[...] = dot(normed, w_ref[2 * HP : 3 * HP], NT).astype(BF)
        da_ref[...] = dot(cot_ref[rows], wo_ref[...], NT).astype(BF)
        for h in range(HEADS):
            two = slice(h * 2 * PAD, (h + 1) * 2 * PAD)
            one = slice(h * 2 * PAD, h * 2 * PAD + PAD)
            lanes = slice(h * PAD, (h + 1) * PAD)
            value, d_att = v_ref[:, lanes], da_ref[:, lanes]
            scores = jnp.where(causal, dot(q_ref[:, one], k_ref[:, one], NT) * scale, -1e30)
            raised = jnp.exp(scores - jnp.max(scores, axis=1, keepdims=True))
            probs = raised / jnp.sum(raised, axis=1, keepdims=True)
            low = probs.astype(BF)
            heads_ref[rows, lanes] = dot(low, value, NN).astype(BF)
            d_ref[rows, 2 * HP + h * PAD : 2 * HP + (h + 1) * PAD] = dot(low, d_att, TN).astype(BF)
            d_probs = dot(d_att, value, NT)
            d_scores = (probs * (d_probs - jnp.sum(probs * d_probs, axis=1, keepdims=True))).astype(BF)
            d_q = dot(d_scores, k_ref[:, two], NN) * scale
            d_k = dot(d_scores, q_ref[:, two], TN) * scale
            for m, pair in ((0, d_q), (1, d_k)):
                at = m * HP + h * PAD
                d_ref[rows, at : at + PAD] = (pair[:, :PAD] * cos - pair[:, PAD:] * sin).astype(BF)

    sums_ref[0] = dot(heads_ref[...], wo_ref[...], NN)
    sums_ref[1] = dot(d_ref[...], w_ref[: 3 * HP], NN)

    for m in range(4):
        if m < 3:
            grad = dot(d_ref[:, m * HP : (m + 1) * HP], normed_ref[...], TN).astype(BF)
        else:
            grad = dot(heads_ref[...], cot_ref[...], TN).astype(BF)
        for h in range(HEADS):
            nat_ref[m * HC + h * HD : m * HC + (h + 1) * HD] = grad[h * PAD : h * PAD + HD]
    place = home_place(at_ref, iota((n_rows, 128), 0))
    pick = jnp.concatenate([one_hot(iota((n_rows, 128), 1) + b == place) for b in range(0, n_rows, 128)], axis=1)
    near_ref[...] = dot(pick, nat_ref[...], NN).astype(BF)
    keep_ref[...] = jnp.zeros_like(keep_ref)
    give_ref[...] = jnp.zeros_like(give_ref)
    for k, (rc, at) in enumerate(needed_blocks(at_ref)):
        (keep_ref, give_ref)[rc][pl.ds(at, block)] = near_ref[k * block : (k + 1) * block]


def forward_kernel(
    at_ref, held0_ref, held1_ref, held2_ref, held3_ref, normed_ref, cot_ref, bias_ref, sums_ref,
    own_ref, peer_ref, gbias_ref, out0_ref, out1_ref, out2_ref, out3_ref,
    win_ref, wback_ref,
):
    span = held0_ref.shape[1]
    for s, ref in enumerate((held0_ref, held1_ref, held2_ref, held3_ref)):
        win_ref[s * span : (s + 1) * span] = ref[0]
        wback_ref[s * span : (s + 1) * span] = ref[1]

    def send(group, grad):
        for s, ref in enumerate((out0_ref, out1_ref, out2_ref, out3_ref)):
            ref[group] = grad[s * span : (s + 1) * span]

    hidden, slope = gelu_parts(dot(normed_ref[...], win_ref[...], NT) + bias_ref[...])
    hidden = hidden.astype(BF)


    def give_rows(k, value):
        own_ref[k] = value[:LEN]
        peer_ref[k] = value[LEN:]

    give_rows(0, sums_ref[0] + dot(hidden, wback_ref[...], NN))
    send(1, dot(hidden, cot_ref[...], TN).astype(BF))
    d_pre = (dot(cot_ref[...], wback_ref[...], NT) * slope).astype(BF)
    grad_bias = jnp.sum(d_pre.astype(F32), axis=0, keepdims=True)
    n_units = win_ref.shape[0]
    bias_row, _ = unit_place(at_ref, iota((8, n_units), 1))
    spread = pieces(jnp.where(bias_row == iota((8, n_units), 0), grad_bias, 0.0), 3)
    _, bias_lane = unit_place(at_ref, iota((n_units, 128), 0))
    to_lane = jnp.concatenate([one_hot(iota((n_units, 128), 1) + b == bias_lane) for b in range(0, D, 128)], axis=1)
    gbias_ref[...] = sum(dot(piece, to_lane, NN) for piece in reversed(spread))
    send(0, dot(d_pre, normed_ref[...], TN).astype(BF))
    give_rows(1, sums_ref[1] + dot(d_pre, win_ref[...], NN))


def out(shape, dtype):
    return jax.ShapeDtypeStruct(shape, dtype)


def low(*shape):
    return pltpu.VMEM(shape, BF)


def attention(at, own, got, normed, cot, cos, sin):
    n = normed.shape[0]
    rows = 4 * own[0].shape[0]
    return pl.pallas_call(
        attention_kernel,
        out_shape=[out((2, n, D), F32), out((rows, D), BF), out((rows, D), BF)],
        in_specs=[SMEM] + [VM] * 12,
        out_specs=[VM] * 3,
        scratch_shapes=[low(2, rows, D), low(4 * HC, D), low(5 * HP, D), low(HP, D)]
        + [low(LEN, 2 * HP), low(LEN, 2 * HP), low(LEN, HP), low(LEN, HP)]
        + [low(n, HP), low(n, 3 * HP), low(4 * HC, D)],
        compiler_params=pltpu.CompilerParams(vmem_limit_bytes=32 << 20),
        cost_estimate=pl.CostEstimate(flops=12 * 10**9, bytes_accessed=16 << 20, transcendentals=10**6),
    )(at, *own, *got, normed, cot, cos, sin)


def feed_forward(at, held, normed, cot, bias, sums):
    n = normed.shape[0]
    span = held[0].shape[1]
    units = 4 * span
    return pl.pallas_call(
        forward_kernel,
        out_shape=[out((2, n // 2, D), F32), out((2, n // 2, D), F32), out((8, D), F32)] + [out((2, span, D), BF)] * 4,
        in_specs=[SMEM] + [VM] * 8,
        out_specs=[VM] * 7,
        scratch_shapes=[low(units, D), low(units, D)],
        compiler_params=pltpu.CompilerParams(vmem_limit_bytes=22 << 20),
        cost_estimate=pl.CostEstimate(flops=10 * 10**9, bytes_accessed=16 << 20, transcendentals=10**6),
    )(at, *held, normed, cot, bias, sums)


def body(tokens, cotangent, qkv_weight, out_weight, fc_weight, vectors, qkv_momentum, out_momentum, fc_momentum, vector_first, vector_second):
    zi, xi, yi, ci, ti = (lax.axis_index(a) for a in ALL)
    rows = tokens.shape[0]
    n_att = qkv_weight.shape[3]
    n_fc = fc_weight.shape[3]
    gain, shift = vectors[:D], vectors[D : 2 * D]
    bias_in, bias_out = vectors[2 * D : 2 * D + FF], vectors[2 * D + FF :]

    first = ci == 0
    attn_rows = jnp.concatenate([jnp.transpose(qkv_weight[:, :, 0, :], (0, 2, 1)), jnp.transpose(out_weight[:, 0, :])[None]])
    fc_rows = jnp.transpose(fc_weight[:, :, 0, :], (0, 2, 1))
    own_rows = jnp.concatenate([attn_rows.reshape(1, n_fc, D), fc_rows]).astype(BF)
    held = jnp.stack(gather_ring(own_rows, pull_yh, 2), axis=1)

    inputs = tokens.astype(F32)
    average = jnp.mean(inputs, axis=-1, keepdims=True)
    deviation = inputs - average
    variance = jnp.mean(deviation * deviation, axis=-1, keepdims=True)
    inv_spread = lax.rsqrt(variance + 1e-05)
    centred = deviation * inv_spread
    normed_own = (centred * gain + shift).astype(BF)
    both = jnp.stack([normed_own, cotangent])
    held, both = lax.optimization_barrier((held, both))
    held = jnp.stack(gather_ring(held, pull_inner, 4), axis=1)
    both = jnp.stack([both, pull(both, "t", 1)], axis=1)
    held, both = lax.optimization_barrier((held, both))
    span = 8 * n_fc
    held = held.reshape(3, span, D)
    att_held = gather_ring(held[0], pull_outer, 4)
    fc_held = gather_ring(held[1:], pull_outer, 4)
    both = jnp.stack([both, pull(both, "c", 1)], axis=1)
    n_all = 4 * rows
    normed, cot = both[0].reshape(n_all, D), both[1].reshape(n_all, D)

    half = jnp.arange(LEN) // rows
    position = ((ti + half) % 2) * rows + jnp.arange(LEN) % rows
    frequency = 10000.0 ** (-2.0 * jnp.arange(ROT // 2, dtype=F32) / ROT)
    angles = position.astype(F32)[:, None] * frequency[None, :]
    cos_t, sin_t = jnp.cos(angles), jnp.sin(angles)
    pad = lambda a, b, fill: jnp.concatenate([a, b, jnp.full((LEN, PAD - ROT), fill, F32)], axis=1)
    cos_full, sin_full = pad(cos_t, cos_t, 1.0), pad(-sin_t, sin_t, 0.0)

    bias6 = bias_in.reshape(2, 4, 4, 2, 2, n_fc)
    bias6 = jnp.concatenate([bias6, bias6], axis=1)
    bias6 = jnp.concatenate([bias6, bias6], axis=2)
    bias6 = jnp.concatenate([bias6, bias6], axis=3)
    bias_own = lax.dynamic_slice(bias6, (ti, zi, xi, yi, ci, 0), (1, 4, 4, 2, 1, n_fc))[0, :, :, :, 0]
    by_turn = lambda v: jnp.where(first, jnp.swapaxes(v, 0, 1), v)
    bias_own = by_turn(bias_own).reshape(1, 32 * n_fc)
    at = jnp.stack([zi, xi, yi, ci, ti]).astype(jnp.int32)
    mom_rows = jnp.concatenate(
        [
            jnp.transpose(qkv_momentum[:, :, 0, :], (0, 2, 1)).reshape(3 * n_att, D),
            jnp.transpose(out_momentum[:, 0, :]),
            jnp.transpose(fc_momentum[:, :, 0, :], (0, 2, 1)).reshape(2 * n_fc, D),
        ]
    )
    att_held[2], normed, cot, bias_own, at, cos_full, sin_full, mom_rows = lax.optimization_barrier(
        (att_held[2], normed, cot, bias_own, at, cos_full, sin_full, mom_rows)
    )
    att_got = [pull(v, "c", 1) for v in att_held]
    sums, att_keep, att_give = attention(at, att_held, att_got, normed, cot, cos_full, sin_full)

    att_grad = (att_keep + pull(att_give, "c", 1)).reshape(4, span, D)
    att_parts = [att_grad[k] for k in range(4)]

    rows_own, rows_peer, grad_bias_in, *fc_parts = feed_forward(at, fc_held, normed, cot, bias_own, sums)
    att_total = sum_ring(att_parts, pull_outer)
    fc_total = sum_ring(fc_parts, pull_outer)
    rows_own = (rows_own + pull(rows_peer, "c", 1)).reshape(2, 2, rows, D)
    rows_own = rows_own[:, 0] + pull(rows_own[:, 1].astype(BF), "t", 1).astype(F32)
    att_total, fc_total, rows_own = lax.optimization_barrier((att_total, fc_total, rows_own))
    total = jnp.concatenate([att_total[None], fc_total]).reshape(3, 4, 2, n_fc, D)
    total = sum_ring([total[:, k] for k in range(4)], pull_inner)
    total = sum_ring([total[:, k] for k in range(2)], pull_yh).reshape(3 * n_fc, D)

    mixed = (inputs + rows_own[0] + bias_out).astype(BF)
    d_rows = rows_own[1]
    d_hat = d_rows * gain
    correction = d_hat - jnp.mean(d_hat, axis=-1, keepdims=True) - centred * jnp.mean(d_hat * centred, axis=-1, keepdims=True)
    own_cot = cotangent.astype(F32)
    input_grad = own_cot + correction * inv_spread

    total_of = lambda v: jnp.sum(v, axis=0, keepdims=True)
    vec_rows = [total_of(d_rows * centred), total_of(d_rows), grad_bias_in[: FF // D], total_of(own_cot), jnp.zeros((VEC_ROWS - VEC // D, D), F32)]

    moment = 0.95 * mom_rows + total
    update = total + 0.95 * moment

    half_fc = n_fc // 2
    att_u = update[: 4 * n_att].reshape(4, n_att, D)
    att_u = jnp.concatenate([att_u, jnp.zeros((4, half_fc - n_att, D), F32)], axis=1)
    fc_u = update[4 * n_att :].reshape(4, half_fc, D)
    vec_rows = jnp.concatenate(vec_rows)
    chunks = jnp.concatenate([att_u, fc_u])
    chunks = jnp.concatenate([chunks, jnp.broadcast_to(vec_rows, (8, VEC_ROWS, D))], axis=1)
    got = lax.all_to_all(chunks, ("z", "t"), split_axis=0, concat_axis=0, tiled=True)
    mine = got[:, :half_fc].reshape(8 * half_fc, D)
    vec_sum = jnp.sum(got[:, half_fc:], axis=0)[:8]
    keep, give = gram_parts(at, mine)
    from_core = pull(jnp.concatenate([give, vec_sum]), "c", 1)
    part = keep + from_core[:BLK]
    vec_sum = vec_sum + from_core[BLK:]
    quarter = lambda k: part[k * QUARTER : (k + 1) * QUARTER]
    along_x = lambda v, k: pull(v, "x", k)
    load = jnp.concatenate([quarter(0), vec_sum])
    for k in (1, 2, 3):
        load = load + along_x(jnp.concatenate([quarter(k), vec_sum]), 4 - k)
    load = load + pull(load, "yh", 1)
    part, vec_sum = load[:QUARTER], load[QUARTER:]
    part = jnp.where(zi >= 2, part + pull(part, "t", 1), part)
    part = gather_ring(part, along_x, 4)
    rest = [pull(v, "c", 1) for v in part]
    x_rows = sweeps(at, part, rest, mine)
    x_rows, moment = lax.optimization_barrier((x_rows, moment))
    vector_grad = vec_sum[: VEC // D].reshape(VEC)
    first_new = 0.9 * vector_first + 0.1 * vector_grad
    second_new = 0.95 * vector_second + 0.05 * vector_grad * vector_grad
    step_size = first_new / (1.0 - 0.9**STEP) / (jnp.sqrt(second_new / (1.0 - 0.95**STEP)) + 1e-08)
    vector_new = vectors - 0.2 * step_size

    back = lax.all_to_all(x_rows, ("z", "t"), split_axis=0, concat_axis=0, tiled=True).astype(F32)
    att_x = back[:4, :n_att]
    fc_x = back[4:].reshape(2, n_fc, D)

    def cols(v):
        return jnp.transpose(v, (0, 2, 1))[:, :, None, :]

    fc_factor = math.sqrt(FF / D)
    qkv_new = qkv_weight * 0.99 - cols(att_x[:3])
    out_new = out_weight * 0.99 - cols(att_x[3:])[0]
    fc_new = fc_weight * 0.99 - fc_factor * cols(fc_x)
    att_m = moment[: 4 * n_att].reshape(4, n_att, D)
    fc_m = moment[4 * n_att :].reshape(2, n_fc, D)
    return (mixed, input_grad, qkv_new, out_new, fc_new, cols(att_m[:3]), cols(att_m[3:])[0], cols(fc_m), first_new, second_new, vector_new)


def solution(mesh):
    mesh = Mesh(mesh.devices.reshape(4, 4, 2, 2, 2), ALL)
    rows = P(ALL, None)
    w3 = P(None, None, "t", DP)
    w2 = P(None, "t", DP)
    vec = P()
    in_specs = (rows, rows, w3, w2, w3, vec, w3, w2, w3, vec, vec)
    out_specs = (rows, rows, w3, w2, w3, w3, w2, w3, vec, vec, vec)
    return jax.shard_map(body, mesh=mesh, in_specs=in_specs, out_specs=out_specs, check_vma=False)
```

```python
import functools
import itertools
import math

import jax
import jax.numpy as jnp
from jax import lax
from jax.experimental import pallas as pl
from jax.experimental.pallas import tpu as pltpu
from jax.sharding import Mesh, PartitionSpec as P

D = 768
H = 12
HD = 64
ROT = 16
FF = 3072
SWEEPS = 5
STEP = 10
LEN = 256
VEC = 2 * D + FF + D
VEC_ROWS = 12

NS = (3.4445, -4.775, 2.0315)
BF = jnp.bfloat16
F32 = jnp.float32
BLK = 256
QUARTER = 64
NB = D // BLK

DP = ("zh", "zl", "xh", "xl", "yh", "c")
ALL = DP + ("t",)
SIZES = (4, 4, 2, 2, 2)


def pull(value, axis, k):
    n = lax.axis_size(axis)
    return lax.ppermute(value, axis, [((i + k) % n, i) for i in range(n)])


def move(value, source):
    sizes = SIZES
    index = lambda at: functools.reduce(lambda total, one: total * one[0] + one[1] % one[0], zip(sizes, at), 0)
    pairs = []
    for here in itertools.product(*map(range, sizes)):
        there = source(*here)
        if there is not None:
            pairs.append((index(there), index(here)))
    return lax.ppermute(value, ALL, pairs)


def pull_outer(value, k):
    return move(value, lambda z, x, y, c, t: (z, x + k, y, c, t) if c == 0 else (z + k, x, y, c, t))


def pull_inner(value, k):
    return move(value, lambda z, x, y, c, t: (z + k, x, y, c, t) if c == 0 else (z, x + k, y, c, t))


def pair_outer(value):
    return move(value, lambda z, x, y, c, t: (z, x ^ 1, y, c, t) if c == 0 else (z ^ 1, x, y, c, t))


def pair_inner(value):
    return move(value, lambda z, x, y, c, t: (z ^ 1, x, y, c, t) if c == 0 else (z, x ^ 1, y, c, t))


def pull_yh(value, k):
    return pull(value, "yh", k)


def gather_ring(value, pulls, n):
    return [value] + [pulls(value, k) for k in range(1, n)]


def sum_ring(parts, pulls):
    n = len(parts)
    total = parts[0].astype(F32)
    for k in range(1, n):
        total = total + pulls(parts[k].astype(BF), n - k).astype(F32)
    return total


def dot(a, b, dims):
    return lax.dot_general(a, b, (dims, ((), ())), preferred_element_type=F32)


def pieces(value, n):
    out = []
    for _ in range(n):
        low = value.astype(BF)
        out.append(low)
        value = value - low.astype(F32)
    return out


def mul(xs, ys, dims=((1,), (0,))):
    n = len(xs)
    total = None
    for order in reversed(range(n)):
        for i in range(order + 1):
            term = lax.dot_general(xs[i], ys[order - i], (dims, ((), ())), preferred_element_type=F32)
            total = term if total is None else total + term
    return total


def quarters(at_ref, core):
    for outer in range(2):
        for inner in range(2):
            dx, dz = (outer, inner) if core == 0 else (inner, outer)
            x = jnp.bitwise_and(at_ref[1] + dx, 1)
            z = jnp.bitwise_and(at_ref[0] + dz, 1)
            yield pl.ds(pl.multiple_of((2 * x + z) * QUARTER, QUARTER), QUARTER)


def gram_kernel(at_ref, rows_ref, keep_ref, give_ref, top_ref, bottom_ref):
    xs = pieces(rows_ref[...], 3)
    dims = ((0,), (0,))
    cut = lambda i: slice(i * BLK, (i + 1) * BLK)
    top_ref[...] = mul([x[:, cut(0)] for x in xs], xs, dims)
    bottom_ref[:, : 2 * BLK] = mul([x[:, cut(1)] for x in xs], [x[:, BLK:] for x in xs], dims)
    bottom_ref[:, 2 * BLK :] = mul([x[:, cut(2)] for x in xs], [x[:, 2 * BLK :] for x in xs], dims)

    def by_place(out_ref, in_ref, core):
        for k, rows in enumerate(quarters(at_ref, core)):
            out_ref[k * QUARTER : (k + 1) * QUARTER] = in_ref[rows]

    first = at_ref[3] == 0

    @pl.when(first)
    def _():
        by_place(keep_ref, top_ref, 0)
        by_place(give_ref, bottom_ref, 1)

    @pl.when(jnp.logical_not(first))
    def _():
        by_place(keep_ref, bottom_ref, 1)
        by_place(give_ref, top_ref, 0)


def blocks(i, j):
    return (slice(i * BLK, (i + 1) * BLK), slice(j * BLK, (j + 1) * BLK))


def put(refs, i, j, value):
    for ref, piece in zip(refs, pieces(value, len(refs))):
        ref[blocks(i, j)] = piece


def put_both(refs, i, j, value):
    put(refs, i, j, value)
    if i != j:
        put(refs, j, i, value.T)


def symmetric_product(xs, ys, emit, start=0):
    for i in range(start, NB):
        rows = slice(i * BLK, (i + 1) * BLK)
        wide = mul([x[rows, :] for x in xs], [y[:, i * BLK :] for y in ys])
        for j in range(i, NB):
            emit(i, j, wide[:, (j - i) * BLK : (j - i + 1) * BLK])


def sweeps_kernel(at_ref, *refs):
    sweeps_math(at_ref, refs[:3], refs[3:6], *refs[6:])


def sweeps_math(at_ref, mine_refs, rest_refs, x_ref, out_ref, top_ref, bottom_ref, gram_ref, a_ref, p_ref, b_ref):
    first = at_ref[3] == 0
    n_x = x_ref.shape[0]

    def by_place(out_ref, in_refs, core):
        near, side, far = in_refs
        pieces_of = (near[...], side[...], far[:QUARTER], far[QUARTER:])
        for rows, value in zip(quarters(at_ref, core), pieces_of):
            out_ref[rows] = value

    @pl.when(first)
    def _():
        by_place(top_ref, mine_refs, 0)
        by_place(bottom_ref, rest_refs, 1)

    @pl.when(jnp.logical_not(first))
    def _():
        by_place(top_ref, rest_refs, 0)
        by_place(bottom_ref, mine_refs, 1)

    def packed(i, j):
        if i == 0:
            return top_ref[:, j * BLK : (j + 1) * BLK]
        at = (j - 1) if i == 1 else 2
        return bottom_ref[:, at * BLK : (at + 1) * BLK]

    eye = (lax.broadcasted_iota(jnp.int32, (BLK, BLK), 0) == lax.broadcasted_iota(jnp.int32, (BLK, BLK), 1)).astype(F32)
    trace = sum(jnp.sum(packed(i, i) * eye) for i in range(NB))
    norm = jnp.sqrt(jnp.full((8, 128), trace, F32)) + 1e-07
    factor = (1.0 / norm)[0:1, 0:1]
    square = factor * factor

    a_rows = lambda n: [a_ref.at[k, n_x : n_x + D] for k in range(n)]
    p_rows = lambda n: [p_ref.at[k] for k in range(n)]
    b_rows = lambda n: [b_ref.at[k] for k in range(n)]

    def put_x(n, value):
        for k, piece in enumerate(pieces(value, n)):
            a_ref[k, :n_x] = piece

    for i in range(NB):
        for j in range(i, NB):
            value = packed(i, j) * square
            gram_ref[blocks(i, j)] = value
            put_both(a_rows(2), i, j, value)
    put_x(2, x_ref[...] * factor)

    def poly(n_p):
        def emit(i, j, block):
            value = NS[1] * gram_ref[blocks(i, j)] + NS[2] * block
            if i == j:
                value = value + NS[0] * eye
            put_both(p_rows(n_p), i, j, value)

        a = a_rows(2)
        symmetric_product(a, a, emit)

    def next_gram(n, keep):
        p = p_rows(n)
        rows = slice(0, n_x + BLK)
        wide = mul([a_ref[k, rows] for k in range(n)], [y[...] for y in p])
        for j in range(NB):
            put_both(b_rows(n), 0, j, wide[n_x:, j * BLK : (j + 1) * BLK])
        symmetric_product(a_rows(n), p, lambda i, j, block: put_both(b_rows(n), i, j, block), 1)
        put_x(keep, wide[:n_x])

        def emit(i, j, block):
            gram_ref[blocks(i, j)] = block
            put_both(a_rows(keep), i, j, block)

        symmetric_product(b_rows(n), p, emit)

    @pl.loop(0, SWEEPS - 1)
    def _(_):
        poly(2)
        next_gram(2, 2)

    poly(2)
    last = mul([a_ref[k, :n_x] for k in range(2)], [y[...] for y in p_rows(2)]).astype(BF)
    n = out_ref.shape[1]
    for k in range(out_ref.shape[0]):
        out_ref[k] = last[k * n : (k + 1) * n]


SMEM = pl.BlockSpec(memory_space=pltpu.SMEM)
VM = pl.BlockSpec(memory_space=pltpu.VMEM)


def gram_parts(at, rows):
    return pl.pallas_call(
        gram_kernel,
        out_shape=[jax.ShapeDtypeStruct((BLK, D), F32)] * 2,
        in_specs=[SMEM, VM],
        out_specs=[VM, VM],
        scratch_shapes=[pltpu.VMEM((BLK, D), F32)] * 2,
        compiler_params=pltpu.CompilerParams(vmem_limit_bytes=14 << 20),
        cost_estimate=pl.CostEstimate(flops=2 * 96 * D * D * 4, bytes_accessed=4 * D * D * 2, transcendentals=0),
    )(at, rows)


def sweeps(at, mine, rest, x_rows):
    return pl.pallas_call(
        sweeps_kernel,
        out_shape=jax.ShapeDtypeStruct((8, x_rows.shape[0] // 8, D), BF),
        in_specs=[SMEM] + [VM] * 7,
        out_specs=VM,
        scratch_shapes=[
            pltpu.VMEM((BLK, D), F32),
            pltpu.VMEM((BLK, D), F32),
            pltpu.VMEM((D, D), F32),
            pltpu.VMEM((3, x_rows.shape[0] + D, D), BF),
            pltpu.VMEM((3, D, D), BF),
            pltpu.VMEM((3, D, D), BF),
        ],
        compiler_params=pltpu.CompilerParams(vmem_limit_bytes=24 << 20),
        cost_estimate=pl.CostEstimate(flops=2 * D * D * D * 32, bytes_accessed=4 * D * D, transcendentals=0),
    )(at, *mine, *rest, x_rows)


def gelu_parts(u):
    k0 = math.sqrt(2.0 / math.pi)
    th = jnp.tanh(k0 * (u + 0.044715 * (u * u * u)))
    value = 0.5 * u * (1.0 + th)
    slope = 0.5 * (1.0 + th) + 0.5 * u * (1.0 - th * th) * (k0 * (1.0 + 3.0 * 0.044715 * u * u))
    return value, slope


HEADS = 3
PAD = 128
HC = HEADS * HD
HP = HEADS * PAD
NN = ((1,), (0,))
NT = ((1,), (1,))
TN = ((0,), (0,))


def iota(shape, dim):
    return lax.broadcasted_iota(jnp.int32, shape, dim)


def one_hot(cond):
    return jnp.where(cond, 1.0, 0.0).astype(BF)


def unit_place(at_ref, n):
    zi, xi, yi, ci, ti = (at_ref[k] for k in range(5))
    width = 24
    group = jnp.right_shift(n * 2731, 16)
    lane = n - width * group
    y = jnp.bitwise_and(group + yi, 1)
    inner = jnp.bitwise_and(jnp.right_shift(group, 1), 3)
    outer = jnp.bitwise_and(jnp.right_shift(group, 3), 3)
    z = jnp.bitwise_and(jnp.where(ci == 0, inner, outer) + zi, 3)
    x = jnp.bitwise_and(jnp.where(ci == 0, outer, inner) + xi, 3)
    row = 2 * ti + jnp.right_shift(z, 1)
    return row, (((jnp.bitwise_and(z, 1) * 4 + x) * 2 + y) * 2 + ci) * width + lane


def needed_blocks(at_ref):
    zi, ci = at_ref[0], at_ref[3]
    for rc in range(2):
        core_0 = jnp.bitwise_xor(ci, rc) == 0
        for x in range(4):
            for j in range(2):
                z = jnp.bitwise_and(2 * ci + j - zi, 3)
                outer, inner = jnp.where(core_0, x, z), jnp.where(core_0, z, x)
                yield rc, pl.multiple_of((outer * 4 + inner) * 48, 48)


def home_place(at_ref, r):
    xi, yi, ci = (at_ref[k] for k in range(1, 4))
    n = 6
    group = jnp.right_shift(r * 10923, 16)
    lane = r - n * group
    mat = jnp.bitwise_and(group, 3)
    y = jnp.bitwise_and(jnp.right_shift(group, 2) + yi, 1)
    j = jnp.bitwise_and(jnp.right_shift(group, 3), 1)
    x = jnp.bitwise_and(jnp.right_shift(group, 4) + xi, 3)
    core = jnp.bitwise_and(jnp.right_shift(group, 6) + ci, 1)
    return mat * HC + (((j * 4 + x) * 2 + y) * 2 + core) * n + lane


def attention_kernel(
    at_ref, own0_ref, own1_ref, own2_ref, own3_ref, got0_ref, got1_ref, got2_ref, got3_ref, normed_ref, cot_ref, cos_ref, sin_ref,
    sums_ref, keep_ref, give_ref,
    att_ref, near_ref, w_ref, wo_ref, q_ref, k_ref, v_ref, da_ref, heads_ref, d_ref, nat_ref,
):
    span = own0_ref.shape[0]
    for k, ref in enumerate((own0_ref, own1_ref, own2_ref, own3_ref, got0_ref, got1_ref, got2_ref, got3_ref)):
        att_ref[k // 4, k % 4 * span : (k % 4 + 1) * span] = ref[...]
    block = span // 4
    for k, (rc, at) in enumerate(needed_blocks(at_ref)):
        near_ref[k * block : (k + 1) * block] = att_ref[rc, pl.ds(at, block)]

    n_rows = 4 * HC
    pick = one_hot(iota((n_rows, n_rows), 0) == home_place(at_ref, iota((8, n_rows), 1))[:1])
    w_att = dot(pick, near_ref[...], NN).astype(BF)
    r = iota((HC, HC), 0)
    e = jnp.bitwise_and(r, HD - 1)
    half = ROT // 2
    source = jnp.where(e < half, r + half, jnp.where(e < ROT, r - half, -1))
    exchange = one_hot(iota((HC, HC), 1) == source)
    blank = jnp.zeros((HD, D), BF)

    def padded(ref, base, rows):
        for h in range(HEADS):
            at = base + h * PAD
            ref[at : at + HD] = rows[h * HD : (h + 1) * HD]
            ref[at + HD : at + PAD] = blank

    for m in range(3):
        padded(w_ref, m * HP, w_att[m * HC : (m + 1) * HC])
    for m in range(2):
        padded(w_ref, (3 + m) * HP, dot(exchange, w_att[m * HC : (m + 1) * HC], NN).astype(BF))
    padded(wo_ref, 0, w_att[3 * HC :])

    cos, sin = cos_ref[...], sin_ref[...]
    turn = at_ref[4] * (LEN // 2)
    at_q = jnp.bitwise_xor(iota((LEN, LEN), 0), turn)
    at_k = jnp.bitwise_xor(iota((LEN, LEN), 1), turn)
    causal = at_q >= at_k
    scale = HD ** (-0.5)

    @pl.loop(0, 2)
    def _(s):
        rows = pl.ds(pl.multiple_of(s * LEN, LEN), LEN)
        normed = normed_ref[rows]
        for m, ref in ((0, q_ref), (1, k_ref)):
            lin = dot(normed, w_ref[m * HP : (m + 1) * HP], NT)
            lin_2 = dot(normed, w_ref[(3 + m) * HP : (4 + m) * HP], NT)
            for h in range(HEADS):
                lanes = slice(h * PAD, (h + 1) * PAD)
                base = h * 2 * PAD
                own, other = lin[:, lanes], lin_2[:, lanes]
                ref[:, base : base + PAD] = (own * cos + other * sin).astype(BF)
                ref[:, base + PAD : base + 2 * PAD] = (other * cos - own * sin).astype(BF)
        v_ref[...] = dot(normed, w_ref[2 * HP : 3 * HP], NT).astype(BF)
        da_ref[...] = dot(cot_ref[rows], wo_ref[...], NT).astype(BF)
        for h in range(HEADS):
            two = slice(h * 2 * PAD, (h + 1) * 2 * PAD)
            one = slice(h * 2 * PAD, h * 2 * PAD + PAD)
            lanes = slice(h * PAD, (h + 1) * PAD)
            value, d_att = v_ref[:, lanes], da_ref[:, lanes]
            scores = jnp.where(causal, dot(q_ref[:, one], k_ref[:, one], NT) * scale, -1e30)
            raised = jnp.exp(scores - jnp.max(scores, axis=1, keepdims=True))
            probs = raised / jnp.sum(raised, axis=1, keepdims=True)
            low = probs.astype(BF)
            heads_ref[rows, lanes] = dot(low, value, NN).astype(BF)
            d_ref[rows, 2 * HP + h * PAD : 2 * HP + (h + 1) * PAD] = dot(low, d_att, TN).astype(BF)
            d_probs = dot(d_att, value, NT)
            d_scores = (probs * (d_probs - jnp.sum(probs * d_probs, axis=1, keepdims=True))).astype(BF)
            d_q = dot(d_scores, k_ref[:, two], NN) * scale
            d_k = dot(d_scores, q_ref[:, two], TN) * scale
            for m, pair in ((0, d_q), (1, d_k)):
                at = m * HP + h * PAD
                d_ref[rows, at : at + PAD] = (pair[:, :PAD] * cos - pair[:, PAD:] * sin).astype(BF)

    sums_ref[0] = dot(heads_ref[...], wo_ref[...], NN)
    sums_ref[1] = dot(d_ref[...], w_ref[: 3 * HP], NN)

    for m in range(4):
        if m < 3:
            grad = dot(d_ref[:, m * HP : (m + 1) * HP], normed_ref[...], TN).astype(BF)
        else:
            grad = dot(heads_ref[...], cot_ref[...], TN).astype(BF)
        for h in range(HEADS):
            nat_ref[m * HC + h * HD : m * HC + (h + 1) * HD] = grad[h * PAD : h * PAD + HD]
    place = home_place(at_ref, iota((n_rows, 128), 0))
    pick = jnp.concatenate([one_hot(iota((n_rows, 128), 1) + b == place) for b in range(0, n_rows, 128)], axis=1)
    near_ref[...] = dot(pick, nat_ref[...], NN).astype(BF)
    keep_ref[...] = jnp.zeros_like(keep_ref)
    give_ref[...] = jnp.zeros_like(give_ref)
    for k, (rc, at) in enumerate(needed_blocks(at_ref)):
        (keep_ref, give_ref)[rc][pl.ds(at, block)] = near_ref[k * block : (k + 1) * block]


def forward_kernel(
    at_ref, held0_ref, held1_ref, held2_ref, held3_ref, normed_ref, cot_ref, bias_ref, sums_ref,
    own_ref, peer_ref, gbias_ref, out0_ref, out1_ref, out2_ref, out3_ref,
    win_ref, wback_ref,
):
    span = held0_ref.shape[1]
    for s, ref in enumerate((held0_ref, held1_ref, held2_ref, held3_ref)):
        win_ref[s * span : (s + 1) * span] = ref[0]
        wback_ref[s * span : (s + 1) * span] = ref[1]

    def send(group, grad):
        for s, ref in enumerate((out0_ref, out1_ref, out2_ref, out3_ref)):
            ref[group] = grad[s * span : (s + 1) * span]

    hidden, slope = gelu_parts(dot(normed_ref[...], win_ref[...], NT) + bias_ref[...])
    hidden = hidden.astype(BF)


    def give_rows(k, value):
        own_ref[k] = value[:LEN]
        peer_ref[k] = value[LEN:]

    give_rows(0, sums_ref[0] + dot(hidden, wback_ref[...], NN))
    send(1, dot(hidden, cot_ref[...], TN).astype(BF))
    d_pre = (dot(cot_ref[...], wback_ref[...], NT) * slope).astype(BF)
    grad_bias = jnp.sum(d_pre.astype(F32), axis=0, keepdims=True)
    n_units = win_ref.shape[0]
    bias_row, _ = unit_place(at_ref, iota((8, n_units), 1))
    spread = pieces(jnp.where(bias_row == iota((8, n_units), 0), grad_bias, 0.0), 3)
    _, bias_lane = unit_place(at_ref, iota((n_units, 128), 0))
    to_lane = jnp.concatenate([one_hot(iota((n_units, 128), 1) + b == bias_lane) for b in range(0, D, 128)], axis=1)
    gbias_ref[...] = sum(dot(piece, to_lane, NN) for piece in reversed(spread))
    send(0, dot(d_pre, normed_ref[...], TN).astype(BF))
    give_rows(1, sums_ref[1] + dot(d_pre, win_ref[...], NN))


def out(shape, dtype):
    return jax.ShapeDtypeStruct(shape, dtype)


def low(*shape):
    return pltpu.VMEM(shape, BF)


def attention(at, own, got, normed, cot, cos, sin):
    n = normed.shape[0]
    rows = 4 * own[0].shape[0]
    return pl.pallas_call(
        attention_kernel,
        out_shape=[out((2, n, D), F32), out((rows, D), BF), out((rows, D), BF)],
        in_specs=[SMEM] + [VM] * 12,
        out_specs=[VM] * 3,
        scratch_shapes=[low(2, rows, D), low(4 * HC, D), low(5 * HP, D), low(HP, D)]
        + [low(LEN, 2 * HP), low(LEN, 2 * HP), low(LEN, HP), low(LEN, HP)]
        + [low(n, HP), low(n, 3 * HP), low(4 * HC, D)],
        compiler_params=pltpu.CompilerParams(vmem_limit_bytes=32 << 20),
        cost_estimate=pl.CostEstimate(flops=12 * 10**9, bytes_accessed=16 << 20, transcendentals=10**6),
    )(at, *own, *got, normed, cot, cos, sin)


def feed_forward(at, held, normed, cot, bias, sums):
    n = normed.shape[0]
    span = held[0].shape[1]
    units = 4 * span
    return pl.pallas_call(
        forward_kernel,
        out_shape=[out((2, n // 2, D), F32), out((2, n // 2, D), F32), out((8, D), F32)] + [out((2, span, D), BF)] * 4,
        in_specs=[SMEM] + [VM] * 8,
        out_specs=[VM] * 7,
        scratch_shapes=[low(units, D), low(units, D)],
        compiler_params=pltpu.CompilerParams(vmem_limit_bytes=22 << 20),
        cost_estimate=pl.CostEstimate(flops=10 * 10**9, bytes_accessed=16 << 20, transcendentals=10**6),
    )(at, *held, normed, cot, bias, sums)


def body(tokens, cotangent, qkv_weight, out_weight, fc_weight, vectors, qkv_momentum, out_momentum, fc_momentum, vector_first, vector_second):
    zh, zl, xh, xl, yi, ci, ti = (lax.axis_index(a) for a in ALL)
    zi, xi = 2 * zh + zl, 2 * xh + xl
    rows = tokens.shape[0]
    n_att = qkv_weight.shape[3]
    n_fc = fc_weight.shape[3]
    gain, shift = vectors[:D], vectors[D : 2 * D]
    bias_in, bias_out = vectors[2 * D : 2 * D + FF], vectors[2 * D + FF :]

    first = ci == 0
    attn_rows = jnp.concatenate([jnp.transpose(qkv_weight[:, :, 0, :], (0, 2, 1)), jnp.transpose(out_weight[:, 0, :])[None]])
    fc_rows = jnp.transpose(fc_weight[:, :, 0, :], (0, 2, 1))
    own_rows = jnp.concatenate([attn_rows.reshape(1, n_fc, D), fc_rows]).astype(BF)
    held = jnp.stack(gather_ring(own_rows, pull_yh, 2), axis=1)

    inputs = tokens.astype(F32)
    average = jnp.mean(inputs, axis=-1, keepdims=True)
    deviation = inputs - average
    variance = jnp.mean(deviation * deviation, axis=-1, keepdims=True)
    inv_spread = lax.rsqrt(variance + 1e-05)
    centred = deviation * inv_spread
    normed_own = (centred * gain + shift).astype(BF)
    both = jnp.stack([normed_own, cotangent])
    held, both = lax.optimization_barrier((held, both))
    held = jnp.stack(gather_ring(held, pull_inner, 4), axis=1)
    both = jnp.stack([both, pull(both, "t", 1)], axis=1)
    held, both = lax.optimization_barrier((held, both))
    span = 8 * n_fc
    held = held.reshape(3, span, D)
    att_held = gather_ring(held[0], pull_outer, 4)
    fc_held = gather_ring(held[1:], pull_outer, 4)
    both = jnp.stack([both, pull(both, "c", 1)], axis=1)
    n_all = 4 * rows
    normed, cot = both[0].reshape(n_all, D), both[1].reshape(n_all, D)

    half = jnp.arange(LEN) // rows
    position = ((ti + half) % 2) * rows + jnp.arange(LEN) % rows
    frequency = 10000.0 ** (-2.0 * jnp.arange(ROT // 2, dtype=F32) / ROT)
    angles = position.astype(F32)[:, None] * frequency[None, :]
    cos_t, sin_t = jnp.cos(angles), jnp.sin(angles)
    pad = lambda a, b, fill: jnp.concatenate([a, b, jnp.full((LEN, PAD - ROT), fill, F32)], axis=1)
    cos_full, sin_full = pad(cos_t, cos_t, 1.0), pad(-sin_t, sin_t, 0.0)

    bias6 = bias_in.reshape(2, 4, 4, 2, 2, n_fc)
    bias6 = jnp.concatenate([bias6, bias6], axis=1)
    bias6 = jnp.concatenate([bias6, bias6], axis=2)
    bias6 = jnp.concatenate([bias6, bias6], axis=3)
    bias_own = lax.dynamic_slice(bias6, (ti, zi, xi, yi, ci, 0), (1, 4, 4, 2, 1, n_fc))[0, :, :, :, 0]
    by_turn = lambda v: jnp.where(first, jnp.swapaxes(v, 0, 1), v)
    bias_own = by_turn(bias_own).reshape(1, 32 * n_fc)
    at = jnp.stack([zi, xi, yi, ci, ti]).astype(jnp.int32)
    mom_rows = jnp.concatenate(
        [
            jnp.transpose(qkv_momentum[:, :, 0, :], (0, 2, 1)).reshape(3 * n_att, D),
            jnp.transpose(out_momentum[:, 0, :]),
            jnp.transpose(fc_momentum[:, :, 0, :], (0, 2, 1)).reshape(2 * n_fc, D),
        ]
    )
    att_held[2], normed, cot, bias_own, at, cos_full, sin_full, mom_rows = lax.optimization_barrier(
        (att_held[2], normed, cot, bias_own, at, cos_full, sin_full, mom_rows)
    )
    att_got = [pull(v, "c", 1) for v in att_held]
    sums, att_keep, att_give = attention(at, att_held, att_got, normed, cot, cos_full, sin_full)

    att_grad = (att_keep + pull(att_give, "c", 1)).reshape(4, span, D)
    att_parts = [att_grad[k] for k in range(4)]

    rows_own, rows_peer, grad_bias_in, *fc_parts = feed_forward(at, fc_held, normed, cot, bias_own, sums)
    att_parts, rows_peer = lax.optimization_barrier((att_parts, rows_peer))
    rows_own = (rows_own + pull(rows_peer, "c", 1)).reshape(2, 2, rows, D)
    att_total = sum_ring(att_parts, pull_outer)
    fc_total = sum_ring(fc_parts, pull_outer)
    rows_own = rows_own[:, 0] + pull(rows_own[:, 1].astype(BF), "t", 1).astype(F32)
    att_total, fc_total, rows_own = lax.optimization_barrier((att_total, fc_total, rows_own))
    total = jnp.concatenate([att_total[None], fc_total]).reshape(3, 4, 2, n_fc, D)
    total = sum_ring([total[:, k] for k in range(4)], pull_inner)
    total = sum_ring([total[:, k] for k in range(2)], pull_yh).reshape(3 * n_fc, D)

    mixed = (inputs + rows_own[0] + bias_out).astype(BF)
    d_rows = rows_own[1]
    d_hat = d_rows * gain
    correction = d_hat - jnp.mean(d_hat, axis=-1, keepdims=True) - centred * jnp.mean(d_hat * centred, axis=-1, keepdims=True)
    own_cot = cotangent.astype(F32)
    input_grad = own_cot + correction * inv_spread

    total_of = lambda v: jnp.sum(v, axis=0, keepdims=True)
    vec_rows = [total_of(d_rows * centred), total_of(d_rows), grad_bias_in[: FF // D], total_of(own_cot), jnp.zeros((VEC_ROWS - VEC // D, D), F32)]

    moment = 0.95 * mom_rows + total
    update = total + 0.95 * moment

    half_fc = n_fc // 2
    att_u = update[: 4 * n_att].reshape(4, n_att, D)
    att_u = jnp.concatenate([att_u, jnp.zeros((4, half_fc - n_att, D), F32)], axis=1)
    fc_u = update[4 * n_att :].reshape(4, half_fc, D)
    vec_rows = jnp.concatenate(vec_rows)
    chunks = jnp.concatenate([att_u, fc_u])
    chunks = jnp.concatenate([chunks, jnp.broadcast_to(vec_rows, (8, VEC_ROWS, D))], axis=1)
    got = lax.all_to_all(chunks, ("zh", "xh", "t"), split_axis=0, concat_axis=0, tiled=True)
    mine = got[:, :half_fc].reshape(8 * half_fc, D)
    vec_sum = jnp.sum(got[:, half_fc:], axis=0)[:8]
    keep, give = gram_parts(at, mine)
    from_core = pull(jnp.concatenate([give, vec_sum]), "c", 1)
    part = keep + from_core[:BLK]
    vec_sum = vec_sum + from_core[BLK:]
    half = BLK // 2
    load = jnp.concatenate([part[:half], vec_sum]) + pair_outer(jnp.concatenate([part[half:], vec_sum]))
    vec_sum = load[half:]
    load = jnp.concatenate([load[:QUARTER], vec_sum]) + pair_inner(jnp.concatenate([load[QUARTER:half], vec_sum]))
    load = load + pull_yh(load, 1)
    part, vec_sum = load[:QUARTER], load[QUARTER:]
    part = jnp.where(zh == 1, part + pull(part, "t", 1), part)
    part = [part, pair_inner(part)]
    part.append(pair_outer(jnp.concatenate(part)))
    rest = [pull(v, "c", 1) for v in part]
    x_rows = sweeps(at, part, rest, mine)
    x_rows, moment = lax.optimization_barrier((x_rows, moment))
    vector_grad = vec_sum[: VEC // D].reshape(VEC)
    first_new = 0.9 * vector_first + 0.1 * vector_grad
    second_new = 0.95 * vector_second + 0.05 * vector_grad * vector_grad
    step_size = first_new / (1.0 - 0.9**STEP) / (jnp.sqrt(second_new / (1.0 - 0.95**STEP)) + 1e-08)
    vector_new = vectors - 0.2 * step_size

    back = lax.all_to_all(x_rows, ("zh", "xh", "t"), split_axis=0, concat_axis=0, tiled=True).astype(F32)
    att_x = back[:4, :n_att]
    fc_x = back[4:].reshape(2, n_fc, D)

    def cols(v):
        return jnp.transpose(v, (0, 2, 1))[:, :, None, :]

    fc_factor = math.sqrt(FF / D)
    qkv_new = qkv_weight * 0.99 - cols(att_x[:3])
    out_new = out_weight * 0.99 - cols(att_x[3:])[0]
    fc_new = fc_weight * 0.99 - fc_factor * cols(fc_x)
    att_m = moment[: 4 * n_att].reshape(4, n_att, D)
    fc_m = moment[4 * n_att :].reshape(2, n_fc, D)
    return (mixed, input_grad, qkv_new, out_new, fc_new, cols(att_m[:3]), cols(att_m[3:])[0], cols(fc_m), first_new, second_new, vector_new)


def solution(mesh):
    mesh = Mesh(mesh.devices.reshape((2,) * 7), ALL)
    rows = P(ALL, None)
    w3 = P(None, None, "t", DP)
    w2 = P(None, "t", DP)
    vec = P()
    in_specs = (rows, rows, w3, w2, w3, vec, w3, w2, w3, vec, vec)
    out_specs = (rows, rows, w3, w2, w3, w3, w2, w3, vec, vec, vec)
    return jax.shard_map(body, mesh=mesh, in_specs=in_specs, out_specs=out_specs, check_vma=False)
```

```python
import functools
import itertools
import math

import jax
import jax.numpy as jnp
from jax import lax
from jax.experimental import pallas as pl
from jax.experimental.pallas import tpu as pltpu
from jax.sharding import Mesh, PartitionSpec as P

D = 768
H = 12
HD = 64
ROT = 16
FF = 3072
SWEEPS = 5
STEP = 10
LEN = 256
VEC = 2 * D + FF + D
VEC_ROWS = 12

NS = (3.4445, -4.775, 2.0315)
BF = jnp.bfloat16
F32 = jnp.float32
BLK = 256
QUARTER = 64
NB = D // BLK

DP = ("z", "x", "yh", "c")
ALL = ("z", "x", "yh", "c", "t")


def pull(value, axis, k):
    n = lax.axis_size(axis)
    return lax.ppermute(value, axis, [((i + k) % n, i) for i in range(n)])


def move(value, source):
    sizes = [lax.axis_size(a) for a in ALL]
    index = lambda at: functools.reduce(lambda total, one: total * one[0] + one[1] % one[0], zip(sizes, at), 0)
    pairs = []
    for here in itertools.product(*map(range, sizes)):
        there = source(*here)
        if there is not None:
            pairs.append((index(there), index(here)))
    return lax.ppermute(value, ALL, pairs)


def pull_outer(value, k):
    return move(value, lambda z, x, y, c, t: (z, x + k, y, c, t) if c == 0 else (z + k, x, y, c, t))


def pull_inner(value, k):
    return move(value, lambda z, x, y, c, t: (z + k, x, y, c, t) if c == 0 else (z, x + k, y, c, t))


def pull_yh(value, k):
    return pull(value, "yh", k)


def gather_ring(value, pulls, n):
    return [value] + [pulls(value, k) for k in range(1, n)]


def sum_ring(parts, pulls):
    n = len(parts)
    total = parts[0].astype(F32)
    for k in range(1, n):
        total = total + pulls(parts[k].astype(BF), n - k).astype(F32)
    return total


def dot(a, b, dims):
    return lax.dot_general(a, b, (dims, ((), ())), preferred_element_type=F32)


def pieces(value, n):
    out = []
    for _ in range(n):
        low = value.astype(BF)
        out.append(low)
        value = value - low.astype(F32)
    return out


def mul(xs, ys, dims=((1,), (0,))):
    n = len(xs)
    total = None
    for order in reversed(range(n)):
        for i in range(order + 1):
            term = lax.dot_general(xs[i], ys[order - i], (dims, ((), ())), preferred_element_type=F32)
            total = term if total is None else total + term
    return total


def gram_kernel(at_ref, rows_ref, keep_ref, give_ref, top_ref, bottom_ref):
    xs = pieces(rows_ref[...], 3)
    dims = ((0,), (0,))
    cut = lambda i: slice(i * BLK, (i + 1) * BLK)
    top_ref[...] = mul([x[:, cut(0)] for x in xs], xs, dims)
    bottom_ref[:, : 2 * BLK] = mul([x[:, cut(1)] for x in xs], [x[:, BLK:] for x in xs], dims)
    bottom_ref[:, 2 * BLK :] = mul([x[:, cut(2)] for x in xs], [x[:, 2 * BLK :] for x in xs], dims)

    def by_place(out_ref, in_ref):
        for k in range(4):
            place = pl.multiple_of(jnp.bitwise_and(at_ref[1] + k, 3) * QUARTER, QUARTER)
            out_ref[k * QUARTER : (k + 1) * QUARTER] = in_ref[pl.ds(place, QUARTER)]

    first = at_ref[3] == 0

    @pl.when(first)
    def _():
        by_place(keep_ref, top_ref)
        by_place(give_ref, bottom_ref)

    @pl.when(jnp.logical_not(first))
    def _():
        by_place(keep_ref, bottom_ref)
        by_place(give_ref, top_ref)


def blocks(i, j):
    return (slice(i * BLK, (i + 1) * BLK), slice(j * BLK, (j + 1) * BLK))


def put(refs, i, j, value):
    for ref, piece in zip(refs, pieces(value, len(refs))):
        ref[blocks(i, j)] = piece


def put_both(refs, i, j, value):
    put(refs, i, j, value)
    if i != j:
        put(refs, j, i, value.T)


def symmetric_product(xs, ys, emit, start=0):
    for i in range(start, NB):
        rows = slice(i * BLK, (i + 1) * BLK)
        wide = mul([x[rows, :] for x in xs], [y[:, i * BLK :] for y in ys])
        for j in range(i, NB):
            emit(i, j, wide[:, (j - i) * BLK : (j - i + 1) * BLK])


def sweeps_kernel(at_ref, *refs):
    sweeps_math(at_ref, refs[:4], refs[4:8], *refs[8:])


def sweeps_math(at_ref, mine_refs, rest_refs, x_ref, out_ref, top_ref, bottom_ref, gram_ref, a_ref, p_ref, b_ref):
    first = at_ref[3] == 0
    n_x = x_ref.shape[0]

    def by_place(out_ref, in_refs):
        for k, ref in enumerate(in_refs):
            place = pl.multiple_of(jnp.bitwise_and(at_ref[1] + k, 3) * QUARTER, QUARTER)
            out_ref[pl.ds(place, QUARTER)] = ref[...]

    @pl.when(first)
    def _():
        by_place(top_ref, mine_refs)
        by_place(bottom_ref, rest_refs)

    @pl.when(jnp.logical_not(first))
    def _():
        by_place(top_ref, rest_refs)
        by_place(bottom_ref, mine_refs)

    def packed(i, j):
        if i == 0:
            return top_ref[:, j * BLK : (j + 1) * BLK]
        at = (j - 1) if i == 1 else 2
        return bottom_ref[:, at * BLK : (at + 1) * BLK]

    eye = (lax.broadcasted_iota(jnp.int32, (BLK, BLK), 0) == lax.broadcasted_iota(jnp.int32, (BLK, BLK), 1)).astype(F32)
    trace = sum(jnp.sum(packed(i, i) * eye) for i in range(NB))
    norm = jnp.sqrt(jnp.full((8, 128), trace, F32)) + 1e-07
    factor = (1.0 / norm)[0:1, 0:1]
    square = factor * factor

    a_rows = lambda n: [a_ref.at[k, n_x : n_x + D] for k in range(n)]
    p_rows = lambda n: [p_ref.at[k] for k in range(n)]
    b_rows = lambda n: [b_ref.at[k] for k in range(n)]

    def put_x(n, value):
        for k, piece in enumerate(pieces(value, n)):
            a_ref[k, :n_x] = piece

    for i in range(NB):
        for j in range(i, NB):
            value = packed(i, j) * square
            gram_ref[blocks(i, j)] = value
            put_both(a_rows(2), i, j, value)
    put_x(2, x_ref[...] * factor)

    def poly(n_p):
        def emit(i, j, block):
            value = NS[1] * gram_ref[blocks(i, j)] + NS[2] * block
            if i == j:
                value = value + NS[0] * eye
            put_both(p_rows(n_p), i, j, value)

        a = a_rows(2)
        symmetric_product(a, a, emit)

    def next_gram(n, keep):
        p = p_rows(n)
        rows = slice(0, n_x + BLK)
        wide = mul([a_ref[k, rows] for k in range(n)], [y[...] for y in p])
        for j in range(NB):
            put_both(b_rows(n), 0, j, wide[n_x:, j * BLK : (j + 1) * BLK])
        symmetric_product(a_rows(n), p, lambda i, j, block: put_both(b_rows(n), i, j, block), 1)
        put_x(keep, wide[:n_x])

        def emit(i, j, block):
            gram_ref[blocks(i, j)] = block
            put_both(a_rows(keep), i, j, block)

        symmetric_product(b_rows(n), p, emit)

    @pl.loop(0, SWEEPS - 1)
    def _(_):
        poly(2)
        next_gram(2, 2)

    poly(2)
    last = mul([a_ref[k, :n_x] for k in range(2)], [y[...] for y in p_rows(2)]).astype(BF)
    n = out_ref.shape[1]
    for k in range(out_ref.shape[0]):
        out_ref[k] = last[k * n : (k + 1) * n]


SMEM = pl.BlockSpec(memory_space=pltpu.SMEM)
VM = pl.BlockSpec(memory_space=pltpu.VMEM)


def gram_parts(at, rows):
    return pl.pallas_call(
        gram_kernel,
        out_shape=[jax.ShapeDtypeStruct((BLK, D), F32)] * 2,
        in_specs=[SMEM, VM],
        out_specs=[VM, VM],
        scratch_shapes=[pltpu.VMEM((BLK, D), F32)] * 2,
        compiler_params=pltpu.CompilerParams(vmem_limit_bytes=14 << 20),
        cost_estimate=pl.CostEstimate(flops=2 * 96 * D * D * 4, bytes_accessed=4 * D * D * 2, transcendentals=0),
    )(at, rows)


def sweeps(at, mine, rest, x_rows):
    return pl.pallas_call(
        sweeps_kernel,
        out_shape=jax.ShapeDtypeStruct((8, x_rows.shape[0] // 8, D), BF),
        in_specs=[SMEM] + [VM] * 9,
        out_specs=VM,
        scratch_shapes=[
            pltpu.VMEM((BLK, D), F32),
            pltpu.VMEM((BLK, D), F32),
            pltpu.VMEM((D, D), F32),
            pltpu.VMEM((3, x_rows.shape[0] + D, D), BF),
            pltpu.VMEM((3, D, D), BF),
            pltpu.VMEM((3, D, D), BF),
        ],
        compiler_params=pltpu.CompilerParams(vmem_limit_bytes=24 << 20),
        cost_estimate=pl.CostEstimate(flops=2 * D * D * D * 32, bytes_accessed=4 * D * D, transcendentals=0),
    )(at, *mine, *rest, x_rows)


def gelu_parts(u):
    k0 = math.sqrt(2.0 / math.pi)
    th = jnp.tanh(k0 * (u + 0.044715 * (u * u * u)))
    value = 0.5 * u * (1.0 + th)
    slope = 0.5 * (1.0 + th) + 0.5 * u * (1.0 - th * th) * (k0 * (1.0 + 3.0 * 0.044715 * u * u))
    return value, slope


HEADS = 3
PAD = 128
HC = HEADS * HD
HP = HEADS * PAD
NN = ((1,), (0,))
NT = ((1,), (1,))
TN = ((0,), (0,))


def iota(shape, dim):
    return lax.broadcasted_iota(jnp.int32, shape, dim)


def one_hot(cond):
    return jnp.where(cond, 1.0, 0.0).astype(BF)


def unit_place(at_ref, n):
    zi, xi, yi, ci, ti = (at_ref[k] for k in range(5))
    width = 24
    group = jnp.right_shift(n * 2731, 16)
    lane = n - width * group
    y = jnp.bitwise_and(group + yi, 1)
    inner = jnp.bitwise_and(jnp.right_shift(group, 1), 3)
    outer = jnp.bitwise_and(jnp.right_shift(group, 3), 3)
    z = jnp.bitwise_and(jnp.where(ci == 0, inner, outer) + zi, 3)
    x = jnp.bitwise_and(jnp.where(ci == 0, outer, inner) + xi, 3)
    row = 2 * ti + jnp.right_shift(z, 1)
    return row, (((jnp.bitwise_and(z, 1) * 4 + x) * 2 + y) * 2 + ci) * width + lane


def needed_blocks(at_ref):
    zi, ci = at_ref[0], at_ref[3]
    for rc in range(2):
        core_0 = jnp.bitwise_xor(ci, rc) == 0
        for x in range(4):
            for j in range(2):
                z = jnp.bitwise_and(2 * ci + j - zi, 3)
                outer, inner = jnp.where(core_0, x, z), jnp.where(core_0, z, x)
                yield rc, pl.multiple_of((outer * 4 + inner) * 48, 48)


def home_place(at_ref, r):
    xi, yi, ci = (at_ref[k] for k in range(1, 4))
    n = 6
    group = jnp.right_shift(r * 10923, 16)
    lane = r - n * group
    mat = jnp.bitwise_and(group, 3)
    y = jnp.bitwise_and(jnp.right_shift(group, 2) + yi, 1)
    j = jnp.bitwise_and(jnp.right_shift(group, 3), 1)
    x = jnp.bitwise_and(jnp.right_shift(group, 4) + xi, 3)
    core = jnp.bitwise_and(jnp.right_shift(group, 6) + ci, 1)
    return mat * HC + (((j * 4 + x) * 2 + y) * 2 + core) * n + lane


def attention_kernel(
    at_ref, own0_ref, own1_ref, own2_ref, own3_ref, got0_ref, got1_ref, got2_ref, got3_ref, normed_ref, cot_ref, cos_ref, sin_ref,
    sums_ref, keep_ref, give_ref,
    att_ref, near_ref, w_ref, wo_ref, q_ref, k_ref, v_ref, da_ref, heads_ref, d_ref, nat_ref,
):
    span = own0_ref.shape[0]
    for k, ref in enumerate((own0_ref, own1_ref, own2_ref, own3_ref, got0_ref, got1_ref, got2_ref, got3_ref)):
        att_ref[k // 4, k % 4 * span : (k % 4 + 1) * span] = ref[...]
    block = span // 4
    for k, (rc, at) in enumerate(needed_blocks(at_ref)):
        near_ref[k * block : (k + 1) * block] = att_ref[rc, pl.ds(at, block)]

    n_rows = 4 * HC
    pick = one_hot(iota((n_rows, n_rows), 0) == home_place(at_ref, iota((8, n_rows), 1))[:1])
    w_att = dot(pick, near_ref[...], NN).astype(BF)
    r = iota((HC, HC), 0)
    e = jnp.bitwise_and(r, HD - 1)
    half = ROT // 2
    source = jnp.where(e < half, r + half, jnp.where(e < ROT, r - half, -1))
    exchange = one_hot(iota((HC, HC), 1) == source)
    blank = jnp.zeros((HD, D), BF)

    def padded(ref, base, rows):
        for h in range(HEADS):
            at = base + h * PAD
            ref[at : at + HD] = rows[h * HD : (h + 1) * HD]
            ref[at + HD : at + PAD] = blank

    for m in range(3):
        padded(w_ref, m * HP, w_att[m * HC : (m + 1) * HC])
    for m in range(2):
        padded(w_ref, (3 + m) * HP, dot(exchange, w_att[m * HC : (m + 1) * HC], NN).astype(BF))
    padded(wo_ref, 0, w_att[3 * HC :])

    cos, sin = cos_ref[...], sin_ref[...]
    turn = at_ref[4] * (LEN // 2)
    at_q = jnp.bitwise_xor(iota((LEN, LEN), 0), turn)
    at_k = jnp.bitwise_xor(iota((LEN, LEN), 1), turn)
    causal = at_q >= at_k
    scale = HD ** (-0.5)

    @pl.loop(0, 2)
    def _(s):
        rows = pl.ds(pl.multiple_of(s * LEN, LEN), LEN)
        normed = normed_ref[rows]
        for m, ref in ((0, q_ref), (1, k_ref)):
            lin = dot(normed, w_ref[m * HP : (m + 1) * HP], NT)
            lin_2 = dot(normed, w_ref[(3 + m) * HP : (4 + m) * HP], NT)
            for h in range(HEADS):
                lanes = slice(h * PAD, (h + 1) * PAD)
                base = h * 2 * PAD
                own, other = lin[:, lanes], lin_2[:, lanes]
                ref[:, base : base + PAD] = (own * cos + other * sin).astype(BF)
                ref[:, base + PAD : base + 2 * PAD] = (other * cos - own * sin).astype(BF)
        v_ref[...] = dot(normed, w_ref[2 * HP : 3 * HP], NT).astype(BF)
        da_ref[...] = dot(cot_ref[rows], wo_ref[...], NT).astype(BF)
        for h in range(HEADS):
            two = slice(h * 2 * PAD, (h + 1) * 2 * PAD)
            one = slice(h * 2 * PAD, h * 2 * PAD + PAD)
            lanes = slice(h * PAD, (h + 1) * PAD)
            value, d_att = v_ref[:, lanes], da_ref[:, lanes]
            scores = jnp.where(causal, dot(q_ref[:, one], k_ref[:, one], NT) * scale, -1e30)
            raised = jnp.exp(scores - jnp.max(scores, axis=1, keepdims=True))
            probs = raised / jnp.sum(raised, axis=1, keepdims=True)
            low = probs.astype(BF)
            heads_ref[rows, lanes] = dot(low, value, NN).astype(BF)
            d_ref[rows, 2 * HP + h * PAD : 2 * HP + (h + 1) * PAD] = dot(low, d_att, TN).astype(BF)
            d_probs = dot(d_att, value, NT)
            d_scores = (probs * (d_probs - jnp.sum(probs * d_probs, axis=1, keepdims=True))).astype(BF)
            d_q = dot(d_scores, k_ref[:, two], NN) * scale
            d_k = dot(d_scores, q_ref[:, two], TN) * scale
            for m, pair in ((0, d_q), (1, d_k)):
                at = m * HP + h * PAD
                d_ref[rows, at : at + PAD] = (pair[:, :PAD] * cos - pair[:, PAD:] * sin).astype(BF)

    sums_ref[0] = dot(heads_ref[...], wo_ref[...], NN)
    sums_ref[1] = dot(d_ref[...], w_ref[: 3 * HP], NN)

    for m in range(4):
        if m < 3:
            grad = dot(d_ref[:, m * HP : (m + 1) * HP], normed_ref[...], TN).astype(BF)
        else:
            grad = dot(heads_ref[...], cot_ref[...], TN).astype(BF)
        for h in range(HEADS):
            nat_ref[m * HC + h * HD : m * HC + (h + 1) * HD] = grad[h * PAD : h * PAD + HD]
    place = home_place(at_ref, iota((n_rows, 128), 0))
    pick = jnp.concatenate([one_hot(iota((n_rows, 128), 1) + b == place) for b in range(0, n_rows, 128)], axis=1)
    near_ref[...] = dot(pick, nat_ref[...], NN).astype(BF)
    keep_ref[...] = jnp.zeros_like(keep_ref)
    give_ref[...] = jnp.zeros_like(give_ref)
    for k, (rc, at) in enumerate(needed_blocks(at_ref)):
        (keep_ref, give_ref)[rc][pl.ds(at, block)] = near_ref[k * block : (k + 1) * block]


def forward_kernel(
    at_ref, held0_ref, held1_ref, held2_ref, held3_ref, normed_ref, cot_ref, bias_ref, sums_ref,
    own_ref, peer_ref, gbias_ref, out0_ref, out1_ref, out2_ref, out3_ref,
    win_ref, wback_ref,
):
    span = held0_ref.shape[1]
    for s, ref in enumerate((held0_ref, held1_ref, held2_ref, held3_ref)):
        win_ref[s * span : (s + 1) * span] = ref[0]
        wback_ref[s * span : (s + 1) * span] = ref[1]

    def send(group, grad):
        for s, ref in enumerate((out0_ref, out1_ref, out2_ref, out3_ref)):
            ref[group] = grad[s * span : (s + 1) * span]

    hidden, slope = gelu_parts(dot(normed_ref[...], win_ref[...], NT) + bias_ref[...])
    hidden = hidden.astype(BF)


    def give_rows(k, value):
        own_ref[k] = value[:LEN]
        peer_ref[k] = value[LEN:]

    give_rows(0, sums_ref[0] + dot(hidden, wback_ref[...], NN))
    send(1, dot(hidden, cot_ref[...], TN).astype(BF))
    d_pre = (dot(cot_ref[...], wback_ref[...], NT) * slope).astype(BF)
    grad_bias = jnp.sum(d_pre.astype(F32), axis=0, keepdims=True)
    n_units = win_ref.shape[0]
    bias_row, _ = unit_place(at_ref, iota((8, n_units), 1))
    spread = pieces(jnp.where(bias_row == iota((8, n_units), 0), grad_bias, 0.0), 3)
    _, bias_lane = unit_place(at_ref, iota((n_units, 128), 0))
    to_lane = jnp.concatenate([one_hot(iota((n_units, 128), 1) + b == bias_lane) for b in range(0, D, 128)], axis=1)
    gbias_ref[...] = sum(dot(piece, to_lane, NN) for piece in reversed(spread))
    send(0, dot(d_pre, normed_ref[...], TN).astype(BF))
    give_rows(1, sums_ref[1] + dot(d_pre, win_ref[...], NN))


def out(shape, dtype):
    return jax.ShapeDtypeStruct(shape, dtype)


def low(*shape):
    return pltpu.VMEM(shape, BF)


def attention(at, own, got, normed, cot, cos, sin):
    n = normed.shape[0]
    rows = 4 * own[0].shape[0]
    return pl.pallas_call(
        attention_kernel,
        out_shape=[out((2, n, D), F32), out((rows, D), BF), out((rows, D), BF)],
        in_specs=[SMEM] + [VM] * 12,
        out_specs=[VM] * 3,
        scratch_shapes=[low(2, rows, D), low(4 * HC, D), low(5 * HP, D), low(HP, D)]
        + [low(LEN, 2 * HP), low(LEN, 2 * HP), low(LEN, HP), low(LEN, HP)]
        + [low(n, HP), low(n, 3 * HP), low(4 * HC, D)],
        compiler_params=pltpu.CompilerParams(vmem_limit_bytes=32 << 20),
        cost_estimate=pl.CostEstimate(flops=12 * 10**9, bytes_accessed=16 << 20, transcendentals=10**6),
    )(at, *own, *got, normed, cot, cos, sin)


def feed_forward(at, held, normed, cot, bias, sums):
    n = normed.shape[0]
    span = held[0].shape[1]
    units = 4 * span
    return pl.pallas_call(
        forward_kernel,
        out_shape=[out((2, n // 2, D), F32), out((2, n // 2, D), F32), out((8, D), F32)] + [out((2, span, D), BF)] * 4,
        in_specs=[SMEM] + [VM] * 8,
        out_specs=[VM] * 7,
        scratch_shapes=[low(units, D), low(units, D)],
        compiler_params=pltpu.CompilerParams(vmem_limit_bytes=22 << 20),
        cost_estimate=pl.CostEstimate(flops=10 * 10**9, bytes_accessed=16 << 20, transcendentals=10**6),
    )(at, *held, normed, cot, bias, sums)


def body(tokens, cotangent, qkv_weight, out_weight, fc_weight, vectors, qkv_momentum, out_momentum, fc_momentum, vector_first, vector_second):
    zi, xi, yi, ci, ti = (lax.axis_index(a) for a in ALL)
    rows = tokens.shape[0]
    n_att = qkv_weight.shape[3]
    n_fc = fc_weight.shape[3]
    gain, shift = vectors[:D], vectors[D : 2 * D]
    bias_in, bias_out = vectors[2 * D : 2 * D + FF], vectors[2 * D + FF :]

    first = ci == 0
    attn_rows = jnp.concatenate([jnp.transpose(qkv_weight[:, :, 0, :], (0, 2, 1)), jnp.transpose(out_weight[:, 0, :])[None]])
    fc_rows = jnp.transpose(fc_weight[:, :, 0, :], (0, 2, 1))
    own_rows = jnp.concatenate([attn_rows.reshape(1, n_fc, D), fc_rows]).astype(BF)
    att_near = jnp.stack(gather_ring(own_rows[0], pull_yh, 2))
    fc_near = jnp.stack(gather_ring(own_rows[1:], pull_yh, 2), axis=1)

    inputs = tokens.astype(F32)
    average = jnp.mean(inputs, axis=-1, keepdims=True)
    deviation = inputs - average
    variance = jnp.mean(deviation * deviation, axis=-1, keepdims=True)
    inv_spread = lax.rsqrt(variance + 1e-05)
    centred = deviation * inv_spread
    normed_own = (centred * gain + shift).astype(BF)
    both = jnp.stack([normed_own, cotangent])
    att_near, fc_near, both = lax.optimization_barrier((att_near, fc_near, both))
    span = 8 * n_fc
    att_near = jnp.stack(gather_ring(att_near, pull_inner, 4)).reshape(span, D)
    both = jnp.stack([both, pull(both, "t", 1)], axis=1)
    att_near, both = lax.optimization_barrier((att_near, both))
    att_held = gather_ring(att_near, pull_outer, 4)
    fc_near = jnp.stack(gather_ring(fc_near, pull_inner, 4), axis=1).reshape(2, span, D)
    fc_held = gather_ring(fc_near, pull_outer, 4)
    both = jnp.stack([both, pull(both, "c", 1)], axis=1)
    n_all = 4 * rows
    normed, cot = both[0].reshape(n_all, D), both[1].reshape(n_all, D)

    half = jnp.arange(LEN) // rows
    position = ((ti + half) % 2) * rows + jnp.arange(LEN) % rows
    frequency = 10000.0 ** (-2.0 * jnp.arange(ROT // 2, dtype=F32) / ROT)
    angles = position.astype(F32)[:, None] * frequency[None, :]
    cos_t, sin_t = jnp.cos(angles), jnp.sin(angles)
    pad = lambda a, b, fill: jnp.concatenate([a, b, jnp.full((LEN, PAD - ROT), fill, F32)], axis=1)
    cos_full, sin_full = pad(cos_t, cos_t, 1.0), pad(-sin_t, sin_t, 0.0)

    bias6 = bias_in.reshape(2, 4, 4, 2, 2, n_fc)
    bias6 = jnp.concatenate([bias6, bias6], axis=1)
    bias6 = jnp.concatenate([bias6, bias6], axis=2)
    bias6 = jnp.concatenate([bias6, bias6], axis=3)
    bias_own = lax.dynamic_slice(bias6, (ti, zi, xi, yi, ci, 0), (1, 4, 4, 2, 1, n_fc))[0, :, :, :, 0]
    by_turn = lambda v: jnp.where(first, jnp.swapaxes(v, 0, 1), v)
    bias_own = by_turn(bias_own).reshape(1, 32 * n_fc)
    at = jnp.stack([zi, xi, yi, ci, ti]).astype(jnp.int32)
    mom_rows = jnp.concatenate(
        [
            jnp.transpose(qkv_momentum[:, :, 0, :], (0, 2, 1)).reshape(3 * n_att, D),
            jnp.transpose(out_momentum[:, 0, :]),
            jnp.transpose(fc_momentum[:, :, 0, :], (0, 2, 1)).reshape(2 * n_fc, D),
        ]
    )
    att_held[2], normed, cot, bias_own, at, cos_full, sin_full, mom_rows = lax.optimization_barrier(
        (att_held[2], normed, cot, bias_own, at, cos_full, sin_full, mom_rows)
    )
    att_got = [pull(v, "c", 1) for v in att_held]
    sums, att_keep, att_give = attention(at, att_held, att_got, normed, cot, cos_full, sin_full)

    att_grad = (att_keep + pull(att_give, "c", 1)).reshape(4, span, D)
    att_parts = [att_grad[k] for k in range(4)]

    rows_own, rows_peer, grad_bias_in, *fc_parts = feed_forward(at, fc_held, normed, cot, bias_own, sums)
    att_parts, rows_peer = lax.optimization_barrier((att_parts, rows_peer))
    rows_own = (rows_own + pull(rows_peer, "c", 1)).reshape(2, 2, rows, D)
    att_total = sum_ring(att_parts, pull_outer)
    fc_total = sum_ring(fc_parts, pull_outer)
    rows_own = rows_own[:, 0] + pull(rows_own[:, 1].astype(BF), "t", 1).astype(F32)
    att_total, fc_total, rows_own = lax.optimization_barrier((att_total, fc_total, rows_own))
    total = jnp.concatenate([att_total[None], fc_total]).reshape(3, 4, 2, n_fc, D)
    total = sum_ring([total[:, k] for k in range(4)], pull_inner)
    total = sum_ring([total[:, k] for k in range(2)], pull_yh).reshape(3 * n_fc, D)

    mixed = (inputs + rows_own[0] + bias_out).astype(BF)
    d_rows = rows_own[1]
    d_hat = d_rows * gain
    correction = d_hat - jnp.mean(d_hat, axis=-1, keepdims=True) - centred * jnp.mean(d_hat * centred, axis=-1, keepdims=True)
    own_cot = cotangent.astype(F32)
    input_grad = own_cot + correction * inv_spread

    total_of = lambda v: jnp.sum(v, axis=0, keepdims=True)
    vec_rows = [total_of(d_rows * centred), total_of(d_rows), grad_bias_in[: FF // D], total_of(own_cot), jnp.zeros((VEC_ROWS - VEC // D, D), F32)]

    moment = 0.95 * mom_rows + total
    update = total + 0.95 * moment

    half_fc = n_fc // 2
    att_u = update[: 4 * n_att].reshape(4, n_att, D)
    att_u = jnp.concatenate([att_u, jnp.zeros((4, half_fc - n_att, D), F32)], axis=1)
    fc_u = update[4 * n_att :].reshape(4, half_fc, D)
    vec_rows = jnp.concatenate(vec_rows)
    chunks = jnp.concatenate([att_u, fc_u])
    chunks = jnp.concatenate([chunks, jnp.broadcast_to(vec_rows, (8, VEC_ROWS, D))], axis=1)
    got = lax.all_to_all(chunks, ("z", "t"), split_axis=0, concat_axis=0, tiled=True)
    mine = got[:, :half_fc].reshape(8 * half_fc, D)
    vec_sum = jnp.sum(got[:, half_fc:], axis=0)[:8]
    keep, give = gram_parts(at, mine)
    from_core = pull(jnp.concatenate([give, vec_sum]), "c", 1)
    part = keep + from_core[:BLK]
    vec_sum = vec_sum + from_core[BLK:]
    quarter = lambda k: part[k * QUARTER : (k + 1) * QUARTER]
    along_x = lambda v, k: pull(v, "x", k)
    load = jnp.concatenate([quarter(0), vec_sum])
    for k in (1, 2, 3):
        load = load + along_x(jnp.concatenate([quarter(k), vec_sum]), 4 - k)
    load = load + pull(load, "yh", 1)
    part, vec_sum = load[:QUARTER], load[QUARTER:]
    part = jnp.where(zi >= 2, part + pull(part, "t", 1), part)
    part = gather_ring(part, along_x, 4)
    rest = [pull(v, "c", 1) for v in part]
    x_rows = sweeps(at, part, rest, mine)
    x_rows, moment = lax.optimization_barrier((x_rows, moment))
    vector_grad = vec_sum[: VEC // D].reshape(VEC)
    first_new = 0.9 * vector_first + 0.1 * vector_grad
    second_new = 0.95 * vector_second + 0.05 * vector_grad * vector_grad
    step_size = first_new / (1.0 - 0.9**STEP) / (jnp.sqrt(second_new / (1.0 - 0.95**STEP)) + 1e-08)
    vector_new = vectors - 0.2 * step_size

    back = lax.all_to_all(x_rows, ("z", "t"), split_axis=0, concat_axis=0, tiled=True).astype(F32)
    att_x = back[:4, :n_att]
    fc_x = back[4:].reshape(2, n_fc, D)

    def cols(v):
        return jnp.transpose(v, (0, 2, 1))[:, :, None, :]

    fc_factor = math.sqrt(FF / D)
    qkv_new = qkv_weight * 0.99 - cols(att_x[:3])
    out_new = out_weight * 0.99 - cols(att_x[3:])[0]
    fc_new = fc_weight * 0.99 - fc_factor * cols(fc_x)
    att_m = moment[: 4 * n_att].reshape(4, n_att, D)
    fc_m = moment[4 * n_att :].reshape(2, n_fc, D)
    return (mixed, input_grad, qkv_new, out_new, fc_new, cols(att_m[:3]), cols(att_m[3:])[0], cols(fc_m), first_new, second_new, vector_new)


def solution(mesh):
    mesh = Mesh(mesh.devices.reshape(4, 4, 2, 2, 2), ALL)
    rows = P(ALL, None)
    w3 = P(None, None, "t", DP)
    w2 = P(None, "t", DP)
    vec = P()
    in_specs = (rows, rows, w3, w2, w3, vec, w3, w2, w3, vec, vec)
    out_specs = (rows, rows, w3, w2, w3, w3, w2, w3, vec, vec, vec)
    return jax.shard_map(body, mesh=mesh, in_specs=in_specs, out_specs=out_specs, check_vma=False)
```

```python
import functools
import itertools
import math

import jax
import jax.numpy as jnp
from jax import lax
from jax.experimental import pallas as pl
from jax.experimental.pallas import tpu as pltpu
from jax.sharding import Mesh, PartitionSpec as P

D = 768
H = 12
HD = 64
ROT = 16
FF = 3072
SWEEPS = 5
STEP = 10
LEN = 256
VEC = 2 * D + FF + D
VEC_ROWS = 12

NS = (3.4445, -4.775, 2.0315)
BF = jnp.bfloat16
F32 = jnp.float32
BLK = 256
QUARTER = 64
NB = D // BLK

DP = ("z", "x", "yh", "c")
ALL = ("z", "x", "yh", "c", "t")


def pull(value, axis, k):
    n = lax.axis_size(axis)
    return lax.ppermute(value, axis, [((i + k) % n, i) for i in range(n)])


def move(value, source):
    sizes = [lax.axis_size(a) for a in ALL]
    index = lambda at: functools.reduce(lambda total, one: total * one[0] + one[1] % one[0], zip(sizes, at), 0)
    pairs = []
    for here in itertools.product(*map(range, sizes)):
        there = source(*here)
        if there is not None:
            pairs.append((index(there), index(here)))
    return lax.ppermute(value, ALL, pairs)


def pull_outer(value, k):
    return move(value, lambda z, x, y, c, t: (z, x + k, y, c, t) if c == 0 else (z + k, x, y, c, t))


def pull_inner(value, k):
    return move(value, lambda z, x, y, c, t: (z + k, x, y, c, t) if c == 0 else (z, x + k, y, c, t))


def pull_yh(value, k):
    return pull(value, "yh", k)


def gather_ring(value, pulls, n):
    return [value] + [pulls(value, k) for k in range(1, n)]


def sum_ring(parts, pulls):
    n = len(parts)
    total = parts[0].astype(F32)
    for k in range(1, n):
        total = total + pulls(parts[k].astype(BF), n - k).astype(F32)
    return total


def dot(a, b, dims):
    return lax.dot_general(a, b, (dims, ((), ())), preferred_element_type=F32)


def pieces(value, n):
    out = []
    for _ in range(n):
        low = value.astype(BF)
        out.append(low)
        value = value - low.astype(F32)
    return out


def mul(xs, ys, dims=((1,), (0,))):
    n = len(xs)
    total = None
    for order in reversed(range(n)):
        for i in range(order + 1):
            term = lax.dot_general(xs[i], ys[order - i], (dims, ((), ())), preferred_element_type=F32)
            total = term if total is None else total + term
    return total


def gram_kernel(at_ref, rows_ref, vec_ref, keep_ref, give0_ref, give1_ref, give2_ref, give3_ref, top_ref, bottom_ref):
    xs = pieces(rows_ref[...], 3)
    dims = ((0,), (0,))
    cut = lambda i: slice(i * BLK, (i + 1) * BLK)
    top_ref[...] = mul([x[:, cut(0)] for x in xs], xs, dims)
    bottom_ref[:, : 2 * BLK] = mul([x[:, cut(1)] for x in xs], [x[:, BLK:] for x in xs], dims)
    bottom_ref[:, 2 * BLK :] = mul([x[:, cut(2)] for x in xs], [x[:, 2 * BLK :] for x in xs], dims)

    def keep(in_ref):
        for k in range(4):
            place = pl.multiple_of(jnp.bitwise_and(at_ref[1] + k, 3) * QUARTER, QUARTER)
            keep_ref[k * QUARTER : (k + 1) * QUARTER] = in_ref[pl.ds(place, QUARTER)]

    def give(in_ref):
        for k, ref in enumerate((give0_ref, give1_ref, give2_ref, give3_ref)):
            place = pl.multiple_of(jnp.bitwise_and(at_ref[1] + k, 3) * QUARTER, QUARTER)
            ref[:QUARTER] = in_ref[pl.ds(place, QUARTER)]
            ref[QUARTER:] = vec_ref[...]

    first = at_ref[3] == 0

    @pl.when(first)
    def _():
        keep(top_ref)
        give(bottom_ref)

    @pl.when(jnp.logical_not(first))
    def _():
        keep(bottom_ref)
        give(top_ref)


def blocks(i, j):
    return (slice(i * BLK, (i + 1) * BLK), slice(j * BLK, (j + 1) * BLK))


def put(refs, i, j, value):
    for ref, piece in zip(refs, pieces(value, len(refs))):
        ref[blocks(i, j)] = piece


def put_both(refs, i, j, value):
    put(refs, i, j, value)
    if i != j:
        put(refs, j, i, value.T)


def symmetric_product(xs, ys, emit, start=0):
    for i in range(start, NB):
        rows = slice(i * BLK, (i + 1) * BLK)
        wide = mul([x[rows, :] for x in xs], [y[:, i * BLK :] for y in ys])
        for j in range(i, NB):
            emit(i, j, wide[:, (j - i) * BLK : (j - i + 1) * BLK])


def sweeps_kernel(at_ref, *refs):
    sweeps_math(at_ref, refs[:4], refs[4:8], *refs[8:])


def sweeps_math(at_ref, mine_refs, rest_refs, x_ref, out_ref, top_ref, bottom_ref, gram_ref, a_ref, p_ref, b_ref):
    first = at_ref[3] == 0
    n_x = x_ref.shape[0]

    def by_place(out_ref, in_refs):
        for k, ref in enumerate(in_refs):
            place = pl.multiple_of(jnp.bitwise_and(at_ref[1] + k, 3) * QUARTER, QUARTER)
            out_ref[pl.ds(place, QUARTER)] = ref[...]

    @pl.when(first)
    def _():
        by_place(top_ref, mine_refs)
        by_place(bottom_ref, rest_refs)

    @pl.when(jnp.logical_not(first))
    def _():
        by_place(top_ref, rest_refs)
        by_place(bottom_ref, mine_refs)

    def packed(i, j):
        if i == 0:
            return top_ref[:, j * BLK : (j + 1) * BLK]
        at = (j - 1) if i == 1 else 2
        return bottom_ref[:, at * BLK : (at + 1) * BLK]

    eye = (lax.broadcasted_iota(jnp.int32, (BLK, BLK), 0) == lax.broadcasted_iota(jnp.int32, (BLK, BLK), 1)).astype(F32)
    trace = sum(jnp.sum(packed(i, i) * eye) for i in range(NB))
    norm = jnp.sqrt(jnp.full((8, 128), trace, F32)) + 1e-07
    factor = (1.0 / norm)[0:1, 0:1]
    square = factor * factor

    a_rows = lambda n: [a_ref.at[k, n_x : n_x + D] for k in range(n)]
    p_rows = lambda n: [p_ref.at[k] for k in range(n)]
    b_rows = lambda n: [b_ref.at[k] for k in range(n)]

    def put_x(n, value):
        for k, piece in enumerate(pieces(value, n)):
            a_ref[k, :n_x] = piece

    for i in range(NB):
        for j in range(i, NB):
            value = packed(i, j) * square
            gram_ref[blocks(i, j)] = value
            put_both(a_rows(2), i, j, value)
    put_x(2, x_ref[...] * factor)

    def poly(n_p):
        def emit(i, j, block):
            value = NS[1] * gram_ref[blocks(i, j)] + NS[2] * block
            if i == j:
                value = value + NS[0] * eye
            put_both(p_rows(n_p), i, j, value)

        a = a_rows(2)
        symmetric_product(a, a, emit)

    def next_gram(n, keep):
        p = p_rows(n)
        rows = slice(0, n_x + BLK)
        wide = mul([a_ref[k, rows] for k in range(n)], [y[...] for y in p])
        for j in range(NB):
            put_both(b_rows(n), 0, j, wide[n_x:, j * BLK : (j + 1) * BLK])
        symmetric_product(a_rows(n), p, lambda i, j, block: put_both(b_rows(n), i, j, block), 1)
        put_x(keep, wide[:n_x])

        def emit(i, j, block):
            gram_ref[blocks(i, j)] = block
            put_both(a_rows(keep), i, j, block)

        symmetric_product(b_rows(n), p, emit)

    @pl.loop(0, SWEEPS - 1)
    def _(_):
        poly(2)
        next_gram(2, 2)

    poly(2)
    last = mul([a_ref[k, :n_x] for k in range(2)], [y[...] for y in p_rows(2)]).astype(BF)
    n = out_ref.shape[1]
    for k in range(out_ref.shape[0]):
        out_ref[k] = last[k * n : (k + 1) * n]


SMEM = pl.BlockSpec(memory_space=pltpu.SMEM)
VM = pl.BlockSpec(memory_space=pltpu.VMEM)


def gram_parts(at, rows, vec):
    return pl.pallas_call(
        gram_kernel,
        out_shape=[jax.ShapeDtypeStruct((BLK, D), F32)] + [jax.ShapeDtypeStruct((QUARTER + 8, D), F32)] * 4,
        in_specs=[SMEM, VM, VM],
        out_specs=[VM] * 5,
        scratch_shapes=[pltpu.VMEM((BLK, D), F32)] * 2,
        compiler_params=pltpu.CompilerParams(vmem_limit_bytes=14 << 20),
        cost_estimate=pl.CostEstimate(flops=2 * 96 * D * D * 4, bytes_accessed=4 * D * D * 2, transcendentals=0),
    )(at, rows, vec)


def sweeps(at, mine, rest, x_rows):
    return pl.pallas_call(
        sweeps_kernel,
        out_shape=jax.ShapeDtypeStruct((8, x_rows.shape[0] // 8, D), BF),
        in_specs=[SMEM] + [VM] * 9,
        out_specs=VM,
        scratch_shapes=[
            pltpu.VMEM((BLK, D), F32),
            pltpu.VMEM((BLK, D), F32),
            pltpu.VMEM((D, D), F32),
            pltpu.VMEM((3, x_rows.shape[0] + D, D), BF),
            pltpu.VMEM((3, D, D), BF),
            pltpu.VMEM((3, D, D), BF),
        ],
        compiler_params=pltpu.CompilerParams(vmem_limit_bytes=24 << 20),
        cost_estimate=pl.CostEstimate(flops=2 * D * D * D * 32, bytes_accessed=4 * D * D, transcendentals=0),
    )(at, *mine, *rest, x_rows)


def gelu_parts(u):
    k0 = math.sqrt(2.0 / math.pi)
    th = jnp.tanh(k0 * (u + 0.044715 * (u * u * u)))
    value = 0.5 * u * (1.0 + th)
    slope = 0.5 * (1.0 + th) + 0.5 * u * (1.0 - th * th) * (k0 * (1.0 + 3.0 * 0.044715 * u * u))
    return value, slope


HEADS = 3
PAD = 128
HC = HEADS * HD
HP = HEADS * PAD
NN = ((1,), (0,))
NT = ((1,), (1,))
TN = ((0,), (0,))


def iota(shape, dim):
    return lax.broadcasted_iota(jnp.int32, shape, dim)


def one_hot(cond):
    return jnp.where(cond, 1.0, 0.0).astype(BF)


def unit_place(at_ref, n):
    zi, xi, yi, ci, ti = (at_ref[k] for k in range(5))
    width = 24
    group = jnp.right_shift(n * 2731, 16)
    lane = n - width * group
    y = jnp.bitwise_and(group + yi, 1)
    inner = jnp.bitwise_and(jnp.right_shift(group, 1), 3)
    outer = jnp.bitwise_and(jnp.right_shift(group, 3), 3)
    z = jnp.bitwise_and(jnp.where(ci == 0, inner, outer) + zi, 3)
    x = jnp.bitwise_and(jnp.where(ci == 0, outer, inner) + xi, 3)
    row = 2 * ti + jnp.right_shift(z, 1)
    return row, (((jnp.bitwise_and(z, 1) * 4 + x) * 2 + y) * 2 + ci) * width + lane


def needed_blocks(at_ref):
    zi, ci = at_ref[0], at_ref[3]
    for rc in range(2):
        core_0 = jnp.bitwise_xor(ci, rc) == 0
        for x in range(4):
            for j in range(2):
                z = jnp.bitwise_and(2 * ci + j - zi, 3)
                outer, inner = jnp.where(core_0, x, z), jnp.where(core_0, z, x)
                yield rc, pl.multiple_of((outer * 4 + inner) * 48, 48)


def home_place(at_ref, r):
    xi, yi, ci = (at_ref[k] for k in range(1, 4))
    n = 6
    group = jnp.right_shift(r * 10923, 16)
    lane = r - n * group
    mat = jnp.bitwise_and(group, 3)
    y = jnp.bitwise_and(jnp.right_shift(group, 2) + yi, 1)
    j = jnp.bitwise_and(jnp.right_shift(group, 3), 1)
    x = jnp.bitwise_and(jnp.right_shift(group, 4) + xi, 3)
    core = jnp.bitwise_and(jnp.right_shift(group, 6) + ci, 1)
    return mat * HC + (((j * 4 + x) * 2 + y) * 2 + core) * n + lane


def attention_kernel(
    at_ref, own0_ref, own1_ref, own2_ref, own3_ref, got0_ref, got1_ref, got2_ref, got3_ref, normed_ref, cot_ref, cos_ref, sin_ref,
    sums_ref, keep_ref, give_ref,
    att_ref, near_ref, w_ref, wo_ref, q_ref, k_ref, v_ref, da_ref, heads_ref, d_ref, nat_ref,
):
    span = own0_ref.shape[0]
    for k, ref in enumerate((own0_ref, own1_ref, own2_ref, own3_ref, got0_ref, got1_ref, got2_ref, got3_ref)):
        att_ref[k // 4, k % 4 * span : (k % 4 + 1) * span] = ref[...]
    block = span // 4
    for k, (rc, at) in enumerate(needed_blocks(at_ref)):
        near_ref[k * block : (k + 1) * block] = att_ref[rc, pl.ds(at, block)]

    n_rows = 4 * HC
    pick = one_hot(iota((n_rows, n_rows), 0) == home_place(at_ref, iota((8, n_rows), 1))[:1])
    w_att = dot(pick, near_ref[...], NN).astype(BF)
    r = iota((HC, HC), 0)
    e = jnp.bitwise_and(r, HD - 1)
    half = ROT // 2
    source = jnp.where(e < half, r + half, jnp.where(e < ROT, r - half, -1))
    exchange = one_hot(iota((HC, HC), 1) == source)
    blank = jnp.zeros((HD, D), BF)

    def padded(ref, base, rows):
        for h in range(HEADS):
            at = base + h * PAD
            ref[at : at + HD] = rows[h * HD : (h + 1) * HD]
            ref[at + HD : at + PAD] = blank

    for m in range(3):
        padded(w_ref, m * HP, w_att[m * HC : (m + 1) * HC])
    for m in range(2):
        padded(w_ref, (3 + m) * HP, dot(exchange, w_att[m * HC : (m + 1) * HC], NN).astype(BF))
    padded(wo_ref, 0, w_att[3 * HC :])

    cos, sin = cos_ref[...], sin_ref[...]
    turn = at_ref[4] * (LEN // 2)
    at_q = jnp.bitwise_xor(iota((LEN, LEN), 0), turn)
    at_k = jnp.bitwise_xor(iota((LEN, LEN), 1), turn)
    causal = at_q >= at_k
    scale = HD ** (-0.5)

    @pl.loop(0, 2)
    def _(s):
        rows = pl.ds(pl.multiple_of(s * LEN, LEN), LEN)
        normed = normed_ref[rows]
        for m, ref in ((0, q_ref), (1, k_ref)):
            lin = dot(normed, w_ref[m * HP : (m + 1) * HP], NT)
            lin_2 = dot(normed, w_ref[(3 + m) * HP : (4 + m) * HP], NT)
            for h in range(HEADS):
                lanes = slice(h * PAD, (h + 1) * PAD)
                base = h * 2 * PAD
                own, other = lin[:, lanes], lin_2[:, lanes]
                ref[:, base : base + PAD] = (own * cos + other * sin).astype(BF)
                ref[:, base + PAD : base + 2 * PAD] = (other * cos - own * sin).astype(BF)
        v_ref[...] = dot(normed, w_ref[2 * HP : 3 * HP], NT).astype(BF)
        da_ref[...] = dot(cot_ref[rows], wo_ref[...], NT).astype(BF)
        for h in range(HEADS):
            two = slice(h * 2 * PAD, (h + 1) * 2 * PAD)
            one = slice(h * 2 * PAD, h * 2 * PAD + PAD)
            lanes = slice(h * PAD, (h + 1) * PAD)
            value, d_att = v_ref[:, lanes], da_ref[:, lanes]
            scores = jnp.where(causal, dot(q_ref[:, one], k_ref[:, one], NT) * scale, -1e30)
            raised = jnp.exp(scores - jnp.max(scores, axis=1, keepdims=True))
            probs = raised / jnp.sum(raised, axis=1, keepdims=True)
            low = probs.astype(BF)
            heads_ref[rows, lanes] = dot(low, value, NN).astype(BF)
            d_ref[rows, 2 * HP + h * PAD : 2 * HP + (h + 1) * PAD] = dot(low, d_att, TN).astype(BF)
            d_probs = dot(d_att, value, NT)
            d_scores = (probs * (d_probs - jnp.sum(probs * d_probs, axis=1, keepdims=True))).astype(BF)
            d_q = dot(d_scores, k_ref[:, two], NN) * scale
            d_k = dot(d_scores, q_ref[:, two], TN) * scale
            for m, pair in ((0, d_q), (1, d_k)):
                at = m * HP + h * PAD
                d_ref[rows, at : at + PAD] = (pair[:, :PAD] * cos - pair[:, PAD:] * sin).astype(BF)

    sums_ref[0] = dot(heads_ref[...], wo_ref[...], NN)
    sums_ref[1] = dot(d_ref[...], w_ref[: 3 * HP], NN)

    for m in range(4):
        if m < 3:
            grad = dot(d_ref[:, m * HP : (m + 1) * HP], normed_ref[...], TN).astype(BF)
        else:
            grad = dot(heads_ref[...], cot_ref[...], TN).astype(BF)
        for h in range(HEADS):
            nat_ref[m * HC + h * HD : m * HC + (h + 1) * HD] = grad[h * PAD : h * PAD + HD]
    place = home_place(at_ref, iota((n_rows, 128), 0))
    pick = jnp.concatenate([one_hot(iota((n_rows, 128), 1) + b == place) for b in range(0, n_rows, 128)], axis=1)
    near_ref[...] = dot(pick, nat_ref[...], NN).astype(BF)
    keep_ref[...] = jnp.zeros_like(keep_ref)
    give_ref[...] = jnp.zeros_like(give_ref)
    for k, (rc, at) in enumerate(needed_blocks(at_ref)):
        (keep_ref, give_ref)[rc][pl.ds(at, block)] = near_ref[k * block : (k + 1) * block]


def forward_kernel(
    at_ref, held0_ref, held1_ref, held2_ref, held3_ref, normed_ref, cot_ref, bias_ref, sums_ref,
    own_ref, peer_ref, gbias_ref, out0_ref, out1_ref, out2_ref, out3_ref,
    win_ref, wback_ref,
):
    span = held0_ref.shape[1]
    for s, ref in enumerate((held0_ref, held1_ref, held2_ref, held3_ref)):
        win_ref[s * span : (s + 1) * span] = ref[0]
        wback_ref[s * span : (s + 1) * span] = ref[1]

    def send(group, grad):
        for s, ref in enumerate((out0_ref, out1_ref, out2_ref, out3_ref)):
            ref[group] = grad[s * span : (s + 1) * span]

    hidden, slope = gelu_parts(dot(normed_ref[...], win_ref[...], NT) + bias_ref[...])
    hidden = hidden.astype(BF)


    def give_rows(k, value):
        own_ref[k] = value[:LEN]
        peer_ref[k] = value[LEN:]

    give_rows(0, sums_ref[0] + dot(hidden, wback_ref[...], NN))
    send(1, dot(hidden, cot_ref[...], TN).astype(BF))
    d_pre = (dot(cot_ref[...], wback_ref[...], NT) * slope).astype(BF)
    grad_bias = jnp.sum(d_pre.astype(F32), axis=0, keepdims=True)
    n_units = win_ref.shape[0]
    bias_row, _ = unit_place(at_ref, iota((8, n_units), 1))
    spread = pieces(jnp.where(bias_row == iota((8, n_units), 0), grad_bias, 0.0), 3)
    _, bias_lane = unit_place(at_ref, iota((n_units, 128), 0))
    to_lane = jnp.concatenate([one_hot(iota((n_units, 128), 1) + b == bias_lane) for b in range(0, D, 128)], axis=1)
    gbias_ref[...] = sum(dot(piece, to_lane, NN) for piece in reversed(spread))
    send(0, dot(d_pre, normed_ref[...], TN).astype(BF))
    give_rows(1, sums_ref[1] + dot(d_pre, win_ref[...], NN))


def out(shape, dtype):
    return jax.ShapeDtypeStruct(shape, dtype)


def low(*shape):
    return pltpu.VMEM(shape, BF)


def attention(at, own, got, normed, cot, cos, sin):
    n = normed.shape[0]
    rows = 4 * own[0].shape[0]
    return pl.pallas_call(
        attention_kernel,
        out_shape=[out((2, n, D), F32), out((rows, D), BF), out((rows, D), BF)],
        in_specs=[SMEM] + [VM] * 12,
        out_specs=[VM] * 3,
        scratch_shapes=[low(2, rows, D), low(4 * HC, D), low(5 * HP, D), low(HP, D)]
        + [low(LEN, 2 * HP), low(LEN, 2 * HP), low(LEN, HP), low(LEN, HP)]
        + [low(n, HP), low(n, 3 * HP), low(4 * HC, D)],
        compiler_params=pltpu.CompilerParams(vmem_limit_bytes=32 << 20),
        cost_estimate=pl.CostEstimate(flops=12 * 10**9, bytes_accessed=16 << 20, transcendentals=10**6),
    )(at, *own, *got, normed, cot, cos, sin)


def feed_forward(at, held, normed, cot, bias, sums):
    n = normed.shape[0]
    span = held[0].shape[1]
    units = 4 * span
    return pl.pallas_call(
        forward_kernel,
        out_shape=[out((2, n // 2, D), F32), out((2, n // 2, D), F32), out((8, D), F32)] + [out((2, span, D), BF)] * 4,
        in_specs=[SMEM] + [VM] * 8,
        out_specs=[VM] * 7,
        scratch_shapes=[low(units, D), low(units, D)],
        compiler_params=pltpu.CompilerParams(vmem_limit_bytes=22 << 20),
        cost_estimate=pl.CostEstimate(flops=10 * 10**9, bytes_accessed=16 << 20, transcendentals=10**6),
    )(at, *held, normed, cot, bias, sums)


def body(tokens, cotangent, qkv_weight, out_weight, fc_weight, vectors, qkv_momentum, out_momentum, fc_momentum, vector_first, vector_second):
    zi, xi, yi, ci, ti = (lax.axis_index(a) for a in ALL)
    rows = tokens.shape[0]
    n_att = qkv_weight.shape[3]
    n_fc = fc_weight.shape[3]
    gain, shift = vectors[:D], vectors[D : 2 * D]
    bias_in, bias_out = vectors[2 * D : 2 * D + FF], vectors[2 * D + FF :]

    first = ci == 0
    attn_rows = jnp.concatenate([jnp.transpose(qkv_weight[:, :, 0, :], (0, 2, 1)), jnp.transpose(out_weight[:, 0, :])[None]])
    fc_rows = jnp.transpose(fc_weight[:, :, 0, :], (0, 2, 1))
    own_rows = jnp.concatenate([attn_rows.reshape(1, n_fc, D), fc_rows]).astype(BF)
    held = jnp.stack(gather_ring(own_rows, pull_yh, 2), axis=1)

    inputs = tokens.astype(F32)
    average = jnp.mean(inputs, axis=-1, keepdims=True)
    deviation = inputs - average
    variance = jnp.mean(deviation * deviation, axis=-1, keepdims=True)
    inv_spread = lax.rsqrt(variance + 1e-05)
    centred = deviation * inv_spread
    normed_own = (centred * gain + shift).astype(BF)
    both = jnp.stack([normed_own, cotangent])
    held = jnp.stack(gather_ring(held, pull_inner, 4), axis=1)
    both = jnp.stack([both, pull(both, "t", 1)], axis=1)
    held, both = lax.optimization_barrier((held, both))
    span = 8 * n_fc
    held = held.reshape(3, span, D)
    att_held = gather_ring(held[0], pull_outer, 4)
    fc_held = gather_ring(held[1:], pull_outer, 4)
    both = jnp.stack([both, pull(both, "c", 1)], axis=1)
    n_all = 4 * rows
    normed, cot = both[0].reshape(n_all, D), both[1].reshape(n_all, D)

    half = jnp.arange(LEN) // rows
    position = ((ti + half) % 2) * rows + jnp.arange(LEN) % rows
    frequency = 10000.0 ** (-2.0 * jnp.arange(ROT // 2, dtype=F32) / ROT)
    angles = position.astype(F32)[:, None] * frequency[None, :]
    cos_t, sin_t = jnp.cos(angles), jnp.sin(angles)
    pad = lambda a, b, fill: jnp.concatenate([a, b, jnp.full((LEN, PAD - ROT), fill, F32)], axis=1)
    cos_full, sin_full = pad(cos_t, cos_t, 1.0), pad(-sin_t, sin_t, 0.0)

    bias6 = bias_in.reshape(2, 4, 4, 2, 2, n_fc)
    bias6 = jnp.concatenate([bias6, bias6], axis=1)
    bias6 = jnp.concatenate([bias6, bias6], axis=2)
    bias6 = jnp.concatenate([bias6, bias6], axis=3)
    bias_own = lax.dynamic_slice(bias6, (ti, zi, xi, yi, ci, 0), (1, 4, 4, 2, 1, n_fc))[0, :, :, :, 0]
    by_turn = lambda v: jnp.where(first, jnp.swapaxes(v, 0, 1), v)
    bias_own = by_turn(bias_own).reshape(1, 32 * n_fc)
    at = jnp.stack([zi, xi, yi, ci, ti]).astype(jnp.int32)
    mom_rows = jnp.concatenate(
        [
            jnp.transpose(qkv_momentum[:, :, 0, :], (0, 2, 1)).reshape(3 * n_att, D),
            jnp.transpose(out_momentum[:, 0, :]),
            jnp.transpose(fc_momentum[:, :, 0, :], (0, 2, 1)).reshape(2 * n_fc, D),
        ]
    )
    att_held[2], normed, cot, bias_own, at, cos_full, sin_full, mom_rows = lax.optimization_barrier(
        (att_held[2], normed, cot, bias_own, at, cos_full, sin_full, mom_rows)
    )
    att_got = [pull(v, "c", 1) for v in att_held]
    sums, att_keep, att_give = attention(at, att_held, att_got, normed, cot, cos_full, sin_full)

    att_grad = (att_keep + pull(att_give, "c", 1)).reshape(4, span, D)
    att_parts = [att_grad[k] for k in range(4)]

    rows_own, rows_peer, grad_bias_in, *fc_parts = feed_forward(at, fc_held, normed, cot, bias_own, sums)
    att_total = sum_ring(att_parts, pull_outer)
    fc_total = sum_ring(fc_parts, pull_outer)
    rows_own = (rows_own + pull(rows_peer, "c", 1)).reshape(2, 2, rows, D)
    rows_own = rows_own[:, 0] + pull(rows_own[:, 1].astype(BF), "t", 1).astype(F32)
    att_total, fc_total, rows_own = lax.optimization_barrier((att_total, fc_total, rows_own))
    total = jnp.concatenate([att_total[None], fc_total]).reshape(3, 4, 2, n_fc, D)
    total = sum_ring([total[:, k] for k in range(4)], pull_inner)
    total = sum_ring([total[:, k] for k in range(2)], pull_yh).reshape(3 * n_fc, D)

    mixed = (inputs + rows_own[0] + bias_out).astype(BF)
    d_rows = rows_own[1]
    d_hat = d_rows * gain
    correction = d_hat - jnp.mean(d_hat, axis=-1, keepdims=True) - centred * jnp.mean(d_hat * centred, axis=-1, keepdims=True)
    own_cot = cotangent.astype(F32)
    input_grad = own_cot + correction * inv_spread

    total_of = lambda v: jnp.sum(v, axis=0, keepdims=True)
    vec_rows = [total_of(d_rows * centred), total_of(d_rows), grad_bias_in[: FF // D], total_of(own_cot), jnp.zeros((VEC_ROWS - VEC // D, D), F32)]

    moment = 0.95 * mom_rows + total
    update = total + 0.95 * moment

    half_fc = n_fc // 2
    att_u = update[: 4 * n_att].reshape(4, n_att, D)
    att_u = jnp.concatenate([att_u, jnp.zeros((4, half_fc - n_att, D), F32)], axis=1)
    fc_u = update[4 * n_att :].reshape(4, half_fc, D)
    vec_rows = jnp.concatenate(vec_rows)
    chunks = jnp.concatenate([att_u, fc_u])
    chunks = jnp.concatenate([chunks, jnp.broadcast_to(vec_rows, (8, VEC_ROWS, D))], axis=1)
    got = lax.all_to_all(chunks, ("z", "t"), split_axis=0, concat_axis=0, tiled=True)
    mine = got[:, :half_fc].reshape(8 * half_fc, D)
    vec_sum = jnp.sum(got[:, half_fc:], axis=0)[:8]
    keep, *give = gram_parts(at, mine, vec_sum)
    along_x = lambda v, k: pull(v, "x", k)
    load = [jnp.concatenate([keep[k * QUARTER : (k + 1) * QUARTER], vec_sum]) + pull(give[k], "c", 1) for k in range(4)]
    load = load[0] + along_x(load[1], 3) + along_x(load[2], 2) + along_x(load[3], 1)
    load = load + pull(load, "yh", 1)
    part, vec_sum = load[:QUARTER], load[QUARTER:]
    part = jnp.where(zi >= 2, part + pull(part, "t", 1), part)
    part = gather_ring(part, along_x, 4)
    rest = [pull(v, "c", 1) for v in part]
    x_rows = sweeps(at, part, rest, mine)
    x_rows, moment = lax.optimization_barrier((x_rows, moment))
    vector_grad = vec_sum[: VEC // D].reshape(VEC)
    first_new = 0.9 * vector_first + 0.1 * vector_grad
    second_new = 0.95 * vector_second + 0.05 * vector_grad * vector_grad
    step_size = first_new / (1.0 - 0.9**STEP) / (jnp.sqrt(second_new / (1.0 - 0.95**STEP)) + 1e-08)
    vector_new = vectors - 0.2 * step_size

    back = lax.all_to_all(x_rows, ("z", "t"), split_axis=0, concat_axis=0, tiled=True).astype(F32)
    att_x = back[:4, :n_att]
    fc_x = back[4:].reshape(2, n_fc, D)

    def cols(v):
        return jnp.transpose(v, (0, 2, 1))[:, :, None, :]

    fc_factor = math.sqrt(FF / D)
    qkv_new = qkv_weight * 0.99 - cols(att_x[:3])
    out_new = out_weight * 0.99 - cols(att_x[3:])[0]
    fc_new = fc_weight * 0.99 - fc_factor * cols(fc_x)
    att_m = moment[: 4 * n_att].reshape(4, n_att, D)
    fc_m = moment[4 * n_att :].reshape(2, n_fc, D)
    return (mixed, input_grad, qkv_new, out_new, fc_new, cols(att_m[:3]), cols(att_m[3:])[0], cols(fc_m), first_new, second_new, vector_new)


def solution(mesh):
    mesh = Mesh(mesh.devices.reshape(4, 4, 2, 2, 2), ALL)
    rows = P(ALL, None)
    w3 = P(None, None, "t", DP)
    w2 = P(None, "t", DP)
    vec = P()
    in_specs = (rows, rows, w3, w2, w3, vec, w3, w2, w3, vec, vec)
    out_specs = (rows, rows, w3, w2, w3, w3, w2, w3, vec, vec, vec)
    return jax.shard_map(body, mesh=mesh, in_specs=in_specs, out_specs=out_specs, check_vma=False)
```

```python
import functools
import itertools
import math

import jax
import jax.numpy as jnp
from jax import lax
from jax.experimental import pallas as pl
from jax.experimental.pallas import tpu as pltpu
from jax.sharding import Mesh, PartitionSpec as P

D = 768
H = 12
HD = 64
ROT = 16
FF = 3072
SWEEPS = 5
STEP = 10
LEN = 256
VEC = 2 * D + FF + D

NS = (3.4445, -4.775, 2.0315)
BF = jnp.bfloat16
F32 = jnp.float32
BLK = 256
QUARTER = 64
NB = D // BLK

DP = ("z", "x", "yh", "c")
ALL = ("z", "x", "yh", "c", "t")


def pull(value, axis, k):
    n = lax.axis_size(axis)
    return lax.ppermute(value, axis, [((i + k) % n, i) for i in range(n)])


def move(value, source):
    sizes = [lax.axis_size(a) for a in ALL]
    index = lambda at: functools.reduce(lambda total, one: total * one[0] + one[1] % one[0], zip(sizes, at), 0)
    pairs = []
    for here in itertools.product(*map(range, sizes)):
        there = source(*here)
        if there is not None:
            pairs.append((index(there), index(here)))
    return lax.ppermute(value, ALL, pairs)


def pull_outer(value, k):
    return move(value, lambda z, x, y, c, t: (z, x + k, y, c, t) if c == 0 else (z + k, x, y, c, t))


def pull_inner(value, k):
    return move(value, lambda z, x, y, c, t: (z + k, x, y, c, t) if c == 0 else (z, x + k, y, c, t))


def pull_yh(value, k):
    return pull(value, "yh", k)


def gather_ring(value, pulls, n):
    return [value] + [pulls(value, k) for k in range(1, n)]


def sum_ring(parts, pulls):
    n = len(parts)
    total = parts[0].astype(F32)
    for k in range(1, n):
        total = total + pulls(parts[k].astype(BF), n - k).astype(F32)
    return total


def dot(a, b, dims):
    return lax.dot_general(a, b, (dims, ((), ())), preferred_element_type=F32)


def pieces(value, n):
    out = []
    for _ in range(n):
        low = value.astype(BF)
        out.append(low)
        value = value - low.astype(F32)
    return out


def mul(xs, ys, dims=((1,), (0,))):
    n = len(xs)
    total = None
    for order in reversed(range(n)):
        for i in range(order + 1):
            term = lax.dot_general(xs[i], ys[order - i], (dims, ((), ())), preferred_element_type=F32)
            total = term if total is None else total + term
    return total


def gram_kernel(at_ref, rows_ref, keep_ref, give0_ref, give1_ref, give2_ref, give3_ref, top_ref, bottom_ref):
    xs = pieces(rows_ref[...], 3)
    dims = ((0,), (0,))
    cut = lambda i: slice(i * BLK, (i + 1) * BLK)
    top_ref[...] = mul([x[:, cut(0)] for x in xs], xs, dims)
    bottom_ref[:, : 2 * BLK] = mul([x[:, cut(1)] for x in xs], [x[:, BLK:] for x in xs], dims)
    bottom_ref[:, 2 * BLK :] = mul([x[:, cut(2)] for x in xs], [x[:, 2 * BLK :] for x in xs], dims)

    def keep(in_ref):
        for k in range(4):
            place = pl.multiple_of(jnp.bitwise_and(at_ref[1] + k, 3) * QUARTER, QUARTER)
            keep_ref[k * QUARTER : (k + 1) * QUARTER] = in_ref[pl.ds(place, QUARTER)]

    def give(in_ref):
        for k, ref in enumerate((give0_ref, give1_ref, give2_ref, give3_ref)):
            place = pl.multiple_of(jnp.bitwise_and(at_ref[1] + k, 3) * QUARTER, QUARTER)
            ref[...] = in_ref[pl.ds(place, QUARTER)]

    first = at_ref[3] == 0

    @pl.when(first)
    def _():
        keep(top_ref)
        give(bottom_ref)

    @pl.when(jnp.logical_not(first))
    def _():
        keep(bottom_ref)
        give(top_ref)


def blocks(i, j):
    return (slice(i * BLK, (i + 1) * BLK), slice(j * BLK, (j + 1) * BLK))


def put(refs, i, j, value):
    for ref, piece in zip(refs, pieces(value, len(refs))):
        ref[blocks(i, j)] = piece


def put_both(refs, i, j, value):
    put(refs, i, j, value)
    if i != j:
        put(refs, j, i, value.T)


def symmetric_product(xs, ys, emit, start=0):
    for i in range(start, NB):
        rows = slice(i * BLK, (i + 1) * BLK)
        wide = mul([x[rows, :] for x in xs], [y[:, i * BLK :] for y in ys])
        for j in range(i, NB):
            emit(i, j, wide[:, (j - i) * BLK : (j - i + 1) * BLK])


def sweeps_kernel(at_ref, *refs):
    sweeps_math(at_ref, refs[:4], refs[4:8], *refs[8:])


def sweeps_math(at_ref, mine_refs, rest_refs, x_ref, out_ref, top_ref, bottom_ref, gram_ref, a_ref, p_ref, b_ref):
    first = at_ref[3] == 0
    n_x = x_ref.shape[0]

    def by_place(out_ref, in_refs):
        for k, ref in enumerate(in_refs):
            place = pl.multiple_of(jnp.bitwise_and(at_ref[1] + k, 3) * QUARTER, QUARTER)
            out_ref[pl.ds(place, QUARTER)] = ref[...]

    @pl.when(first)
    def _():
        by_place(top_ref, mine_refs)
        by_place(bottom_ref, rest_refs)

    @pl.when(jnp.logical_not(first))
    def _():
        by_place(top_ref, rest_refs)
        by_place(bottom_ref, mine_refs)

    def packed(i, j):
        if i == 0:
            return top_ref[:, j * BLK : (j + 1) * BLK]
        at = (j - 1) if i == 1 else 2
        return bottom_ref[:, at * BLK : (at + 1) * BLK]

    eye = (lax.broadcasted_iota(jnp.int32, (BLK, BLK), 0) == lax.broadcasted_iota(jnp.int32, (BLK, BLK), 1)).astype(F32)
    trace = sum(jnp.sum(packed(i, i) * eye) for i in range(NB))
    norm = jnp.sqrt(jnp.full((8, 128), trace, F32)) + 1e-07
    factor = (1.0 / norm)[0:1, 0:1]
    square = factor * factor

    a_rows = lambda n: [a_ref.at[k, n_x : n_x + D] for k in range(n)]
    p_rows = lambda n: [p_ref.at[k] for k in range(n)]
    b_rows = lambda n: [b_ref.at[k] for k in range(n)]

    def put_x(n, value):
        for k, piece in enumerate(pieces(value, n)):
            a_ref[k, :n_x] = piece

    for i in range(NB):
        for j in range(i, NB):
            value = packed(i, j) * square
            gram_ref[blocks(i, j)] = value
            put_both(a_rows(2), i, j, value)
    put_x(2, x_ref[...] * factor)

    def poly(n_p):
        def emit(i, j, block):
            value = NS[1] * gram_ref[blocks(i, j)] + NS[2] * block
            if i == j:
                value = value + NS[0] * eye
            put_both(p_rows(n_p), i, j, value)

        a = a_rows(2)
        symmetric_product(a, a, emit)

    def next_gram(n, keep):
        p = p_rows(n)
        rows = slice(0, n_x + BLK)
        wide = mul([a_ref[k, rows] for k in range(n)], [y[...] for y in p])
        for j in range(NB):
            put_both(b_rows(n), 0, j, wide[n_x:, j * BLK : (j + 1) * BLK])
        symmetric_product(a_rows(n), p, lambda i, j, block: put_both(b_rows(n), i, j, block), 1)
        put_x(keep, wide[:n_x])

        def emit(i, j, block):
            gram_ref[blocks(i, j)] = block
            put_both(a_rows(keep), i, j, block)

        symmetric_product(b_rows(n), p, emit)

    @pl.loop(0, SWEEPS - 1)
    def _(_):
        poly(2)
        next_gram(2, 2)

    poly(2)
    last = mul([a_ref[k, :n_x] for k in range(2)], [y[...] for y in p_rows(2)]).astype(BF)
    n = out_ref.shape[1]
    for k in range(out_ref.shape[0]):
        out_ref[k] = last[k * n : (k + 1) * n]


SMEM = pl.BlockSpec(memory_space=pltpu.SMEM)
VM = pl.BlockSpec(memory_space=pltpu.VMEM)


def gram_parts(at, rows):
    return pl.pallas_call(
        gram_kernel,
        out_shape=[jax.ShapeDtypeStruct((BLK, D), F32)] + [jax.ShapeDtypeStruct((QUARTER, D), F32)] * 4,
        in_specs=[SMEM, VM],
        out_specs=[VM] * 5,
        scratch_shapes=[pltpu.VMEM((BLK, D), F32)] * 2,
        compiler_params=pltpu.CompilerParams(vmem_limit_bytes=14 << 20),
        cost_estimate=pl.CostEstimate(flops=2 * 96 * D * D * 4, bytes_accessed=4 * D * D * 2, transcendentals=0),
    )(at, rows)


def sweeps(at, mine, rest, x_rows):
    return pl.pallas_call(
        sweeps_kernel,
        out_shape=jax.ShapeDtypeStruct((8, x_rows.shape[0] // 8, D), BF),
        in_specs=[SMEM] + [VM] * 9,
        out_specs=VM,
        scratch_shapes=[
            pltpu.VMEM((BLK, D), F32),
            pltpu.VMEM((BLK, D), F32),
            pltpu.VMEM((D, D), F32),
            pltpu.VMEM((3, x_rows.shape[0] + D, D), BF),
            pltpu.VMEM((3, D, D), BF),
            pltpu.VMEM((3, D, D), BF),
        ],
        compiler_params=pltpu.CompilerParams(vmem_limit_bytes=24 << 20),
        cost_estimate=pl.CostEstimate(flops=2 * D * D * D * 32, bytes_accessed=4 * D * D, transcendentals=0),
    )(at, *mine, *rest, x_rows)


def gelu_parts(u):
    k0 = math.sqrt(2.0 / math.pi)
    th = jnp.tanh(k0 * (u + 0.044715 * (u * u * u)))
    value = 0.5 * u * (1.0 + th)
    slope = 0.5 * (1.0 + th) + 0.5 * u * (1.0 - th * th) * (k0 * (1.0 + 3.0 * 0.044715 * u * u))
    return value, slope


HEADS = 3
PAD = 128
HC = HEADS * HD
HP = HEADS * PAD
NN = ((1,), (0,))
NT = ((1,), (1,))
TN = ((0,), (0,))


def iota(shape, dim):
    return lax.broadcasted_iota(jnp.int32, shape, dim)


def one_hot(cond):
    return jnp.where(cond, 1.0, 0.0).astype(BF)


def unit_place(at_ref, n):
    zi, xi, yi, ci, ti = (at_ref[k] for k in range(5))
    width = 24
    group = jnp.right_shift(n * 2731, 16)
    lane = n - width * group
    y = jnp.bitwise_and(group + yi, 1)
    inner = jnp.bitwise_and(jnp.right_shift(group, 1), 3)
    outer = jnp.bitwise_and(jnp.right_shift(group, 3), 3)
    z = jnp.bitwise_and(jnp.where(ci == 0, inner, outer) + zi, 3)
    x = jnp.bitwise_and(jnp.where(ci == 0, outer, inner) + xi, 3)
    row = 2 * ti + jnp.right_shift(z, 1)
    return row, (((jnp.bitwise_and(z, 1) * 4 + x) * 2 + y) * 2 + ci) * width + lane


def needed_blocks(at_ref):
    zi, ci = at_ref[0], at_ref[3]
    for rc in range(2):
        core_0 = jnp.bitwise_xor(ci, rc) == 0
        for x in range(4):
            for j in range(2):
                z = jnp.bitwise_and(2 * ci + j - zi, 3)
                outer, inner = jnp.where(core_0, x, z), jnp.where(core_0, z, x)
                yield rc, pl.multiple_of((outer * 4 + inner) * 48, 48)


def home_place(at_ref, r):
    xi, yi, ci = (at_ref[k] for k in range(1, 4))
    n = 6
    group = jnp.right_shift(r * 10923, 16)
    lane = r - n * group
    mat = jnp.bitwise_and(group, 3)
    y = jnp.bitwise_and(jnp.right_shift(group, 2) + yi, 1)
    j = jnp.bitwise_and(jnp.right_shift(group, 3), 1)
    x = jnp.bitwise_and(jnp.right_shift(group, 4) + xi, 3)
    core = jnp.bitwise_and(jnp.right_shift(group, 6) + ci, 1)
    return mat * HC + (((j * 4 + x) * 2 + y) * 2 + core) * n + lane


def attention_kernel(
    at_ref, own0_ref, own1_ref, own2_ref, own3_ref, got0_ref, got1_ref, got2_ref, got3_ref, normed_ref, cot_ref, cos_ref, sin_ref,
    sums_ref, keep_ref, give_ref,
    att_ref, near_ref, w_ref, wo_ref, q_ref, k_ref, v_ref, da_ref, heads_ref, d_ref, nat_ref,
):
    span = own0_ref.shape[0]
    for k, ref in enumerate((own0_ref, own1_ref, own2_ref, own3_ref, got0_ref, got1_ref, got2_ref, got3_ref)):
        att_ref[k // 4, k % 4 * span : (k % 4 + 1) * span] = ref[...]
    block = span // 4
    for k, (rc, at) in enumerate(needed_blocks(at_ref)):
        near_ref[k * block : (k + 1) * block] = att_ref[rc, pl.ds(at, block)]

    n_rows = 4 * HC
    pick = one_hot(iota((n_rows, n_rows), 0) == home_place(at_ref, iota((8, n_rows), 1))[:1])
    w_att = dot(pick, near_ref[...], NN).astype(BF)
    r = iota((HC, HC), 0)
    e = jnp.bitwise_and(r, HD - 1)
    half = ROT // 2
    source = jnp.where(e < half, r + half, jnp.where(e < ROT, r - half, -1))
    exchange = one_hot(iota((HC, HC), 1) == source)
    blank = jnp.zeros((HD, D), BF)

    def padded(ref, base, rows):
        for h in range(HEADS):
            at = base + h * PAD
            ref[at : at + HD] = rows[h * HD : (h + 1) * HD]
            ref[at + HD : at + PAD] = blank

    for m in range(3):
        padded(w_ref, m * HP, w_att[m * HC : (m + 1) * HC])
    for m in range(2):
        padded(w_ref, (3 + m) * HP, dot(exchange, w_att[m * HC : (m + 1) * HC], NN).astype(BF))
    padded(wo_ref, 0, w_att[3 * HC :])

    cos, sin = cos_ref[...], sin_ref[...]
    turn = at_ref[4] * (LEN // 2)
    at_q = jnp.bitwise_xor(iota((LEN, LEN), 0), turn)
    at_k = jnp.bitwise_xor(iota((LEN, LEN), 1), turn)
    causal = at_q >= at_k
    scale = HD ** (-0.5)

    @pl.loop(0, 2)
    def _(s):
        rows = pl.ds(pl.multiple_of(s * LEN, LEN), LEN)
        normed = normed_ref[rows]
        for m, ref in ((0, q_ref), (1, k_ref)):
            lin = dot(normed, w_ref[m * HP : (m + 1) * HP], NT)
            lin_2 = dot(normed, w_ref[(3 + m) * HP : (4 + m) * HP], NT)
            for h in range(HEADS):
                lanes = slice(h * PAD, (h + 1) * PAD)
                base = h * 2 * PAD
                own, other = lin[:, lanes], lin_2[:, lanes]
                ref[:, base : base + PAD] = (own * cos + other * sin).astype(BF)
                ref[:, base + PAD : base + 2 * PAD] = (other * cos - own * sin).astype(BF)
        v_ref[...] = dot(normed, w_ref[2 * HP : 3 * HP], NT).astype(BF)
        da_ref[...] = dot(cot_ref[rows], wo_ref[...], NT).astype(BF)
        for h in range(HEADS):
            two = slice(h * 2 * PAD, (h + 1) * 2 * PAD)
            one = slice(h * 2 * PAD, h * 2 * PAD + PAD)
            lanes = slice(h * PAD, (h + 1) * PAD)
            value, d_att = v_ref[:, lanes], da_ref[:, lanes]
            scores = jnp.where(causal, dot(q_ref[:, one], k_ref[:, one], NT) * scale, -1e30)
            raised = jnp.exp(scores - jnp.max(scores, axis=1, keepdims=True))
            probs = raised / jnp.sum(raised, axis=1, keepdims=True)
            low = probs.astype(BF)
            heads_ref[rows, lanes] = dot(low, value, NN).astype(BF)
            d_ref[rows, 2 * HP + h * PAD : 2 * HP + (h + 1) * PAD] = dot(low, d_att, TN).astype(BF)
            d_probs = dot(d_att, value, NT)
            d_scores = (probs * (d_probs - jnp.sum(probs * d_probs, axis=1, keepdims=True))).astype(BF)
            d_q = dot(d_scores, k_ref[:, two], NN) * scale
            d_k = dot(d_scores, q_ref[:, two], TN) * scale
            for m, pair in ((0, d_q), (1, d_k)):
                at = m * HP + h * PAD
                d_ref[rows, at : at + PAD] = (pair[:, :PAD] * cos - pair[:, PAD:] * sin).astype(BF)

    sums_ref[0] = dot(heads_ref[...], wo_ref[...], NN)
    sums_ref[1] = dot(d_ref[...], w_ref[: 3 * HP], NN)

    for m in range(4):
        if m < 3:
            grad = dot(d_ref[:, m * HP : (m + 1) * HP], normed_ref[...], TN).astype(BF)
        else:
            grad = dot(heads_ref[...], cot_ref[...], TN).astype(BF)
        for h in range(HEADS):
            nat_ref[m * HC + h * HD : m * HC + (h + 1) * HD] = grad[h * PAD : h * PAD + HD]
    place = home_place(at_ref, iota((n_rows, 128), 0))
    pick = jnp.concatenate([one_hot(iota((n_rows, 128), 1) + b == place) for b in range(0, n_rows, 128)], axis=1)
    near_ref[...] = dot(pick, nat_ref[...], NN).astype(BF)
    keep_ref[...] = jnp.zeros_like(keep_ref)
    give_ref[...] = jnp.zeros_like(give_ref)
    for k, (rc, at) in enumerate(needed_blocks(at_ref)):
        (keep_ref, give_ref)[rc][pl.ds(at, block)] = near_ref[k * block : (k + 1) * block]


def forward_kernel(
    at_ref, held0_ref, held1_ref, held2_ref, held3_ref, normed_ref, cot_ref, bias_ref, sums_ref,
    own_ref, peer_ref, gbias_ref, out0_ref, out1_ref, out2_ref, out3_ref,
    win_ref, wback_ref,
):
    span = held0_ref.shape[1]
    for s, ref in enumerate((held0_ref, held1_ref, held2_ref, held3_ref)):
        win_ref[s * span : (s + 1) * span] = ref[0]
        wback_ref[s * span : (s + 1) * span] = ref[1]

    def send(group, grad):
        for s, ref in enumerate((out0_ref, out1_ref, out2_ref, out3_ref)):
            ref[group] = grad[s * span : (s + 1) * span]

    hidden, slope = gelu_parts(dot(normed_ref[...], win_ref[...], NT) + bias_ref[...])
    hidden = hidden.astype(BF)


    def give_rows(k, value):
        own_ref[k] = value[:LEN]
        peer_ref[k] = value[LEN:]

    give_rows(0, sums_ref[0] + dot(hidden, wback_ref[...], NN))
    send(1, dot(hidden, cot_ref[...], TN).astype(BF))
    d_pre = (dot(cot_ref[...], wback_ref[...], NT) * slope).astype(BF)
    grad_bias = jnp.sum(d_pre.astype(F32), axis=0, keepdims=True)
    n_units = win_ref.shape[0]
    bias_row, _ = unit_place(at_ref, iota((8, n_units), 1))
    spread = pieces(jnp.where(bias_row == iota((8, n_units), 0), grad_bias, 0.0), 3)
    _, bias_lane = unit_place(at_ref, iota((n_units, 128), 0))
    to_lane = jnp.concatenate([one_hot(iota((n_units, 128), 1) + b == bias_lane) for b in range(0, D, 128)], axis=1)
    gbias_ref[...] = sum(dot(piece, to_lane, NN) for piece in reversed(spread))
    send(0, dot(d_pre, normed_ref[...], TN).astype(BF))
    give_rows(1, sums_ref[1] + dot(d_pre, win_ref[...], NN))


def out(shape, dtype):
    return jax.ShapeDtypeStruct(shape, dtype)


def low(*shape):
    return pltpu.VMEM(shape, BF)


def attention(at, own, got, normed, cot, cos, sin):
    n = normed.shape[0]
    rows = 4 * own[0].shape[0]
    return pl.pallas_call(
        attention_kernel,
        out_shape=[out((2, n, D), F32), out((rows, D), BF), out((rows, D), BF)],
        in_specs=[SMEM] + [VM] * 12,
        out_specs=[VM] * 3,
        scratch_shapes=[low(2, rows, D), low(4 * HC, D), low(5 * HP, D), low(HP, D)]
        + [low(LEN, 2 * HP), low(LEN, 2 * HP), low(LEN, HP), low(LEN, HP)]
        + [low(n, HP), low(n, 3 * HP), low(4 * HC, D)],
        compiler_params=pltpu.CompilerParams(vmem_limit_bytes=32 << 20),
        cost_estimate=pl.CostEstimate(flops=12 * 10**9, bytes_accessed=16 << 20, transcendentals=10**6),
    )(at, *own, *got, normed, cot, cos, sin)


def feed_forward(at, held, normed, cot, bias, sums):
    n = normed.shape[0]
    span = held[0].shape[1]
    units = 4 * span
    return pl.pallas_call(
        forward_kernel,
        out_shape=[out((2, n // 2, D), F32), out((2, n // 2, D), F32), out((8, D), F32)] + [out((2, span, D), BF)] * 4,
        in_specs=[SMEM] + [VM] * 8,
        out_specs=[VM] * 7,
        scratch_shapes=[low(units, D), low(units, D)],
        compiler_params=pltpu.CompilerParams(vmem_limit_bytes=22 << 20),
        cost_estimate=pl.CostEstimate(flops=10 * 10**9, bytes_accessed=16 << 20, transcendentals=10**6),
    )(at, *held, normed, cot, bias, sums)


def body(tokens, cotangent, qkv_weight, out_weight, fc_weight, vectors, qkv_momentum, out_momentum, fc_momentum, vector_first, vector_second):
    zi, xi, yi, ci, ti = (lax.axis_index(a) for a in ALL)
    rows = tokens.shape[0]
    n_att = qkv_weight.shape[3]
    n_fc = fc_weight.shape[3]
    gain, shift = vectors[:D], vectors[D : 2 * D]
    bias_in, bias_out = vectors[2 * D : 2 * D + FF], vectors[2 * D + FF :]

    first = ci == 0
    attn_rows = jnp.concatenate([jnp.transpose(qkv_weight[:, :, 0, :], (0, 2, 1)), jnp.transpose(out_weight[:, 0, :])[None]])
    fc_rows = jnp.transpose(fc_weight[:, :, 0, :], (0, 2, 1))
    own_rows = jnp.concatenate([attn_rows.reshape(1, n_fc, D), fc_rows]).astype(BF)
    held = jnp.stack(gather_ring(own_rows, pull_yh, 2), axis=1)

    inputs = tokens.astype(F32)
    average = jnp.mean(inputs, axis=-1, keepdims=True)
    deviation = inputs - average
    variance = jnp.mean(deviation * deviation, axis=-1, keepdims=True)
    inv_spread = lax.rsqrt(variance + 1e-05)
    centred = deviation * inv_spread
    normed_own = (centred * gain + shift).astype(BF)
    both = jnp.stack([normed_own, cotangent])
    held = jnp.stack(gather_ring(held, pull_inner, 4), axis=1)
    both = jnp.stack([both, pull(both, "t", 1)], axis=1)
    held, both = lax.optimization_barrier((held, both))
    span = 8 * n_fc
    held = held.reshape(3, span, D)
    att_held = gather_ring(held[0], pull_outer, 4)
    fc_held = gather_ring(held[1:], pull_outer, 4)
    both = jnp.stack([both, pull(both, "c", 1)], axis=1)
    n_all = 4 * rows
    normed, cot = both[0].reshape(n_all, D), both[1].reshape(n_all, D)

    half = jnp.arange(LEN) // rows
    position = ((ti + half) % 2) * rows + jnp.arange(LEN) % rows
    frequency = 10000.0 ** (-2.0 * jnp.arange(ROT // 2, dtype=F32) / ROT)
    angles = position.astype(F32)[:, None] * frequency[None, :]
    cos_t, sin_t = jnp.cos(angles), jnp.sin(angles)
    pad = lambda a, b, fill: jnp.concatenate([a, b, jnp.full((LEN, PAD - ROT), fill, F32)], axis=1)
    cos_full, sin_full = pad(cos_t, cos_t, 1.0), pad(-sin_t, sin_t, 0.0)

    bias6 = bias_in.reshape(2, 4, 4, 2, 2, n_fc)
    bias6 = jnp.concatenate([bias6, bias6], axis=1)
    bias6 = jnp.concatenate([bias6, bias6], axis=2)
    bias6 = jnp.concatenate([bias6, bias6], axis=3)
    bias_own = lax.dynamic_slice(bias6, (ti, zi, xi, yi, ci, 0), (1, 4, 4, 2, 1, n_fc))[0, :, :, :, 0]
    by_turn = lambda v: jnp.where(first, jnp.swapaxes(v, 0, 1), v)
    bias_own = by_turn(bias_own).reshape(1, 32 * n_fc)
    at = jnp.stack([zi, xi, yi, ci, ti]).astype(jnp.int32)
    mom_rows = jnp.concatenate(
        [
            jnp.transpose(qkv_momentum[:, :, 0, :], (0, 2, 1)).reshape(3 * n_att, D),
            jnp.transpose(out_momentum[:, 0, :]),
            jnp.transpose(fc_momentum[:, :, 0, :], (0, 2, 1)).reshape(2 * n_fc, D),
        ]
    )
    att_held[2], normed, cot, bias_own, at, cos_full, sin_full, mom_rows = lax.optimization_barrier(
        (att_held[2], normed, cot, bias_own, at, cos_full, sin_full, mom_rows)
    )
    att_got = [pull(v, "c", 1) for v in att_held]
    sums, att_keep, att_give = attention(at, att_held, att_got, normed, cot, cos_full, sin_full)

    att_grad = (att_keep + pull(att_give, "c", 1)).reshape(4, span, D)
    att_parts = [att_grad[k] for k in range(4)]

    rows_own, rows_peer, grad_bias_in, *fc_parts = feed_forward(at, fc_held, normed, cot, bias_own, sums)
    att_total = sum_ring(att_parts, pull_outer)
    fc_total = sum_ring(fc_parts, pull_outer)
    rows_own = (rows_own + pull(rows_peer, "c", 1)).reshape(2, 2, rows, D)
    rows_own = rows_own[:, 0] + pull(rows_own[:, 1].astype(BF), "t", 1).astype(F32)
    att_total, fc_total, rows_own = lax.optimization_barrier((att_total, fc_total, rows_own))
    mixed = (inputs + rows_own[0] + bias_out).astype(BF)
    d_rows = rows_own[1]
    d_hat = d_rows * gain
    correction = d_hat - jnp.mean(d_hat, axis=-1, keepdims=True) - centred * jnp.mean(d_hat * centred, axis=-1, keepdims=True)
    own_cot = cotangent.astype(F32)
    input_grad = own_cot + correction * inv_spread

    total_of = lambda v: jnp.sum(v, axis=0, keepdims=True)
    vec_rows = [total_of(d_rows * centred), total_of(d_rows), grad_bias_in[: FF // D], total_of(own_cot), jnp.zeros((1, D), F32)]
    vec_sum = jnp.concatenate(vec_rows)
    beside = lambda value, flip, axis: value + (pull(value, axis, 1) if axis in ("c", "t", "yh") else lax.ppermute(value, axis, [(i, i ^ flip) for i in range(4)]))

    total = jnp.concatenate([att_total[None], fc_total]).reshape(3, 4, 2, n_fc, D)
    total = sum_ring([total[:, k] for k in range(4)], pull_inner)
    total, vec_sum = lax.optimization_barrier((total, beside(beside(vec_sum, 1, "c"), 1, "t")))
    total = sum_ring([total[:, k] for k in range(2)], pull_yh).reshape(3 * n_fc, D)
    total, vec_sum = lax.optimization_barrier((total, beside(vec_sum, 1, "yh")))
    moment = 0.95 * mom_rows + total
    update = total + 0.95 * moment

    half_fc = n_fc // 2
    att_u = update[: 4 * n_att].reshape(4, n_att, D)
    att_u = jnp.concatenate([att_u, jnp.zeros((4, half_fc - n_att, D), F32)], axis=1)
    fc_u = update[4 * n_att :].reshape(4, half_fc, D)
    chunks = jnp.concatenate([att_u, fc_u])
    got = lax.all_to_all(chunks, ("z", "t"), split_axis=0, concat_axis=0, tiled=True)
    mine = got.reshape(8 * half_fc, D)
    keep, *give = gram_parts(at, mine)
    along_x = lambda v, k: pull(v, "x", k)
    load = [keep[k * QUARTER : (k + 1) * QUARTER] + pull(give[k], "c", 1) for k in range(4)]
    part = load[0] + along_x(load[1], 3) + along_x(load[2], 2) + along_x(load[3], 1)
    part, vec_sum = lax.optimization_barrier((part, beside(beside(vec_sum, 1, "z"), 2, "z")))
    part = part + pull(part, "yh", 1)
    part, vec_sum = lax.optimization_barrier((part, beside(vec_sum, 1, "x")))
    part = jnp.where(zi >= 2, part + pull(part, "t", 1), part)
    part, vec_sum = lax.optimization_barrier((part, beside(vec_sum, 2, "x")))
    part = gather_ring(part, along_x, 4)
    rest = [pull(v, "c", 1) for v in part]
    x_rows = sweeps(at, part, rest, mine)
    x_rows, moment = lax.optimization_barrier((x_rows, moment))
    vector_grad = vec_sum[: VEC // D].reshape(VEC)
    first_new = 0.9 * vector_first + 0.1 * vector_grad
    second_new = 0.95 * vector_second + 0.05 * vector_grad * vector_grad
    step_size = first_new / (1.0 - 0.9**STEP) / (jnp.sqrt(second_new / (1.0 - 0.95**STEP)) + 1e-08)
    vector_new = vectors - 0.2 * step_size

    back = lax.all_to_all(x_rows, ("z", "t"), split_axis=0, concat_axis=0, tiled=True).astype(F32)
    att_x = back[:4, :n_att]
    fc_x = back[4:].reshape(2, n_fc, D)

    def cols(v):
        return jnp.transpose(v, (0, 2, 1))[:, :, None, :]

    fc_factor = math.sqrt(FF / D)
    qkv_new = qkv_weight * 0.99 - cols(att_x[:3])
    out_new = out_weight * 0.99 - cols(att_x[3:])[0]
    fc_new = fc_weight * 0.99 - fc_factor * cols(fc_x)
    att_m = moment[: 4 * n_att].reshape(4, n_att, D)
    fc_m = moment[4 * n_att :].reshape(2, n_fc, D)
    return (mixed, input_grad, qkv_new, out_new, fc_new, cols(att_m[:3]), cols(att_m[3:])[0], cols(fc_m), first_new, second_new, vector_new)


def solution(mesh):
    mesh = Mesh(mesh.devices.reshape(4, 4, 2, 2, 2), ALL)
    rows = P(ALL, None)
    w3 = P(None, None, "t", DP)
    w2 = P(None, "t", DP)
    vec = P()
    in_specs = (rows, rows, w3, w2, w3, vec, w3, w2, w3, vec, vec)
    out_specs = (rows, rows, w3, w2, w3, w3, w2, w3, vec, vec, vec)
    return jax.shard_map(body, mesh=mesh, in_specs=in_specs, out_specs=out_specs, check_vma=False)
```

```python
import functools
import itertools
import math

import jax
import jax.numpy as jnp
from jax import lax
from jax.experimental import pallas as pl
from jax.experimental.pallas import tpu as pltpu
from jax.sharding import Mesh, PartitionSpec as P

D = 768
H = 12
HD = 64
ROT = 16
FF = 3072
SWEEPS = 5
STEP = 10
LEN = 256
VEC = 2 * D + FF + D

NS = (3.4445, -4.775, 2.0315)
BF = jnp.bfloat16
F32 = jnp.float32
BLK = 256
QUARTER = 64
NB = D // BLK

DP = ("z", "x", "yh", "c")
ALL = ("z", "x", "yh", "c", "t")


def pull(value, axis, k):
    n = lax.axis_size(axis)
    return lax.ppermute(value, axis, [((i + k) % n, i) for i in range(n)])


def move(value, source):
    sizes = [lax.axis_size(a) for a in ALL]
    index = lambda at: functools.reduce(lambda total, one: total * one[0] + one[1] % one[0], zip(sizes, at), 0)
    pairs = []
    for here in itertools.product(*map(range, sizes)):
        there = source(*here)
        if there is not None:
            pairs.append((index(there), index(here)))
    return lax.ppermute(value, ALL, pairs)


def pull_outer(value, k):
    return move(value, lambda z, x, y, c, t: (z, x + k, y, c, t) if c == 0 else (z + k, x, y, c, t))


def pull_inner(value, k):
    return move(value, lambda z, x, y, c, t: (z + k, x, y, c, t) if c == 0 else (z, x + k, y, c, t))


def pull_yh(value, k):
    return pull(value, "yh", k)


def gather_ring(value, pulls, n):
    return [value] + [pulls(value, k) for k in range(1, n)]


def sum_ring(parts, pulls):
    n = len(parts)
    total = parts[0].astype(F32)
    for k in range(1, n):
        total = total + pulls(parts[k].astype(BF), n - k).astype(F32)
    return total


def dot(a, b, dims):
    return lax.dot_general(a, b, (dims, ((), ())), preferred_element_type=F32)


def pieces(value, n):
    out = []
    for _ in range(n):
        low = value.astype(BF)
        out.append(low)
        value = value - low.astype(F32)
    return out


def mul(xs, ys, dims=((1,), (0,))):
    n = len(xs)
    total = None
    for order in reversed(range(n)):
        for i in range(order + 1):
            term = lax.dot_general(xs[i], ys[order - i], (dims, ((), ())), preferred_element_type=F32)
            total = term if total is None else total + term
    return total


def gram_kernel(at_ref, rows_ref, keep_ref, give0_ref, give1_ref, give2_ref, give3_ref, top_ref, bottom_ref):
    xs = pieces(rows_ref[...], 3)
    dims = ((0,), (0,))
    cut = lambda i: slice(i * BLK, (i + 1) * BLK)
    top_ref[...] = mul([x[:, cut(0)] for x in xs], xs, dims)
    bottom_ref[:, : 2 * BLK] = mul([x[:, cut(1)] for x in xs], [x[:, BLK:] for x in xs], dims)
    bottom_ref[:, 2 * BLK :] = mul([x[:, cut(2)] for x in xs], [x[:, 2 * BLK :] for x in xs], dims)

    def keep(in_ref):
        for k in range(4):
            place = pl.multiple_of(jnp.bitwise_and(at_ref[1] + k, 3) * QUARTER, QUARTER)
            keep_ref[k * QUARTER : (k + 1) * QUARTER] = in_ref[pl.ds(place, QUARTER)]

    def give(in_ref):
        for k, ref in enumerate((give0_ref, give1_ref, give2_ref, give3_ref)):
            place = pl.multiple_of(jnp.bitwise_and(at_ref[1] + k, 3) * QUARTER, QUARTER)
            ref[...] = in_ref[pl.ds(place, QUARTER)]

    first = at_ref[3] == 0

    @pl.when(first)
    def _():
        keep(top_ref)
        give(bottom_ref)

    @pl.when(jnp.logical_not(first))
    def _():
        keep(bottom_ref)
        give(top_ref)


def blocks(i, j):
    return (slice(i * BLK, (i + 1) * BLK), slice(j * BLK, (j + 1) * BLK))


def put(refs, i, j, value):
    for ref, piece in zip(refs, pieces(value, len(refs))):
        ref[blocks(i, j)] = piece


def put_both(refs, i, j, value):
    put(refs, i, j, value)
    if i != j:
        put(refs, j, i, value.T)


def symmetric_product(xs, ys, emit, start=0):
    for i in range(start, NB):
        rows = slice(i * BLK, (i + 1) * BLK)
        wide = mul([x[rows, :] for x in xs], [y[:, i * BLK :] for y in ys])
        for j in range(i, NB):
            emit(i, j, wide[:, (j - i) * BLK : (j - i + 1) * BLK])


def sweeps_kernel(at_ref, *refs):
    sweeps_math(at_ref, refs[:4], refs[4:8], *refs[8:])


def sweeps_math(at_ref, mine_refs, rest_refs, x_ref, out_ref, top_ref, bottom_ref, gram_ref, a_ref, p_ref, b_ref):
    first = at_ref[3] == 0
    n_x = x_ref.shape[0]

    def by_place(out_ref, in_refs):
        for k, ref in enumerate(in_refs):
            place = pl.multiple_of(jnp.bitwise_and(at_ref[1] + k, 3) * QUARTER, QUARTER)
            out_ref[pl.ds(place, QUARTER)] = ref[...]

    @pl.when(first)
    def _():
        by_place(top_ref, mine_refs)
        by_place(bottom_ref, rest_refs)

    @pl.when(jnp.logical_not(first))
    def _():
        by_place(top_ref, rest_refs)
        by_place(bottom_ref, mine_refs)

    def packed(i, j):
        if i == 0:
            return top_ref[:, j * BLK : (j + 1) * BLK]
        at = (j - 1) if i == 1 else 2
        return bottom_ref[:, at * BLK : (at + 1) * BLK]

    eye = (lax.broadcasted_iota(jnp.int32, (BLK, BLK), 0) == lax.broadcasted_iota(jnp.int32, (BLK, BLK), 1)).astype(F32)
    trace = sum(jnp.sum(packed(i, i) * eye) for i in range(NB))
    norm = jnp.sqrt(jnp.full((8, 128), trace, F32)) + 1e-07
    factor = (1.0 / norm)[0:1, 0:1]
    square = factor * factor

    a_rows = lambda n: [a_ref.at[k, n_x : n_x + D] for k in range(n)]
    p_rows = lambda n: [p_ref.at[k] for k in range(n)]
    b_rows = lambda n: [b_ref.at[k] for k in range(n)]

    def put_x(n, value):
        for k, piece in enumerate(pieces(value, n)):
            a_ref[k, :n_x] = piece

    for i in range(NB):
        for j in range(i, NB):
            value = packed(i, j) * square
            gram_ref[blocks(i, j)] = value
            put_both(a_rows(2), i, j, value)
    put_x(2, x_ref[...] * factor)

    def poly(n_p):
        def emit(i, j, block):
            value = NS[1] * gram_ref[blocks(i, j)] + NS[2] * block
            if i == j:
                value = value + NS[0] * eye
            put_both(p_rows(n_p), i, j, value)

        a = a_rows(2)
        symmetric_product(a, a, emit)

    def next_gram(n, keep):
        p = p_rows(n)
        rows = slice(0, n_x + BLK)
        wide = mul([a_ref[k, rows] for k in range(n)], [y[...] for y in p])
        for j in range(NB):
            put_both(b_rows(n), 0, j, wide[n_x:, j * BLK : (j + 1) * BLK])
        symmetric_product(a_rows(n), p, lambda i, j, block: put_both(b_rows(n), i, j, block), 1)
        put_x(keep, wide[:n_x])

        def emit(i, j, block):
            gram_ref[blocks(i, j)] = block
            put_both(a_rows(keep), i, j, block)

        symmetric_product(b_rows(n), p, emit)

    @pl.loop(0, SWEEPS - 1)
    def _(_):
        poly(2)
        next_gram(2, 2)

    poly(2)
    last = mul([a_ref[k, :n_x] for k in range(2)], [y[...] for y in p_rows(2)]).astype(BF)
    n = out_ref.shape[1]
    for k in range(out_ref.shape[0]):
        out_ref[k] = last[k * n : (k + 1) * n]


SMEM = pl.BlockSpec(memory_space=pltpu.SMEM)
VM = pl.BlockSpec(memory_space=pltpu.VMEM)


def gram_parts(at, rows):
    return pl.pallas_call(
        gram_kernel,
        out_shape=[jax.ShapeDtypeStruct((BLK, D), F32)] + [jax.ShapeDtypeStruct((QUARTER, D), F32)] * 4,
        in_specs=[SMEM, VM],
        out_specs=[VM] * 5,
        scratch_shapes=[pltpu.VMEM((BLK, D), F32)] * 2,
        compiler_params=pltpu.CompilerParams(vmem_limit_bytes=14 << 20),
        cost_estimate=pl.CostEstimate(flops=2 * 96 * D * D * 4, bytes_accessed=4 * D * D * 2, transcendentals=0),
    )(at, rows)


def sweeps(at, mine, rest, x_rows):
    return pl.pallas_call(
        sweeps_kernel,
        out_shape=jax.ShapeDtypeStruct((8, x_rows.shape[0] // 8, D), BF),
        in_specs=[SMEM] + [VM] * 9,
        out_specs=VM,
        scratch_shapes=[
            pltpu.VMEM((BLK, D), F32),
            pltpu.VMEM((BLK, D), F32),
            pltpu.VMEM((D, D), F32),
            pltpu.VMEM((3, x_rows.shape[0] + D, D), BF),
            pltpu.VMEM((3, D, D), BF),
            pltpu.VMEM((3, D, D), BF),
        ],
        compiler_params=pltpu.CompilerParams(vmem_limit_bytes=24 << 20),
        cost_estimate=pl.CostEstimate(flops=2 * D * D * D * 32, bytes_accessed=4 * D * D, transcendentals=0),
    )(at, *mine, *rest, x_rows)


def gelu_parts(u):
    k0 = math.sqrt(2.0 / math.pi)
    th = jnp.tanh(k0 * (u + 0.044715 * (u * u * u)))
    value = 0.5 * u * (1.0 + th)
    slope = 0.5 * (1.0 + th) + 0.5 * u * (1.0 - th * th) * (k0 * (1.0 + 3.0 * 0.044715 * u * u))
    return value, slope


HEADS = 3
PAD = 128
HC = HEADS * HD
HP = HEADS * PAD
NN = ((1,), (0,))
NT = ((1,), (1,))
TN = ((0,), (0,))


def iota(shape, dim):
    return lax.broadcasted_iota(jnp.int32, shape, dim)


def one_hot(cond):
    return jnp.where(cond, 1.0, 0.0).astype(BF)


def unit_place(at_ref, n):
    zi, xi, yi, ci, ti = (at_ref[k] for k in range(5))
    width = 24
    group = jnp.right_shift(n * 2731, 16)
    lane = n - width * group
    y = jnp.bitwise_and(group + yi, 1)
    inner = jnp.bitwise_and(jnp.right_shift(group, 1), 3)
    outer = jnp.bitwise_and(jnp.right_shift(group, 3), 3)
    z = jnp.bitwise_and(jnp.where(ci == 0, inner, outer) + zi, 3)
    x = jnp.bitwise_and(jnp.where(ci == 0, outer, inner) + xi, 3)
    row = 2 * ti + jnp.right_shift(z, 1)
    return row, (((jnp.bitwise_and(z, 1) * 4 + x) * 2 + y) * 2 + ci) * width + lane


def needed_blocks(at_ref):
    zi, ci = at_ref[0], at_ref[3]
    for rc in range(2):
        core_0 = jnp.bitwise_xor(ci, rc) == 0
        for x in range(4):
            for j in range(2):
                z = jnp.bitwise_and(2 * ci + j - zi, 3)
                outer, inner = jnp.where(core_0, x, z), jnp.where(core_0, z, x)
                yield rc, pl.multiple_of((outer * 4 + inner) * 48, 48)


def home_place(at_ref, r):
    xi, yi, ci = (at_ref[k] for k in range(1, 4))
    n = 6
    group = jnp.right_shift(r * 10923, 16)
    lane = r - n * group
    mat = jnp.bitwise_and(group, 3)
    y = jnp.bitwise_and(jnp.right_shift(group, 2) + yi, 1)
    j = jnp.bitwise_and(jnp.right_shift(group, 3), 1)
    x = jnp.bitwise_and(jnp.right_shift(group, 4) + xi, 3)
    core = jnp.bitwise_and(jnp.right_shift(group, 6) + ci, 1)
    return mat * HC + (((j * 4 + x) * 2 + y) * 2 + core) * n + lane


def attention_kernel(
    at_ref, own0_ref, own1_ref, own2_ref, own3_ref, got0_ref, got1_ref, got2_ref, got3_ref, normed_ref, cot_ref, cos_ref, sin_ref,
    sums_ref, keep_ref, give_ref,
    att_ref, near_ref, w_ref, wo_ref, q_ref, k_ref, v_ref, da_ref, heads_ref, d_ref, nat_ref,
):
    span = own0_ref.shape[0]
    for k, ref in enumerate((own0_ref, own1_ref, own2_ref, own3_ref, got0_ref, got1_ref, got2_ref, got3_ref)):
        att_ref[k // 4, k % 4 * span : (k % 4 + 1) * span] = ref[...]
    block = span // 4
    for k, (rc, at) in enumerate(needed_blocks(at_ref)):
        near_ref[k * block : (k + 1) * block] = att_ref[rc, pl.ds(at, block)]

    n_rows = 4 * HC
    pick = one_hot(iota((n_rows, n_rows), 0) == home_place(at_ref, iota((8, n_rows), 1))[:1])
    w_att = dot(pick, near_ref[...], NN).astype(BF)
    r = iota((HC, HC), 0)
    e = jnp.bitwise_and(r, HD - 1)
    half = ROT // 2
    source = jnp.where(e < half, r + half, jnp.where(e < ROT, r - half, -1))
    exchange = one_hot(iota((HC, HC), 1) == source)
    blank = jnp.zeros((HD, D), BF)

    def padded(ref, base, rows):
        for h in range(HEADS):
            at = base + h * PAD
            ref[at : at + HD] = rows[h * HD : (h + 1) * HD]
            ref[at + HD : at + PAD] = blank

    for m in range(3):
        padded(w_ref, m * HP, w_att[m * HC : (m + 1) * HC])
    for m in range(2):
        padded(w_ref, (3 + m) * HP, dot(exchange, w_att[m * HC : (m + 1) * HC], NN).astype(BF))
    padded(wo_ref, 0, w_att[3 * HC :])

    cos, sin = cos_ref[...], sin_ref[...]
    turn = at_ref[4] * (LEN // 2)
    at_q = jnp.bitwise_xor(iota((LEN, LEN), 0), turn)
    at_k = jnp.bitwise_xor(iota((LEN, LEN), 1), turn)
    causal = at_q >= at_k
    scale = HD ** (-0.5)

    @pl.loop(0, 2)
    def _(s):
        rows = pl.ds(pl.multiple_of(s * LEN, LEN), LEN)
        normed = normed_ref[rows]
        for m, ref in ((0, q_ref), (1, k_ref)):
            lin = dot(normed, w_ref[m * HP : (m + 1) * HP], NT)
            lin_2 = dot(normed, w_ref[(3 + m) * HP : (4 + m) * HP], NT)
            for h in range(HEADS):
                lanes = slice(h * PAD, (h + 1) * PAD)
                base = h * 2 * PAD
                own, other = lin[:, lanes], lin_2[:, lanes]
                ref[:, base : base + PAD] = (own * cos + other * sin).astype(BF)
                ref[:, base + PAD : base + 2 * PAD] = (other * cos - own * sin).astype(BF)
        v_ref[...] = dot(normed, w_ref[2 * HP : 3 * HP], NT).astype(BF)
        da_ref[...] = dot(cot_ref[rows], wo_ref[...], NT).astype(BF)
        for h in range(HEADS):
            two = slice(h * 2 * PAD, (h + 1) * 2 * PAD)
            one = slice(h * 2 * PAD, h * 2 * PAD + PAD)
            lanes = slice(h * PAD, (h + 1) * PAD)
            value, d_att = v_ref[:, lanes], da_ref[:, lanes]
            scores = jnp.where(causal, dot(q_ref[:, one], k_ref[:, one], NT) * scale, -1e30)
            raised = jnp.exp(scores - jnp.max(scores, axis=1, keepdims=True))
            probs = raised / jnp.sum(raised, axis=1, keepdims=True)
            low = probs.astype(BF)
            heads_ref[rows, lanes] = dot(low, value, NN).astype(BF)
            d_ref[rows, 2 * HP + h * PAD : 2 * HP + (h + 1) * PAD] = dot(low, d_att, TN).astype(BF)
            d_probs = dot(d_att, value, NT)
            d_scores = (probs * (d_probs - jnp.sum(probs * d_probs, axis=1, keepdims=True))).astype(BF)
            d_q = dot(d_scores, k_ref[:, two], NN) * scale
            d_k = dot(d_scores, q_ref[:, two], TN) * scale
            for m, pair in ((0, d_q), (1, d_k)):
                at = m * HP + h * PAD
                d_ref[rows, at : at + PAD] = (pair[:, :PAD] * cos - pair[:, PAD:] * sin).astype(BF)

    sums_ref[0] = dot(heads_ref[...], wo_ref[...], NN)
    sums_ref[1] = dot(d_ref[...], w_ref[: 3 * HP], NN)

    for m in range(4):
        if m < 3:
            grad = dot(d_ref[:, m * HP : (m + 1) * HP], normed_ref[...], TN).astype(BF)
        else:
            grad = dot(heads_ref[...], cot_ref[...], TN).astype(BF)
        for h in range(HEADS):
            nat_ref[m * HC + h * HD : m * HC + (h + 1) * HD] = grad[h * PAD : h * PAD + HD]
    place = home_place(at_ref, iota((n_rows, 128), 0))
    pick = jnp.concatenate([one_hot(iota((n_rows, 128), 1) + b == place) for b in range(0, n_rows, 128)], axis=1)
    near_ref[...] = dot(pick, nat_ref[...], NN).astype(BF)
    keep_ref[...] = jnp.zeros_like(keep_ref)
    give_ref[...] = jnp.zeros_like(give_ref)
    for k, (rc, at) in enumerate(needed_blocks(at_ref)):
        (keep_ref, give_ref)[rc][pl.ds(at, block)] = near_ref[k * block : (k + 1) * block]


def forward_kernel(
    at_ref, held0_ref, held1_ref, held2_ref, held3_ref, normed_ref, cot_ref, bias_ref, sums_ref,
    own_ref, peer_ref, gbias_ref, out0_ref, out1_ref, out2_ref, out3_ref,
    win_ref, wback_ref,
):
    span = held0_ref.shape[1]
    for s, ref in enumerate((held0_ref, held1_ref, held2_ref, held3_ref)):
        win_ref[s * span : (s + 1) * span] = ref[0]
        wback_ref[s * span : (s + 1) * span] = ref[1]

    def send(group, grad):
        for s, ref in enumerate((out0_ref, out1_ref, out2_ref, out3_ref)):
            ref[group] = grad[s * span : (s + 1) * span]

    hidden, slope = gelu_parts(dot(normed_ref[...], win_ref[...], NT) + bias_ref[...])
    hidden = hidden.astype(BF)


    def give_rows(k, value):
        own_ref[k] = value[:LEN]
        peer_ref[k] = value[LEN:]

    give_rows(0, sums_ref[0] + dot(hidden, wback_ref[...], NN))
    send(1, dot(hidden, cot_ref[...], TN).astype(BF))
    d_pre = (dot(cot_ref[...], wback_ref[...], NT) * slope).astype(BF)
    grad_bias = jnp.sum(d_pre.astype(F32), axis=0, keepdims=True)
    n_units = win_ref.shape[0]
    bias_row, _ = unit_place(at_ref, iota((8, n_units), 1))
    spread = pieces(jnp.where(bias_row == iota((8, n_units), 0), grad_bias, 0.0), 3)
    _, bias_lane = unit_place(at_ref, iota((n_units, 128), 0))
    to_lane = jnp.concatenate([one_hot(iota((n_units, 128), 1) + b == bias_lane) for b in range(0, D, 128)], axis=1)
    gbias_ref[...] = sum(dot(piece, to_lane, NN) for piece in reversed(spread))
    send(0, dot(d_pre, normed_ref[...], TN).astype(BF))
    give_rows(1, sums_ref[1] + dot(d_pre, win_ref[...], NN))


def out(shape, dtype):
    return jax.ShapeDtypeStruct(shape, dtype)


def low(*shape):
    return pltpu.VMEM(shape, BF)


def attention(at, own, got, normed, cot, cos, sin):
    n = normed.shape[0]
    rows = 4 * own[0].shape[0]
    return pl.pallas_call(
        attention_kernel,
        out_shape=[out((2, n, D), F32), out((rows, D), BF), out((rows, D), BF)],
        in_specs=[SMEM] + [VM] * 12,
        out_specs=[VM] * 3,
        scratch_shapes=[low(2, rows, D), low(4 * HC, D), low(5 * HP, D), low(HP, D)]
        + [low(LEN, 2 * HP), low(LEN, 2 * HP), low(LEN, HP), low(LEN, HP)]
        + [low(n, HP), low(n, 3 * HP), low(4 * HC, D)],
        compiler_params=pltpu.CompilerParams(vmem_limit_bytes=32 << 20),
        cost_estimate=pl.CostEstimate(flops=12 * 10**9, bytes_accessed=16 << 20, transcendentals=10**6),
    )(at, *own, *got, normed, cot, cos, sin)


def feed_forward(at, held, normed, cot, bias, sums):
    n = normed.shape[0]
    span = held[0].shape[1]
    units = 4 * span
    return pl.pallas_call(
        forward_kernel,
        out_shape=[out((2, n // 2, D), F32), out((2, n // 2, D), F32), out((8, D), F32)] + [out((2, span, D), BF)] * 4,
        in_specs=[SMEM] + [VM] * 8,
        out_specs=[VM] * 7,
        scratch_shapes=[low(units, D), low(units, D)],
        compiler_params=pltpu.CompilerParams(vmem_limit_bytes=22 << 20),
        cost_estimate=pl.CostEstimate(flops=10 * 10**9, bytes_accessed=16 << 20, transcendentals=10**6),
    )(at, *held, normed, cot, bias, sums)


def body(tokens, cotangent, qkv_weight, out_weight, fc_weight, vectors, qkv_momentum, out_momentum, fc_momentum, vector_first, vector_second):
    zi, xi, yi, ci, ti = (lax.axis_index(a) for a in ALL)
    rows = tokens.shape[0]
    n_att = qkv_weight.shape[3]
    n_fc = fc_weight.shape[3]
    gain, shift = vectors[:D], vectors[D : 2 * D]
    bias_in, bias_out = vectors[2 * D : 2 * D + FF], vectors[2 * D + FF :]

    first = ci == 0
    attn_rows = jnp.concatenate([jnp.transpose(qkv_weight[:, :, 0, :], (0, 2, 1)), jnp.transpose(out_weight[:, 0, :])[None]])
    fc_rows = jnp.transpose(fc_weight[:, :, 0, :], (0, 2, 1))
    own_rows = jnp.concatenate([attn_rows.reshape(1, n_fc, D), fc_rows]).astype(BF)
    held = jnp.stack(gather_ring(own_rows, pull_yh, 2), axis=1)

    inputs = tokens.astype(F32)
    average = jnp.mean(inputs, axis=-1, keepdims=True)
    deviation = inputs - average
    variance = jnp.mean(deviation * deviation, axis=-1, keepdims=True)
    inv_spread = lax.rsqrt(variance + 1e-05)
    centred = deviation * inv_spread
    normed_own = (centred * gain + shift).astype(BF)
    both = jnp.stack([normed_own, cotangent])
    held = jnp.stack(gather_ring(held, pull_inner, 4), axis=1)
    both = jnp.stack([both, pull(both, "t", 1)], axis=1)
    held, both = lax.optimization_barrier((held, both))
    span = 8 * n_fc
    held = held.reshape(3, span, D)
    att_held = gather_ring(held[0], pull_outer, 4)
    fc_held = gather_ring(held[1:], pull_outer, 4)
    both = jnp.stack([both, pull(both, "c", 1)], axis=1)
    n_all = 4 * rows
    normed, cot = both[0].reshape(n_all, D), both[1].reshape(n_all, D)

    half = jnp.arange(LEN) // rows
    position = ((ti + half) % 2) * rows + jnp.arange(LEN) % rows
    frequency = 10000.0 ** (-2.0 * jnp.arange(ROT // 2, dtype=F32) / ROT)
    angles = position.astype(F32)[:, None] * frequency[None, :]
    cos_t, sin_t = jnp.cos(angles), jnp.sin(angles)
    pad = lambda a, b, fill: jnp.concatenate([a, b, jnp.full((LEN, PAD - ROT), fill, F32)], axis=1)
    cos_full, sin_full = pad(cos_t, cos_t, 1.0), pad(-sin_t, sin_t, 0.0)

    bias6 = bias_in.reshape(2, 4, 4, 2, 2, n_fc)
    bias6 = jnp.concatenate([bias6, bias6], axis=1)
    bias6 = jnp.concatenate([bias6, bias6], axis=2)
    bias6 = jnp.concatenate([bias6, bias6], axis=3)
    bias_own = lax.dynamic_slice(bias6, (ti, zi, xi, yi, ci, 0), (1, 4, 4, 2, 1, n_fc))[0, :, :, :, 0]
    by_turn = lambda v: jnp.where(first, jnp.swapaxes(v, 0, 1), v)
    bias_own = by_turn(bias_own).reshape(1, 32 * n_fc)
    at = jnp.stack([zi, xi, yi, ci, ti]).astype(jnp.int32)
    mom_rows = jnp.concatenate(
        [
            jnp.transpose(qkv_momentum[:, :, 0, :], (0, 2, 1)).reshape(3 * n_att, D),
            jnp.transpose(out_momentum[:, 0, :]),
            jnp.transpose(fc_momentum[:, :, 0, :], (0, 2, 1)).reshape(2 * n_fc, D),
        ]
    )
    att_held[2], normed, cot, bias_own, at, cos_full, sin_full, mom_rows = lax.optimization_barrier(
        (att_held[2], normed, cot, bias_own, at, cos_full, sin_full, mom_rows)
    )
    att_got = [pull(v, "c", 1) for v in att_held]
    sums, att_keep, att_give = attention(at, att_held, att_got, normed, cot, cos_full, sin_full)

    att_grad = (att_keep + pull(att_give, "c", 1)).reshape(4, span, D)
    att_parts = [att_grad[k] for k in range(4)]

    rows_own, rows_peer, grad_bias_in, *fc_parts = feed_forward(at, fc_held, normed, cot, bias_own, sums)
    att_total = sum_ring(att_parts, pull_outer)
    fc_total = sum_ring(fc_parts, pull_outer)
    rows_own = (rows_own + pull(rows_peer, "c", 1)).reshape(2, 2, rows, D)
    rows_own = rows_own[:, 0] + pull(rows_own[:, 1].astype(BF), "t", 1).astype(F32)
    att_total, fc_total, rows_own = lax.optimization_barrier((att_total, fc_total, rows_own))
    mixed = (inputs + rows_own[0] + bias_out).astype(BF)
    d_rows = rows_own[1]
    d_hat = d_rows * gain
    correction = d_hat - jnp.mean(d_hat, axis=-1, keepdims=True) - centred * jnp.mean(d_hat * centred, axis=-1, keepdims=True)
    own_cot = cotangent.astype(F32)
    input_grad = own_cot + correction * inv_spread

    total_of = lambda v: jnp.sum(v, axis=0, keepdims=True)
    vec_rows = [total_of(d_rows * centred), total_of(d_rows), grad_bias_in[: FF // D], total_of(own_cot), jnp.zeros((1, D), F32)]
    vec_sum = jnp.concatenate(vec_rows)
    beside = lambda value, flip, axis: value + (pull(value, axis, 1) if axis in ("c", "t", "yh") else lax.ppermute(value, axis, [(i, i ^ flip) for i in range(4)]))

    total = jnp.concatenate([att_total[None], fc_total]).reshape(3, 4, 2, n_fc, D)
    total = sum_ring([total[:, k] for k in range(4)], pull_inner)
    total, vec_sum = lax.optimization_barrier((total, beside(beside(vec_sum, 1, "c"), 1, "t")))
    total = sum_ring([total[:, k] for k in range(2)], pull_yh).reshape(3 * n_fc, D)
    moment = 0.95 * mom_rows + total
    update = total + 0.95 * moment

    half_fc = n_fc // 2
    att_u = update[: 4 * n_att].reshape(4, n_att, D)
    att_u = jnp.concatenate([att_u, jnp.zeros((4, half_fc - n_att, D), F32)], axis=1)
    fc_u = update[4 * n_att :].reshape(4, half_fc, D)
    chunks = jnp.concatenate([att_u, fc_u])
    got = lax.all_to_all(chunks, ("z", "t"), split_axis=0, concat_axis=0, tiled=True)
    mine = got.reshape(8 * half_fc, D)
    keep, *give = gram_parts(at, mine)
    along_x = lambda v, k: pull(v, "x", k)
    load = [keep[k * QUARTER : (k + 1) * QUARTER] + pull(give[k], "c", 1) for k in range(4)]
    part = load[0] + along_x(load[1], 3) + along_x(load[2], 2) + along_x(load[3], 1)
    part, vec_sum = lax.optimization_barrier((part, beside(beside(vec_sum, 1, "z"), 2, "z")))
    part = part + pull(part, "yh", 1)
    part, vec_sum = lax.optimization_barrier((part, beside(vec_sum, 1, "x")))
    part = jnp.where(zi >= 2, part + pull(part, "t", 1), part)
    part, vec_sum = lax.optimization_barrier((part, beside(vec_sum, 2, "x")))
    part = gather_ring(part, along_x, 4)
    part[2], vec_sum = lax.optimization_barrier((part[2], beside(vec_sum, 1, "yh")))
    rest = [pull(v, "c", 1) for v in part]
    x_rows = sweeps(at, part, rest, mine)
    x_rows, moment = lax.optimization_barrier((x_rows, moment))
    vector_grad = vec_sum[: VEC // D].reshape(VEC)
    first_new = 0.9 * vector_first + 0.1 * vector_grad
    second_new = 0.95 * vector_second + 0.05 * vector_grad * vector_grad
    step_size = first_new / (1.0 - 0.9**STEP) / (jnp.sqrt(second_new / (1.0 - 0.95**STEP)) + 1e-08)
    vector_new = vectors - 0.2 * step_size

    back = lax.all_to_all(x_rows, ("z", "t"), split_axis=0, concat_axis=0, tiled=True).astype(F32)
    att_x = back[:4, :n_att]
    fc_x = back[4:].reshape(2, n_fc, D)

    def cols(v):
        return jnp.transpose(v, (0, 2, 1))[:, :, None, :]

    fc_factor = math.sqrt(FF / D)
    qkv_new = qkv_weight * 0.99 - cols(att_x[:3])
    out_new = out_weight * 0.99 - cols(att_x[3:])[0]
    fc_new = fc_weight * 0.99 - fc_factor * cols(fc_x)
    att_m = moment[: 4 * n_att].reshape(4, n_att, D)
    fc_m = moment[4 * n_att :].reshape(2, n_fc, D)
    return (mixed, input_grad, qkv_new, out_new, fc_new, cols(att_m[:3]), cols(att_m[3:])[0], cols(fc_m), first_new, second_new, vector_new)


def solution(mesh):
    mesh = Mesh(mesh.devices.reshape(4, 4, 2, 2, 2), ALL)
    rows = P(ALL, None)
    w3 = P(None, None, "t", DP)
    w2 = P(None, "t", DP)
    vec = P()
    in_specs = (rows, rows, w3, w2, w3, vec, w3, w2, w3, vec, vec)
    out_specs = (rows, rows, w3, w2, w3, w3, w2, w3, vec, vec, vec)
    return jax.shard_map(body, mesh=mesh, in_specs=in_specs, out_specs=out_specs, check_vma=False)
```

```python
import functools
import itertools
import math

import jax
import jax.numpy as jnp
from jax import lax
from jax.experimental import pallas as pl
from jax.experimental.pallas import tpu as pltpu
from jax.sharding import Mesh, PartitionSpec as P

D = 768
H = 12
HD = 64
ROT = 16
FF = 3072
SWEEPS = 5
STEP = 10
LEN = 256
VEC = 2 * D + FF + D

NS = (3.4445, -4.775, 2.0315)
BF = jnp.bfloat16
F32 = jnp.float32
BLK = 256
QUARTER = 64
NB = D // BLK

DP = ("z", "x", "yh", "c")
ALL = ("z", "x", "yh", "c", "t")


def pull(value, axis, k):
    n = lax.axis_size(axis)
    return lax.ppermute(value, axis, [((i + k) % n, i) for i in range(n)])


def move(value, source):
    sizes = [lax.axis_size(a) for a in ALL]
    index = lambda at: functools.reduce(lambda total, one: total * one[0] + one[1] % one[0], zip(sizes, at), 0)
    pairs = []
    for here in itertools.product(*map(range, sizes)):
        there = source(*here)
        if there is not None:
            pairs.append((index(there), index(here)))
    return lax.ppermute(value, ALL, pairs)


def pull_outer(value, k):
    return move(value, lambda z, x, y, c, t: (z, x + k, y, c, t) if c == 0 else (z + k, x, y, c, t))


def pull_inner(value, k):
    return move(value, lambda z, x, y, c, t: (z + k, x, y, c, t) if c == 0 else (z, x + k, y, c, t))


def pull_yh(value, k):
    return pull(value, "yh", k)


def gather_ring(value, pulls, n):
    return [value] + [pulls(value, k) for k in range(1, n)]


def sum_ring(parts, pulls):
    n = len(parts)
    total = parts[0].astype(F32)
    for k in range(1, n):
        total = total + pulls(parts[k].astype(BF), n - k).astype(F32)
    return total


def dot(a, b, dims):
    return lax.dot_general(a, b, (dims, ((), ())), preferred_element_type=F32)


def pieces(value, n):
    out = []
    for _ in range(n):
        low = value.astype(BF)
        out.append(low)
        value = value - low.astype(F32)
    return out


def mul(xs, ys, dims=((1,), (0,))):
    n = len(xs)
    total = None
    for order in reversed(range(n)):
        for i in range(order + 1):
            term = lax.dot_general(xs[i], ys[order - i], (dims, ((), ())), preferred_element_type=F32)
            total = term if total is None else total + term
    return total


def gram_kernel(at_ref, rows_ref, keep_ref, give0_ref, give1_ref, give2_ref, give3_ref, top_ref, bottom_ref):
    xs = pieces(rows_ref[...], 3)
    dims = ((0,), (0,))
    cut = lambda i: slice(i * BLK, (i + 1) * BLK)
    top_ref[...] = mul([x[:, cut(0)] for x in xs], xs, dims)
    bottom_ref[:, : 2 * BLK] = mul([x[:, cut(1)] for x in xs], [x[:, BLK:] for x in xs], dims)
    bottom_ref[:, 2 * BLK :] = mul([x[:, cut(2)] for x in xs], [x[:, 2 * BLK :] for x in xs], dims)

    def keep(in_ref):
        for k in range(4):
            place = pl.multiple_of(jnp.bitwise_and(at_ref[1] + k, 3) * QUARTER, QUARTER)
            keep_ref[k * QUARTER : (k + 1) * QUARTER] = in_ref[pl.ds(place, QUARTER)]

    def give(in_ref):
        for k, ref in enumerate((give0_ref, give1_ref, give2_ref, give3_ref)):
            place = pl.multiple_of(jnp.bitwise_and(at_ref[1] + k, 3) * QUARTER, QUARTER)
            ref[...] = in_ref[pl.ds(place, QUARTER)]

    first = at_ref[3] == 0

    @pl.when(first)
    def _():
        keep(top_ref)
        give(bottom_ref)

    @pl.when(jnp.logical_not(first))
    def _():
        keep(bottom_ref)
        give(top_ref)


def blocks(i, j):
    return (slice(i * BLK, (i + 1) * BLK), slice(j * BLK, (j + 1) * BLK))


def put(refs, i, j, value):
    for ref, piece in zip(refs, pieces(value, len(refs))):
        ref[blocks(i, j)] = piece


def put_both(refs, i, j, value):
    put(refs, i, j, value)
    if i != j:
        put(refs, j, i, value.T)


def symmetric_product(xs, ys, emit, start=0):
    for i in range(start, NB):
        rows = slice(i * BLK, (i + 1) * BLK)
        wide = mul([x[rows, :] for x in xs], [y[:, i * BLK :] for y in ys])
        for j in range(i, NB):
            emit(i, j, wide[:, (j - i) * BLK : (j - i + 1) * BLK])


def sweeps_kernel(at_ref, *refs):
    sweeps_math(at_ref, refs[:4], refs[4:8], *refs[8:])


def sweeps_math(at_ref, mine_refs, rest_refs, x_ref, out_ref, top_ref, bottom_ref, gram_ref, a_ref, p_ref, b_ref):
    first = at_ref[3] == 0
    n_x = x_ref.shape[0]

    def by_place(out_ref, in_refs):
        for k, ref in enumerate(in_refs):
            place = pl.multiple_of(jnp.bitwise_and(at_ref[1] + k, 3) * QUARTER, QUARTER)
            out_ref[pl.ds(place, QUARTER)] = ref[...]

    @pl.when(first)
    def _():
        by_place(top_ref, mine_refs)
        by_place(bottom_ref, rest_refs)

    @pl.when(jnp.logical_not(first))
    def _():
        by_place(top_ref, rest_refs)
        by_place(bottom_ref, mine_refs)

    def packed(i, j):
        if i == 0:
            return top_ref[:, j * BLK : (j + 1) * BLK]
        at = (j - 1) if i == 1 else 2
        return bottom_ref[:, at * BLK : (at + 1) * BLK]

    eye = (lax.broadcasted_iota(jnp.int32, (BLK, BLK), 0) == lax.broadcasted_iota(jnp.int32, (BLK, BLK), 1)).astype(F32)
    trace = sum(jnp.sum(packed(i, i) * eye) for i in range(NB))
    norm = jnp.sqrt(jnp.full((8, 128), trace, F32)) + 1e-07
    factor = (1.0 / norm)[0:1, 0:1]
    square = factor * factor

    a_rows = lambda n: [a_ref.at[k, n_x : n_x + D] for k in range(n)]
    p_rows = lambda n: [p_ref.at[k] for k in range(n)]
    b_rows = lambda n: [b_ref.at[k] for k in range(n)]

    def put_x(n, value):
        for k, piece in enumerate(pieces(value, n)):
            a_ref[k, :n_x] = piece

    for i in range(NB):
        for j in range(i, NB):
            value = packed(i, j) * square
            gram_ref[blocks(i, j)] = value
            put_both(a_rows(2), i, j, value)
    put_x(2, x_ref[...] * factor)

    def poly(n_p):
        def emit(i, j, block):
            value = NS[1] * gram_ref[blocks(i, j)] + NS[2] * block
            if i == j:
                value = value + NS[0] * eye
            put_both(p_rows(n_p), i, j, value)

        a = a_rows(2)
        symmetric_product(a, a, emit)

    def next_gram(n, keep):
        p = p_rows(n)
        rows = slice(0, n_x + BLK)
        wide = mul([a_ref[k, rows] for k in range(n)], [y[...] for y in p])
        for j in range(NB):
            put_both(b_rows(n), 0, j, wide[n_x:, j * BLK : (j + 1) * BLK])
        symmetric_product(a_rows(n), p, lambda i, j, block: put_both(b_rows(n), i, j, block), 1)
        put_x(keep, wide[:n_x])

        def emit(i, j, block):
            gram_ref[blocks(i, j)] = block
            put_both(a_rows(keep), i, j, block)

        symmetric_product(b_rows(n), p, emit)

    @pl.loop(0, SWEEPS - 1)
    def _(_):
        poly(2)
        next_gram(2, 2)

    poly(2)
    last = mul([a_ref[k, :n_x] for k in range(2)], [y[...] for y in p_rows(2)]).astype(BF)
    n = out_ref.shape[1]
    for k in range(out_ref.shape[0]):
        out_ref[k] = last[k * n : (k + 1) * n]


SMEM = pl.BlockSpec(memory_space=pltpu.SMEM)
VM = pl.BlockSpec(memory_space=pltpu.VMEM)


def gram_parts(at, rows):
    return pl.pallas_call(
        gram_kernel,
        out_shape=[jax.ShapeDtypeStruct((BLK, D), F32)] + [jax.ShapeDtypeStruct((QUARTER, D), F32)] * 4,
        in_specs=[SMEM, VM],
        out_specs=[VM] * 5,
        scratch_shapes=[pltpu.VMEM((BLK, D), F32)] * 2,
        compiler_params=pltpu.CompilerParams(vmem_limit_bytes=14 << 20),
        cost_estimate=pl.CostEstimate(flops=2 * 96 * D * D * 4, bytes_accessed=4 * D * D * 2, transcendentals=0),
    )(at, rows)


def sweeps(at, mine, rest, x_rows):
    return pl.pallas_call(
        sweeps_kernel,
        out_shape=jax.ShapeDtypeStruct((8, x_rows.shape[0] // 8, D), BF),
        in_specs=[SMEM] + [VM] * 9,
        out_specs=VM,
        scratch_shapes=[
            pltpu.VMEM((BLK, D), F32),
            pltpu.VMEM((BLK, D), F32),
            pltpu.VMEM((D, D), F32),
            pltpu.VMEM((3, x_rows.shape[0] + D, D), BF),
            pltpu.VMEM((3, D, D), BF),
            pltpu.VMEM((3, D, D), BF),
        ],
        compiler_params=pltpu.CompilerParams(vmem_limit_bytes=24 << 20),
        cost_estimate=pl.CostEstimate(flops=2 * D * D * D * 32, bytes_accessed=4 * D * D, transcendentals=0),
    )(at, *mine, *rest, x_rows)


def gelu_parts(u):
    k0 = math.sqrt(2.0 / math.pi)
    th = jnp.tanh(k0 * (u + 0.044715 * (u * u * u)))
    value = 0.5 * u * (1.0 + th)
    slope = 0.5 * (1.0 + th) + 0.5 * u * (1.0 - th * th) * (k0 * (1.0 + 3.0 * 0.044715 * u * u))
    return value, slope


HEADS = 3
PAD = 128
HC = HEADS * HD
HP = HEADS * PAD
NN = ((1,), (0,))
NT = ((1,), (1,))
TN = ((0,), (0,))


def iota(shape, dim):
    return lax.broadcasted_iota(jnp.int32, shape, dim)


def one_hot(cond):
    return jnp.where(cond, 1.0, 0.0).astype(BF)


def unit_place(at_ref, n):
    zi, xi, yi, ci, ti = (at_ref[k] for k in range(5))
    width = 24
    group = jnp.right_shift(n * 2731, 16)
    lane = n - width * group
    y = jnp.bitwise_and(group + yi, 1)
    inner = jnp.bitwise_and(jnp.right_shift(group, 1), 3)
    outer = jnp.bitwise_and(jnp.right_shift(group, 3), 3)
    z = jnp.bitwise_and(jnp.where(ci == 0, inner, outer) + zi, 3)
    x = jnp.bitwise_and(jnp.where(ci == 0, outer, inner) + xi, 3)
    row = 2 * ti + jnp.right_shift(z, 1)
    return row, (((jnp.bitwise_and(z, 1) * 4 + x) * 2 + y) * 2 + ci) * width + lane


def needed_blocks(at_ref):
    zi, ci = at_ref[0], at_ref[3]
    for rc in range(2):
        core_0 = jnp.bitwise_xor(ci, rc) == 0
        for x in range(4):
            for j in range(2):
                z = jnp.bitwise_and(2 * ci + j - zi, 3)
                outer, inner = jnp.where(core_0, x, z), jnp.where(core_0, z, x)
                yield rc, pl.multiple_of((outer * 4 + inner) * 48, 48)


def home_place(at_ref, r):
    xi, yi, ci = (at_ref[k] for k in range(1, 4))
    n = 6
    group = jnp.right_shift(r * 10923, 16)
    lane = r - n * group
    mat = jnp.bitwise_and(group, 3)
    y = jnp.bitwise_and(jnp.right_shift(group, 2) + yi, 1)
    j = jnp.bitwise_and(jnp.right_shift(group, 3), 1)
    x = jnp.bitwise_and(jnp.right_shift(group, 4) + xi, 3)
    core = jnp.bitwise_and(jnp.right_shift(group, 6) + ci, 1)
    return mat * HC + (((j * 4 + x) * 2 + y) * 2 + core) * n + lane


def attention_kernel(
    at_ref, own0_ref, own1_ref, own2_ref, own3_ref, got0_ref, got1_ref, got2_ref, got3_ref, normed_ref, cot_ref, cos_ref, sin_ref,
    sums_ref, keep_ref, give_ref,
    att_ref, near_ref, w_ref, wo_ref, q_ref, k_ref, v_ref, da_ref, heads_ref, d_ref, nat_ref,
):
    span = own0_ref.shape[0]
    for k, ref in enumerate((own0_ref, own1_ref, own2_ref, own3_ref, got0_ref, got1_ref, got2_ref, got3_ref)):
        att_ref[k // 4, k % 4 * span : (k % 4 + 1) * span] = ref[...]
    block = span // 4
    for k, (rc, at) in enumerate(needed_blocks(at_ref)):
        near_ref[k * block : (k + 1) * block] = att_ref[rc, pl.ds(at, block)]

    n_rows = 4 * HC
    pick = one_hot(iota((n_rows, n_rows), 0) == home_place(at_ref, iota((8, n_rows), 1))[:1])
    w_att = dot(pick, near_ref[...], NN).astype(BF)
    r = iota((HC, HC), 0)
    e = jnp.bitwise_and(r, HD - 1)
    half = ROT // 2
    source = jnp.where(e < half, r + half, jnp.where(e < ROT, r - half, -1))
    exchange = one_hot(iota((HC, HC), 1) == source)
    blank = jnp.zeros((HD, D), BF)

    def padded(ref, base, rows):
        for h in range(HEADS):
            at = base + h * PAD
            ref[at : at + HD] = rows[h * HD : (h + 1) * HD]
            ref[at + HD : at + PAD] = blank

    for m in range(3):
        padded(w_ref, m * HP, w_att[m * HC : (m + 1) * HC])
    for m in range(2):
        padded(w_ref, (3 + m) * HP, dot(exchange, w_att[m * HC : (m + 1) * HC], NN).astype(BF))
    padded(wo_ref, 0, w_att[3 * HC :])

    cos, sin = cos_ref[...], sin_ref[...]
    turn = at_ref[4] * (LEN // 2)
    at_q = jnp.bitwise_xor(iota((LEN, LEN), 0), turn)
    at_k = jnp.bitwise_xor(iota((LEN, LEN), 1), turn)
    causal = at_q >= at_k
    scale = HD ** (-0.5)

    @pl.loop(0, 2)
    def _(s):
        rows = pl.ds(pl.multiple_of(s * LEN, LEN), LEN)
        normed = normed_ref[rows]
        for m, ref in ((0, q_ref), (1, k_ref)):
            lin = dot(normed, w_ref[m * HP : (m + 1) * HP], NT)
            lin_2 = dot(normed, w_ref[(3 + m) * HP : (4 + m) * HP], NT)
            for h in range(HEADS):
                lanes = slice(h * PAD, (h + 1) * PAD)
                base = h * 2 * PAD
                own, other = lin[:, lanes], lin_2[:, lanes]
                ref[:, base : base + PAD] = (own * cos + other * sin).astype(BF)
                ref[:, base + PAD : base + 2 * PAD] = (other * cos - own * sin).astype(BF)
        v_ref[...] = dot(normed, w_ref[2 * HP : 3 * HP], NT).astype(BF)
        da_ref[...] = dot(cot_ref[rows], wo_ref[...], NT).astype(BF)
        for h in range(HEADS):
            two = slice(h * 2 * PAD, (h + 1) * 2 * PAD)
            one = slice(h * 2 * PAD, h * 2 * PAD + PAD)
            lanes = slice(h * PAD, (h + 1) * PAD)
            value, d_att = v_ref[:, lanes], da_ref[:, lanes]
            scores = jnp.where(causal, dot(q_ref[:, one], k_ref[:, one], NT) * scale, -1e30)
            raised = jnp.exp(scores - jnp.max(scores, axis=1, keepdims=True))
            probs = raised / jnp.sum(raised, axis=1, keepdims=True)
            low = probs.astype(BF)
            heads_ref[rows, lanes] = dot(low, value, NN).astype(BF)
            d_ref[rows, 2 * HP + h * PAD : 2 * HP + (h + 1) * PAD] = dot(low, d_att, TN).astype(BF)
            d_probs = dot(d_att, value, NT)
            d_scores = (probs * (d_probs - jnp.sum(probs * d_probs, axis=1, keepdims=True))).astype(BF)
            d_q = dot(d_scores, k_ref[:, two], NN) * scale
            d_k = dot(d_scores, q_ref[:, two], TN) * scale
            for m, pair in ((0, d_q), (1, d_k)):
                at = m * HP + h * PAD
                d_ref[rows, at : at + PAD] = (pair[:, :PAD] * cos - pair[:, PAD:] * sin).astype(BF)

    sums_ref[0] = dot(heads_ref[...], wo_ref[...], NN)
    sums_ref[1] = dot(d_ref[...], w_ref[: 3 * HP], NN)

    for m in range(4):
        if m < 3:
            grad = dot(d_ref[:, m * HP : (m + 1) * HP], normed_ref[...], TN).astype(BF)
        else:
            grad = dot(heads_ref[...], cot_ref[...], TN).astype(BF)
        for h in range(HEADS):
            nat_ref[m * HC + h * HD : m * HC + (h + 1) * HD] = grad[h * PAD : h * PAD + HD]
    place = home_place(at_ref, iota((n_rows, 128), 0))
    pick = jnp.concatenate([one_hot(iota((n_rows, 128), 1) + b == place) for b in range(0, n_rows, 128)], axis=1)
    near_ref[...] = dot(pick, nat_ref[...], NN).astype(BF)
    keep_ref[...] = jnp.zeros_like(keep_ref)
    give_ref[...] = jnp.zeros_like(give_ref)
    for k, (rc, at) in enumerate(needed_blocks(at_ref)):
        (keep_ref, give_ref)[rc][pl.ds(at, block)] = near_ref[k * block : (k + 1) * block]


def forward_kernel(
    at_ref, held0_ref, held1_ref, held2_ref, held3_ref, normed_ref, cot_ref, bias_ref, sums_ref,
    own_ref, peer_ref, gbias_ref, out0_ref, out1_ref, out2_ref, out3_ref,
    win_ref, wback_ref,
):
    span = held0_ref.shape[1]
    for s, ref in enumerate((held0_ref, held1_ref, held2_ref, held3_ref)):
        win_ref[s * span : (s + 1) * span] = ref[0]
        wback_ref[s * span : (s + 1) * span] = ref[1]

    def send(group, grad):
        for s, ref in enumerate((out0_ref, out1_ref, out2_ref, out3_ref)):
            ref[group] = grad[s * span : (s + 1) * span]

    hidden, slope = gelu_parts(dot(normed_ref[...], win_ref[...], NT) + bias_ref[...])
    hidden = hidden.astype(BF)


    def give_rows(k, value):
        own_ref[k] = value[:LEN]
        peer_ref[k] = value[LEN:]

    give_rows(0, sums_ref[0] + dot(hidden, wback_ref[...], NN))
    send(1, dot(hidden, cot_ref[...], TN).astype(BF))
    d_pre = (dot(cot_ref[...], wback_ref[...], NT) * slope).astype(BF)
    grad_bias = jnp.sum(d_pre.astype(F32), axis=0, keepdims=True)
    n_units = win_ref.shape[0]
    bias_row, _ = unit_place(at_ref, iota((8, n_units), 1))
    spread = pieces(jnp.where(bias_row == iota((8, n_units), 0), grad_bias, 0.0), 3)
    _, bias_lane = unit_place(at_ref, iota((n_units, 128), 0))
    to_lane = jnp.concatenate([one_hot(iota((n_units, 128), 1) + b == bias_lane) for b in range(0, D, 128)], axis=1)
    gbias_ref[...] = sum(dot(piece, to_lane, NN) for piece in reversed(spread))
    send(0, dot(d_pre, normed_ref[...], TN).astype(BF))
    give_rows(1, sums_ref[1] + dot(d_pre, win_ref[...], NN))


def out(shape, dtype):
    return jax.ShapeDtypeStruct(shape, dtype)


def low(*shape):
    return pltpu.VMEM(shape, BF)


def attention(at, own, got, normed, cot, cos, sin):
    n = normed.shape[0]
    rows = 4 * own[0].shape[0]
    return pl.pallas_call(
        attention_kernel,
        out_shape=[out((2, n, D), F32), out((rows, D), BF), out((rows, D), BF)],
        in_specs=[SMEM] + [VM] * 12,
        out_specs=[VM] * 3,
        scratch_shapes=[low(2, rows, D), low(4 * HC, D), low(5 * HP, D), low(HP, D)]
        + [low(LEN, 2 * HP), low(LEN, 2 * HP), low(LEN, HP), low(LEN, HP)]
        + [low(n, HP), low(n, 3 * HP), low(4 * HC, D)],
        compiler_params=pltpu.CompilerParams(vmem_limit_bytes=32 << 20),
        cost_estimate=pl.CostEstimate(flops=12 * 10**9, bytes_accessed=16 << 20, transcendentals=10**6),
    )(at, *own, *got, normed, cot, cos, sin)


def feed_forward(at, held, normed, cot, bias, sums):
    n = normed.shape[0]
    span = held[0].shape[1]
    units = 4 * span
    return pl.pallas_call(
        forward_kernel,
        out_shape=[out((2, n // 2, D), F32), out((2, n // 2, D), F32), out((8, D), F32)] + [out((2, span, D), BF)] * 4,
        in_specs=[SMEM] + [VM] * 8,
        out_specs=[VM] * 7,
        scratch_shapes=[low(units, D), low(units, D)],
        compiler_params=pltpu.CompilerParams(vmem_limit_bytes=22 << 20),
        cost_estimate=pl.CostEstimate(flops=10 * 10**9, bytes_accessed=16 << 20, transcendentals=10**6),
    )(at, *held, normed, cot, bias, sums)


def body(tokens, cotangent, qkv_weight, out_weight, fc_weight, vectors, qkv_momentum, out_momentum, fc_momentum, vector_first, vector_second):
    zi, xi, yi, ci, ti = (lax.axis_index(a) for a in ALL)
    rows = tokens.shape[0]
    n_att = qkv_weight.shape[3]
    n_fc = fc_weight.shape[3]
    gain, shift = vectors[:D], vectors[D : 2 * D]
    bias_in, bias_out = vectors[2 * D : 2 * D + FF], vectors[2 * D + FF :]

    first = ci == 0
    attn_rows = jnp.concatenate([jnp.transpose(qkv_weight[:, :, 0, :], (0, 2, 1)), jnp.transpose(out_weight[:, 0, :])[None]])
    fc_rows = jnp.transpose(fc_weight[:, :, 0, :], (0, 2, 1))
    own_rows = jnp.concatenate([attn_rows.reshape(1, n_fc, D), fc_rows]).astype(BF)
    held = jnp.stack(gather_ring(own_rows, pull_yh, 2), axis=1)

    inputs = tokens.astype(F32)
    average = jnp.mean(inputs, axis=-1, keepdims=True)
    deviation = inputs - average
    variance = jnp.mean(deviation * deviation, axis=-1, keepdims=True)
    inv_spread = lax.rsqrt(variance + 1e-05)
    centred = deviation * inv_spread
    normed_own = (centred * gain + shift).astype(BF)
    both = jnp.stack([normed_own, cotangent])
    held = jnp.stack(gather_ring(held, pull_inner, 4), axis=1)
    both = jnp.stack([both, pull(both, "t", 1)], axis=1)
    held, both = lax.optimization_barrier((held, both))
    span = 8 * n_fc
    held = held.reshape(3, span, D)
    att_held = gather_ring(held[0], pull_outer, 4)
    fc_held = gather_ring(held[1:], pull_outer, 4)
    both = jnp.stack([both, pull(both, "c", 1)], axis=1)
    n_all = 4 * rows
    normed, cot = both[0].reshape(n_all, D), both[1].reshape(n_all, D)

    half = jnp.arange(LEN) // rows
    position = ((ti + half) % 2) * rows + jnp.arange(LEN) % rows
    frequency = 10000.0 ** (-2.0 * jnp.arange(ROT // 2, dtype=F32) / ROT)
    angles = position.astype(F32)[:, None] * frequency[None, :]
    cos_t, sin_t = jnp.cos(angles), jnp.sin(angles)
    pad = lambda a, b, fill: jnp.concatenate([a, b, jnp.full((LEN, PAD - ROT), fill, F32)], axis=1)
    cos_full, sin_full = pad(cos_t, cos_t, 1.0), pad(-sin_t, sin_t, 0.0)

    bias6 = bias_in.reshape(2, 4, 4, 2, 2, n_fc)
    bias6 = jnp.concatenate([bias6, bias6], axis=1)
    bias6 = jnp.concatenate([bias6, bias6], axis=2)
    bias6 = jnp.concatenate([bias6, bias6], axis=3)
    bias_own = lax.dynamic_slice(bias6, (ti, zi, xi, yi, ci, 0), (1, 4, 4, 2, 1, n_fc))[0, :, :, :, 0]
    by_turn = lambda v: jnp.where(first, jnp.swapaxes(v, 0, 1), v)
    bias_own = by_turn(bias_own).reshape(1, 32 * n_fc)
    at = jnp.stack([zi, xi, yi, ci, ti]).astype(jnp.int32)
    mom_rows = jnp.concatenate(
        [
            jnp.transpose(qkv_momentum[:, :, 0, :], (0, 2, 1)).reshape(3 * n_att, D),
            jnp.transpose(out_momentum[:, 0, :]),
            jnp.transpose(fc_momentum[:, :, 0, :], (0, 2, 1)).reshape(2 * n_fc, D),
        ]
    )
    att_held[2], normed, cot, bias_own, at, cos_full, sin_full, mom_rows = lax.optimization_barrier(
        (att_held[2], normed, cot, bias_own, at, cos_full, sin_full, mom_rows)
    )
    att_got = [pull(v, "c", 1) for v in att_held]
    sums, att_keep, att_give = attention(at, att_held, att_got, normed, cot, cos_full, sin_full)

    att_grad = (att_keep + pull(att_give, "c", 1)).reshape(4, span, D)
    att_parts = [att_grad[k] for k in range(4)]

    rows_own, rows_peer, grad_bias_in, *fc_parts = feed_forward(at, fc_held, normed, cot, bias_own, sums)
    att_total = sum_ring(att_parts, pull_outer)
    fc_total = sum_ring(fc_parts, pull_outer)
    rows_own = (rows_own + pull(rows_peer, "c", 1)).reshape(2, 2, rows, D)
    rows_own = rows_own[:, 0] + pull(rows_own[:, 1].astype(BF), "t", 1).astype(F32)
    att_total, fc_total, rows_own = lax.optimization_barrier((att_total, fc_total, rows_own))
    mixed = (inputs + rows_own[0] + bias_out).astype(BF)
    d_rows = rows_own[1]
    d_hat = d_rows * gain
    correction = d_hat - jnp.mean(d_hat, axis=-1, keepdims=True) - centred * jnp.mean(d_hat * centred, axis=-1, keepdims=True)
    own_cot = cotangent.astype(F32)
    input_grad = own_cot + correction * inv_spread

    total_of = lambda v: jnp.sum(v, axis=0, keepdims=True)
    vec_rows = [total_of(d_rows * centred), total_of(d_rows), grad_bias_in[: FF // D], total_of(own_cot), jnp.zeros((1, D), F32)]
    vec_sum = jnp.concatenate(vec_rows)
    beside = lambda value, flip, axis: value + (pull(value, axis, 1) if axis in ("c", "t", "yh") else lax.ppermute(value, axis, [(i, i ^ flip) for i in range(4)]))

    total = jnp.concatenate([att_total[None], fc_total]).reshape(3, 4, 2, n_fc, D)
    total = sum_ring([total[:, k] for k in range(4)], pull_inner)
    total, vec_sum = lax.optimization_barrier((total, beside(vec_sum, 1, "t")))
    total = sum_ring([total[:, k] for k in range(2)], pull_yh).reshape(3 * n_fc, D)
    moment = 0.95 * mom_rows + total
    update = total + 0.95 * moment

    half_fc = n_fc // 2
    att_u = update[: 4 * n_att].reshape(4, n_att, D)
    att_u = jnp.concatenate([att_u, jnp.zeros((4, half_fc - n_att, D), F32)], axis=1)
    fc_u = update[4 * n_att :].reshape(4, half_fc, D)
    chunks = jnp.concatenate([att_u, fc_u])
    got = lax.all_to_all(chunks, ("z", "t"), split_axis=0, concat_axis=0, tiled=True)
    mine = got.reshape(8 * half_fc, D)
    keep, *give = gram_parts(at, mine)
    along_x = lambda v, k: pull(v, "x", k)
    load = [keep[k * QUARTER : (k + 1) * QUARTER] + pull(give[k], "c", 1) for k in range(4)]
    part = load[0] + along_x(load[1], 3) + along_x(load[2], 2) + along_x(load[3], 1)
    part, vec_sum = lax.optimization_barrier((part, beside(beside(beside(vec_sum, 1, "c"), 1, "z"), 2, "z")))
    part = part + pull(part, "yh", 1)
    part, vec_sum = lax.optimization_barrier((part, beside(vec_sum, 1, "x")))
    part = jnp.where(zi >= 2, part + pull(part, "t", 1), part)
    part, vec_sum = lax.optimization_barrier((part, beside(vec_sum, 2, "x")))
    part = gather_ring(part, along_x, 4)
    part[2], vec_sum = lax.optimization_barrier((part[2], beside(vec_sum, 1, "yh")))
    rest = [pull(v, "c", 1) for v in part]
    x_rows = sweeps(at, part, rest, mine)
    x_rows, moment = lax.optimization_barrier((x_rows, moment))
    vector_grad = vec_sum[: VEC // D].reshape(VEC)
    first_new = 0.9 * vector_first + 0.1 * vector_grad
    second_new = 0.95 * vector_second + 0.05 * vector_grad * vector_grad
    step_size = first_new / (1.0 - 0.9**STEP) / (jnp.sqrt(second_new / (1.0 - 0.95**STEP)) + 1e-08)
    vector_new = vectors - 0.2 * step_size

    back = lax.all_to_all(x_rows, ("z", "t"), split_axis=0, concat_axis=0, tiled=True).astype(F32)
    att_x = back[:4, :n_att]
    fc_x = back[4:].reshape(2, n_fc, D)

    def cols(v):
        return jnp.transpose(v, (0, 2, 1))[:, :, None, :]

    fc_factor = math.sqrt(FF / D)
    qkv_new = qkv_weight * 0.99 - cols(att_x[:3])
    out_new = out_weight * 0.99 - cols(att_x[3:])[0]
    fc_new = fc_weight * 0.99 - fc_factor * cols(fc_x)
    att_m = moment[: 4 * n_att].reshape(4, n_att, D)
    fc_m = moment[4 * n_att :].reshape(2, n_fc, D)
    return (mixed, input_grad, qkv_new, out_new, fc_new, cols(att_m[:3]), cols(att_m[3:])[0], cols(fc_m), first_new, second_new, vector_new)


def solution(mesh):
    mesh = Mesh(mesh.devices.reshape(4, 4, 2, 2, 2), ALL)
    rows = P(ALL, None)
    w3 = P(None, None, "t", DP)
    w2 = P(None, "t", DP)
    vec = P()
    in_specs = (rows, rows, w3, w2, w3, vec, w3, w2, w3, vec, vec)
    out_specs = (rows, rows, w3, w2, w3, w3, w2, w3, vec, vec, vec)
    return jax.shard_map(body, mesh=mesh, in_specs=in_specs, out_specs=out_specs, check_vma=False)
```
